32 devices in a mesh: grp: 2 (over core), dp: 16 (over z, y, x).
Axes of the slice: x: 2, y: 2, z: 4, core: 2. Of those that a mesh axis runs over, the one named last changes fastest.
Arguments:
- question_ids: int32 [512, 64], P(('grp', 'dp')), may hold values from 0 to 30719
- passage_ids: int32 [1024, 256], P(('grp', 'dp')), may hold values from 0 to 30719
- question_lengths: int32 [512], P(('grp', 'dp')), may hold values from 16 to 64
- passage_lengths: int32 [1024], P(('grp', 'dp')), may hold values from 64 to 256
- question_keys: int32 [512], P(('grp', 'dp')), may hold values from 0 to 15
- passage_keys: int32 [1024], P(('grp', 'dp')), may hold values from 0 to 15
- question_valid: int32 [512], P(('grp', 'dp')), may hold values 0 or 1
- word_table: float32 [2, 30720, 128], P('grp', 'dp'), may hold values from -0.3125 to 0.3125
- positions: float32 [2, 2, 256, 128], P('grp'), may hold values from -0.3125 to 0.3125
- attention: float32 [2, 2, 128, 512], P('grp'), may hold values from -0.5 to 0.5
- feedforward: float32 [2, 2, 2, 128, 512], P('grp'), may hold values from -0.5 to 0.5
- vectors: float32 [2, 2, 14, 128], P('grp'), as said below
- word_first: float32 [2, 30720, 128], P('grp', 'dp'), may hold values from -8.940697e-08 to 8.940697e-08
- positions_first: float32 [2, 2, 256, 128], P('grp'), may hold values from -3.33786e-06 to 3.33786e-06
- attention_first: float32 [2, 2, 128, 512], P('grp'), may hold values from -3.33786e-06 to 3.33786e-06
- feedforward_first: float32 [2, 2, 2, 128, 512], P('grp'), may hold values from -3.33786e-06 to 3.33786e-06
- vectors_first: float32 [2, 2, 14, 128], P('grp'), may hold values from -1.335144e-05 to 1.335144e-05
- word_second: float32 [2, 30720, 128], P('grp', 'dp'), may hold values from 1.0240082e-15 to 1.6384131e-14
- positions_second: float32 [2, 2, 256, 128], P('grp'), may hold values from 1.1377869e-14 to 1.820459e-13
- attention_second: float32 [2, 2, 128, 512], P('grp'), may hold values from 1.1377869e-14 to 1.820459e-13
- feedforward_second: float32 [2, 2, 2, 128, 512], P('grp'), may hold values from 1.1377869e-14 to 1.820459e-13
- vectors_second: float32 [2, 2, 14, 128], P('grp'), may hold values from 1.820459e-13 to 2.9127345e-12
- word_anchor: float32 [30720, 128], P('dp'), may hold values from -0.3125 to 0.3125
- positions_anchor: float32 [2, 256, 128], replicated, may hold values from -0.3125 to 0.3125
- attention_anchor: float32 [2, 128, 512], replicated, may hold values from -0.5 to 0.5
- feedforward_anchor: float32 [2, 2, 128, 512], replicated, may hold values from -0.5 to 0.5
- vectors_anchor: float32 [2, 14, 128], replicated, as said below
- word_outer: float32 [30720, 128], P('dp'), may hold values from -0.3125 to 0.3125
- positions_outer: float32 [2, 256, 128], replicated, may hold values from -0.3125 to 0.3125
- attention_outer: float32 [2, 128, 512], replicated, may hold values from -0.3125 to 0.3125
- feedforward_outer: float32 [2, 2, 128, 512], replicated, may hold values from -0.3125 to 0.3125
- vectors_outer: float32 [2, 14, 128], replicated, may hold values from -1.25 to 1.25
Outputs:
- loss_sum: float32 [2], P('grp')
- loss_count: float32 [2], P('grp')
- grad_norm: float32 [2], P('grp')
- word_first_next: float32 [2, 30720, 128], P('grp', 'dp')
- positions_first_next: float32 [2, 2, 256, 128], P('grp')
- attention_first_next: float32 [2, 2, 128, 512], P('grp')
- feedforward_first_next: float32 [2, 2, 2, 128, 512], P('grp')
- vectors_first_next: float32 [2, 2, 14, 128], P('grp')
- word_second_next: float32 [2, 30720, 128], P('grp', 'dp')
- positions_second_next: float32 [2, 2, 256, 128], P('grp')
- attention_second_next: float32 [2, 2, 128, 512], P('grp')
- feedforward_second_next: float32 [2, 2, 2, 128, 512], P('grp')
- vectors_second_next: float32 [2, 2, 14, 128], P('grp')
- word_average: float32 [30720, 128], P('dp')
- positions_average: float32 [2, 256, 128], replicated
- attention_average: float32 [2, 128, 512], replicated
- feedforward_average: float32 [2, 2, 128, 512], replicated
- vectors_average: float32 [2, 14, 128], replicated
- word_outer_next: float32 [30720, 128], P('dp')
- positions_outer_next: float32 [2, 256, 128], replicated
- attention_outer_next: float32 [2, 128, 512], replicated
- feedforward_outer_next: float32 [2, 2, 128, 512], replicated
- vectors_outer_next: float32 [2, 14, 128], replicated
- word_weight_next: float32 [2, 30720, 128], P('grp', 'dp')
- positions_weight_next: float32 [2, 2, 256, 128], P('grp')
- attention_weight_next: float32 [2, 2, 128, 512], P('grp')
- feedforward_weight_next: float32 [2, 2, 2, 128, 512], P('grp')
- vectors_weight_next: float32 [2, 2, 14, 128], P('grp')
The draws below stay inside these ranges and needn't reach their ends.
Inputs may be any that keep to these rules, and one draw needn't show every extreme that they name: `vectors`: rows 0, 5 and 8 are norm gains near one, the others biases. `vectors_anchor`: rows 0, 5 and 8 are norm gains near one, the others biases.
All inputs are finite; a program needn't handle non-finite values. No bound on the sum of `question_valid` on one device may be relied on, other than what follows from the above.
Results may differ from the reference program's by a relative error of at most 0.018.
The reference program's roundings to bfloat16 on the way count: a program that leaves them out, or rounds other values in their place, can miss the bound.
Values may be sent and summed in bfloat16 or wider, within the bound.
A program may use at most 256 MiB of HBM per device.

```python
import math
import jax
import jax.numpy as jnp
import numpy as np
from jax import lax

D = 128
HEAD = 64
FF = 512
VOCAB = 30720
LQ = 64
LP = 256
STEP = 5
QUESTIONS = 256
PASSAGES = 512
ALL_Q = 512
ALL_P = 1024
NV = 14
N_GRP = 2


def vector_rows(key, shape):
    noise = jax.random.normal(key, shape, jnp.float32)
    row_index = lax.broadcasted_iota(jnp.int32, shape, len(shape) - 2)
    gain_row = (row_index == 0) | (row_index == 5) | (row_index == 8)
    return jnp.where(gain_row, 1.0 + 0.15 * noise, 0.3 * noise)


def draw_vectors(key, part):
    key = jax.random.fold_in(key, 11)
    return vector_rows(key, (N_GRP, 2, NV, D))


def draw_vectors_anchor(key, part):
    key = jax.random.fold_in(key, 23)
    return vector_rows(key, (2, NV, D))


def with_ends(entries, rng, smallest, high):
    longest = entries.shape.index(max(entries.shape))
    spots = []
    for shift in (0, 1):
        where = [jax.random.randint(jax.random.fold_in(rng, axis), (), 0, length) for axis, length in enumerate(entries.shape)]
        where[longest] = (where[longest] + shift) % entries.shape[longest]
        spots.append(tuple(where))
    return entries.at[spots[0]].set(smallest).at[spots[1]].set(high)


def block_levels(stream_key, extent, pieces, low, largest):
    def one(dim, parts):
        draws = jax.random.uniform(jax.random.fold_in(jax.random.fold_in(stream_key, 6), dim), (parts,), jnp.float32, low / len(pieces), largest / len(pieces))
        return jnp.repeat(jnp.exp(draws), extent[dim] // parts).reshape((-1,) + (1,) * (len(extent) - dim - 1))

    factor_of = one(*pieces[0])
    for cut in pieces[1:]:
        factor_of = factor_of * one(*cut)
    return factor_of


def rank_table(number_of, slope):
    weights = [(1 << 20) // math.isqrt(grade ** slope) + 1 for grade in range(1, number_of + 1)]
    scale = 1 + sum(weights) // (1 << 30)
    return np.cumsum(np.array([max(1, weight // scale) for weight in weights]))


def skewed_ids(rng, extent, count, lean):
    table = rank_table(count, lean)
    pick = jax.random.randint(jax.random.fold_in(rng, 1), extent, 0, int(table[count - 1]))
    grade = jnp.searchsorted(jnp.asarray(table, jnp.int32), pick, side="right")
    return jax.random.permutation(jax.random.fold_in(rng, 2), count)[grade].astype(jnp.int32)


def centred(key, dims, scale, limit, pieces=(), held_as=jnp.bfloat16):
    values = scale * jax.random.normal(key, dims, jnp.float32)
    if pieces:
        values = values * block_levels(key, dims, pieces, -0.22, 0.18)
    return jnp.clip(values, -limit, limit).astype(held_as)


def setup_inputs(seed: int = 0) -> dict:
    seeds = jax.random.split(jax.random.key(seed), 33)
    question_ids = with_ends(skewed_ids(seeds[0], (ALL_Q, LQ), VOCAB, 1), jax.random.fold_in(seeds[0], 3), 0, VOCAB - 1).astype(jnp.int32)
    passage_ids = with_ends(skewed_ids(seeds[1], (ALL_P, LP), VOCAB, 1), jax.random.fold_in(seeds[1], 3), 0, VOCAB - 1).astype(jnp.int32)
    question_lengths = with_ends(jax.random.randint(seeds[2], (ALL_Q,), LQ // 4, LQ + 1), jax.random.fold_in(seeds[2], 1), LQ // 4, LQ).astype(jnp.int32)
    passage_lengths = with_ends(jax.random.randint(seeds[3], (ALL_P,), LP // 4, LP + 1), jax.random.fold_in(seeds[3], 1), LP // 4, LP).astype(jnp.int32)
    question_keys = with_ends(jax.random.randint(seeds[4], (ALL_Q,), 0, 16), jax.random.fold_in(seeds[4], 1), 0, 15).astype(jnp.int32)
    passage_keys = with_ends(jax.random.randint(seeds[5], (ALL_P,), 0, 16), jax.random.fold_in(seeds[5], 1), 0, 15).astype(jnp.int32)
    question_valid = with_ends((jax.random.randint(seeds[6], (ALL_Q,), 0, 8) < 7).astype(jnp.int32), jax.random.fold_in(seeds[6], 1), 0, 1)
    word_table = centred(seeds[7], (N_GRP, VOCAB, D), 0.05, 0.3125, ((0, 2), (1, 16)), jnp.float32)
    positions = centred(seeds[8], (N_GRP, 2, LP, D), 0.05, 0.3125, ((0, 2),), jnp.float32)
    attention = centred(seeds[9], (N_GRP, 2, D, 4 * D), D ** -0.5, 0.5, ((0, 2),), jnp.float32)
    feedforward = centred(seeds[10], (N_GRP, 2, 2, D, FF), D ** -0.5, 0.5, ((0, 2),), jnp.float32)
    vectors = draw_vectors(jax.random.fold_in(seeds[32], 71), 0)
    word_first = centred(seeds[12], (N_GRP, VOCAB, D), (0.0033 * 0.01 * (VOCAB * D + 2 * (LP * D + 4 * D * D + 2 * D * FF + NV * D)) ** -0.5), 8.940696716308594e-08, ((0, 2), (1, 16)), jnp.float32)
    positions_first = centred(seeds[13], (N_GRP, 2, LP, D), (0.11 * 0.01 * (VOCAB * D + 2 * (LP * D + 4 * D * D + 2 * D * FF + NV * D)) ** -0.5), 3.337860107421875e-06, ((0, 2),), jnp.float32)
    attention_first = centred(seeds[14], (N_GRP, 2, D, 4 * D), (0.11 * 0.01 * (VOCAB * D + 2 * (LP * D + 4 * D * D + 2 * D * FF + NV * D)) ** -0.5), 3.337860107421875e-06, ((0, 2),), jnp.float32)
    feedforward_first = centred(seeds[15], (N_GRP, 2, 2, D, FF), (0.11 * 0.01 * (VOCAB * D + 2 * (LP * D + 4 * D * D + 2 * D * FF + NV * D)) ** -0.5), 3.337860107421875e-06, ((0, 2),), jnp.float32)
    vectors_first = centred(seeds[16], (N_GRP, 2, NV, D), (0.44 * 0.01 * (VOCAB * D + 2 * (LP * D + 4 * D * D + 2 * D * FF + NV * D)) ** -0.5), 1.33514404296875e-05, ((0, 2),), jnp.float32)
    word_second = jnp.clip(jnp.exp(math.log(1.638413119368562e-14) - 2.7725887 * jax.random.uniform(seeds[17], (N_GRP, VOCAB, D), jnp.float32) ** block_levels(seeds[17], (N_GRP, VOCAB, D), ((0, 2), (1, 16)), -0.2, 0.2)), 1.0240081996053512e-15, 1.638413119368562e-14)
    positions_second = jnp.clip(jnp.exp(math.log(1.820459066695715e-13) - 2.7725887 * jax.random.uniform(seeds[18], (N_GRP, 2, LP, D), jnp.float32) ** block_levels(seeds[18], (N_GRP, 2, LP, D), ((0, 2),), -0.2, 0.2)), 1.1377869166848218e-14, 1.820459066695715e-13)
    attention_second = jnp.clip(jnp.exp(math.log(1.820459066695715e-13) - 2.7725887 * jax.random.uniform(seeds[19], (N_GRP, 2, D, 4 * D), jnp.float32) ** block_levels(seeds[19], (N_GRP, 2, D, 4 * D), ((0, 2),), -0.2, 0.2)), 1.1377869166848218e-14, 1.820459066695715e-13)
    feedforward_second = jnp.clip(jnp.exp(math.log(1.820459066695715e-13) - 2.7725887 * jax.random.uniform(seeds[20], (N_GRP, 2, 2, D, FF), jnp.float32) ** block_levels(seeds[20], (N_GRP, 2, 2, D, FF), ((0, 2),), -0.2, 0.2)), 1.1377869166848218e-14, 1.820459066695715e-13)
    vectors_second = jnp.clip(jnp.exp(math.log(2.912734506713144e-12) - 2.7725887 * jax.random.uniform(seeds[21], (N_GRP, 2, NV, D), jnp.float32) ** block_levels(seeds[21], (N_GRP, 2, NV, D), ((0, 2),), -0.2, 0.2)), 1.820459066695715e-13, 2.912734506713144e-12)
    word_anchor = centred(seeds[22], (VOCAB, D), 0.05, 0.3125, ((0, 16),), jnp.float32)
    positions_anchor = centred(seeds[23], (2, LP, D), 0.05, 0.3125, (), jnp.float32)
    attention_anchor = centred(seeds[24], (2, D, 4 * D), D ** -0.5, 0.5, (), jnp.float32)
    feedforward_anchor = centred(seeds[25], (2, 2, D, FF), D ** -0.5, 0.5, (), jnp.float32)
    vectors_anchor = draw_vectors_anchor(jax.random.fold_in(seeds[32], 71), 0)
    word_outer = centred(seeds[27], (VOCAB, D), 0.05, 0.3125, ((0, 16),), jnp.float32)
    positions_outer = centred(seeds[28], (2, LP, D), 0.05, 0.3125, (), jnp.float32)
    attention_outer = centred(seeds[29], (2, D, 4 * D), 0.05, 0.3125, (), jnp.float32)
    feedforward_outer = centred(seeds[30], (2, 2, D, FF), 0.05, 0.3125, (), jnp.float32)
    vectors_outer = centred(seeds[31], (2, NV, D), 0.2, 1.25, (), jnp.float32)
    return {"question_ids": question_ids, "passage_ids": passage_ids, "question_lengths": question_lengths, "passage_lengths": passage_lengths, "question_keys": question_keys, "passage_keys": passage_keys, "question_valid": question_valid, "word_table": word_table, "positions": positions, "attention": attention, "feedforward": feedforward, "vectors": vectors, "word_first": word_first, "positions_first": positions_first, "attention_first": attention_first, "feedforward_first": feedforward_first, "vectors_first": vectors_first, "word_second": word_second, "positions_second": positions_second, "attention_second": attention_second, "feedforward_second": feedforward_second, "vectors_second": vectors_second, "word_anchor": word_anchor, "positions_anchor": positions_anchor, "attention_anchor": attention_anchor, "feedforward_anchor": feedforward_anchor, "vectors_anchor": vectors_anchor, "word_outer": word_outer, "positions_outer": positions_outer, "attention_outer": attention_outer, "feedforward_outer": feedforward_outer, "vectors_outer": vectors_outer}


@jax.custom_vjp
def low(v):
    return lax.optimization_barrier(v.astype(jnp.bfloat16)).astype(jnp.float32)

@jax.custom_vjp
def low_back(v):
    return v

def low_keep(v):
    return (low(v), None)

def low_pass(kept, grad):
    return (grad,)

def back_keep(v):
    return (v, None)

def back_low(kept, grad):
    return (low(grad),)
low.defvjp(low_keep, low_pass)
low_back.defvjp(back_keep, back_low)
HIGH = lax.Precision.HIGHEST
NORM_EPS = 1e-05
MASKED = -1000000000.0
BETA_ONE = 0.9
BETA_TWO = 0.999
INNER_RATE = 0.05
WEIGHT_DECAY = 0.01
ADAM_EPS = 1e-08
CLIP_LIMIT = 0.01
OUTER_RATE = 0.7
OUTER_MU = 0.9

def layer_norm(values, gain, shift):
    center = values - lax.optimization_barrier(jnp.mean(values, -1, keepdims=True))
    spread = lax.optimization_barrier(jnp.mean(center * center, -1, keepdims=True))
    return center * lax.rsqrt(spread + NORM_EPS) * gain + shift

def encode_block(table_low, weights, token_ids, lengths):
    place, attn_w, ffn_w, vec = weights
    sequences, seq = token_ids.shape
    width = attn_w.shape[0]
    heads = width // HEAD
    x_embed = table_low[token_ids] + place[:seq]
    h_embed = layer_norm(x_embed, vec[0], vec[1])
    bias_row = jnp.concatenate([vec[2], jnp.zeros_like(vec[2]), vec[3]])
    qkv = jnp.einsum('bld,de->ble', low(h_embed), low(attn_w[:, :3 * width]), precision=HIGH) + bias_row
    qkv = low_back(low(qkv)).reshape(sequences, seq, 3, heads, HEAD)
    scores = jnp.einsum('bqhe,bkhe->bhqk', qkv[:, :, 0], qkv[:, :, 1], precision=HIGH) * HEAD ** (-0.5)
    scores = low_back(scores)
    keep = jnp.arange(seq)[None, None, None, :] < lengths[:, None, None, None]
    probs = jax.nn.softmax(jnp.where(keep, scores, MASKED), -1)
    mixed = jnp.einsum('bhqk,bkhe->bqhe', low(probs), qkv[:, :, 2], precision=HIGH).reshape(sequences, seq, width)
    mixed = low_back(low(mixed))
    branch = low_back(jnp.einsum('bld,de->ble', mixed, low(attn_w[:, 3 * width:]), precision=HIGH) + vec[4])
    h_attn = layer_norm(h_embed + branch, vec[5], vec[6])
    pre = jnp.einsum('bld,df->blf', low(h_attn), low(ffn_w[0]), precision=HIGH) + vec[10:].reshape(-1)
    pre = low_back(pre)
    act = low(jax.nn.gelu(pre, approximate=True))
    out_branch = low_back(jnp.einsum('blf,df->bld', act, low(ffn_w[1]), precision=HIGH) + vec[7])
    h_out = layer_norm(h_attn + out_branch, vec[8], vec[9])
    return h_out[:, 0]

def encode_all(table_low, weights, token_ids, lengths):
    count_seq, seq = token_ids.shape
    block = math.gcd(count_seq, max(1, 4096 // seq))
    run = jax.checkpoint(lambda pair: encode_block(table_low, weights, pair[0], pair[1]))
    found = lax.map(run, (token_ids.reshape(-1, block, seq), lengths.reshape(-1, block)))
    return found.reshape(count_seq, -1)

def softmax_loss(scores, drop, target, weight):
    lse = jax.nn.logsumexp(jnp.where(drop, MASKED, scores), -1)
    picked = lax.optimization_barrier(jnp.sum(jnp.where(target, scores, 0.0), -1))
    return jnp.sum(weight * (lse - picked))

def group_loss(params, question_ids, passage_ids, question_lengths, passage_lengths, question_keys, passage_keys, question_valid):
    table, places, attn, ffn, vectors = params
    table_low = low(table)
    every_q = low(encode_all(table_low, (places[0], attn[0], ffn[0], vectors[0]), question_ids, question_lengths))
    every_p = low(encode_all(table_low, (places[1], attn[1], ffn[1], vectors[1]), passage_ids, passage_lengths))
    scale = every_q.shape[1] ** (-0.5)
    scores_qp = low_back(jnp.dot(every_q, every_p.T, precision=HIGH) * scale)
    scores_pq = low_back(jnp.dot(every_p, every_q.T, precision=HIGH) * scale)
    index_q = jnp.arange(every_q.shape[0])
    index_p = jnp.arange(every_p.shape[0])
    target_qp = index_p[None, :] == 2 * index_q[:, None]
    drop_qp = (question_keys[:, None] == passage_keys[None, :]) & ~target_qp
    owner = index_p // 2
    target_pq = index_q[None, :] == owner[:, None]
    drop_pq = ((passage_keys[:, None] == question_keys[None, :]) | (question_valid[None, :] == 0)) & ~target_pq
    valid = question_valid.astype(jnp.float32)
    weight_p = jnp.where(index_p % 2 == 0, valid[owner], 0.0)
    total = softmax_loss(scores_qp, drop_qp, target_qp, valid) + softmax_loss(scores_pq, drop_pq, target_pq, weight_p)
    count = jnp.maximum(jnp.sum(valid), 1.0)
    return (total / count, (total, count))

def adam(weight, grad, first, second):
    first_new = BETA_ONE * first + (1.0 - BETA_ONE) * grad
    second_new = BETA_TWO * second + (1.0 - BETA_TWO) * grad * grad
    fix_one = 1.0 - BETA_ONE ** STEP
    fix_two = 1.0 - BETA_TWO ** STEP
    ratio = first_new / fix_one / (jnp.sqrt(second_new / fix_two) + ADAM_EPS)
    return (first_new, second_new, weight - INNER_RATE * (ratio + WEIGHT_DECAY * weight))

def reference(question_ids, passage_ids, question_lengths, passage_lengths, question_keys, passage_keys, question_valid, word_table, positions, attention, feedforward, vectors, word_first, positions_first, attention_first, feedforward_first, vectors_first, word_second, positions_second, attention_second, feedforward_second, vectors_second, word_anchor, positions_anchor, attention_anchor, feedforward_anchor, vectors_anchor, word_outer, positions_outer, attention_outer, feedforward_outer, vectors_outer):
    weights = (word_table, positions, attention, feedforward, vectors)
    firsts = (word_first, positions_first, attention_first, feedforward_first, vectors_first)
    seconds = (word_second, positions_second, attention_second, feedforward_second, vectors_second)
    anchors = (word_anchor, positions_anchor, attention_anchor, feedforward_anchor, vectors_anchor)
    outers = (word_outer, positions_outer, attention_outer, feedforward_outer, vectors_outer)
    sums, counts, norms = ([], [], [])
    first_new = [[] for kind in range(5)]
    second_new = [[] for kind in range(5)]
    inner_new = [[] for kind in range(5)]
    for group in range(N_GRP):
        low_q = group * QUESTIONS
        low_p = group * PASSAGES
        params = tuple((w[group] for w in weights))

        def loss_fn(values):
            return group_loss(values, question_ids[low_q:low_q + QUESTIONS], passage_ids[low_p:low_p + PASSAGES], question_lengths[low_q:low_q + QUESTIONS], passage_lengths[low_p:low_p + PASSAGES], question_keys[low_q:low_q + QUESTIONS], passage_keys[low_p:low_p + PASSAGES], question_valid[low_q:low_q + QUESTIONS])
        loss_value, pull, aux = jax.vjp(loss_fn, params, has_aux=True)
        grads = pull(jnp.ones((), jnp.float32))[0]
        norm = jnp.sqrt(sum((jnp.sum(g * g) for g in grads)))
        factor = CLIP_LIMIT / jnp.maximum(norm, CLIP_LIMIT)
        sums.append(aux[0])
        counts.append(aux[1])
        norms.append(norm)
        for kind in range(5):
            fresh_first, fresh_second, stepped = adam(params[kind], grads[kind] * factor, firsts[kind][group], seconds[kind][group])
            first_new[kind].append(fresh_first)
            second_new[kind].append(fresh_second)
            inner_new[kind].append(stepped)
    averages, outer_next, weight_next = ([], [], [])
    for kind in range(5):
        inner = jnp.stack(inner_new[kind])
        average = lax.optimization_barrier(jnp.mean(anchors[kind][None] - inner, 0))
        momentum = OUTER_MU * outers[kind] + average
        outer_weight = anchors[kind] - OUTER_RATE * (average + OUTER_MU * momentum)
        averages.append(average)
        outer_next.append(momentum)
        weight_next.append(jnp.broadcast_to(outer_weight[None], inner.shape))
    fs = [jnp.stack(v) for v in first_new]
    ss = [jnp.stack(v) for v in second_new]
    return (jnp.stack(sums), jnp.stack(counts), jnp.stack(norms), fs[0], fs[1], fs[2], fs[3], fs[4], ss[0], ss[1], ss[2], ss[3], ss[4], averages[0], averages[1], averages[2], averages[3], averages[4], outer_next[0], outer_next[1], outer_next[2], outer_next[3], outer_next[4], weight_next[0], weight_next[1], weight_next[2], weight_next[3], weight_next[4])
```

```python
import jax
import jax.numpy as jnp
from jax import lax
from jax.sharding import PartitionSpec as P

HEAD = 64
STEP = 5


NORM_EPS = 1e-05
MASKED = -1000000000.0
BETA_ONE = 0.9
BETA_TWO = 0.999
INNER_RATE = 0.05
WEIGHT_DECAY = 0.01
ADAM_EPS = 1e-08
CLIP_LIMIT = 0.01
OUTER_RATE = 0.7
OUTER_MU = 0.9
CONTRACT_ROWS = (((0,), (0,)), ((), ()))
CONTRACT_LAST = (((1,), (1,)), ((), ()))


def layer_norm(values, gain, shift):
    center = values - jnp.mean(values, -1, keepdims=True)
    spread = jnp.mean(center * center, -1, keepdims=True)
    return center * lax.rsqrt(spread + NORM_EPS) * gain + shift


def gelu_tanh(values):
    return jax.nn.gelu(values, approximate=True)


def low16(values):
    return values.astype(jnp.bfloat16)


def dot(left, right):
    return jnp.dot(left, right, preferred_element_type=jnp.float32)


def dot_rows(left, right):
    return lax.dot_general(left, right, CONTRACT_ROWS, preferred_element_type=jnp.float32)


def dot_last(left, right):
    return lax.dot_general(left, right, CONTRACT_LAST, preferred_element_type=jnp.float32)


def token_forward(rows, place, attn_w, vec, lengths):
    sequences, seq, width = rows.shape
    heads = width // HEAD
    x_embed = rows.astype(jnp.float32) + place[:seq]
    a_low = low16(layer_norm(x_embed, vec[0], vec[1]))
    w_kv = low16(attn_w[:, width : 3 * width])
    bias = jnp.concatenate([jnp.zeros_like(vec[3]), vec[3]])
    kv = low16(
        jnp.einsum("bld,de->ble", a_low, w_kv, preferred_element_type=jnp.float32) + bias
    ).reshape(sequences, seq, 2, heads, HEAD)
    query = low16(dot(a_low[:, 0], low16(attn_w[:, :width])) + vec[2]).reshape(
        sequences, heads, HEAD
    )
    keys_all, values_all = kv[:, :, 0], kv[:, :, 1]
    scores = jnp.einsum(
        "bhe,bkhe->bhk", query, keys_all, preferred_element_type=jnp.float32
    ) * HEAD ** (-0.5)
    keep = jnp.arange(seq)[None, None, :] < lengths[:, None, None]
    scores = jnp.where(keep, scores, MASKED)
    top = jnp.max(scores, -1, keepdims=True)
    expo = jnp.exp(scores - top)
    probs = expo / jnp.sum(expo, -1, keepdims=True)
    mixed = jnp.einsum(
        "bhk,bkhe->bhe", low16(probs), values_all, preferred_element_type=jnp.float32
    )
    mixed = low16(mixed.reshape(sequences, width))
    return mixed, (x_embed, a_low, query, keys_all, values_all, probs)


def token_backward(kept, attn_w, vec, d_mixed, d_x_attn):
    x_embed, a_low, query, keys_all, values_all, probs = kept
    sequences, seq, width = x_embed.shape
    heads = width // HEAD
    dm = d_mixed.reshape(sequences, heads, HEAD)
    d_probs = jnp.einsum("bhe,bkhe->bhk", dm, values_all, preferred_element_type=jnp.float32)
    d_values = low16(probs).astype(jnp.float32).transpose(0, 2, 1)[..., None] * dm.astype(
        jnp.float32
    )[:, None]
    d_scores = low16(probs * (d_probs - jnp.sum(probs * d_probs, -1, keepdims=True)))
    d_query = jnp.einsum(
        "bhk,bkhe->bhe", d_scores, keys_all, preferred_element_type=jnp.float32
    ) * HEAD ** (-0.5)
    d_keys = (
        d_scores.astype(jnp.float32).transpose(0, 2, 1)[..., None]
        * query.astype(jnp.float32)[:, None]
        * HEAD ** (-0.5)
    )
    d_query = low16(d_query.reshape(sequences, width))
    d_kv = low16(
        jnp.concatenate(
            [
                d_keys.reshape(sequences, seq, width),
                d_values.reshape(sequences, seq, width),
            ],
            -1,
        )
    )
    d_query_bias = jnp.sum(d_query.astype(jnp.float32), 0)
    d_value_bias = jnp.sum(d_kv[..., width:], (0, 1), dtype=jnp.float32)
    d_w_kv = jnp.einsum("bld,ble->de", a_low, d_kv, preferred_element_type=jnp.float32)
    d_w_q = dot_rows(a_low[:, 0], d_query)
    w_low = low16(attn_w)
    d_h = jnp.einsum(
        "ble,de->bld", d_kv, w_low[:, width : 3 * width], preferred_element_type=jnp.float32
    )
    first = d_x_attn + dot_last(d_query, w_low[:, :width])
    d_h = d_h.at[:, 0].add(first)
    unused, embed_back = jax.vjp(layer_norm, x_embed, vec[0], vec[1])
    d_x_embed, d_gain, d_shift = embed_back(d_h)
    return d_x_embed, jnp.concatenate([d_w_q, d_w_kv], 1), (d_gain, d_shift, d_query_bias, d_value_bias)


def class_forward(rows, mixed, place, attn_w, ffn_w, vec):
    width = rows.shape[1]
    h_embed = layer_norm(rows.astype(jnp.float32) + place[:1], vec[0], vec[1])
    x_attn = h_embed + (dot(mixed, low16(attn_w[:, 3 * width :])) + vec[4])
    h_attn = layer_norm(x_attn, vec[5], vec[6])
    h_low = low16(h_attn)
    pre = dot(h_low, low16(ffn_w[0])) + vec[10:].reshape(-1)
    act = low16(gelu_tanh(pre))
    x_ffn = h_attn + (dot_last(act, low16(ffn_w[1])) + vec[7])
    h_out = layer_norm(x_ffn, vec[8], vec[9])
    return low16(h_out), (x_attn, h_low, pre, act, x_ffn)


def class_backward(kept, mixed, attn_w, ffn_w, vec, d_cls):
    x_attn, h_low, pre, act, x_ffn = kept
    width = x_attn.shape[1]
    unused, out_back = jax.vjp(layer_norm, x_ffn, vec[8], vec[9])
    d_x_ffn, d_gain_two, d_shift_two = out_back(d_cls)
    d_branch = low16(d_x_ffn)
    d_down_bias = jnp.sum(d_branch, 0, dtype=jnp.float32)
    d_down = dot_rows(d_branch, act)
    d_act = dot(d_branch, low16(ffn_w[1]))
    unused, gelu_back = jax.vjp(gelu_tanh, pre)
    d_pre = low16(gelu_back(d_act)[0])
    d_up_bias = jnp.sum(d_pre, 0, dtype=jnp.float32)
    d_up = dot_rows(h_low, d_pre)
    d_h_attn = d_x_ffn + dot_last(d_pre, low16(ffn_w[0]))
    unused, attn_back = jax.vjp(layer_norm, x_attn, vec[5], vec[6])
    d_x_attn, d_gain_one, d_shift_one = attn_back(d_h_attn)
    d_proj = low16(d_x_attn)
    d_out_bias = jnp.sum(d_proj, 0, dtype=jnp.float32)
    d_w_out = dot_rows(mixed, d_proj)
    d_mixed = low16(dot_last(d_proj, low16(attn_w[:, 3 * width :])))
    rows = (d_out_bias, d_gain_one, d_shift_one, d_down_bias, d_gain_two, d_shift_two)
    return d_mixed, d_x_attn, d_w_out, jnp.stack([d_up, d_down]), rows, d_up_bias


def softmax_terms(scores, drop, target, weight, count, axis):
    masked = jnp.where(drop, MASKED, scores)
    top = jnp.max(masked, axis, keepdims=True)
    expo = jnp.exp(masked - top)
    total = jnp.sum(expo, axis, keepdims=True)
    lse = top + jnp.log(total)
    picked = jnp.sum(jnp.where(target, scores, 0.0), axis, keepdims=True)
    loss = jnp.sum(weight * (lse - picked))
    grad = low16((weight / count) * (expo / total - target.astype(jnp.float32)))
    return grad, loss


def score_stage(every_q, every_p, keys_q, keys_p, valid_q):
    count = jnp.maximum(jnp.sum(valid_q).astype(jnp.float32), 1.0)
    scale = every_q.shape[1] ** (-0.5)
    index_q = jnp.arange(every_q.shape[0])[:, None]
    index_p = jnp.arange(every_p.shape[0])[None, :]
    scores = dot_last(every_q, every_p) * scale
    same = keys_q[:, None] == keys_p[None, :]
    target_qp = index_p == 2 * index_q
    valid = valid_q.astype(jnp.float32)[:, None]
    grad_qp, loss_qp = softmax_terms(scores, same & ~target_qp, target_qp, valid, count, 1)
    target_pq = index_p // 2 == index_q
    drop_pq = (same | (valid_q[:, None] == 0)) & ~target_pq
    owner_valid = jnp.repeat(valid_q, 2)
    weight_p = jnp.where(index_p[0] % 2 == 0, owner_valid, 0).astype(jnp.float32)[None, :]
    grad_pq, loss_pq = softmax_terms(scores, drop_pq, target_pq, weight_p, count, 0)
    d_q = (dot(grad_qp, every_p) + dot(grad_pq, every_p)) * scale
    d_p = (dot_rows(grad_pq, every_q) + dot_rows(grad_qp, every_q)) * scale
    return d_q, d_p, loss_qp + loss_pq, count


def adam(weight, grad, first, second):
    first_new = BETA_ONE * first + (1.0 - BETA_ONE) * grad
    second_new = BETA_TWO * second + (1.0 - BETA_TWO) * grad * grad
    fix_one = 1.0 - BETA_ONE**STEP
    fix_two = 1.0 - BETA_TWO**STEP
    ratio = first_new / fix_one / (jnp.sqrt(second_new / fix_two) + ADAM_EPS)
    return (first_new, second_new, weight - INNER_RATE * (ratio + WEIGHT_DECAY * weight))


def body(
    question_ids,
    passage_ids,
    question_lengths,
    passage_lengths,
    question_keys,
    passage_keys,
    question_valid,
    word_table,
    positions,
    attention,
    feedforward,
    vectors,
    word_first,
    positions_first,
    attention_first,
    feedforward_first,
    vectors_first,
    word_second,
    positions_second,
    attention_second,
    feedforward_second,
    vectors_second,
    word_anchor,
    positions_anchor,
    attention_anchor,
    feedforward_anchor,
    vectors_anchor,
    word_outer,
    positions_outer,
    attention_outer,
    feedforward_outer,
    vectors_outer,
):
    width = word_table.shape[2]
    wide = lax.all_gather(low16(word_table[0]), "dp", axis=0, tiled=True)
    device = lax.axis_index("dp")
    many = lax.axis_size("dp")
    ids = (question_ids, passage_ids)
    lengths = (question_lengths, passage_lengths)
    counts = (question_ids.shape[0], passage_ids.shape[0])
    flags = jnp.concatenate([question_keys, question_valid, passage_keys])
    flags_all = lax.all_gather(flags, "dp")
    keys_q = flags_all[:, : counts[0]].reshape(-1)
    valid_all = flags_all[:, counts[0] : 2 * counts[0]].reshape(-1)
    keys_p = flags_all[:, 2 * counts[0] :].reshape(-1)
    packs, kepts = ([], [])
    for enc in range(2):
        rows = jnp.take(wide, ids[enc], axis=0)
        mixed, kept = token_forward(
            rows, positions[0, enc], attention[0, enc], vectors[0, enc], lengths[enc]
        )
        packs.append(jnp.concatenate([rows[:, 0], mixed], 1))
        kepts.append(kept)
    every = lax.all_gather(jnp.concatenate(packs), "dp")
    cls, class_kept, mixes = ([], [], [])
    for enc in range(2):
        part = every[:, : counts[0]] if enc == 0 else every[:, counts[0] :]
        part = part.reshape(-1, 2 * width)
        low_cls, kept = class_forward(
            part[:, :width],
            part[:, width:],
            positions[0, enc],
            attention[0, enc],
            feedforward[0, enc],
            vectors[0, enc],
        )
        cls.append(low_cls)
        class_kept.append(kept)
        mixes.append(part[:, width:])
    d_q, d_p, loss_total, count = score_stage(cls[0], cls[1], keys_q, keys_p, valid_all)
    d_cls = (d_q, d_p)
    token_grads, partials, finals = ([], [], [])
    for enc in range(2):
        d_mixed, d_x_attn, d_w_out, d_ffn, rows_mid, d_up_bias = class_backward(
            class_kept[enc], mixes[enc], attention[0, enc], feedforward[0, enc], vectors[0, enc], d_cls[enc]
        )
        begin = device * counts[enc]
        own_mixed = lax.dynamic_slice_in_dim(d_mixed, begin, counts[enc])
        own_x = lax.dynamic_slice_in_dim(d_x_attn, begin, counts[enc])
        d_x_embed, d_w_qkv, rows_first = token_backward(
            kepts[enc], attention[0, enc], vectors[0, enc], own_mixed, own_x
        )
        token_grads.append(d_x_embed)
        place_sum = jnp.sum(d_x_embed, 0)
        d_place = jnp.pad(place_sum, ((0, positions.shape[2] - place_sum.shape[0]), (0, 0)))
        partials.append((d_place, d_w_qkv, jnp.stack(rows_first)))
        finals.append((d_w_out, d_ffn, rows_mid, d_up_bias))
    token_ids = jnp.concatenate([ids[0].reshape(-1), ids[1].reshape(-1)])
    token_all = jnp.concatenate([token_grads[0].reshape(-1, width), token_grads[1].reshape(-1, width)])
    table_full = jax.ops.segment_sum(token_all, token_ids, num_segments=wide.shape[0])
    table_grad = lax.psum_scatter(
        low16(table_full), "dp", scatter_dimension=0, tiled=True
    ).astype(jnp.float32)
    table_sq = jnp.sum(table_grad * table_grad)
    flat = jnp.concatenate(
        [table_sq.reshape(1)] + [v.reshape(-1) for part in partials for v in part]
    )
    flat = lax.psum(flat, "dp")
    table_sq = flat[0]
    spot = 1
    places, attns, vecs = ([], [], [])
    for enc in range(2):
        got = []
        for piece in partials[enc]:
            got.append(flat[spot : spot + piece.size].reshape(piece.shape))
            spot += piece.size
        d_w_out, d_ffn, rows_mid, d_up_bias = finals[enc]
        places.append(got[0])
        attns.append(jnp.concatenate([got[1], d_w_out], 1))
        vecs.append(
            jnp.concatenate([got[2], jnp.stack(rows_mid), d_up_bias.reshape(-1, width)])
        )
    place_grad, attn_grad, vec_grad = (jnp.stack(places), jnp.stack(attns), jnp.stack(vecs))
    ffn_grad = jnp.stack([finals[0][1], finals[1][1]])
    grads = (table_grad[None], place_grad[None], attn_grad[None], ffn_grad[None], vec_grad[None])
    norm = jnp.sqrt(table_sq + sum((jnp.sum(g * g) for g in grads[1:])))
    factor = CLIP_LIMIT / jnp.maximum(norm, CLIP_LIMIT)
    weights = (word_table, positions, attention, feedforward, vectors)
    firsts = (word_first, positions_first, attention_first, feedforward_first, vectors_first)
    seconds = (word_second, positions_second, attention_second, feedforward_second, vectors_second)
    anchors = (word_anchor, positions_anchor, attention_anchor, feedforward_anchor, vectors_anchor)
    outers = (word_outer, positions_outer, attention_outer, feedforward_outer, vectors_outer)
    first_new, second_new, inner_new = ([], [], [])
    for kind in range(5):
        fresh_first, fresh_second, stepped = adam(
            weights[kind], grads[kind] * factor, firsts[kind], seconds[kind]
        )
        first_new.append(fresh_first)
        second_new.append(fresh_second)
        inner_new.append(stepped)
    differences = tuple((anchors[kind] - inner_new[kind][0] for kind in range(5)))
    summed = lax.psum(
        (differences[0], differences[1], differences[2], differences[3], differences[4]), "grp"
    )
    groups = lax.axis_size("grp")
    averages, outer_next, weight_next = ([], [], [])
    for kind in range(5):
        average = summed[kind] / groups
        momentum = OUTER_MU * outers[kind] + average
        outer_weight = anchors[kind] - OUTER_RATE * (average + OUTER_MU * momentum)
        averages.append(average)
        outer_next.append(momentum)
        weight_next.append(outer_weight[None])
    return (
        loss_total.reshape(1),
        count.reshape(1),
        norm.reshape(1),
        first_new[0],
        first_new[1],
        first_new[2],
        first_new[3],
        first_new[4],
        second_new[0],
        second_new[1],
        second_new[2],
        second_new[3],
        second_new[4],
        averages[0],
        averages[1],
        averages[2],
        averages[3],
        averages[4],
        outer_next[0],
        outer_next[1],
        outer_next[2],
        outer_next[3],
        outer_next[4],
        weight_next[0],
        weight_next[1],
        weight_next[2],
        weight_next[3],
        weight_next[4],
    )


def solution(mesh):
    placed = (
        P(("grp", "dp"), None),
        P(("grp", "dp"), None),
        P(("grp", "dp")),
        P(("grp", "dp")),
        P(("grp", "dp")),
        P(("grp", "dp")),
        P(("grp", "dp")),
        P("grp", "dp", None),
        P("grp", None, None, None),
        P("grp", None, None, None),
        P("grp", None, None, None, None),
        P("grp", None, None, None),
        P("grp", "dp", None),
        P("grp", None, None, None),
        P("grp", None, None, None),
        P("grp", None, None, None, None),
        P("grp", None, None, None),
        P("grp", "dp", None),
        P("grp", None, None, None),
        P("grp", None, None, None),
        P("grp", None, None, None, None),
        P("grp", None, None, None),
        P("dp", None),
        P(),
        P(),
        P(),
        P(),
        P("dp", None),
        P(),
        P(),
        P(),
        P(),
    )
    return jax.shard_map(
        body,
        mesh=mesh,
        in_specs=placed,
        out_specs=(
            P("grp"),
            P("grp"),
            P("grp"),
            P("grp", "dp", None),
            P("grp", None, None, None),
            P("grp", None, None, None),
            P("grp", None, None, None, None),
            P("grp", None, None, None),
            P("grp", "dp", None),
            P("grp", None, None, None),
            P("grp", None, None, None),
            P("grp", None, None, None, None),
            P("grp", None, None, None),
            P("dp", None),
            P(),
            P(),
            P(),
            P(),
            P("dp", None),
            P(),
            P(),
            P(),
            P(),
            P("grp", "dp", None),
            P("grp", None, None, None),
            P("grp", None, None, None),
            P("grp", None, None, None, None),
            P("grp", None, None, None),
        ),
        check_vma=False,
    )
```

```python
import functools

import jax
import jax.numpy as jnp
from jax import lax
from jax.experimental import pallas as pl
from jax.experimental.pallas import tpu as pltpu
from jax.sharding import PartitionSpec as P

HEAD = 64
STEP = 5


NORM_EPS = 1e-05
MASKED = -1000000000.0
BETA_ONE = 0.9
BETA_TWO = 0.999
INNER_RATE = 0.05
WEIGHT_DECAY = 0.01
ADAM_EPS = 1e-08
CLIP_LIMIT = 0.01
OUTER_RATE = 0.7
OUTER_MU = 0.9
CONTRACT_ROWS = (((0,), (0,)), ((), ()))
CONTRACT_LAST = (((1,), (1,)), ((), ()))


def layer_norm(values, gain, shift):
    center = values - jnp.mean(values, -1, keepdims=True)
    spread = jnp.mean(center * center, -1, keepdims=True)
    return center * lax.rsqrt(spread + NORM_EPS) * gain + shift


def gelu_tanh(values):
    return jax.nn.gelu(values, approximate=True)


def low16(values):
    return values.astype(jnp.bfloat16)


NEG = -1e30
MESH = pl.DeviceIdType.MESH
VMEM_LIMIT = 60 * 1024 * 1024
WAYS = 4
SLOTS = 128
SPAN = WAYS * SLOTS
CHUNK = 256
RAW_Q = 64
RAW_FLAGS = 72
RAW_ROWS = 80


def enter(many):
    me = lax.axis_index("dp")
    barrier = pltpu.get_barrier_semaphore()

    def greet(step, carry):
        peer = lax.rem(me + step, many)
        pl.semaphore_signal(barrier, inc=1, device_id={"dp": peer}, device_id_type=MESH)
        return carry

    lax.fori_loop(1, many, greet, 0)
    pl.semaphore_wait(barrier, many - 1)
    return me


def copy_to(peer, src, dst, send, recv):
    return pltpu.make_async_remote_copy(
        src_ref=src,
        dst_ref=dst,
        send_sem=send,
        recv_sem=recv,
        device_id={"dp": peer},
        device_id_type=MESH,
    )


def spread_start(many, me, pairs, send, recv, slot):
    def step_start(step, carry):
        peer = lax.rem(me + step, many)
        for index, (source, landing) in enumerate(pairs):
            copy_to(
                peer,
                source(peer),
                landing.at[me],
                send.at[slot + index, peer],
                recv.at[slot + index, me],
            ).start()
        return carry

    lax.fori_loop(1, many, step_start, 0)


def spread_wait(many, me, pairs, send, recv, slot):
    def step_wait(step, carry):
        peer = lax.rem(me + step, many)
        for index, (source, landing) in enumerate(pairs):
            copy = copy_to(
                peer,
                source(peer),
                landing.at[peer],
                send.at[slot + index, peer],
                recv.at[slot + index, peer],
            )
            copy.wait_recv()
            copy.wait_send()
        return carry

    lax.fori_loop(1, many, step_wait, 0)


def dot(left, right):
    return jnp.dot(left, right, preferred_element_type=jnp.float32)


def dot_rows(left, right):
    return lax.dot_general(left, right, CONTRACT_ROWS, preferred_element_type=jnp.float32)


def dot_last(left, right):
    return lax.dot_general(left, right, CONTRACT_LAST, preferred_element_type=jnp.float32)


def iota(shape, axis):
    return lax.broadcasted_iota(jnp.int32, shape, axis)


def hot(mask):
    return jnp.where(mask, 1.0, 0.0).astype(jnp.bfloat16)


def rows_kernel(
    many, count_q, raw_ref, table_ref, every_ref, rows_ref, low_ref, offer, landed, own, send, recv
):
    me = enter(many)
    raw_pairs = [(lambda peer: raw_ref, every_ref)]
    spread_start(many, me, raw_pairs, send, recv, 0)
    every_ref[me] = raw_ref[...]
    depth = table_ref.shape[0]
    low_ref[...] = jnp.zeros_like(low_ref)
    low_ref[0:depth, :] = low16(table_ref[...])
    padded = low_ref.shape[0]
    spread_wait(many, me, raw_pairs, send, recv, 0)
    first = me * depth

    def pick(step, carry):
        peer = lax.rem(me + step, many)
        found = every_ref[peer].astype(jnp.int32)
        ask = jnp.concatenate(
            [
                found[RAW_Q : RAW_Q + count_q // 2, 0:1],
                found[RAW_Q : RAW_Q + count_q // 2, 64:65],
                found[0 : RAW_Q // 2, 0:1],
            ],
            0,
        )
        place = ask - first
        inside = (place >= 0) & (place < depth)
        spot = jnp.where(inside, place, -1)
        total = jnp.zeros((spot.shape[0], 128), jnp.float32)
        for cut in range(padded // CHUNK):
            wide = jnp.broadcast_to(spot, (spot.shape[0], CHUNK))
            chosen = hot(wide == iota(wide.shape, 1) + cut * CHUNK)
            total += dot(chosen, low_ref[cut * CHUNK : (cut + 1) * CHUNK, :])
        offer[peer] = low16(total)
        return carry

    lax.fori_loop(0, many, pick, 0)
    pairs = [(lambda peer: offer.at[peer], landed)]
    spread_start(many, me, pairs, send, recv, 1)
    landed[me] = offer[me]
    spread_wait(many, me, pairs, send, recv, 1)
    own[...] = low16(jnp.sum(landed[...].astype(jnp.float32), 0))
    pairs = [(lambda peer: own, rows_ref)]
    spread_start(many, me, pairs, send, recv, 2)
    rows_ref[me] = own[...]
    spread_wait(many, me, pairs, send, recv, 2)


def exchange_rows(many, count_q, count_p, raw, table):
    depth = table.shape[0]
    padded = -(-depth // CHUNK) * CHUNK
    both = count_q + count_p
    return pl.pallas_call(
        functools.partial(rows_kernel, many, count_q),
        out_shape=(
            jax.ShapeDtypeStruct((many, RAW_ROWS, 128), jnp.int16),
            jax.ShapeDtypeStruct((many, both, 128), jnp.bfloat16),
        ),
        in_specs=[pl.BlockSpec(memory_space=pltpu.VMEM)] * 2,
        out_specs=[pl.BlockSpec(memory_space=pltpu.VMEM)] * 2,
        scratch_shapes=[
            pltpu.VMEM((padded, 128), jnp.bfloat16),
            pltpu.VMEM((many, both, 128), jnp.bfloat16),
            pltpu.VMEM((many, both, 128), jnp.bfloat16),
            pltpu.VMEM((both, 128), jnp.bfloat16),
            pltpu.SemaphoreType.DMA((3, many)),
            pltpu.SemaphoreType.DMA((3, many)),
        ],
        compiler_params=pltpu.CompilerParams(
            collective_id=1, has_side_effects=True, vmem_limit_bytes=VMEM_LIMIT
        ),
        name="exchange_rows",
    )(raw, table)


def norm_rows(values, gain, shift):
    center = values - jnp.mean(values, -1, keepdims=True)
    spread = jnp.mean(center * center, -1, keepdims=True)
    return center * lax.rsqrt(spread + NORM_EPS) * gain + shift


def two_heads(values):
    lane = iota(values.shape, 1)
    low = jnp.where(lane < HEAD, values, jnp.zeros_like(values))
    high = jnp.where(lane >= HEAD, values, jnp.zeros_like(values))
    return jnp.concatenate([low, high], 0)


def merge_heads(both):
    half = both.shape[0] // 2
    lane = iota((half, both.shape[1]), 1)
    return jnp.where(lane < HEAD, both[:half], both[half:])


class Sizes:
    def __init__(self, many, count_q, count_p, depth):
        self.many = many
        self.count = (count_q, count_p)
        self.depth = depth
        self.padded = -(-depth // CHUNK) * CHUNK
        self.steps = (many // (2 * WAYS), many)
        self.spans = self.steps[0] + self.steps[1]
        self.devices = (2 * WAYS, 1)
        self.queries = (2 * WAYS * count_q, count_p)
        self.keep = self.spans * 128 * SPAN * 4 <= 8 * 1024 * 1024


def prepare_tokens(sizes, table_ref, place_ref, attn_ref, vec_ref, table_t, place_t, w_kv, vec_t, codes):
    table_t[...] = jnp.zeros_like(table_t)
    depth = sizes.depth
    for cut in range(0, depth, 128):
        top = min(cut + 128, depth)
        piece = table_ref[cut:top, :]
        if top - cut < 128:
            piece = jnp.concatenate([piece, jnp.zeros((128 - (top - cut), 128), jnp.float32)], 0)
        table_t[:, cut : cut + 128] = low16(jnp.transpose(piece))
    for enc in range(2):
        place = place_ref[0, enc]
        high = low16(place)
        rest = low16(place - high.astype(jnp.float32))
        for cut in range(0, place.shape[0], 128):
            place_t[enc, 0, :, cut : cut + 128] = jnp.transpose(high[cut : cut + 128].astype(jnp.float32)).astype(jnp.bfloat16)
            place_t[enc, 1, :, cut : cut + 128] = jnp.transpose(rest[cut : cut + 128].astype(jnp.float32)).astype(jnp.bfloat16)
        for cut in range(2):
            w_kv[enc, cut * 128 : (cut + 1) * 128, :] = low16(
                jnp.transpose(attn_ref[0, enc, :, (cut + 1) * 128 : (cut + 2) * 128])
            )
        rows = jnp.concatenate(
            [vec_ref[0, enc, 0:10, :], jnp.zeros((118, 128), jnp.float32)], 0
        )
        vec_t[enc] = jnp.transpose(rows)
    row = iota((8, 128), 0)
    lane = iota((8, 128), 1)
    for way in range(WAYS):
        for line in range(16):
            where_q = lane % 64
            seq_q = (2 * way + line // 8) * sizes.count[0] + lane // 64 * 8 + line % 8 + 1
            where_p = line // 8 * 128 + lane
            seq_p = way * 8 + line % 8 + 1
            for enc, (where, seq) in enumerate(((where_q, seq_q), (where_p, seq_p))):
                codes[enc, way, :, line * 128 : (line + 1) * 128] = jnp.where(
                    row == 2, where, jnp.where(row == 3, seq, 0)
                ).astype(jnp.float32)


def gather_span(sizes, enc, step, level, first, raw_ref, table_t, place_t, codes, ranks, entries, counts):
    tri = hot(iota((128, 128), 0) < iota((128, 128), 1))
    ones = jnp.ones((128, 128), jnp.bfloat16)
    above = hot(iota((16, 16), 1) < iota((16, 16), 0))
    if enc == 1:
        found = raw_ref[step, 0:RAW_Q, :].astype(jnp.int32)
    for way in range(WAYS):
        if enc == 1:
            ids = jnp.concatenate(
                [found[way * 8 : way * 8 + 8], found[32 + way * 8 : 32 + way * 8 + 8]], 0
            )
        else:
            base = step * 2 * WAYS + 2 * way
            ids = jnp.concatenate(
                [
                    raw_ref[base, RAW_Q:RAW_ROWS, :].astype(jnp.int32)[0:8],
                    raw_ref[base + 1, RAW_Q:RAW_ROWS, :].astype(jnp.int32)[0:8],
                ],
                0,
            )
        place = ids - first
        owned = (place >= 0) & (place < sizes.depth)
        flag = hot(owned)
        inside = dot(flag, tri)
        total = dot(flag, ones)
        before = dot(above, low16(total))
        rank = jnp.where(owned, (inside + before).astype(jnp.int32) - level * SLOTS, -1)
        counts[...] = jnp.maximum(counts[...], (before + total)[8:16])
        ranks[...] = rank
        for line in range(16):
            spot = slice(line * 128, (line + 1) * 128)
            codes[enc, way, 0:1, spot] = (place[line : line + 1] // 256).astype(jnp.float32)
            codes[enc, way, 1:2, spot] = (place[line : line + 1] % 256).astype(jnp.float32)
        got = jnp.zeros((8, SLOTS), jnp.float32)
        for line in range(16):
            wide = jnp.broadcast_to(ranks[line : line + 1, :], (SLOTS, 128))
            chosen = hot(wide == iota((SLOTS, 128), 0))
            got += dot_last(low16(codes[enc, way, :, line * 128 : (line + 1) * 128]), chosen)
        entries[:, way * SLOTS : (way + 1) * SLOTS] = got
    rows = (entries[0:1, :] * 256.0 + entries[1:2, :]).astype(jnp.int32)
    where = entries[2:3, :].astype(jnp.int32)
    x = jnp.zeros((128, SPAN), jnp.float32)
    wide = jnp.broadcast_to(rows, (CHUNK, SPAN))
    for cut in range(sizes.padded // CHUNK):
        chosen = hot(wide == iota((CHUNK, SPAN), 0) + cut * CHUNK)
        x += dot(table_t[:, cut * CHUNK : (cut + 1) * CHUNK], chosen)
    chosen = hot(jnp.broadcast_to(where, (CHUNK, SPAN)) == iota((CHUNK, SPAN), 0))
    x += dot(place_t[enc, 0], chosen) + dot(place_t[enc, 1], chosen)
    center = x - jnp.mean(x, 0, keepdims=True)
    rate = lax.rsqrt(jnp.mean(center * center, 0, keepdims=True) + NORM_EPS)
    entries[7:8, :] = rate
    return center * rate


def project(enc, scaled, vec_t, w_kv):
    a_t = low16(scaled * vec_t[enc, :, 0:1] + vec_t[enc, :, 1:2])
    kv = dot(w_kv[enc], a_t)
    keys_t = low16(kv[:128])
    values_t = low16(kv[128:] + vec_t[enc, :, 3:4])
    return a_t, keys_t, values_t


def forward_kernel(
    sizes,
    raw_ref,
    rows_ref,
    table_ref,
    place_ref,
    attn_ref,
    vec_ref,
    out_ref,
    lse_ref,
    query_ref,
    kept_ref,
    entry_ref,
    levels_ref,
    table_t,
    place_t,
    w_kv,
    vec_t,
    codes,
    ranks,
    entries,
    counts,
    query_q,
    total_q,
    top_q,
    mass_q,
    total_p,
    top_p,
    mass_p,
):
    first = lax.axis_index("dp") * sizes.depth
    count_q, count_p = sizes.count
    prepare_tokens(sizes, table_ref, place_ref, attn_ref, vec_ref, table_t, place_t, w_kv, vec_t, codes)
    counts[...] = jnp.zeros_like(counts)
    for enc in range(2):
        low, high = (0, count_q) if enc == 0 else (count_q, count_q + count_p)
        w_q = low16(attn_ref[0, enc, :, 0:128])

        def ask(step, carry):
            if enc == 0:
                held = jnp.concatenate(
                    [rows_ref[step * 8 + i, low:high, :] for i in range(8)], 0
                )
            else:
                held = rows_ref[step, low:high, :]
            x = held.astype(jnp.float32) + place_ref[0, enc, 0:1, :]
            h = norm_rows(x, vec_ref[0, enc, 0:1, :], vec_ref[0, enc, 1:2, :])
            query = low16(dot(low16(h), w_q) + vec_ref[0, enc, 2:3, :])
            if enc == 0:
                query_q[step] = query
                for i in range(8):
                    query_ref[step * 8 + i, low:high, :] = query[i * count_q : (i + 1) * count_q]
            else:
                query_ref[step, low:high, :] = query
            return carry

        lax.fori_loop(0, sizes.steps[enc], ask, 0)
    total_q[...] = jnp.zeros_like(total_q)
    total_p[...] = jnp.zeros_like(total_p)
    mass_q[...] = jnp.zeros_like(mass_q)
    mass_p[...] = jnp.zeros_like(mass_p)
    top_q[...] = jnp.full_like(top_q, NEG)
    top_p[...] = jnp.full_like(top_p, NEG)

    def one_level(state):
        level = state[0]
        for enc in range(2):
            total, top, mass = (total_q, top_q, mass_q) if enc == 0 else (total_p, top_p, mass_p)

            def one_span(step, carry):
                scaled = gather_span(
                    sizes, enc, step, level, first, raw_ref, table_t, place_t, codes, ranks, entries, counts
                )
                if sizes.keep:
                    at = step if enc == 0 else sizes.steps[0] + step

                    @pl.when(level == 0)
                    def _():
                        kept_ref[at] = scaled
                        entry_ref[at] = entries[...]

                a_t, keys_t, values_t = project(enc, scaled, vec_t, w_kv)
                query = query_q[step] if enc == 0 else query_ref[step, count_q:, :]
                both = two_heads(query)
                number = query.shape[0]
                scores = dot(both, keys_t) * HEAD ** (-0.5)
                seq = entries[3:4, :].astype(jnp.int32) - 1
                line = iota(scores.shape, 0)
                line = jnp.where(line >= number, line - number, line)
                mine = line == seq
                scores = jnp.where(mine, scores, NEG)
                old = top[step][:, 0:1]
                new = jnp.maximum(old, jnp.max(scores, 1, keepdims=True))
                fade = jnp.exp(old - new)
                expo = jnp.where(mine, jnp.exp(scores - new), 0.0)
                mass[step] = mass[step] * fade + jnp.sum(expo, 1, keepdims=True)
                top[step] = jnp.broadcast_to(new, top.shape[1:])
                mixed = dot_last(low16(expo), values_t)
                total[step] = total[step] * fade + mixed
                return carry

            lax.fori_loop(0, sizes.steps[enc], one_span, 0)
        need = (jnp.max(counts[...]).astype(jnp.int32) + SLOTS - 1) // SLOTS
        return level + 1, jnp.maximum(need, 1)

    last = lax.while_loop(lambda state: state[0] < state[1], one_level, (jnp.int32(0), jnp.int32(1)))
    levels_ref[0] = last[1]
    lse_ref[...] = jnp.full_like(lse_ref, NEG)
    for enc in range(2):
        total, top, mass = (total_q, top_q, mass_q) if enc == 0 else (total_p, top_p, mass_p)

        def close(step, carry):
            bulk = mass[step]
            some = bulk > 0.0
            safe = jnp.where(some, bulk, 1.0)
            mixed = merge_heads(total[step] / safe)
            lse = jnp.where(some, top[step] + jnp.log(safe), NEG)
            if enc == 1:
                out_ref[step, count_q:, :] = low16(mixed)
                tall = jnp.concatenate([lse, jnp.full((128 - 2 * count_p, 128), NEG, jnp.float32)], 0)
                lse_ref[step, 0:1, :] = jnp.transpose(tall)[0:1, :]
            else:
                half = lse.shape[0] // 2
                for i in range(8):
                    out_ref[step * 8 + i, 0:count_q, :] = low16(mixed[i * count_q : (i + 1) * count_q])
                    tall = jnp.concatenate(
                        [
                            lse[i * count_q : (i + 1) * count_q],
                            lse[half + i * count_q : half + (i + 1) * count_q],
                            jnp.full((128 - 2 * count_q, 128), NEG, jnp.float32),
                        ],
                        0,
                    )
                    lse_ref[step * 8 + i, 1:2, :] = jnp.transpose(tall)[0:1, :]
            return carry

        lax.fori_loop(0, sizes.steps[enc], close, 0)


def token_scratch(sizes):
    return [
        pltpu.VMEM((128, sizes.padded), jnp.bfloat16),
        pltpu.VMEM((2, 2, 128, CHUNK), jnp.bfloat16),
        pltpu.VMEM((2, 256, 128), jnp.bfloat16),
        pltpu.VMEM((2, 128, 128), jnp.float32),
        pltpu.VMEM((2, WAYS, 8, 2048), jnp.float32),
        pltpu.VMEM((16, 128), jnp.int32),
        pltpu.VMEM((8, SPAN), jnp.float32),
        pltpu.VMEM((8, 128), jnp.float32),
    ]


def local_call(kernel, out_shape, inputs, scratch, name, smem_in=(), smem_out=()):
    vm = pl.BlockSpec(memory_space=pltpu.VMEM)
    sm = pl.BlockSpec(memory_space=pltpu.SMEM)
    return pl.pallas_call(
        kernel,
        out_shape=out_shape,
        in_specs=[sm if i in smem_in else vm for i in range(len(inputs))],
        out_specs=[sm if i in smem_out else vm for i in range(len(out_shape))],
        scratch_shapes=scratch,
        compiler_params=pltpu.CompilerParams(vmem_limit_bytes=VMEM_LIMIT),
        name=name,
    )(*inputs)


def tokens_forward(sizes, every, rows, table, positions, attention, vectors):
    many = sizes.many
    both = sum(sizes.count)
    kept = sizes.spans if sizes.keep else 1
    state = []
    for enc in range(2):
        tall = 2 * sizes.queries[enc]
        state += [pltpu.VMEM((sizes.steps[enc], tall, 128), jnp.float32)] * 3
    return local_call(
        functools.partial(forward_kernel, sizes),
        (
            jax.ShapeDtypeStruct((many, both, 128), jnp.bfloat16),
            jax.ShapeDtypeStruct((many, 8, 128), jnp.float32),
            jax.ShapeDtypeStruct((many, both, 128), jnp.bfloat16),
            jax.ShapeDtypeStruct((kept, 128, SPAN), jnp.float32),
            jax.ShapeDtypeStruct((kept, 8, SPAN), jnp.float32),
            jax.ShapeDtypeStruct((1,), jnp.int32),
        ),
        (every, rows, table, positions, attention, vectors),
        token_scratch(sizes)
        + [pltpu.VMEM((sizes.steps[0], sizes.queries[0], 128), jnp.bfloat16)]
        + state,
        "tokens_forward",
        smem_out=(5,),
    )


def mix_kernel(
    many, count_q, part_ref, lse_ref, mixed_ref, total_ref, landed, landed_lse, own, own_lse, send, recv
):
    me = enter(many)
    pairs = [
        (lambda peer: part_ref.at[peer], landed),
        (lambda peer: lse_ref.at[peer], landed_lse),
    ]
    spread_start(many, me, pairs, send, recv, 0)
    landed[me] = part_ref[me]
    landed_lse[me] = lse_ref[me]
    spread_wait(many, me, pairs, send, recv, 0)
    parts = landed_lse[...]
    top = jnp.max(parts, 0)
    total = top + jnp.log(jnp.sum(jnp.exp(parts - top[None]), 0))
    own_lse[...] = total
    share = jnp.exp(parts - total[None])
    columns = jnp.transpose(share.reshape(many * 8, 128))
    count_p = part_ref.shape[1] - count_q
    mixed = jnp.zeros((count_q + count_p, 128), jnp.float32)
    lane_q = iota((count_q, 128), 1)
    lane_p = iota((count_p, 128), 1)
    for peer in range(many):
        factor_p = jnp.where(
            lane_p < HEAD,
            columns[0:count_p, peer * 8 : peer * 8 + 1],
            columns[count_p : 2 * count_p, peer * 8 : peer * 8 + 1],
        )
        factor_q = jnp.where(
            lane_q < HEAD,
            columns[0:count_q, peer * 8 + 1 : peer * 8 + 2],
            columns[count_q : 2 * count_q, peer * 8 + 1 : peer * 8 + 2],
        )
        mixed += jnp.concatenate([factor_q, factor_p], 0) * landed[peer].astype(jnp.float32)
    own[...] = low16(mixed)
    pairs = [(lambda peer: own, mixed_ref), (lambda peer: own_lse, total_ref)]
    spread_start(many, me, pairs, send, recv, 2)
    mixed_ref[me] = own[...]
    total_ref[me] = own_lse[...]
    spread_wait(many, me, pairs, send, recv, 2)


def remote_call(kernel, out_shape, inputs, scratch, lanes, many, ident, name):
    return pl.pallas_call(
        kernel,
        out_shape=out_shape,
        in_specs=[pl.BlockSpec(memory_space=pltpu.VMEM)] * len(inputs),
        out_specs=[pl.BlockSpec(memory_space=pltpu.VMEM)] * len(out_shape),
        scratch_shapes=scratch
        + [pltpu.SemaphoreType.DMA((lanes, many)), pltpu.SemaphoreType.DMA((lanes, many))],
        compiler_params=pltpu.CompilerParams(
            collective_id=ident, has_side_effects=True, vmem_limit_bytes=VMEM_LIMIT
        ),
        name=name,
    )(*inputs)


def exchange_mixed(sizes, part, lse):
    many = sizes.many
    both = sum(sizes.count)
    return remote_call(
        functools.partial(mix_kernel, many, sizes.count[0]),
        (
            jax.ShapeDtypeStruct((many, both, 128), jnp.bfloat16),
            jax.ShapeDtypeStruct((many, 8, 128), jnp.float32),
        ),
        (part, lse),
        [
            pltpu.VMEM((many, both, 128), jnp.bfloat16),
            pltpu.VMEM((many, 8, 128), jnp.float32),
            pltpu.VMEM((both, 128), jnp.bfloat16),
            pltpu.VMEM((8, 128), jnp.float32),
        ],
        4,
        many,
        2,
        "exchange_mixed",
    )


def backward_kernel(
    sizes,
    levels_ref,
    raw_ref,
    query_ref,
    mixed_ref,
    lse_ref,
    grad_ref,
    kept_ref,
    entry_ref,
    table_ref,
    place_ref,
    attn_ref,
    vec_ref,
    d_query_ref,
    d_table_ref,
    d_place_ref,
    d_attn_ref,
    d_vec_ref,
    table_t,
    place_t,
    w_kv,
    vec_t,
    codes,
    ranks,
    entries,
    counts,
    lse_cols,
    acc_gain,
    acc_shift,
    acc_value,
    scaled_ref,
    d_query_q,
):
    first = lax.axis_index("dp") * sizes.depth
    count_q, count_p = sizes.count
    prepare_tokens(sizes, table_ref, place_ref, attn_ref, vec_ref, table_t, place_t, w_kv, vec_t, codes)
    counts[...] = jnp.zeros_like(counts)
    lse_cols[...] = jnp.transpose(lse_ref[...].reshape(sizes.many * 8, 128))
    d_table_ref[...] = jnp.zeros_like(d_table_ref)
    d_place_ref[...] = jnp.zeros_like(d_place_ref)
    d_attn_ref[...] = jnp.zeros_like(d_attn_ref)
    d_query_ref[...] = jnp.zeros_like(d_query_ref)
    d_query_q[...] = jnp.zeros_like(d_query_q)
    acc_gain[...] = jnp.zeros_like(acc_gain)
    acc_shift[...] = jnp.zeros_like(acc_shift)
    acc_value[...] = jnp.zeros_like(acc_value)

    def one_level(level, carry_level):
        for enc in range(2):
            w_all = low16(attn_ref[0, enc, :, 128:384])

            def one_span(step, carry):
                at = step if enc == 0 else sizes.steps[0] + step
                if sizes.keep:

                    @pl.when(level == 0)
                    def _():
                        scaled_ref[...] = kept_ref[at]
                        entries[...] = entry_ref[at]

                    @pl.when(level > 0)
                    def _():
                        scaled_ref[...] = gather_span(
                            sizes, enc, step, level, first, raw_ref, table_t, place_t, codes, ranks, entries, counts
                        )

                else:
                    scaled_ref[...] = gather_span(
                        sizes, enc, step, level, first, raw_ref, table_t, place_t, codes, ranks, entries, counts
                    )
                scaled = scaled_ref[...]
                a_t, keys_t, values_t = project(enc, scaled, vec_t, w_kv)
                if enc == 0:
                    query = jnp.concatenate([query_ref[step * 8 + i, 0:count_q, :] for i in range(8)], 0)
                    grad = jnp.concatenate([grad_ref[step * 8 + i, 0:count_q, :] for i in range(8)], 0)
                    mixed = jnp.concatenate([mixed_ref[step * 8 + i, 0:count_q, :] for i in range(8)], 0)
                    pieces = []
                    for head in range(2):
                        for i in range(8):
                            line = lse_ref[step * 8 + i]
                            tall = jnp.transpose(
                                jnp.concatenate([line, jnp.zeros((120, 128), jnp.float32)], 0)
                            )
                            pieces.append(tall[head * count_q : (head + 1) * count_q, 1:2])
                    lse = jnp.concatenate(pieces, 0)
                else:
                    query = query_ref[step, count_q:, :]
                    grad = grad_ref[step, count_q:, :]
                    mixed = mixed_ref[step, count_q:, :]
                    tall = jnp.transpose(
                        jnp.concatenate([lse_ref[step], jnp.zeros((120, 128), jnp.float32)], 0)
                    )
                    lse = tall[0 : 2 * count_p, 0:1]
                number = query.shape[0]
                both = two_heads(query)
                grads = two_heads(grad)
                level_sum = jnp.sum(
                    grads.astype(jnp.float32) * jnp.concatenate([mixed, mixed], 0).astype(jnp.float32),
                    1,
                    keepdims=True,
                )
                scores = dot(both, keys_t) * HEAD ** (-0.5)
                seq = entries[3:4, :].astype(jnp.int32) - 1
                line = iota(scores.shape, 0)
                line = jnp.where(line >= number, line - number, line)
                mine = line == seq
                probs = jnp.where(mine, jnp.exp(jnp.where(mine, scores, NEG) - lse), 0.0)
                d_probs = dot(grads, values_t)
                d_scores = low16(probs * (d_probs - level_sum))
                d_values = low16(dot_rows(grads, low16(probs)))
                d_keys = low16(dot_rows(both, d_scores) * HEAD ** (-0.5))
                d_query = merge_heads(dot_last(d_scores, keys_t)) * HEAD ** (-0.5)
                if enc == 0:
                    d_query_q[step] += d_query
                else:
                    d_query_ref[step, count_q:, :] += d_query
                d_kv = jnp.concatenate([d_keys, d_values], 0)
                d_attn_ref[enc] += dot_last(a_t, d_kv)
                acc_value[enc] += d_values.astype(jnp.float32)
                d_h = dot(w_all, d_kv)
                acc_gain[enc] += d_h * scaled
                acc_shift[enc] += d_h
                d_scaled = d_h * vec_t[enc, :, 0:1]
                center = d_scaled - jnp.mean(d_scaled, 0, keepdims=True)
                slope = jnp.mean(d_scaled * scaled, 0, keepdims=True)
                d_x = low16((center - scaled * slope) * entries[7:8, :])
                rows = (entries[0:1, :] * 256.0 + entries[1:2, :]).astype(jnp.int32)
                where = entries[2:3, :].astype(jnp.int32)
                chosen = hot(jnp.broadcast_to(where, (CHUNK, SPAN)) == iota((CHUNK, SPAN), 0))
                d_place_ref[enc] += dot_last(d_x, chosen)
                wide = jnp.broadcast_to(rows, (CHUNK, SPAN))
                for cut in range(sizes.padded // CHUNK):
                    spot = slice(cut * CHUNK, (cut + 1) * CHUNK)
                    chosen = hot(wide == iota((CHUNK, SPAN), 0) + cut * CHUNK)
                    d_table_ref[:, spot] += dot_last(d_x, chosen)
                return carry

            lax.fori_loop(0, sizes.steps[enc], one_span, 0)
        return carry_level

    lax.fori_loop(0, levels_ref[0], one_level, 0)

    def give(step, carry):
        for i in range(8):
            d_query_ref[step * 8 + i, 0:count_q, :] = d_query_q[step][i * count_q : (i + 1) * count_q]
        return carry

    lax.fori_loop(0, sizes.steps[0], give, 0)
    d_vec_ref[...] = jnp.zeros_like(d_vec_ref)
    for enc in range(2):
        for row, acc in enumerate((acc_gain, acc_shift, acc_value)):
            tall = jnp.broadcast_to(jnp.sum(acc[enc], 1, keepdims=True), (128, 128))
            d_vec_ref[enc * 4 + row : enc * 4 + row + 1, :] = jnp.transpose(tall)[0:1, :]


def tokens_backward(sizes, levels, every, query, mixed, lse, grad, kept, entry, table, positions, attention, vectors):
    many = sizes.many
    both = sum(sizes.count)
    return local_call(
        functools.partial(backward_kernel, sizes),
        (
            jax.ShapeDtypeStruct((many, both, 128), jnp.float32),
            jax.ShapeDtypeStruct((128, sizes.padded), jnp.float32),
            jax.ShapeDtypeStruct((2, 128, CHUNK), jnp.float32),
            jax.ShapeDtypeStruct((2, 128, 256), jnp.float32),
            jax.ShapeDtypeStruct((8, 128), jnp.float32),
        ),
        (levels, every, query, mixed, lse, grad, kept, entry, table, positions, attention, vectors),
        token_scratch(sizes)
        + [
            pltpu.VMEM((128, many * 8), jnp.float32),
            pltpu.VMEM((2, 128, SPAN), jnp.float32),
            pltpu.VMEM((2, 128, SPAN), jnp.float32),
            pltpu.VMEM((2, 128, SPAN), jnp.float32),
            pltpu.VMEM((128, SPAN), jnp.float32),
            pltpu.VMEM((sizes.steps[0], sizes.queries[0], 128), jnp.float32),
        ],
        "tokens_backward",
        smem_in=(0,),
    )


def sum_kernel(
    many,
    query_ref,
    slice_ref,
    vec_ref,
    query_out,
    slice_out,
    vec_out,
    landed_query,
    landed_slice,
    own_query,
    own_slice,
    send,
    recv,
):
    me = enter(many)
    pairs = [
        (lambda peer: query_ref.at[peer], landed_query),
        (lambda peer: slice_ref.at[peer], landed_slice),
        (lambda peer: vec_ref, vec_out),
    ]
    spread_start(many, me, pairs, send, recv, 0)
    landed_query[me] = query_ref[me]
    landed_slice[me] = slice_ref[me]
    vec_out[me] = vec_ref[...]
    spread_wait(many, me, pairs, send, recv, 0)
    own_query[...] = low16(jnp.sum(landed_query[...].astype(jnp.float32), 0))
    own_slice[...] = jnp.sum(landed_slice[...].astype(jnp.float32), 0).astype(own_slice.dtype)
    pairs = [(lambda peer: own_query, query_out), (lambda peer: own_slice, slice_out)]
    spread_start(many, me, pairs, send, recv, 3)
    query_out[me] = own_query[...]
    slice_out[me] = own_slice[...]
    spread_wait(many, me, pairs, send, recv, 3)


def exchange_sums(many, query, slices, vec):
    one = query.shape[1:]
    cut = slices.shape[1:]
    return remote_call(
        functools.partial(sum_kernel, many),
        (
            jax.ShapeDtypeStruct((many,) + one, jnp.bfloat16),
            jax.ShapeDtypeStruct((many,) + cut, slices.dtype),
            jax.ShapeDtypeStruct((many,) + vec.shape, jnp.float32),
        ),
        (query, slices, vec),
        [
            pltpu.VMEM((many,) + one, query.dtype),
            pltpu.VMEM((many,) + cut, slices.dtype),
            pltpu.VMEM(one, jnp.bfloat16),
            pltpu.VMEM(cut, slices.dtype),
        ],
        5,
        many,
        3,
        "exchange_sums",
    )


def scalar_kernel(many, value_ref, out_ref, send, recv):
    me = enter(many)
    pairs = [(lambda peer: value_ref, out_ref)]
    spread_start(many, me, pairs, send, recv, 0)
    out_ref[me] = value_ref[...]
    spread_wait(many, me, pairs, send, recv, 0)


def exchange_scalar(many, value):
    tile = jnp.broadcast_to(value.reshape(1, 1), (8, 128))
    (got,) = remote_call(
        functools.partial(scalar_kernel, many),
        (jax.ShapeDtypeStruct((many, 8, 128), jnp.float32),),
        (tile,),
        [],
        1,
        many,
        4,
        "exchange_scalar",
    )
    return jnp.sum(got[:, 0, 0])


def class_forward(rows, mixed, place, attn_w, ffn_w, vec):
    width = rows.shape[1]
    h_embed = layer_norm(rows.astype(jnp.float32) + place[:1], vec[0], vec[1])
    x_attn = h_embed + (dot(mixed, low16(attn_w[:, 3 * width :])) + vec[4])
    h_attn = layer_norm(x_attn, vec[5], vec[6])
    h_low = low16(h_attn)
    pre = dot(h_low, low16(ffn_w[0])) + vec[10:].reshape(-1)
    act = low16(gelu_tanh(pre))
    x_ffn = h_attn + (dot_last(act, low16(ffn_w[1])) + vec[7])
    h_out = layer_norm(x_ffn, vec[8], vec[9])
    return low16(h_out), (x_attn, h_low, pre, act, x_ffn)


def class_backward(kept, mixed, attn_w, ffn_w, vec, d_cls):
    x_attn, h_low, pre, act, x_ffn = kept
    width = x_attn.shape[1]
    unused, out_back = jax.vjp(layer_norm, x_ffn, vec[8], vec[9])
    d_x_ffn, d_gain_two, d_shift_two = out_back(d_cls)
    d_branch = low16(d_x_ffn)
    d_down_bias = jnp.sum(d_branch, 0, dtype=jnp.float32)
    d_down = dot_rows(d_branch, act)
    d_act = dot(d_branch, low16(ffn_w[1]))
    unused, gelu_back = jax.vjp(gelu_tanh, pre)
    d_pre = low16(gelu_back(d_act)[0])
    d_up_bias = jnp.sum(d_pre, 0, dtype=jnp.float32)
    d_up = dot_rows(h_low, d_pre)
    d_h_attn = d_x_ffn + dot_last(d_pre, low16(ffn_w[0]))
    unused, attn_back = jax.vjp(layer_norm, x_attn, vec[5], vec[6])
    d_x_attn, d_gain_one, d_shift_one = attn_back(d_h_attn)
    d_proj = low16(d_x_attn)
    d_out_bias = jnp.sum(d_proj, 0, dtype=jnp.float32)
    d_w_out = dot_rows(mixed, d_proj)
    d_mixed = low16(dot_last(d_proj, low16(attn_w[:, 3 * width :])))
    rows = (d_out_bias, d_gain_one, d_shift_one, d_down_bias, d_gain_two, d_shift_two)
    return d_mixed, d_x_attn, d_w_out, jnp.stack([d_up, d_down]), rows, d_up_bias


def softmax_terms(scores, drop, target, weight, count, axis):
    masked = jnp.where(drop, MASKED, scores)
    top = jnp.max(masked, axis, keepdims=True)
    expo = jnp.exp(masked - top)
    total = jnp.sum(expo, axis, keepdims=True)
    lse = top + jnp.log(total)
    picked = jnp.sum(jnp.where(target, scores, 0.0), axis, keepdims=True)
    loss = jnp.sum(weight * (lse - picked))
    grad = low16((weight / count) * (expo / total - target.astype(jnp.float32)))
    return grad, loss


def score_stage(every_q, every_p, keys_q, keys_p, valid_q):
    count = jnp.maximum(jnp.sum(valid_q).astype(jnp.float32), 1.0)
    scale = every_q.shape[1] ** (-0.5)
    index_q = jnp.arange(every_q.shape[0])[:, None]
    index_p = jnp.arange(every_p.shape[0])[None, :]
    scores = dot_last(every_q, every_p) * scale
    same = keys_q[:, None] == keys_p[None, :]
    target_qp = index_p == 2 * index_q
    valid = valid_q.astype(jnp.float32)[:, None]
    grad_qp, loss_qp = softmax_terms(scores, same & ~target_qp, target_qp, valid, count, 1)
    target_pq = index_p // 2 == index_q
    drop_pq = (same | (valid_q[:, None] == 0)) & ~target_pq
    owner_valid = jnp.repeat(valid_q, 2)
    weight_p = jnp.where(index_p[0] % 2 == 0, owner_valid, 0).astype(jnp.float32)[None, :]
    grad_pq, loss_pq = softmax_terms(scores, drop_pq, target_pq, weight_p, count, 0)
    d_q = (dot(grad_qp, every_p) + dot(grad_pq, every_p)) * scale
    d_p = (dot_rows(grad_pq, every_q) + dot_rows(grad_qp, every_q)) * scale
    return d_q, d_p, loss_qp + loss_pq, count


def adam(weight, grad, first, second):
    first_new = BETA_ONE * first + (1.0 - BETA_ONE) * grad
    second_new = BETA_TWO * second + (1.0 - BETA_TWO) * grad * grad
    fix_one = 1.0 - BETA_ONE**STEP
    fix_two = 1.0 - BETA_TWO**STEP
    ratio = first_new / fix_one / (jnp.sqrt(second_new / fix_two) + ADAM_EPS)
    return (first_new, second_new, weight - INNER_RATE * (ratio + WEIGHT_DECAY * weight))


def body(
    question_ids,
    passage_ids,
    question_lengths,
    passage_lengths,
    question_keys,
    passage_keys,
    question_valid,
    word_table,
    positions,
    attention,
    feedforward,
    vectors,
    word_first,
    positions_first,
    attention_first,
    feedforward_first,
    vectors_first,
    word_second,
    positions_second,
    attention_second,
    feedforward_second,
    vectors_second,
    word_anchor,
    positions_anchor,
    attention_anchor,
    feedforward_anchor,
    vectors_anchor,
    word_outer,
    positions_outer,
    attention_outer,
    feedforward_outer,
    vectors_outer,
):
    width = word_table.shape[2]
    many = lax.axis_size("dp")
    count_q, seq_q = question_ids.shape
    count_p, seq_p = passage_ids.shape
    counts = (count_q, count_p)
    table = word_table[0]
    sizes = Sizes(many, count_q, count_p, table.shape[0])
    ids_q = jnp.where(jnp.arange(seq_q)[None, :] < question_lengths[:, None], question_ids, -1)
    ids_p = jnp.where(jnp.arange(seq_p)[None, :] < passage_lengths[:, None], passage_ids, -1)
    half = count_q // 2
    flags = jnp.concatenate([question_keys, question_valid, passage_keys])
    flags = jnp.pad(flags, (0, 8 * 128 - flags.size)).reshape(8, 128)
    raw = jnp.concatenate(
        [
            ids_p[:, :128],
            ids_p[:, 128:],
            jnp.concatenate([ids_q[:half], ids_q[half:]], 1),
            flags,
        ]
    ).astype(jnp.int16)
    every, class_rows = exchange_rows(many, count_q, count_p, raw, table)
    flags_all = every[:, RAW_FLAGS, :].astype(jnp.int32)
    keys_q = flags_all[:, :count_q].reshape(-1)
    valid_all = flags_all[:, count_q : 2 * count_q].reshape(-1)
    keys_p = flags_all[:, 2 * count_q : 2 * count_q + count_p].reshape(-1)
    part, lse_part, query, kept, entry, levels = tokens_forward(
        sizes, every, class_rows, table, positions, attention, vectors
    )
    mixed_all, lse_all = exchange_mixed(sizes, part, lse_part)
    cuts = ((0, count_q), (count_q, count_q + count_p))
    cls, class_kept, mixes, class_x = ([], [], [], [])
    for enc in range(2):
        low, high = cuts[enc]
        rows = class_rows[:, low:high].reshape(-1, width)
        mixed = mixed_all[:, low:high].reshape(-1, width)
        low_cls, kept_cls = class_forward(
            rows, mixed, positions[0, enc], attention[0, enc], feedforward[0, enc], vectors[0, enc]
        )
        cls.append(low_cls)
        class_kept.append(kept_cls)
        mixes.append(mixed)
        class_x.append(rows.astype(jnp.float32) + positions[0, enc, :1])
    d_q, d_p, loss_total, count = score_stage(cls[0], cls[1], keys_q, keys_p, valid_all)
    d_cls = (d_q, d_p)
    finals, grad_parts, firsts_x = ([], [], [])
    for enc in range(2):
        d_mixed, d_x_attn, d_w_out, d_ffn, rows_mid, d_up_bias = class_backward(
            class_kept[enc], mixes[enc], attention[0, enc], feedforward[0, enc], vectors[0, enc], d_cls[enc]
        )
        grad_parts.append(d_mixed.reshape(many, counts[enc], width))
        firsts_x.append(d_x_attn)
        finals.append((d_w_out, d_ffn, rows_mid, d_up_bias))
    grad_all = jnp.concatenate(grad_parts, 1)
    d_query, d_table_t, d_place_t, d_kv, d_first = tokens_backward(
        sizes, levels, every, query, mixed_all, lse_all, grad_all, kept, entry, table, positions, attention, vectors
    )
    lines = 1024 // many
    kind = jnp.bfloat16 if lines % 16 == 0 else jnp.float32
    slices = jnp.concatenate(
        [d_place_t[:, :, :128], d_place_t[:, :, 128:], d_kv[:, :, :128], d_kv[:, :, 128:]], 1
    )
    slices = slices.reshape(many, lines, 128).astype(kind)
    query_sum, slice_sum, first_sum = exchange_sums(many, low16(d_query), slices, d_first)
    slice_sum = slice_sum.reshape(2, 4, 128, 128).astype(jnp.float32)
    first_sum = jnp.sum(first_sum, 0)
    first_row = lax.axis_index("dp") * table.shape[0]
    table_grad = d_table_t[:, : table.shape[0]].T
    places, attns, vecs = ([], [], [])
    for enc in range(2):
        low, high = cuts[enc]
        d_w_out, d_ffn, rows_mid, d_up_bias = finals[enc]
        dq = query_sum[:, low:high].reshape(-1, width)
        a_low = low16(layer_norm(class_x[enc], vectors[0, enc, 0], vectors[0, enc, 1]))
        d_w_q = dot_rows(a_low, dq)
        d_h = firsts_x[enc] + dot_last(dq, low16(attention[0, enc, :, :width]))
        unused, embed_back = jax.vjp(layer_norm, class_x[enc], vectors[0, enc, 0], vectors[0, enc, 1])
        d_x, d_gain, d_shift = embed_back(d_h)
        if enc == 0:
            first_ids = jnp.concatenate([every[:, RAW_Q:RAW_FLAGS, 0], every[:, RAW_Q:RAW_FLAGS, 64]], 1)
        else:
            first_ids = every[:, :32, 0]
        chosen = first_ids.reshape(-1)[None, :].astype(jnp.int32) == first_row + jnp.arange(table.shape[0])[:, None]
        high_part = low16(d_x)
        rest = low16(d_x - high_part.astype(jnp.float32))
        chosen = chosen.astype(jnp.bfloat16)
        table_grad = table_grad + dot(chosen, high_part) + dot(chosen, rest)
        d_place = jnp.concatenate([slice_sum[enc, 0].T, slice_sum[enc, 1].T], 0)
        d_place = d_place.at[0].add(jnp.sum(d_x, 0))
        places.append(d_place)
        attns.append(jnp.concatenate([d_w_q, slice_sum[enc, 2], slice_sum[enc, 3], d_w_out], 1))
        top_rows = [
            first_sum[enc * 4] + d_gain,
            first_sum[enc * 4 + 1] + d_shift,
            jnp.sum(dq.astype(jnp.float32), 0),
            first_sum[enc * 4 + 2],
        ]
        vecs.append(jnp.concatenate([jnp.stack(top_rows + list(rows_mid)), d_up_bias.reshape(-1, width)]))
    table_sq = exchange_scalar(many, jnp.sum(table_grad * table_grad))
    place_grad, attn_grad, vec_grad = (jnp.stack(places), jnp.stack(attns), jnp.stack(vecs))
    ffn_grad = jnp.stack([finals[0][1], finals[1][1]])
    grads = (table_grad[None], place_grad[None], attn_grad[None], ffn_grad[None], vec_grad[None])
    norm = jnp.sqrt(table_sq + sum((jnp.sum(g * g) for g in grads[1:])))
    factor = CLIP_LIMIT / jnp.maximum(norm, CLIP_LIMIT)
    weights = (word_table, positions, attention, feedforward, vectors)
    firsts = (word_first, positions_first, attention_first, feedforward_first, vectors_first)
    seconds = (word_second, positions_second, attention_second, feedforward_second, vectors_second)
    anchors = (word_anchor, positions_anchor, attention_anchor, feedforward_anchor, vectors_anchor)
    outers = (word_outer, positions_outer, attention_outer, feedforward_outer, vectors_outer)
    first_new, second_new, inner_new = ([], [], [])
    for kind in range(5):
        fresh_first, fresh_second, stepped = adam(
            weights[kind], grads[kind] * factor, firsts[kind], seconds[kind]
        )
        first_new.append(fresh_first)
        second_new.append(fresh_second)
        inner_new.append(stepped)
    differences = tuple((anchors[kind] - inner_new[kind][0] for kind in range(5)))
    summed = lax.psum(
        (differences[0], differences[1], differences[2], differences[3], differences[4]), "grp"
    )
    groups = lax.axis_size("grp")
    averages, outer_next, weight_next = ([], [], [])
    for kind in range(5):
        average = summed[kind] / groups
        momentum = OUTER_MU * outers[kind] + average
        outer_weight = anchors[kind] - OUTER_RATE * (average + OUTER_MU * momentum)
        averages.append(average)
        outer_next.append(momentum)
        weight_next.append(outer_weight[None])
    return (
        loss_total.reshape(1),
        count.reshape(1),
        norm.reshape(1),
        first_new[0],
        first_new[1],
        first_new[2],
        first_new[3],
        first_new[4],
        second_new[0],
        second_new[1],
        second_new[2],
        second_new[3],
        second_new[4],
        averages[0],
        averages[1],
        averages[2],
        averages[3],
        averages[4],
        outer_next[0],
        outer_next[1],
        outer_next[2],
        outer_next[3],
        outer_next[4],
        weight_next[0],
        weight_next[1],
        weight_next[2],
        weight_next[3],
        weight_next[4],
    )


def solution(mesh):
    placed = (
        P(("grp", "dp"), None),
        P(("grp", "dp"), None),
        P(("grp", "dp")),
        P(("grp", "dp")),
        P(("grp", "dp")),
        P(("grp", "dp")),
        P(("grp", "dp")),
        P("grp", "dp", None),
        P("grp", None, None, None),
        P("grp", None, None, None),
        P("grp", None, None, None, None),
        P("grp", None, None, None),
        P("grp", "dp", None),
        P("grp", None, None, None),
        P("grp", None, None, None),
        P("grp", None, None, None, None),
        P("grp", None, None, None),
        P("grp", "dp", None),
        P("grp", None, None, None),
        P("grp", None, None, None),
        P("grp", None, None, None, None),
        P("grp", None, None, None),
        P("dp", None),
        P(),
        P(),
        P(),
        P(),
        P("dp", None),
        P(),
        P(),
        P(),
        P(),
    )
    return jax.shard_map(
        body,
        mesh=mesh,
        in_specs=placed,
        out_specs=(
            P("grp"),
            P("grp"),
            P("grp"),
            P("grp", "dp", None),
            P("grp", None, None, None),
            P("grp", None, None, None),
            P("grp", None, None, None, None),
            P("grp", None, None, None),
            P("grp", "dp", None),
            P("grp", None, None, None),
            P("grp", None, None, None),
            P("grp", None, None, None, None),
            P("grp", None, None, None),
            P("dp", None),
            P(),
            P(),
            P(),
            P(),
            P("dp", None),
            P(),
            P(),
            P(),
            P(),
            P("grp", "dp", None),
            P("grp", None, None, None),
            P("grp", None, None, None),
            P("grp", None, None, None, None),
            P("grp", None, None, None),
        ),
        check_vma=False,
    )
```

```python
import functools
import math

import jax
import jax.numpy as jnp
from jax import lax
from jax.experimental import pallas as pl
from jax.experimental.pallas import tpu as pltpu
from jax.sharding import PartitionSpec as P

HEAD = 64
STEP = 5


NORM_EPS = 1e-05
MASKED = -1000000000.0
BETA_ONE = 0.9
BETA_TWO = 0.999
INNER_RATE = 0.05
WEIGHT_DECAY = 0.01
ADAM_EPS = 1e-08
CLIP_LIMIT = 0.01
OUTER_RATE = 0.7
OUTER_MU = 0.9
CONTRACT_ROWS = (((0,), (0,)), ((), ()))
CONTRACT_LAST = (((1,), (1,)), ((), ()))


def layer_norm(values, gain, shift):
    center = values - jnp.mean(values, -1, keepdims=True)
    spread = jnp.mean(center * center, -1, keepdims=True)
    return center * lax.rsqrt(spread + NORM_EPS) * gain + shift


def gelu_tanh(values):
    return jax.nn.gelu(values, approximate=True)


def low16(values):
    return values.astype(jnp.bfloat16)


NEG = -1e30
MESH = pl.DeviceIdType.MESH
VMEM_LIMIT = 60 * 1024 * 1024
WAYS = 4
SLOTS = 128
SPAN = WAYS * SLOTS
CHUNK = 256
RAW_Q = 64
RAW_FLAGS = 72
RAW_ROWS = 80


def enter(many):
    me = lax.axis_index("dp")
    barrier = pltpu.get_barrier_semaphore()

    def greet(step, carry):
        peer = lax.rem(me + step, many)
        pl.semaphore_signal(barrier, inc=1, device_id={"dp": peer}, device_id_type=MESH)
        return carry

    lax.fori_loop(1, many, greet, 0)
    pl.semaphore_wait(barrier, many - 1)
    return me


def copy_to(peer, src, dst, send, recv):
    return pltpu.make_async_remote_copy(
        src_ref=src,
        dst_ref=dst,
        send_sem=send,
        recv_sem=recv,
        device_id={"dp": peer},
        device_id_type=MESH,
    )


def spread_start(many, me, pairs, send, recv, slot):
    def step_start(step, carry):
        peer = lax.rem(me + step, many)
        for index, (source, landing) in enumerate(pairs):
            copy_to(
                peer,
                source(peer),
                landing.at[me],
                send.at[slot + index, peer],
                recv.at[slot + index, me],
            ).start()
        return carry

    lax.fori_loop(1, many, step_start, 0)


def spread_wait(many, me, pairs, send, recv, slot):
    def step_wait(step, carry):
        peer = lax.rem(me + step, many)
        for index, (source, landing) in enumerate(pairs):
            copy = copy_to(
                peer,
                source(peer),
                landing.at[peer],
                send.at[slot + index, peer],
                recv.at[slot + index, peer],
            )
            copy.wait_recv()
            copy.wait_send()
        return carry

    lax.fori_loop(1, many, step_wait, 0)


def dot(left, right):
    return jnp.dot(left, right, preferred_element_type=jnp.float32)


def dot_rows(left, right):
    return lax.dot_general(left, right, CONTRACT_ROWS, preferred_element_type=jnp.float32)


def dot_last(left, right):
    return lax.dot_general(left, right, CONTRACT_LAST, preferred_element_type=jnp.float32)


def iota(shape, axis):
    return lax.broadcasted_iota(jnp.int32, shape, axis)


def hot(mask):
    return jnp.where(mask, 1.0, 0.0).astype(jnp.bfloat16)


def rows_kernel(
    many, count_q, raw_ref, table_ref, every_ref, rows_ref, low_ref, offer, landed, own, send, recv
):
    me = enter(many)
    raw_pairs = [(lambda peer: raw_ref, every_ref)]
    spread_start(many, me, raw_pairs, send, recv, 0)
    every_ref[me] = raw_ref[...]
    depth = table_ref.shape[0]
    low_ref[...] = jnp.zeros_like(low_ref)
    low_ref[0:depth, :] = low16(table_ref[...])
    padded = low_ref.shape[0]
    spread_wait(many, me, raw_pairs, send, recv, 0)
    first = me * depth

    def pick(step, carry):
        peer = lax.rem(me + step, many)
        found = every_ref[peer].astype(jnp.int32)
        ask = jnp.concatenate(
            [
                found[RAW_Q : RAW_Q + count_q // 2, 0:1],
                found[RAW_Q : RAW_Q + count_q // 2, 64:65],
                found[0 : RAW_Q // 2, 0:1],
            ],
            0,
        )
        place = ask - first
        inside = (place >= 0) & (place < depth)
        spot = jnp.where(inside, place, -1)
        total = jnp.zeros((spot.shape[0], 128), jnp.float32)
        for cut in range(padded // CHUNK):
            wide = jnp.broadcast_to(spot, (spot.shape[0], CHUNK))
            chosen = hot(wide == iota(wide.shape, 1) + cut * CHUNK)
            total += dot(chosen, low_ref[cut * CHUNK : (cut + 1) * CHUNK, :])
        offer[peer] = low16(total)
        return carry

    lax.fori_loop(0, many, pick, 0)
    pairs = [(lambda peer: offer.at[peer], landed)]
    spread_start(many, me, pairs, send, recv, 1)
    landed[me] = offer[me]
    spread_wait(many, me, pairs, send, recv, 1)
    own[...] = low16(jnp.sum(landed[...].astype(jnp.float32), 0))
    pairs = [(lambda peer: own, rows_ref)]
    spread_start(many, me, pairs, send, recv, 2)
    rows_ref[me] = own[...]
    spread_wait(many, me, pairs, send, recv, 2)


def exchange_rows(many, count_q, count_p, raw, table):
    depth = table.shape[0]
    padded = -(-depth // CHUNK) * CHUNK
    both = count_q + count_p
    return pl.pallas_call(
        functools.partial(rows_kernel, many, count_q),
        out_shape=(
            jax.ShapeDtypeStruct((many, RAW_ROWS, 128), jnp.int16),
            jax.ShapeDtypeStruct((many, both, 128), jnp.bfloat16),
        ),
        in_specs=[pl.BlockSpec(memory_space=pltpu.VMEM)] * 2,
        out_specs=[pl.BlockSpec(memory_space=pltpu.VMEM)] * 2,
        scratch_shapes=[
            pltpu.VMEM((padded, 128), jnp.bfloat16),
            pltpu.VMEM((many, both, 128), jnp.bfloat16),
            pltpu.VMEM((many, both, 128), jnp.bfloat16),
            pltpu.VMEM((both, 128), jnp.bfloat16),
            pltpu.SemaphoreType.DMA((3, many)),
            pltpu.SemaphoreType.DMA((3, many)),
        ],
        compiler_params=pltpu.CompilerParams(
            collective_id=1, has_side_effects=True, vmem_limit_bytes=VMEM_LIMIT
        ),
        name="exchange_rows",
    )(raw, table)


def norm_rows(values, gain, shift):
    center = values - jnp.mean(values, -1, keepdims=True)
    spread = jnp.mean(center * center, -1, keepdims=True)
    return center * lax.rsqrt(spread + NORM_EPS) * gain + shift


def two_heads(values):
    lane = iota(values.shape, 1)
    low = jnp.where(lane < HEAD, values, jnp.zeros_like(values))
    high = jnp.where(lane >= HEAD, values, jnp.zeros_like(values))
    return jnp.concatenate([low, high], 0)


def merge_heads(both):
    half = both.shape[0] // 2
    lane = iota((half, both.shape[1]), 1)
    return jnp.where(lane < HEAD, both[:half], both[half:])


class Sizes:
    def __init__(self, many, count_q, count_p, depth):
        self.many = many
        self.count = (count_q, count_p)
        self.depth = depth
        self.padded = -(-depth // CHUNK) * CHUNK
        self.steps = (many // (2 * WAYS), many)
        self.spans = self.steps[0] + self.steps[1]
        self.devices = (2 * WAYS, 1)
        self.queries = (2 * WAYS * count_q, count_p)
        self.lines = 1024 // many
        self.kind = jnp.bfloat16 if self.lines % 16 == 0 else jnp.float32
        self.keep = self.spans * 136 * SPAN * 4 <= 8 * 1024 * 1024


def prepare_tokens(sizes, table_ref, place_ref, attn_ref, vec_ref, table_t, place_t, w_kv, vec_t):
    table_t[...] = jnp.zeros_like(table_t)
    depth = sizes.depth
    for cut in range(0, depth, 128):
        top = min(cut + 128, depth)
        piece = table_ref[cut:top, :]
        if top - cut < 128:
            piece = jnp.concatenate([piece, jnp.zeros((128 - (top - cut), 128), jnp.float32)], 0)
        table_t[:, cut : cut + 128] = low16(jnp.transpose(piece))
    for enc in range(2):
        place = place_ref[0, enc]
        for cut in range(0, place.shape[0], 128):
            turned = jnp.transpose(place[cut : cut + 128])
            high = low16(turned)
            place_t[enc, 0, :, cut : cut + 128] = high
            place_t[enc, 1, :, cut : cut + 128] = low16(turned - high.astype(jnp.float32))


def prepare_weights(attn_ref, vec_ref, w_kv, vec_t):
    for enc in range(2):
        for cut in range(2):
            w_kv[enc, cut * 128 : (cut + 1) * 128, :] = low16(
                jnp.transpose(attn_ref[0, enc, :, (cut + 1) * 128 : (cut + 2) * 128])
            )
        rows = jnp.concatenate(
            [vec_ref[0, enc, 0:10, :], jnp.zeros((118, 128), jnp.float32)], 0
        )
        vec_t[enc] = jnp.transpose(rows)


def lane_pick(values, lanes):
    return jnp.take_along_axis(values, lanes, axis=1, mode="promise_in_bounds")


def pack_span(sizes, enc, step, level, first, raw_ref, entries, counts):
    if enc == 1:
        ids = raw_ref[step, 0:RAW_Q, :].astype(jnp.int32)
    else:
        ids = jnp.concatenate(
            [
                raw_ref[step * 8 + i, RAW_Q:RAW_ROWS, :].astype(jnp.int32)[0:8]
                for i in range(8)
            ],
            0,
        )
    place = ids - first
    owned = (place >= 0) & (place < sizes.depth)
    flag = hot(owned)
    tall = iota((64, 64), 0)
    inside = dot(flag, hot(iota((128, 128), 0) <= iota((128, 128), 1)))
    total = dot(flag, jnp.ones((128, 128), jnp.bfloat16))
    before = dot(hot(iota((64, 64), 1) < tall), low16(total))
    counts[...] = jnp.maximum(counts[...], (before + total)[56:64])
    reached = (inside + before).astype(jnp.int32)
    start = before.astype(jnp.int32)
    stop = (before + total).astype(jnp.int32)
    line = iota((64, 128), 0)
    for window in range(WAYS):
        slot = iota((64, 128), 1) + (window * SLOTS + level * SPAN)
        lane = jnp.zeros((64, 128), jnp.int32)
        for jump in (64, 32, 16, 8, 4, 2, 1):
            seen = lane_pick(reached, lane + (jump - 1))
            lane = jnp.where(seen <= slot, lane + jump, lane)
        row = lane_pick(place, lane)
        if enc == 1:
            where = (line >> 5) * 128 + lane
            seq = (line & 31) + 1
        else:
            where = lane & 63
            seq = (line >> 3) * sizes.count[0] + (lane >> 6) * 8 + (line & 7) + 1
        code = (row << 16) + (where << 8) + seq
        code = jnp.where((slot >= start) & (slot < stop), code, 0)
        entries[0:1, window * SLOTS : (window + 1) * SLOTS] = jnp.sum(code, 0, keepdims=True)


def gather_span(sizes, enc, step, level, first, raw_ref, table_t, place_t, entries, counts, scaled_ref):
    pack_span(sizes, enc, step, level, first, raw_ref, entries, counts)
    code = entries[0:1, :]
    rows = code >> 16
    where = (code >> 8) & 255
    x = jnp.zeros((128, SPAN), jnp.float32)
    wide = jnp.broadcast_to(rows, (CHUNK, SPAN))
    for cut in range(sizes.padded // CHUNK):
        chosen = hot(wide == iota((CHUNK, SPAN), 0) + cut * CHUNK)
        x += dot(table_t[:, cut * CHUNK : (cut + 1) * CHUNK], chosen)
    chosen = hot(jnp.broadcast_to(where, (CHUNK, SPAN)) == iota((CHUNK, SPAN), 0))
    x += dot(place_t[enc, 0], chosen) + dot(place_t[enc, 1], chosen)
    center = x - jnp.mean(x, 0, keepdims=True)
    rate = lax.rsqrt(jnp.mean(center * center, 0, keepdims=True) + NORM_EPS)
    scaled_ref[0:128, :] = center * rate
    scaled_ref[128:129, :] = rate


def project(enc, scaled, vec_t, w_kv):
    a_t = low16(scaled * vec_t[enc, :, 0:1] + vec_t[enc, :, 1:2])
    kv = dot(w_kv[enc], a_t)
    keys_t = low16(kv[:128])
    values_t = low16(kv[128:] + vec_t[enc, :, 3:4])
    return a_t, keys_t, values_t


def forward_kernel(
    sizes,
    raw_ref,
    rows_ref,
    table_ref,
    place_ref,
    attn_ref,
    vec_ref,
    out_ref,
    lse_ref,
    query_ref,
    kept_ref,
    entry_ref,
    levels_ref,
    table_t,
    place_t,
    w_kv,
    vec_t,
    entries,
    counts,
    scaled_ref,
    query_q,
    total_q,
    top_q,
    mass_q,
    total_p,
    top_p,
    mass_p,
):
    first = lax.axis_index("dp") * sizes.depth
    count_q, count_p = sizes.count
    prepare_tokens(sizes, table_ref, place_ref, attn_ref, vec_ref, table_t, place_t, w_kv, vec_t)
    prepare_weights(attn_ref, vec_ref, w_kv, vec_t)
    counts[...] = jnp.zeros_like(counts)
    for enc in range(2):
        low, high = (0, count_q) if enc == 0 else (count_q, count_q + count_p)
        w_q = low16(attn_ref[0, enc, :, 0:128])

        def ask(step, carry):
            if enc == 0:
                held = jnp.concatenate(
                    [rows_ref[step * 8 + i, low:high, :] for i in range(8)], 0
                )
            else:
                held = rows_ref[step, low:high, :]
            x = held.astype(jnp.float32) + place_ref[0, enc, 0:1, :]
            h = norm_rows(x, vec_ref[0, enc, 0:1, :], vec_ref[0, enc, 1:2, :])
            query = low16(dot(low16(h), w_q) + vec_ref[0, enc, 2:3, :])
            if enc == 0:
                query_q[step] = query
                for i in range(8):
                    query_ref[step * 8 + i, low:high, :] = query[i * count_q : (i + 1) * count_q]
            else:
                query_ref[step, low:high, :] = query
            return carry

        lax.fori_loop(0, sizes.steps[enc], ask, 0)
    total_q[...] = jnp.zeros_like(total_q)
    total_p[...] = jnp.zeros_like(total_p)
    mass_q[...] = jnp.zeros_like(mass_q)
    mass_p[...] = jnp.zeros_like(mass_p)
    top_q[...] = jnp.full_like(top_q, NEG)
    top_p[...] = jnp.full_like(top_p, NEG)

    def one_level(state):
        level = state[0]
        for enc in range(2):
            total, top, mass = (total_q, top_q, mass_q) if enc == 0 else (total_p, top_p, mass_p)

            def one_span(step, carry):
                gather_span(
                    sizes, enc, step, level, first, raw_ref, table_t, place_t, entries, counts, scaled_ref
                )
                scaled = scaled_ref[0:128, :]
                if sizes.keep:
                    at = step if enc == 0 else sizes.steps[0] + step

                    @pl.when(level == 0)
                    def _():
                        kept_ref[at] = scaled_ref[...]
                        entry_ref[at] = entries[...]

                a_t, keys_t, values_t = project(enc, scaled, vec_t, w_kv)
                query = query_q[step] if enc == 0 else query_ref[step, count_q:, :]
                both = two_heads(query)
                number = query.shape[0]
                scores = dot(both, keys_t) * HEAD ** (-0.5)
                seq = (entries[0:1, :] & 255) - 1
                line = iota(scores.shape, 0)
                line = jnp.where(line >= number, line - number, line)
                mine = line == seq
                scores = jnp.where(mine, scores, NEG)
                old = top[step][:, 0:1]
                new = jnp.maximum(old, jnp.max(scores, 1, keepdims=True))
                fade = jnp.exp(old - new)
                expo = jnp.where(mine, jnp.exp(scores - new), 0.0)
                mass[step] = mass[step] * fade + jnp.sum(expo, 1, keepdims=True)
                top[step] = jnp.broadcast_to(new, top.shape[1:])
                mixed = dot_last(low16(expo), values_t)
                total[step] = total[step] * fade + mixed
                return carry

            lax.fori_loop(0, sizes.steps[enc], one_span, 0)
        need = (jnp.max(counts[...]).astype(jnp.int32) + SPAN - 1) // SPAN
        return level + 1, jnp.maximum(need, 1)

    last = lax.while_loop(lambda state: state[0] < state[1], one_level, (jnp.int32(0), jnp.int32(1)))
    levels_ref[0] = last[1]
    lse_ref[...] = jnp.full_like(lse_ref, NEG)
    for enc in range(2):
        total, top, mass = (total_q, top_q, mass_q) if enc == 0 else (total_p, top_p, mass_p)

        def close(step, carry):
            bulk = mass[step]
            some = bulk > 0.0
            safe = jnp.where(some, bulk, 1.0)
            mixed = merge_heads(total[step] / safe)
            lse = jnp.where(some, top[step] + jnp.log(safe), NEG)
            if enc == 1:
                out_ref[step, count_q:, :] = low16(mixed)
                tall = jnp.concatenate([lse, jnp.full((128 - 2 * count_p, 128), NEG, jnp.float32)], 0)
                lse_ref[step, 0:1, :] = jnp.transpose(tall)[0:1, :]
            else:
                half = lse.shape[0] // 2
                for i in range(8):
                    out_ref[step * 8 + i, 0:count_q, :] = low16(mixed[i * count_q : (i + 1) * count_q])
                    tall = jnp.concatenate(
                        [
                            lse[i * count_q : (i + 1) * count_q],
                            lse[half + i * count_q : half + (i + 1) * count_q],
                            jnp.full((128 - 2 * count_q, 128), NEG, jnp.float32),
                        ],
                        0,
                    )
                    lse_ref[step * 8 + i, 1:2, :] = jnp.transpose(tall)[0:1, :]
            return carry

        lax.fori_loop(0, sizes.steps[enc], close, 0)


def token_scratch(sizes):
    return [
        pltpu.VMEM((128, sizes.padded), jnp.bfloat16),
        pltpu.VMEM((2, 2, 128, CHUNK), jnp.bfloat16),
        pltpu.VMEM((2, 256, 128), jnp.bfloat16),
        pltpu.VMEM((2, 128, 128), jnp.float32),
        pltpu.VMEM((8, SPAN), jnp.int32),
        pltpu.VMEM((8, 128), jnp.float32),
        pltpu.VMEM((136, SPAN), jnp.float32),
    ]


def local_call(kernel, out_shape, inputs, scratch, name, smem_in=(), smem_out=()):
    vm = pl.BlockSpec(memory_space=pltpu.VMEM)
    sm = pl.BlockSpec(memory_space=pltpu.SMEM)
    return pl.pallas_call(
        kernel,
        out_shape=out_shape,
        in_specs=[sm if i in smem_in else vm for i in range(len(inputs))],
        out_specs=[sm if i in smem_out else vm for i in range(len(out_shape))],
        scratch_shapes=scratch,
        compiler_params=pltpu.CompilerParams(vmem_limit_bytes=VMEM_LIMIT),
        name=name,
    )(*inputs)


def tokens_forward(sizes, every, rows, table, positions, attention, vectors):
    many = sizes.many
    both = sum(sizes.count)
    kept = sizes.spans if sizes.keep else 1
    state = []
    for enc in range(2):
        tall = 2 * sizes.queries[enc]
        state += [pltpu.VMEM((sizes.steps[enc], tall, 128), jnp.float32)] * 3
    return local_call(
        functools.partial(forward_kernel, sizes),
        (
            jax.ShapeDtypeStruct((many, both, 128), jnp.bfloat16),
            jax.ShapeDtypeStruct((many, 8, 128), jnp.float32),
            jax.ShapeDtypeStruct((many, both, 128), jnp.bfloat16),
            jax.ShapeDtypeStruct((kept, 136, SPAN), jnp.float32),
            jax.ShapeDtypeStruct((kept, 8, SPAN), jnp.int32),
            jax.ShapeDtypeStruct((1,), jnp.int32),
        ),
        (every, rows, table, positions, attention, vectors),
        token_scratch(sizes)
        + [pltpu.VMEM((sizes.steps[0], sizes.queries[0], 128), jnp.bfloat16)]
        + state,
        "tokens_forward",
        smem_out=(5,),
    )


def mix_kernel(
    many, count_q, part_ref, lse_ref, mixed_ref, total_ref, landed, landed_lse, own, own_lse, send, recv
):
    me = enter(many)
    pairs = [
        (lambda peer: part_ref.at[peer], landed),
        (lambda peer: lse_ref.at[peer], landed_lse),
    ]
    spread_start(many, me, pairs, send, recv, 0)
    landed[me] = part_ref[me]
    landed_lse[me] = lse_ref[me]
    spread_wait(many, me, pairs, send, recv, 0)
    parts = landed_lse[...]
    top = jnp.max(parts, 0)
    total = top + jnp.log(jnp.sum(jnp.exp(parts - top[None]), 0))
    own_lse[...] = total
    share = jnp.exp(parts - total[None])
    columns = jnp.transpose(share.reshape(many * 8, 128))
    count_p = part_ref.shape[1] - count_q
    mixed = jnp.zeros((count_q + count_p, 128), jnp.float32)
    lane_q = iota((count_q, 128), 1)
    lane_p = iota((count_p, 128), 1)
    for peer in range(many):
        factor_p = jnp.where(
            lane_p < HEAD,
            columns[0:count_p, peer * 8 : peer * 8 + 1],
            columns[count_p : 2 * count_p, peer * 8 : peer * 8 + 1],
        )
        factor_q = jnp.where(
            lane_q < HEAD,
            columns[0:count_q, peer * 8 + 1 : peer * 8 + 2],
            columns[count_q : 2 * count_q, peer * 8 + 1 : peer * 8 + 2],
        )
        mixed += jnp.concatenate([factor_q, factor_p], 0) * landed[peer].astype(jnp.float32)
    own[...] = low16(mixed)
    pairs = [(lambda peer: own, mixed_ref), (lambda peer: own_lse, total_ref)]
    spread_start(many, me, pairs, send, recv, 2)
    mixed_ref[me] = own[...]
    total_ref[me] = own_lse[...]
    spread_wait(many, me, pairs, send, recv, 2)


def remote_call(kernel, out_shape, inputs, scratch, lanes, many, ident, name):
    return pl.pallas_call(
        kernel,
        out_shape=out_shape,
        in_specs=[pl.BlockSpec(memory_space=pltpu.VMEM)] * len(inputs),
        out_specs=[pl.BlockSpec(memory_space=pltpu.VMEM)] * len(out_shape),
        scratch_shapes=scratch
        + [pltpu.SemaphoreType.DMA((lanes, many)), pltpu.SemaphoreType.DMA((lanes, many))],
        compiler_params=pltpu.CompilerParams(
            collective_id=ident, has_side_effects=True, vmem_limit_bytes=VMEM_LIMIT
        ),
        name=name,
    )(*inputs)


def exchange_mixed(sizes, part, lse):
    many = sizes.many
    both = sum(sizes.count)
    return remote_call(
        functools.partial(mix_kernel, many, sizes.count[0]),
        (
            jax.ShapeDtypeStruct((many, both, 128), jnp.bfloat16),
            jax.ShapeDtypeStruct((many, 8, 128), jnp.float32),
        ),
        (part, lse),
        [
            pltpu.VMEM((many, both, 128), jnp.bfloat16),
            pltpu.VMEM((many, 8, 128), jnp.float32),
            pltpu.VMEM((both, 128), jnp.bfloat16),
            pltpu.VMEM((8, 128), jnp.float32),
        ],
        4,
        many,
        2,
        "exchange_mixed",
    )


def backward_kernel(
    sizes,
    levels_ref,
    raw_ref,
    query_ref,
    mixed_ref,
    lse_ref,
    grad_ref,
    kept_ref,
    entry_ref,
    table_ref,
    place_ref,
    attn_ref,
    vec_ref,
    d_query_ref,
    d_table_ref,
    slice_ref,
    d_vec_ref,
    table_t,
    place_t,
    w_kv,
    vec_t,
    entries,
    counts,
    scaled_ref,
    d_place_ref,
    d_attn_ref,
    acc_gain,
    acc_shift,
    acc_value,
    d_query_q,
    d_query_p,
):
    first = lax.axis_index("dp") * sizes.depth
    count_q, count_p = sizes.count
    prepare_weights(attn_ref, vec_ref, w_kv, vec_t)
    again = levels_ref[0] > 1 if sizes.keep else levels_ref[0] > 0

    @pl.when(again)
    def _():
        prepare_tokens(sizes, table_ref, place_ref, attn_ref, vec_ref, table_t, place_t, w_kv, vec_t)

    counts[...] = jnp.zeros_like(counts)
    d_table_ref[...] = jnp.zeros_like(d_table_ref)
    d_place_ref[...] = jnp.zeros_like(d_place_ref)
    d_attn_ref[...] = jnp.zeros_like(d_attn_ref)
    d_query_p[...] = jnp.zeros_like(d_query_p)
    d_query_q[...] = jnp.zeros_like(d_query_q)
    acc_gain[...] = jnp.zeros_like(acc_gain)
    acc_shift[...] = jnp.zeros_like(acc_shift)
    acc_value[...] = jnp.zeros_like(acc_value)

    def one_level(level, carry_level):
        for enc in range(2):
            w_all = low16(attn_ref[0, enc, :, 128:384])

            def one_span(step, carry):
                at = step if enc == 0 else sizes.steps[0] + step
                again_span = functools.partial(
                    gather_span, sizes, enc, step, level, first, raw_ref, table_t, place_t, entries, counts, scaled_ref
                )
                if sizes.keep:

                    @pl.when(level == 0)
                    def _():
                        scaled_ref[...] = kept_ref[at]
                        entries[...] = entry_ref[at]

                    pl.when(level > 0)(again_span)
                else:
                    again_span()
                scaled = scaled_ref[0:128, :]
                a_t, keys_t, values_t = project(enc, scaled, vec_t, w_kv)
                if enc == 0:
                    query = jnp.concatenate([query_ref[step * 8 + i, 0:count_q, :] for i in range(8)], 0)
                    grad = jnp.concatenate([grad_ref[step * 8 + i, 0:count_q, :] for i in range(8)], 0)
                    mixed = jnp.concatenate([mixed_ref[step * 8 + i, 0:count_q, :] for i in range(8)], 0)
                    pieces = []
                    for head in range(2):
                        for i in range(8):
                            line = lse_ref[step * 8 + i]
                            tall = jnp.transpose(
                                jnp.concatenate([line, jnp.zeros((120, 128), jnp.float32)], 0)
                            )
                            pieces.append(tall[head * count_q : (head + 1) * count_q, 1:2])
                    lse = jnp.concatenate(pieces, 0)
                else:
                    query = query_ref[step, count_q:, :]
                    grad = grad_ref[step, count_q:, :]
                    mixed = mixed_ref[step, count_q:, :]
                    tall = jnp.transpose(
                        jnp.concatenate([lse_ref[step], jnp.zeros((120, 128), jnp.float32)], 0)
                    )
                    lse = tall[0 : 2 * count_p, 0:1]
                number = query.shape[0]
                both = two_heads(query)
                grads = two_heads(grad)
                level_sum = jnp.sum(
                    grads.astype(jnp.float32) * jnp.concatenate([mixed, mixed], 0).astype(jnp.float32),
                    1,
                    keepdims=True,
                )
                scores = dot(both, keys_t) * HEAD ** (-0.5)
                seq = (entries[0:1, :] & 255) - 1
                line = iota(scores.shape, 0)
                line = jnp.where(line >= number, line - number, line)
                mine = line == seq
                probs = jnp.where(mine, jnp.exp(jnp.where(mine, scores, NEG) - lse), 0.0)
                d_probs = dot(grads, values_t)
                d_scores = low16(probs * (d_probs - level_sum))
                d_values = low16(dot_rows(grads, low16(probs)))
                d_keys = low16(dot_rows(both, d_scores) * HEAD ** (-0.5))
                d_query = merge_heads(dot_last(d_scores, keys_t)) * HEAD ** (-0.5)
                if enc == 0:
                    d_query_q[step] += d_query
                else:
                    d_query_p[step] += d_query
                d_kv = jnp.concatenate([d_keys, d_values], 0)
                d_attn_ref[enc] += dot_last(a_t, d_kv)
                acc_value[enc] += d_values.astype(jnp.float32)
                d_h = dot(w_all, d_kv)
                acc_gain[enc] += d_h * scaled
                acc_shift[enc] += d_h
                d_scaled = d_h * vec_t[enc, :, 0:1]
                center = d_scaled - jnp.mean(d_scaled, 0, keepdims=True)
                slope = jnp.mean(d_scaled * scaled, 0, keepdims=True)
                d_x = low16((center - scaled * slope) * scaled_ref[128:129, :])
                rows = entries[0:1, :] >> 16
                where = (entries[0:1, :] >> 8) & 255
                chosen = hot(jnp.broadcast_to(where, (CHUNK, SPAN)) == iota((CHUNK, SPAN), 0))
                d_place_ref[enc] += dot_last(d_x, chosen)
                wide = jnp.broadcast_to(rows, (CHUNK, SPAN))
                for cut in range(sizes.padded // CHUNK):
                    spot = slice(cut * CHUNK, (cut + 1) * CHUNK)
                    chosen = hot(wide == iota((CHUNK, SPAN), 0) + cut * CHUNK)
                    d_table_ref[:, spot] += dot_last(d_x, chosen)
                return carry

            lax.fori_loop(0, sizes.steps[enc], one_span, 0)
        return carry_level

    lax.fori_loop(0, levels_ref[0], one_level, 0)

    def give(step, carry):
        for i in range(8):
            d_query_ref[step * 8 + i, 0:count_q, :] = low16(
                d_query_q[step][i * count_q : (i + 1) * count_q]
            )
        return carry

    lax.fori_loop(0, sizes.steps[0], give, 0)
    d_query_ref[:, count_q:, :] = low16(d_query_p[...])
    for enc in range(2):
        for part, block in enumerate((d_place_ref, d_attn_ref)):
            for cut in range(2):
                slice_ref[enc, 2 * part + cut] = block[enc, :, cut * 128 : (cut + 1) * 128].astype(
                    slice_ref.dtype
                )
    d_vec_ref[...] = jnp.zeros_like(d_vec_ref)
    for enc in range(2):
        for row, acc in enumerate((acc_gain, acc_shift, acc_value)):
            tall = jnp.broadcast_to(jnp.sum(acc[enc], 1, keepdims=True), (128, 128))
            d_vec_ref[enc * 4 + row : enc * 4 + row + 1, :] = jnp.transpose(tall)[0:1, :]


def tokens_backward(sizes, levels, every, query, mixed, lse, grad, kept, entry, table, positions, attention, vectors):
    many = sizes.many
    count_p = sizes.count[1]
    both = sum(sizes.count)
    return local_call(
        functools.partial(backward_kernel, sizes),
        (
            jax.ShapeDtypeStruct((many, both, 128), jnp.bfloat16),
            jax.ShapeDtypeStruct((128, sizes.padded), jnp.float32),
            jax.ShapeDtypeStruct((2, 4, 128, 128), sizes.kind),
            jax.ShapeDtypeStruct((8, 128), jnp.float32),
        ),
        (levels, every, query, mixed, lse, grad, kept, entry, table, positions, attention, vectors),
        token_scratch(sizes)
        + [
            pltpu.VMEM((2, 128, CHUNK), jnp.float32),
            pltpu.VMEM((2, 128, 256), jnp.float32),
            pltpu.VMEM((2, 128, SPAN), jnp.float32),
            pltpu.VMEM((2, 128, SPAN), jnp.float32),
            pltpu.VMEM((2, 128, SPAN), jnp.float32),
            pltpu.VMEM((sizes.steps[0], sizes.queries[0], 128), jnp.float32),
            pltpu.VMEM((many, count_p, 128), jnp.float32),
        ],
        "tokens_backward",
        smem_in=(0,),
    )


def adam(weight, grad, first, second):
    first_new = BETA_ONE * first + (1.0 - BETA_ONE) * grad
    second_new = BETA_TWO * second + (1.0 - BETA_TWO) * grad * grad
    fix_one = 1.0 - BETA_ONE**STEP
    fix_two = 1.0 - BETA_TWO**STEP
    ratio = first_new / fix_one / (jnp.sqrt(second_new / fix_two) + ADAM_EPS)
    return (first_new, second_new, weight - INNER_RATE * (ratio + WEIGHT_DECAY * weight))


def pieces_of(depth):
    blocks = [(1, (enc,)) for enc in range(2)] + [(2, (enc,)) for enc in range(2)]
    blocks += [(3, (enc, side)) for enc in range(2) for side in range(2)]
    blocks += [(4, (enc,)) for enc in range(2)]
    return blocks


def square_sum(values):
    return jnp.sum(jnp.sum(values * values, 0, keepdims=True), 1, keepdims=True)


def finish_kernel(sizes, *refs):
    many = sizes.many
    count_q, count_p = sizes.count
    depth = sizes.depth
    (query_ref, slice_ref, first_ref, d_table_ref, rows_ref, raw_ref, xa_q, xa_p, d_out, d_ffn, d_mid) = refs[:11]
    place_ref, attn_ref, vec_ref = refs[11:14]
    state = refs[14:34]
    norm_ref, g_word, g_place, g_attn, g_vec = refs[34:39]
    theirs = refs[39:44]
    held = refs[44:64]
    mine = refs[64:69]
    (query_all, slice_all, first_all, scalar_all, land_query, land_slice, own_query, own_slice, tile, table_t) = refs[69:79]
    send, recv, load, pair_send, pair_recv = refs[79:84]
    loads = []
    for index in range(20):
        copy = pltpu.make_async_copy(state[index], held[index], load.at[index])
        copy.start()
        loads.append(copy)
    me = lax.axis_index("dp")
    other = 1 - lax.axis_index("grp")
    barrier = pltpu.get_barrier_semaphore()

    def greet(step, carry):
        peer = lax.rem(me + step, many)
        pl.semaphore_signal(barrier, inc=1, device_id={"dp": peer}, device_id_type=MESH)
        return carry

    lax.fori_loop(1, many, greet, 0)
    pl.semaphore_signal(barrier, inc=1, device_id={"grp": other}, device_id_type=MESH)
    pl.semaphore_wait(barrier, many)
    pairs = [
        (lambda peer: query_ref.at[peer], land_query),
        (lambda peer: slice_ref.at[peer], land_slice),
        (lambda peer: first_ref, first_all),
    ]
    spread_start(many, me, pairs, send, recv, 0)
    land_query[me] = query_ref[me]
    land_slice[me] = slice_ref[me]
    first_all[me] = first_ref[...]
    spread_wait(many, me, pairs, send, recv, 0)
    own_query[...] = low16(jnp.sum(land_query[...].astype(jnp.float32), 0))
    own_slice[...] = jnp.sum(land_slice[...].astype(jnp.float32), 0).astype(own_slice.dtype)
    pairs = [(lambda peer: own_query, query_all), (lambda peer: own_slice, slice_all)]
    spread_start(many, me, pairs, send, recv, 3)
    query_all[me] = own_query[...]
    slice_all[me] = own_slice[...]
    spread_wait(many, me, pairs, send, recv, 3)

    first_sum = jnp.sum(first_all[...], 0)
    first = me * depth
    table_t[...] = d_table_ref[...]
    blocks = slice_all[...].astype(jnp.float32).reshape(8, 128, 128)
    rest = jnp.zeros((1, 1), jnp.float32)
    for enc in range(2):
        low, high = (0, count_q) if enc == 0 else (count_q, count_q + count_p)
        number = many * (high - low)
        d_query = query_all[:, low:high, :].reshape(number, 128)
        x = rows_ref[:, low:high, :].reshape(number, 128).astype(jnp.float32) + place_ref[0, enc, 0:1, :]
        center = x - jnp.mean(x, -1, keepdims=True)
        rate = lax.rsqrt(jnp.mean(center * center, -1, keepdims=True) + NORM_EPS)
        scaled = center * rate
        gain = vec_ref[0, enc, 0:1, :]
        a_low = low16(scaled * gain + vec_ref[0, enc, 1:2, :])
        xa = xa_q if enc == 0 else xa_p
        d_h = xa[...] + dot_last(d_query, low16(attn_ref[0, enc, :, 0:128]))
        d_scaled = d_h * gain
        slope = jnp.mean(d_scaled * scaled, -1, keepdims=True)
        d_x = (d_scaled - jnp.mean(d_scaled, -1, keepdims=True) - scaled * slope) * rate
        g_place[enc, 0:128, :] = jnp.transpose(blocks[enc * 4])
        g_place[enc, 128:256, :] = jnp.transpose(blocks[enc * 4 + 1])
        g_place[enc, 0:1, :] += jnp.sum(d_x, 0, keepdims=True)
        g_attn[enc, :, 0:128] = dot_rows(a_low, d_query)
        g_attn[enc, :, 128:256] = blocks[enc * 4 + 2]
        g_attn[enc, :, 256:384] = blocks[enc * 4 + 3]
        g_attn[enc, :, 384:512] = d_out[enc]
        g_vec[enc] = d_mid[enc]
        g_vec[enc, 0:1, :] = first_sum[enc * 4 : enc * 4 + 1] + jnp.sum(d_h * scaled, 0, keepdims=True)
        g_vec[enc, 1:2, :] = first_sum[enc * 4 + 1 : enc * 4 + 2] + jnp.sum(d_h, 0, keepdims=True)
        g_vec[enc, 2:3, :] = jnp.sum(d_query.astype(jnp.float32), 0, keepdims=True)
        g_vec[enc, 3:4, :] = first_sum[enc * 4 + 2 : enc * 4 + 3]
        if enc == 0:
            columns = [
                part
                for peer in range(many)
                for part in (
                    raw_ref[peer, RAW_Q : RAW_Q + 16, 0:1].astype(jnp.int32)[0 : count_q // 2],
                    raw_ref[peer, RAW_Q : RAW_Q + 16, 64:65].astype(jnp.int32)[0 : count_q // 2],
                )
            ]
        else:
            columns = [raw_ref[peer, 0:count_p, 0:1].astype(jnp.int32) for peer in range(many)]
        spot = jnp.concatenate(columns, 0) - first
        spot = jnp.where(spot < depth, spot, -1)
        d_low = low16(d_x)
        wide = jnp.broadcast_to(spot, (number, CHUNK))
        for cut in range(sizes.padded // CHUNK):
            chosen = hot(wide == iota((number, CHUNK), 1) + cut * CHUNK)
            table_t[:, cut * CHUNK : (cut + 1) * CHUNK] += dot_rows(d_low, chosen)
        rest += square_sum(g_place[enc]) + square_sum(g_attn[enc]) + square_sum(g_vec[enc])
        rest += square_sum(d_ffn[enc, 0]) + square_sum(d_ffn[enc, 1])
    for cut in range(0, depth, 128):
        top = min(cut + 128, depth)
        g_word[cut:top, :] = jnp.transpose(table_t[:, cut : cut + 128])[0 : top - cut]
    tile[...] = jnp.broadcast_to(square_sum(table_t[...]), (8, 128))
    pairs = [(lambda peer: tile, scalar_all)]
    spread_start(many, me, pairs, send, recv, 5)
    scalar_all[me] = tile[...]
    for copy in loads:
        copy.wait()
    spread_wait(many, me, pairs, send, recv, 5)
    norm = jnp.sqrt(jnp.sum(scalar_all[...], 0)[0:1, 0:1] + rest)
    norm_ref[...] = jnp.broadcast_to(norm, (8, 128))
    factor = CLIP_LIMIT / jnp.maximum(norm, CLIP_LIMIT)
    grads = (g_word, g_place, g_attn, d_ffn, g_vec)

    def differ(kind, at, rows):
        weight, moment, square, anchor = (held[kind * 4 + j] for j in range(4))
        grad = grads[kind][at + (rows,)] * factor
        inner = adam(weight[(0,) + at + (rows,)], grad, moment[(0,) + at + (rows,)], square[(0,) + at + (rows,)])[2]
        mine[kind][at + (rows,)] = anchor[at + (rows,)] - inner

    size = math.gcd(depth, 128)

    def table_block(step, carry):
        differ(0, (), pl.ds(pl.multiple_of(step * size, size), size))
        return carry

    lax.fori_loop(0, depth // size, table_block, 0)
    ways = []

    def hand(kind):
        copy = pltpu.make_async_remote_copy(
            src_ref=mine[kind],
            dst_ref=theirs[kind],
            send_sem=pair_send.at[kind],
            recv_sem=pair_recv.at[kind],
            device_id={"grp": other},
            device_id_type=MESH,
        )
        copy.start()
        ways.append(copy)

    hand(0)
    for kind in range(1, 5):
        for found, at in pieces_of(depth):
            if found == kind:
                differ(kind, at, slice(0, 14) if kind == 4 else slice(None))
        hand(kind)
    for kind in range(5):
        ways[kind].wait()


    def table_add(step, carry):
        rows = pl.ds(pl.multiple_of(step * size, size), size)
        theirs[0][rows] += mine[0][rows]
        return carry

    lax.fori_loop(0, depth // size, table_add, 0)
    for kind, at in pieces_of(depth):
        theirs[kind][at] += mine[kind][at]


def finish(sizes, query, slices, first, d_table, rows, every, xa_q, xa_p, d_out, d_ffn, d_mid, params, state):
    many = sizes.many
    both = sum(sizes.count)
    inputs = (query, slices, first, d_table, rows, every, xa_q, xa_p, d_out, d_ffn, d_mid) + params
    flat = tuple(state[j][kind] for kind in range(5) for j in range(4))
    shapes = [state[3][kind].shape for kind in range(5)]
    vm = pl.BlockSpec(memory_space=pltpu.VMEM)
    hbm = pl.BlockSpec(memory_space=pl.ANY)
    f32 = jnp.float32
    return pl.pallas_call(
        functools.partial(finish_kernel, sizes),
        out_shape=tuple(
            jax.ShapeDtypeStruct(shape, f32)
            for shape in [(8, 128), shapes[0], shapes[1], shapes[2], (2, 16, 128)] + shapes
        ),
        in_specs=[vm] * len(inputs) + [hbm] * 20,
        out_specs=[vm] * 10,
        scratch_shapes=[pltpu.VMEM(value.shape, f32) for value in flat]
        + [pltpu.VMEM(shape, f32) for shape in shapes]
        + [
            pltpu.VMEM((many, both, 128), jnp.bfloat16),
            pltpu.VMEM((many, sizes.lines, 128), sizes.kind),
            pltpu.VMEM((many, 8, 128), f32),
            pltpu.VMEM((many, 8, 128), f32),
            pltpu.VMEM((many, both, 128), jnp.bfloat16),
            pltpu.VMEM((many, sizes.lines, 128), sizes.kind),
            pltpu.VMEM((both, 128), jnp.bfloat16),
            pltpu.VMEM((sizes.lines, 128), sizes.kind),
            pltpu.VMEM((8, 128), f32),
            pltpu.VMEM((128, sizes.padded), f32),
            pltpu.SemaphoreType.DMA((6, many)),
            pltpu.SemaphoreType.DMA((6, many)),
            pltpu.SemaphoreType.DMA((20,)),
            pltpu.SemaphoreType.DMA((5,)),
            pltpu.SemaphoreType.DMA((5,)),
        ],
        compiler_params=pltpu.CompilerParams(
            collective_id=3, has_side_effects=True, vmem_limit_bytes=VMEM_LIMIT
        ),
        name="finish",
    )(*inputs, *flat)


def outputs_kernel(depth, groups, *refs):
    norm_ref, g_vec = refs[:2]
    ins = refs[2:31]
    outs = refs[31:56]
    held = refs[56:85]
    made = refs[85:110]
    load, store = refs[110:112]
    loads, stores = ([], [])
    for index in range(29):
        copy = pltpu.make_async_copy(ins[index], held[index], load.at[index])
        copy.start()
        loads.append(copy)
    norm = norm_ref[0:1, 0:1]
    factor = CLIP_LIMIT / jnp.maximum(norm, CLIP_LIMIT)
    grads = tuple(held[25:29]) + (g_vec,)

    def work(kind, at, rows):
        moment, square, anchor, outer, summed = (held[kind * 5 + j] for j in range(5))
        first, second, average, momentum, weight = (made[kind * 5 + j] for j in range(5))
        spot = at + (rows,)
        deep = (0,) + spot
        grad = grads[kind][spot] * factor
        first[deep] = BETA_ONE * moment[deep] + (1.0 - BETA_ONE) * grad
        second[deep] = BETA_TWO * square[deep] + (1.0 - BETA_TWO) * grad * grad
        mean = summed[spot] / groups
        speed = OUTER_MU * outer[spot] + mean
        average[spot] = mean
        momentum[spot] = speed
        weight[deep] = anchor[spot] - OUTER_RATE * (mean + OUTER_MU * speed)

    def give(kind):
        for j in range(5):
            index = kind * 5 + j
            copy = pltpu.make_async_copy(made[index], outs[index], store.at[index])
            copy.start()
            stores.append(copy)

    size = math.gcd(depth, 128)

    def table_block(step, carry):
        work(0, (), pl.ds(pl.multiple_of(step * size, size), size))
        return carry

    for kind in range(5):
        for j in range(5):
            loads[kind * 5 + j].wait()
        if kind < 4:
            loads[25 + kind].wait()
        if kind == 0:
            lax.fori_loop(0, depth // size, table_block, 0)
        else:
            for found, at in pieces_of(depth):
                if found == kind:
                    work(kind, at, slice(0, 14) if kind == 4 else slice(None))
        give(kind)
    for copy in stores:
        copy.wait()


def make_outputs(norm, grads, firsts, seconds, anchors, outers, summed, groups):
    kinds = range(5)
    flat = tuple(v for kind in kinds for v in (firsts[kind], seconds[kind], anchors[kind], outers[kind], summed[kind]))
    flat += tuple(grads[:4])
    out = tuple(
        jax.ShapeDtypeStruct(shape, jnp.float32)
        for kind in kinds
        for shape in (firsts[kind].shape, firsts[kind].shape, anchors[kind].shape, anchors[kind].shape, firsts[kind].shape)
    )
    vm = pl.BlockSpec(memory_space=pltpu.VMEM)
    hbm = pl.BlockSpec(memory_space=pl.ANY)
    got = pl.pallas_call(
        functools.partial(outputs_kernel, anchors[0].shape[0], groups),
        out_shape=out,
        in_specs=[vm] * 2 + [hbm] * 29,
        out_specs=[hbm] * 25,
        scratch_shapes=[pltpu.VMEM(v.shape, jnp.float32) for v in flat]
        + [pltpu.VMEM(v.shape, jnp.float32) for v in out]
        + [pltpu.SemaphoreType.DMA((29,)), pltpu.SemaphoreType.DMA((25,))],
        compiler_params=pltpu.CompilerParams(vmem_limit_bytes=VMEM_LIMIT),
        name="make_outputs",
    )(norm, grads[4], *flat)
    return [[got[kind * 5 + j] for kind in kinds] for j in range(5)]


def class_forward(rows, mixed, place, attn_w, ffn_w, vec):
    width = rows.shape[1]
    h_embed = layer_norm(rows.astype(jnp.float32) + place[:1], vec[0], vec[1])
    x_attn = h_embed + (dot(mixed, low16(attn_w[:, 3 * width :])) + vec[4])
    h_attn = layer_norm(x_attn, vec[5], vec[6])
    h_low = low16(h_attn)
    pre = dot(h_low, low16(ffn_w[0])) + vec[10:].reshape(-1)
    act = low16(gelu_tanh(pre))
    x_ffn = h_attn + (dot_last(act, low16(ffn_w[1])) + vec[7])
    h_out = layer_norm(x_ffn, vec[8], vec[9])
    return low16(h_out), (x_attn, h_low, pre, act, x_ffn)


def class_backward(kept, mixed, attn_w, ffn_w, vec, d_cls):
    x_attn, h_low, pre, act, x_ffn = kept
    width = x_attn.shape[1]
    unused, out_back = jax.vjp(layer_norm, x_ffn, vec[8], vec[9])
    d_x_ffn, d_gain_two, d_shift_two = out_back(d_cls)
    d_branch = low16(d_x_ffn)
    d_down_bias = jnp.sum(d_branch, 0, dtype=jnp.float32)
    d_down = dot_rows(d_branch, act)
    d_act = dot(d_branch, low16(ffn_w[1]))
    unused, gelu_back = jax.vjp(gelu_tanh, pre)
    d_pre = low16(gelu_back(d_act)[0])
    d_up_bias = jnp.sum(d_pre, 0, dtype=jnp.float32)
    d_up = dot_rows(h_low, d_pre)
    d_h_attn = d_x_ffn + dot_last(d_pre, low16(ffn_w[0]))
    unused, attn_back = jax.vjp(layer_norm, x_attn, vec[5], vec[6])
    d_x_attn, d_gain_one, d_shift_one = attn_back(d_h_attn)
    d_proj = low16(d_x_attn)
    d_out_bias = jnp.sum(d_proj, 0, dtype=jnp.float32)
    d_w_out = dot_rows(mixed, d_proj)
    d_mixed = low16(dot_last(d_proj, low16(attn_w[:, 3 * width :])))
    rows = (d_out_bias, d_gain_one, d_shift_one, d_down_bias, d_gain_two, d_shift_two)
    return d_mixed, d_x_attn, d_w_out, jnp.stack([d_up, d_down]), rows, d_up_bias


def softmax_terms(scores, drop, target, weight, count, axis):
    masked = jnp.where(drop, MASKED, scores)
    top = jnp.max(masked, axis, keepdims=True)
    expo = jnp.exp(masked - top)
    total = jnp.sum(expo, axis, keepdims=True)
    lse = top + jnp.log(total)
    picked = jnp.sum(jnp.where(target, scores, 0.0), axis, keepdims=True)
    loss = jnp.sum(weight * (lse - picked))
    grad = low16((weight / count) * (expo / total - target.astype(jnp.float32)))
    return grad, loss


def score_stage(every_q, every_p, keys_q, keys_p, valid_q):
    count = jnp.maximum(jnp.sum(valid_q).astype(jnp.float32), 1.0)
    scale = every_q.shape[1] ** (-0.5)
    index_q = jnp.arange(every_q.shape[0])[:, None]
    index_p = jnp.arange(every_p.shape[0])[None, :]
    scores = dot_last(every_q, every_p) * scale
    same = keys_q[:, None] == keys_p[None, :]
    target_qp = index_p == 2 * index_q
    valid = valid_q.astype(jnp.float32)[:, None]
    grad_qp, loss_qp = softmax_terms(scores, same & ~target_qp, target_qp, valid, count, 1)
    target_pq = index_p // 2 == index_q
    drop_pq = (same | (valid_q[:, None] == 0)) & ~target_pq
    owner_valid = jnp.repeat(valid_q, 2)
    weight_p = jnp.where(index_p[0] % 2 == 0, owner_valid, 0).astype(jnp.float32)[None, :]
    grad_pq, loss_pq = softmax_terms(scores, drop_pq, target_pq, weight_p, count, 0)
    d_q = (dot(grad_qp, every_p) + dot(grad_pq, every_p)) * scale
    d_p = (dot_rows(grad_pq, every_q) + dot_rows(grad_qp, every_q)) * scale
    return d_q, d_p, loss_qp + loss_pq, count


def body(
    question_ids,
    passage_ids,
    question_lengths,
    passage_lengths,
    question_keys,
    passage_keys,
    question_valid,
    word_table,
    positions,
    attention,
    feedforward,
    vectors,
    word_first,
    positions_first,
    attention_first,
    feedforward_first,
    vectors_first,
    word_second,
    positions_second,
    attention_second,
    feedforward_second,
    vectors_second,
    word_anchor,
    positions_anchor,
    attention_anchor,
    feedforward_anchor,
    vectors_anchor,
    word_outer,
    positions_outer,
    attention_outer,
    feedforward_outer,
    vectors_outer,
):
    width = word_table.shape[2]
    many = lax.axis_size("dp")
    count_q, seq_q = question_ids.shape
    count_p, seq_p = passage_ids.shape
    counts = (count_q, count_p)
    table = word_table[0]
    sizes = Sizes(many, count_q, count_p, table.shape[0])
    ids_q = jnp.where(jnp.arange(seq_q)[None, :] < question_lengths[:, None], question_ids, -1)
    ids_p = jnp.where(jnp.arange(seq_p)[None, :] < passage_lengths[:, None], passage_ids, -1)
    half = count_q // 2
    flags = jnp.concatenate([question_keys, question_valid, passage_keys])
    flags = jnp.pad(flags, (0, 8 * 128 - flags.size)).reshape(8, 128)
    raw = jnp.concatenate(
        [
            ids_p[:, :128],
            ids_p[:, 128:],
            jnp.concatenate([ids_q[:half], ids_q[half:]], 1),
            flags,
        ]
    ).astype(jnp.int16)
    every, class_rows = exchange_rows(many, count_q, count_p, raw, table)
    flags_all = every[:, RAW_FLAGS, :].astype(jnp.int32)
    keys_q = flags_all[:, :count_q].reshape(-1)
    valid_all = flags_all[:, count_q : 2 * count_q].reshape(-1)
    keys_p = flags_all[:, 2 * count_q : 2 * count_q + count_p].reshape(-1)
    part, lse_part, query, kept, entry, levels = tokens_forward(
        sizes, every, class_rows, table, positions, attention, vectors
    )
    mixed_all, lse_all = exchange_mixed(sizes, part, lse_part)
    cuts = ((0, count_q), (count_q, count_q + count_p))
    cls, class_kept, mixes, class_x = ([], [], [], [])
    for enc in range(2):
        low, high = cuts[enc]
        rows = class_rows[:, low:high].reshape(-1, width)
        mixed = mixed_all[:, low:high].reshape(-1, width)
        low_cls, kept_cls = class_forward(
            rows, mixed, positions[0, enc], attention[0, enc], feedforward[0, enc], vectors[0, enc]
        )
        cls.append(low_cls)
        class_kept.append(kept_cls)
        mixes.append(mixed)
        class_x.append(rows.astype(jnp.float32) + positions[0, enc, :1])
    d_q, d_p, loss_total, count = score_stage(cls[0], cls[1], keys_q, keys_p, valid_all)
    d_cls = (d_q, d_p)
    finals, grad_parts, firsts_x = ([], [], [])
    for enc in range(2):
        d_mixed, d_x_attn, d_w_out, d_ffn, rows_mid, d_up_bias = class_backward(
            class_kept[enc], mixes[enc], attention[0, enc], feedforward[0, enc], vectors[0, enc], d_cls[enc]
        )
        grad_parts.append(d_mixed.reshape(many, counts[enc], width))
        firsts_x.append(d_x_attn)
        finals.append((d_w_out, d_ffn, rows_mid, d_up_bias))
    grad_all = jnp.concatenate(grad_parts, 1)
    d_query, d_table_t, slices, d_first = tokens_backward(
        sizes, levels, every, query, mixed_all, lse_all, grad_all, kept, entry, table, positions, attention, vectors
    )
    d_out = jnp.stack([finals[0][0], finals[1][0]])
    d_ffn = jnp.stack([finals[0][1], finals[1][1]])
    d_mid = jnp.stack(
        [
            jnp.concatenate(
                [
                    jnp.zeros((4, width), jnp.float32),
                    jnp.stack(list(part[2])),
                    part[3].reshape(-1, width),
                    jnp.zeros((2, width), jnp.float32),
                ]
            )
            for part in finals
        ]
    )
    weights = (word_table, positions, attention, feedforward, vectors)
    firsts = (word_first, positions_first, attention_first, feedforward_first, vectors_first)
    seconds = (word_second, positions_second, attention_second, feedforward_second, vectors_second)
    anchors = (word_anchor, positions_anchor, attention_anchor, feedforward_anchor, vectors_anchor)
    outers = (word_outer, positions_outer, attention_outer, feedforward_outer, vectors_outer)
    done = finish(
        sizes,
        d_query,
        slices.reshape(many, sizes.lines, 128),
        d_first,
        d_table_t,
        class_rows,
        every,
        firsts_x[0],
        firsts_x[1],
        d_out,
        d_ffn,
        d_mid,
        (positions, attention, vectors),
        (weights, firsts, seconds, anchors),
    )
    norm = done[0]
    grads = (done[1], done[2], done[3], d_ffn, done[4])
    first_new, second_new, averages, outer_next, weight_next = make_outputs(
        norm, grads, firsts, seconds, anchors, outers, done[5:10], lax.axis_size("grp")
    )
    norm = norm[0, 0]
    return (
        loss_total.reshape(1),
        count.reshape(1),
        norm.reshape(1),
        first_new[0],
        first_new[1],
        first_new[2],
        first_new[3],
        first_new[4],
        second_new[0],
        second_new[1],
        second_new[2],
        second_new[3],
        second_new[4],
        averages[0],
        averages[1],
        averages[2],
        averages[3],
        averages[4],
        outer_next[0],
        outer_next[1],
        outer_next[2],
        outer_next[3],
        outer_next[4],
        weight_next[0],
        weight_next[1],
        weight_next[2],
        weight_next[3],
        weight_next[4],
    )


def solution(mesh):
    placed = (
        P(("grp", "dp"), None),
        P(("grp", "dp"), None),
        P(("grp", "dp")),
        P(("grp", "dp")),
        P(("grp", "dp")),
        P(("grp", "dp")),
        P(("grp", "dp")),
        P("grp", "dp", None),
        P("grp", None, None, None),
        P("grp", None, None, None),
        P("grp", None, None, None, None),
        P("grp", None, None, None),
        P("grp", "dp", None),
        P("grp", None, None, None),
        P("grp", None, None, None),
        P("grp", None, None, None, None),
        P("grp", None, None, None),
        P("grp", "dp", None),
        P("grp", None, None, None),
        P("grp", None, None, None),
        P("grp", None, None, None, None),
        P("grp", None, None, None),
        P("dp", None),
        P(),
        P(),
        P(),
        P(),
        P("dp", None),
        P(),
        P(),
        P(),
        P(),
    )
    return jax.shard_map(
        body,
        mesh=mesh,
        in_specs=placed,
        out_specs=(
            P("grp"),
            P("grp"),
            P("grp"),
            P("grp", "dp", None),
            P("grp", None, None, None),
            P("grp", None, None, None),
            P("grp", None, None, None, None),
            P("grp", None, None, None),
            P("grp", "dp", None),
            P("grp", None, None, None),
            P("grp", None, None, None),
            P("grp", None, None, None, None),
            P("grp", None, None, None),
            P("dp", None),
            P(),
            P(),
            P(),
            P(),
            P("dp", None),
            P(),
            P(),
            P(),
            P(),
            P("grp", "dp", None),
            P("grp", None, None, None),
            P("grp", None, None, None),
            P("grp", None, None, None, None),
            P("grp", None, None, None),
        ),
        check_vma=False,
    )
```

```python
import functools
import math

import jax
import jax.numpy as jnp
from jax import lax
from jax.experimental import pallas as pl
from jax.experimental.pallas import tpu as pltpu
from jax.sharding import PartitionSpec as P

HEAD = 64
STEP = 5


NORM_EPS = 1e-05
MASKED = -1000000000.0
BETA_ONE = 0.9
BETA_TWO = 0.999
INNER_RATE = 0.05
WEIGHT_DECAY = 0.01
ADAM_EPS = 1e-08
CLIP_LIMIT = 0.01
OUTER_RATE = 0.7
OUTER_MU = 0.9
CONTRACT_ROWS = (((0,), (0,)), ((), ()))
CONTRACT_LAST = (((1,), (1,)), ((), ()))


def layer_norm(values, gain, shift):
    center = values - jnp.mean(values, -1, keepdims=True)
    spread = jnp.mean(center * center, -1, keepdims=True)
    return center * lax.rsqrt(spread + NORM_EPS) * gain + shift


def gelu_tanh(values):
    return jax.nn.gelu(values, approximate=True)


def low16(values):
    return values.astype(jnp.bfloat16)


NEG = -1e30
MESH = pl.DeviceIdType.MESH
VMEM_LIMIT = 60 * 1024 * 1024
WAYS = 4
SLOTS = 128
SPAN = WAYS * SLOTS
CHUNK = 256
UNROLL = 2
RAW_Q = 64
RAW_FLAGS = 72
RAW_ROWS = 80


def enter(many):
    me = lax.axis_index("dp")
    barrier = pltpu.get_barrier_semaphore()

    def greet(step, carry):
        peer = lax.rem(me + step, many)
        pl.semaphore_signal(barrier, inc=1, device_id={"dp": peer}, device_id_type=MESH)
        return carry

    lax.fori_loop(1, many, greet, 0)
    pl.semaphore_wait(barrier, many - 1)
    return me


def copy_to(peer, src, dst, send, recv):
    return pltpu.make_async_remote_copy(
        src_ref=src,
        dst_ref=dst,
        send_sem=send,
        recv_sem=recv,
        device_id={"dp": peer},
        device_id_type=MESH,
    )


def spread_start(many, me, pairs, send, recv, slot):
    def step_start(step, carry):
        peer = lax.rem(me + step, many)
        for index, (source, landing) in enumerate(pairs):
            copy_to(
                peer,
                source(peer),
                landing.at[me],
                send.at[slot + index, peer],
                recv.at[slot + index, me],
            ).start()
        return carry

    lax.fori_loop(1, many, step_start, 0)


def spread_wait(many, me, pairs, send, recv, slot):
    def step_wait(step, carry):
        peer = lax.rem(me + step, many)
        for index, (source, landing) in enumerate(pairs):
            copy = copy_to(
                peer,
                source(peer),
                landing.at[peer],
                send.at[slot + index, peer],
                recv.at[slot + index, peer],
            )
            copy.wait_recv()
            copy.wait_send()
        return carry

    lax.fori_loop(1, many, step_wait, 0)


def dot(left, right):
    return jnp.dot(left, right, preferred_element_type=jnp.float32)


def dot_rows(left, right):
    return lax.dot_general(left, right, CONTRACT_ROWS, preferred_element_type=jnp.float32)


def dot_last(left, right):
    return lax.dot_general(left, right, CONTRACT_LAST, preferred_element_type=jnp.float32)


def iota(shape, axis):
    return lax.broadcasted_iota(jnp.int32, shape, axis)


def hot(mask):
    return jnp.where(mask, 1.0, 0.0).astype(jnp.bfloat16)


def rows_kernel(
    many,
    question_ref,
    passage_ref,
    length_q,
    length_p,
    key_q,
    valid_q,
    key_p,
    table_ref,
    every_ref,
    rows_ref,
    stage,
    raw,
    low_ref,
    offer,
    landed,
    own,
    send,
    recv,
):
    count_q, count_p = (question_ref.shape[0], passage_ref.shape[0])
    half = count_q // 2
    lane = iota((1, 128), 1)
    for seq in range(count_p):
        stop = length_p[seq]
        stage[seq : seq + 1, :] = jnp.where(lane < stop, passage_ref[seq : seq + 1, 0:128], -1)
        stage[count_p + seq : count_p + seq + 1, :] = jnp.where(
            lane + 128 < stop, passage_ref[seq : seq + 1, 128:256], -1
        )
    both = jnp.concatenate([question_ref[0:half, :], question_ref[half:count_q, :]], 1)
    for seq in range(half):
        stop = jnp.where(lane < 64, length_q[seq], length_q[half + seq] + 64)
        stage[RAW_Q + seq : RAW_Q + seq + 1, :] = jnp.where(lane < stop, both[seq : seq + 1], -1)
    flags = jnp.zeros((1, 128), jnp.int32)
    for spot in range(count_q):
        flags = jnp.where(lane == spot, key_q[spot], flags)
        flags = jnp.where(lane == count_q + spot, valid_q[spot], flags)
    for spot in range(count_p):
        flags = jnp.where(lane == 2 * count_q + spot, key_p[spot], flags)
    stage[RAW_FLAGS:RAW_ROWS, :] = jnp.broadcast_to(flags, (8, 128))
    raw[...] = stage[...].astype(jnp.int16)
    me = enter(many)
    raw_pairs = [(lambda peer: raw, every_ref)]
    spread_start(many, me, raw_pairs, send, recv, 0)
    every_ref[me] = raw[...]
    depth = table_ref.shape[0]
    low_ref[...] = jnp.zeros_like(low_ref)
    low_ref[0:depth, :] = low16(table_ref[...])
    padded = low_ref.shape[0]
    spread_wait(many, me, raw_pairs, send, recv, 0)
    first = me * depth
    block = math.gcd(many, 16)

    def pick(step, carry):
        asks = []
        for i in range(block):
            found = every_ref[step * block + i].astype(jnp.int32)
            asks += [
                found[RAW_Q : RAW_Q + half, 0:1],
                found[RAW_Q : RAW_Q + half, 64:65],
                found[0:count_p, 0:1],
            ]
        place = jnp.concatenate(asks, 0) - first
        spot = jnp.where((place >= 0) & (place < depth), place, -1)
        number = spot.shape[0]
        total = jnp.zeros((number, 128), jnp.float32)
        wide = jnp.broadcast_to(spot, (number, CHUNK))
        for at in range(padded // CHUNK):
            chosen = hot(wide == iota((number, CHUNK), 1) + at * CHUNK)
            total += dot(chosen, low_ref[at * CHUNK : (at + 1) * CHUNK, :])
        each = count_q + count_p
        for i in range(block):
            offer[step * block + i] = low16(total[i * each : (i + 1) * each])
        return carry

    lax.fori_loop(0, many // block, pick, 0)
    pairs = [(lambda peer: offer.at[peer], landed)]
    spread_start(many, me, pairs, send, recv, 1)
    landed[me] = offer[me]
    spread_wait(many, me, pairs, send, recv, 1)
    own[...] = low16(jnp.sum(landed[...].astype(jnp.float32), 0))
    pairs = [(lambda peer: own, rows_ref)]
    spread_start(many, me, pairs, send, recv, 2)
    rows_ref[me] = own[...]
    spread_wait(many, me, pairs, send, recv, 2)


def exchange_rows(many, ids_q, ids_p, length_q, length_p, key_q, valid_q, key_p, table):
    count_q, count_p = (ids_q.shape[0], ids_p.shape[0])
    depth = table.shape[0]
    padded = -(-depth // CHUNK) * CHUNK
    both = count_q + count_p
    vm = pl.BlockSpec(memory_space=pltpu.VMEM)
    sm = pl.BlockSpec(memory_space=pltpu.SMEM)
    return pl.pallas_call(
        functools.partial(rows_kernel, many),
        out_shape=(
            jax.ShapeDtypeStruct((many, RAW_ROWS, 128), jnp.int16),
            jax.ShapeDtypeStruct((many, both, 128), jnp.bfloat16),
        ),
        in_specs=[vm, vm, sm, sm, sm, sm, sm, vm],
        out_specs=[vm, vm],
        scratch_shapes=[
            pltpu.VMEM((RAW_ROWS, 128), jnp.int32),
            pltpu.VMEM((RAW_ROWS, 128), jnp.int16),
            pltpu.VMEM((padded, 128), jnp.bfloat16),
            pltpu.VMEM((many, both, 128), jnp.bfloat16),
            pltpu.VMEM((many, both, 128), jnp.bfloat16),
            pltpu.VMEM((both, 128), jnp.bfloat16),
            pltpu.SemaphoreType.DMA((3, many)),
            pltpu.SemaphoreType.DMA((3, many)),
        ],
        compiler_params=pltpu.CompilerParams(
            collective_id=1, has_side_effects=True, vmem_limit_bytes=VMEM_LIMIT
        ),
        name="exchange_rows",
    )(ids_q, ids_p, length_q, length_p, key_q, valid_q, key_p, table)


def norm_rows(values, gain, shift):
    center = values - jnp.mean(values, -1, keepdims=True)
    spread = jnp.mean(center * center, -1, keepdims=True)
    return center * lax.rsqrt(spread + NORM_EPS) * gain + shift


def two_heads(values):
    lane = iota(values.shape, 1)
    low = jnp.where(lane < HEAD, values, jnp.zeros_like(values))
    high = jnp.where(lane >= HEAD, values, jnp.zeros_like(values))
    return jnp.concatenate([low, high], 0)


def merge_heads(both):
    half = both.shape[0] // 2
    lane = iota((half, both.shape[1]), 1)
    return jnp.where(lane < HEAD, both[:half], both[half:])


class Sizes:
    def __init__(self, many, count_q, count_p, depth):
        self.many = many
        self.count = (count_q, count_p)
        self.depth = depth
        self.padded = -(-depth // CHUNK) * CHUNK
        self.steps = (many // (2 * WAYS), many)
        self.spans = self.steps[0] + self.steps[1]
        self.devices = (2 * WAYS, 1)
        self.queries = (2 * WAYS * count_q, count_p)
        self.lines = 1024 // many
        self.kind = jnp.bfloat16 if self.lines % 16 == 0 else jnp.float32
        self.keep = self.spans * 136 * SPAN * 4 <= 8 * 1024 * 1024


def vector_row(vec_ref, enc, row):
    return vec_ref[0, row, enc : enc + 1, :]


def prepare_tokens(sizes, table_ref, place_ref, table_t, place_t):
    depth = sizes.depth
    if sizes.padded > depth:
        table_t[...] = jnp.zeros_like(table_t)
    for cut in range(0, depth, 128):
        top = min(cut + 128, depth)
        piece = table_ref[cut:top, :]
        if top - cut < 128:
            piece = jnp.concatenate([piece, jnp.zeros((128 - (top - cut), 128), jnp.float32)], 0)
        table_t[:, cut : cut + 128] = low16(jnp.transpose(piece))
    for enc in range(2):
        place = place_ref[0, enc]
        for cut in range(0, place.shape[0], 128):
            turned = jnp.transpose(place[cut : cut + 128])
            high = low16(turned)
            place_t[enc, 0, :, cut : cut + 128] = high
            place_t[enc, 1, :, cut : cut + 128] = low16(turned - high.astype(jnp.float32))


def prepare_weights(attn_ref, vec_ref, w_kv, vec_t):
    for enc in range(2):
        for cut in range(2):
            w_kv[enc, cut * 128 : (cut + 1) * 128, :] = low16(
                jnp.transpose(attn_ref[0, enc, :, (cut + 1) * 128 : (cut + 2) * 128])
            )
        rows = [vector_row(vec_ref, enc, row) for row in range(4)]
        rows = jnp.concatenate(rows + [jnp.zeros((124, 128), jnp.float32)], 0)
        vec_t[enc] = jnp.transpose(rows)


def lane_pick(values, lanes):
    return jnp.take_along_axis(values, lanes, axis=1, mode="promise_in_bounds")


def pack_span(sizes, enc, step, level, first, raw_ref):
    if enc == 1:
        ids = raw_ref[step, 0:RAW_Q, :].astype(jnp.int32)
    else:
        ids = jnp.concatenate(
            [
                raw_ref[step * 8 + i, RAW_Q:RAW_ROWS, :].astype(jnp.int32)[0:8]
                for i in range(8)
            ],
            0,
        )
    place = ids - first
    owned = (place >= 0) & (place < sizes.depth)
    flag = hot(owned)
    inside = dot(flag, hot(iota((128, 128), 0) <= iota((128, 128), 1)))
    total = dot(flag, jnp.ones((128, 128), jnp.bfloat16))
    before = dot(hot(iota((64, 64), 1) < iota((64, 64), 0)), low16(total))
    reached = (inside + before).astype(jnp.int32)
    start = before.astype(jnp.int32)
    stop = (before + total).astype(jnp.int32)
    line = iota((64, 128), 0)
    codes = []
    for window in range(WAYS):
        slot = iota((64, 128), 1) + (window * SLOTS + level * SPAN)
        lane = jnp.zeros((64, 128), jnp.int32)
        for jump in (64, 32, 16, 8, 4, 2, 1):
            seen = lane_pick(reached, lane + (jump - 1))
            lane = jnp.where(seen <= slot, lane + jump, lane)
        row = lane_pick(place, lane)
        if enc == 1:
            where = (line >> 5) * 128 + lane
            seq = (line & 31) + 1
        else:
            where = lane & 63
            seq = (line >> 3) * sizes.count[0] + (lane >> 6) * 8 + (line & 7) + 1
        code = (row << 16) + (where << 8) + seq
        code = jnp.where((slot >= start) & (slot < stop), code, 0)
        codes.append(jnp.sum(code, 0, keepdims=True))
    return jnp.concatenate(codes, 1), (before + total)[56:64]


def gather_span(sizes, enc, code, table_t, place_t):
    rows = code >> 16
    where = (code >> 8) & 255
    x = jnp.zeros((128, SPAN), jnp.float32)
    wide = jnp.broadcast_to(rows, (CHUNK, SPAN))
    for cut in range(sizes.padded // CHUNK):
        chosen = hot(wide == iota((CHUNK, SPAN), 0) + cut * CHUNK)
        x += dot(table_t[:, cut * CHUNK : (cut + 1) * CHUNK], chosen)
    chosen = hot(jnp.broadcast_to(where, (CHUNK, SPAN)) == iota((CHUNK, SPAN), 0))
    x += dot(place_t[enc, 0], chosen) + dot(place_t[enc, 1], chosen)
    center = x - jnp.mean(x, 0, keepdims=True)
    rate = lax.rsqrt(jnp.mean(center * center, 0, keepdims=True) + NORM_EPS)
    return center * rate, rate


def project(enc, scaled, vec_t, w_kv):
    a_t = low16(scaled * vec_t[enc, :, 0:1] + vec_t[enc, :, 1:2])
    kv = dot(w_kv[enc], a_t)
    keys_t = low16(kv[:128])
    values_t = low16(kv[128:] + vec_t[enc, :, 3:4])
    return a_t, keys_t, values_t


def own_slots(code, number):
    line = iota((2 * number, SPAN), 0)
    line = jnp.where(line >= number, line - number, line)
    return line == (code & 255) - 1


def forward_kernel(
    sizes,
    raw_ref,
    rows_ref,
    table_ref,
    place_ref,
    attn_ref,
    vec_ref,
    out_ref,
    lse_ref,
    query_ref,
    kept_ref,
    entry_ref,
    levels_ref,
    table_t,
    place_t,
    w_kv,
    vec_t,
    query_q,
    total_q,
    top_q,
    mass_q,
    total_p,
    top_p,
    mass_p,
):
    first = lax.axis_index("dp") * sizes.depth
    count_q, count_p = sizes.count
    prepare_tokens(sizes, table_ref, place_ref, table_t, place_t)
    prepare_weights(attn_ref, vec_ref, w_kv, vec_t)
    block = math.gcd(sizes.many, 16)
    for enc in range(2):
        low, high = (0, count_q) if enc == 0 else (count_q, count_q + count_p)
        w_q = low16(attn_ref[0, enc, :, 0:128])

        def ask(step, carry):
            spot = pl.ds(step * block, block)
            held = rows_ref[spot, low:high, :].reshape(block * (high - low), 128)
            x = held.astype(jnp.float32) + place_ref[0, enc, 0:1, :]
            h = norm_rows(x, vector_row(vec_ref, enc, 0), vector_row(vec_ref, enc, 1))
            query = low16(dot(low16(h), w_q) + vector_row(vec_ref, enc, 2))
            query_ref[spot, low:high, :] = query.reshape(block, high - low, 128)
            if enc == 0:
                for half in range(block // 8):
                    query_q[step * (block // 8) + half] = query[half * 8 * count_q : (half + 1) * 8 * count_q]
            return carry

        lax.fori_loop(0, sizes.many // block, ask, 0)
    states = ((total_q, top_q, mass_q), (total_p, top_p, mass_p))
    for total, top, mass in states:
        total[...] = jnp.zeros_like(total)
        mass[...] = jnp.zeros_like(mass)
        top[...] = jnp.full_like(top, NEG)

    def one_level(state):
        level = state[0]
        count = state[2]
        for enc in range(2):
            total, top, mass = states[enc]

            def spans(turn, count):
                steps = [turn * UNROLL + u for u in range(UNROLL)]
                old = [(total[s], top[s][:, 0:1], mass[s]) for s in steps]
                queries = [query_q[s] if enc == 0 else query_ref[s, count_q:, :] for s in steps]
                packed = [pack_span(sizes, enc, s, level, first, raw_ref) for s in steps]
                codes = [part[0] for part in packed]
                for part in packed:
                    count = jnp.maximum(count, part[1])
                found = [gather_span(sizes, enc, code, table_t, place_t) for code in codes]
                made = [project(enc, part[0], vec_t, w_kv) for part in found]
                scores = [
                    dot(two_heads(query), part[1]) * HEAD ** (-0.5) for query, part in zip(queries, made)
                ]
                news = []
                for u in range(UNROLL):
                    mine = own_slots(codes[u], queries[u].shape[0])
                    score = jnp.where(mine, scores[u], NEG)
                    new = jnp.maximum(old[u][1], jnp.max(score, 1, keepdims=True))
                    fade = jnp.exp(old[u][1] - new)
                    expo = jnp.where(mine, jnp.exp(score - new), 0.0)
                    news.append(
                        (
                            old[u][0] * fade + dot_last(low16(expo), made[u][2]),
                            jnp.broadcast_to(new, top.shape[1:]),
                            old[u][2] * fade + jnp.sum(expo, 1, keepdims=True),
                        )
                    )
                for u, s in enumerate(steps):
                    total[s] = news[u][0]
                    top[s] = news[u][1]
                    mass[s] = news[u][2]
                    if sizes.keep:
                        at = s if enc == 0 else sizes.steps[0] + s
                        at = jnp.where(level == 0, at, sizes.spans)
                        kept_ref[at, 0:128, :] = found[u][0]
                        kept_ref[at, 128:129, :] = found[u][1]
                        entry_ref[at, 0:1, :] = codes[u]
                return count

            count = lax.fori_loop(0, sizes.steps[enc] // UNROLL, spans, count)
        need = (jnp.max(count).astype(jnp.int32) + SPAN - 1) // SPAN
        return level + 1, jnp.maximum(need, 1), count

    last = lax.while_loop(
        lambda state: state[0] < state[1],
        one_level,
        (jnp.int32(0), jnp.int32(1), jnp.zeros((8, 128), jnp.float32)),
    )
    levels_ref[0] = last[1]
    lse_ref[...] = jnp.full_like(lse_ref, NEG)
    for enc in range(2):
        total, top, mass = states[enc]

        def close(turn, carry):
            for u in range(UNROLL):
                step = turn * UNROLL + u
                bulk = mass[step]
                some = bulk > 0.0
                safe = jnp.where(some, bulk, 1.0)
                mixed = merge_heads(total[step] / safe)
                lse = jnp.where(some, top[step] + jnp.log(safe), NEG)
                if enc == 1:
                    out_ref[step, count_q:, :] = low16(mixed)
                    at = iota(lse.shape, 0) == iota(lse.shape, 1)
                    lse_ref[step, 0:1, :] = jnp.sum(jnp.where(at, lse, 0.0), 0, keepdims=True)
                else:
                    half = lse.shape[0] // 2
                    row = iota((count_q, 128), 0)
                    lane = iota((count_q, 128), 1)
                    for i in range(8):
                        spot = slice(i * count_q, (i + 1) * count_q)
                        out_ref[step * 8 + i, 0:count_q, :] = low16(mixed[spot])
                        line = jnp.where(lane == row, lse[spot], 0.0) + jnp.where(
                            lane == row + count_q, lse[half + i * count_q : half + (i + 1) * count_q], 0.0
                        )
                        lse_ref[step * 8 + i, 1:2, :] = jnp.sum(line, 0, keepdims=True)
            return carry

        lax.fori_loop(0, sizes.steps[enc] // UNROLL, close, 0)


def token_scratch(sizes):
    return [
        pltpu.VMEM((128, sizes.padded), jnp.bfloat16),
        pltpu.VMEM((2, 2, 128, CHUNK), jnp.bfloat16),
        pltpu.VMEM((2, 256, 128), jnp.bfloat16),
        pltpu.VMEM((2, 128, 128), jnp.float32),
    ]


def local_call(kernel, out_shape, inputs, scratch, name, smem_in=(), smem_out=()):
    vm = pl.BlockSpec(memory_space=pltpu.VMEM)
    sm = pl.BlockSpec(memory_space=pltpu.SMEM)
    return pl.pallas_call(
        kernel,
        out_shape=out_shape,
        in_specs=[sm if i in smem_in else vm for i in range(len(inputs))],
        out_specs=[sm if i in smem_out else vm for i in range(len(out_shape))],
        scratch_shapes=scratch,
        compiler_params=pltpu.CompilerParams(vmem_limit_bytes=VMEM_LIMIT),
        name=name,
    )(*inputs)


def tokens_forward(sizes, every, rows, table, positions, attention, vectors):
    many = sizes.many
    both = sum(sizes.count)
    kept = sizes.spans + 1 if sizes.keep else 1
    state = []
    for enc in range(2):
        tall = 2 * sizes.queries[enc]
        state += [pltpu.VMEM((sizes.steps[enc], tall, 128), jnp.float32)] * 3
    return local_call(
        functools.partial(forward_kernel, sizes),
        (
            jax.ShapeDtypeStruct((many, both, 128), jnp.bfloat16),
            jax.ShapeDtypeStruct((many, 8, 128), jnp.float32),
            jax.ShapeDtypeStruct((many, both, 128), jnp.bfloat16),
            jax.ShapeDtypeStruct((kept, 136, SPAN), jnp.float32),
            jax.ShapeDtypeStruct((kept, 8, SPAN), jnp.int32),
            jax.ShapeDtypeStruct((1,), jnp.int32),
        ),
        (every, rows, table, positions, attention, vectors),
        token_scratch(sizes)
        + [pltpu.VMEM((sizes.steps[0], sizes.queries[0], 128), jnp.bfloat16)]
        + state,
        "tokens_forward",
        smem_out=(5,),
    )


def mix_kernel(
    many, count_q, part_ref, lse_ref, mixed_ref, total_ref, landed, landed_lse, own, own_lse, send, recv
):
    me = enter(many)
    pairs = [
        (lambda peer: part_ref.at[peer], landed),
        (lambda peer: lse_ref.at[peer], landed_lse),
    ]
    spread_start(many, me, pairs, send, recv, 0)
    landed[me] = part_ref[me]
    landed_lse[me] = lse_ref[me]
    spread_wait(many, me, pairs, send, recv, 0)
    parts = landed_lse[...]
    top = jnp.max(parts, 0)
    total = top + jnp.log(jnp.sum(jnp.exp(parts - top[None]), 0))
    own_lse[...] = total
    share = jnp.exp(parts - total[None])
    columns = jnp.transpose(share.reshape(many * 8, 128))
    count_p = part_ref.shape[1] - count_q
    mixed = jnp.zeros((count_q + count_p, 128), jnp.float32)
    lane_q = iota((count_q, 128), 1)
    lane_p = iota((count_p, 128), 1)
    for peer in range(many):
        factor_p = jnp.where(
            lane_p < HEAD,
            columns[0:count_p, peer * 8 : peer * 8 + 1],
            columns[count_p : 2 * count_p, peer * 8 : peer * 8 + 1],
        )
        factor_q = jnp.where(
            lane_q < HEAD,
            columns[0:count_q, peer * 8 + 1 : peer * 8 + 2],
            columns[count_q : 2 * count_q, peer * 8 + 1 : peer * 8 + 2],
        )
        mixed += jnp.concatenate([factor_q, factor_p], 0) * landed[peer].astype(jnp.float32)
    own[...] = low16(mixed)
    pairs = [(lambda peer: own, mixed_ref), (lambda peer: own_lse, total_ref)]
    spread_start(many, me, pairs, send, recv, 2)
    mixed_ref[me] = own[...]
    total_ref[me] = own_lse[...]
    spread_wait(many, me, pairs, send, recv, 2)


def remote_call(kernel, out_shape, inputs, scratch, lanes, many, ident, name):
    return pl.pallas_call(
        kernel,
        out_shape=out_shape,
        in_specs=[pl.BlockSpec(memory_space=pltpu.VMEM)] * len(inputs),
        out_specs=[pl.BlockSpec(memory_space=pltpu.VMEM)] * len(out_shape),
        scratch_shapes=scratch
        + [pltpu.SemaphoreType.DMA((lanes, many)), pltpu.SemaphoreType.DMA((lanes, many))],
        compiler_params=pltpu.CompilerParams(
            collective_id=ident, has_side_effects=True, vmem_limit_bytes=VMEM_LIMIT
        ),
        name=name,
    )(*inputs)


def exchange_mixed(sizes, part, lse):
    many = sizes.many
    both = sum(sizes.count)
    return remote_call(
        functools.partial(mix_kernel, many, sizes.count[0]),
        (
            jax.ShapeDtypeStruct((many, both, 128), jnp.bfloat16),
            jax.ShapeDtypeStruct((many, 8, 128), jnp.float32),
        ),
        (part, lse),
        [
            pltpu.VMEM((many, both, 128), jnp.bfloat16),
            pltpu.VMEM((many, 8, 128), jnp.float32),
            pltpu.VMEM((both, 128), jnp.bfloat16),
            pltpu.VMEM((8, 128), jnp.float32),
        ],
        4,
        many,
        2,
        "exchange_mixed",
    )


def backward_kernel(
    sizes,
    levels_ref,
    raw_ref,
    query_ref,
    mixed_ref,
    lse_ref,
    grad_ref,
    kept_ref,
    entry_ref,
    table_ref,
    place_ref,
    attn_ref,
    vec_ref,
    d_query_ref,
    d_table_ref,
    slice_ref,
    d_vec_ref,
    table_t,
    place_t,
    w_kv,
    vec_t,
    d_place_ref,
    d_attn_ref,
    acc_gain,
    acc_shift,
    acc_value,
    d_query_q,
    d_query_p,
):
    first = lax.axis_index("dp") * sizes.depth
    count_q, count_p = sizes.count
    prepare_weights(attn_ref, vec_ref, w_kv, vec_t)
    begin = 1 if sizes.keep else 0
    again = levels_ref[0] > begin

    @pl.when(again)
    def _():
        prepare_tokens(sizes, table_ref, place_ref, table_t, place_t)

    for ref in (d_table_ref, d_place_ref, d_attn_ref, d_query_q, d_query_p, acc_gain, acc_shift, acc_value):
        ref[...] = jnp.zeros_like(ref)

    def ask_span(enc, step):
        if enc == 0:
            spot = pl.ds(step * 8, 8)
            shape = (8 * count_q, 128)
            found = [ref[spot, 0:count_q, :].reshape(shape) for ref in (query_ref, grad_ref, mixed_ref)]
            lines = [jnp.broadcast_to(lse_ref[step * 8 + i, 1:2, :], (count_q, 128)) for i in range(8)]
            lines = jnp.concatenate(lines, 0)
            row = iota(lines.shape, 0) % count_q
            lane = iota(lines.shape, 1)
            lse = [
                jnp.sum(jnp.where(lane == row + head * count_q, lines, 0.0), 1, keepdims=True)
                for head in range(2)
            ]
            lse = jnp.concatenate(lse, 0)
        else:
            found = [ref[step, count_q:, :] for ref in (query_ref, grad_ref, mixed_ref)]
            lines = jnp.broadcast_to(lse_ref[step, 0:1, :], (2 * count_p, 128))
            lse = jnp.sum(jnp.where(iota(lines.shape, 1) == iota(lines.shape, 0), lines, 0.0), 1, keepdims=True)
        return found + [lse]

    def work(enc, steps, codes, scaleds, rates):
        w_all = low16(attn_ref[0, enc, :, 128:384])
        asked = [ask_span(enc, step) for step in steps]
        made = [project(enc, scaled, vec_t, w_kv) for scaled in scaleds]
        d_queries, d_kvs = ([], [])
        for (query, grad, mixed, lse), code, (a_t, keys_t, values_t) in zip(asked, codes, made):
            both = two_heads(query)
            grads = two_heads(grad)
            base = jnp.sum(
                grads.astype(jnp.float32) * jnp.concatenate([mixed, mixed], 0).astype(jnp.float32),
                1,
                keepdims=True,
            )
            scores = dot(both, keys_t) * HEAD ** (-0.5)
            mine = own_slots(code, query.shape[0])
            probs = jnp.where(mine, jnp.exp(jnp.where(mine, scores, NEG) - lse), 0.0)
            d_probs = dot(grads, values_t)
            d_scores = low16(probs * (d_probs - base))
            d_values = low16(dot_rows(grads, low16(probs)))
            d_keys = low16(dot_rows(both, d_scores) * HEAD ** (-0.5))
            d_queries.append(merge_heads(dot_last(d_scores, keys_t)) * HEAD ** (-0.5))
            d_kvs.append(jnp.concatenate([d_keys, d_values], 0))
        for step, d_query in zip(steps, d_queries):
            if enc == 0:
                d_query_q[step] += d_query
            else:
                d_query_p[step] += d_query
        d_kv = jnp.concatenate(d_kvs, 1)
        a_t = jnp.concatenate([part[0] for part in made], 1)
        scaled = jnp.concatenate(scaleds, 1)
        rate = jnp.concatenate(rates, 1)
        code = jnp.concatenate(codes, 1)
        width = code.shape[1]
        d_attn_ref[enc] += dot_last(a_t, d_kv)
        d_h = dot(w_all, d_kv)
        fold = lambda values: sum(values[:, i * SPAN : (i + 1) * SPAN] for i in range(width // SPAN))
        acc_value[enc] += fold(d_kv[128:].astype(jnp.float32))
        acc_gain[enc] += fold(d_h * scaled)
        acc_shift[enc] += fold(d_h)
        d_scaled = d_h * vec_t[enc, :, 0:1]
        center = d_scaled - jnp.mean(d_scaled, 0, keepdims=True)
        slope = jnp.mean(d_scaled * scaled, 0, keepdims=True)
        d_x = low16((center - scaled * slope) * rate)
        rows = code >> 16
        where = (code >> 8) & 255
        chosen = hot(jnp.broadcast_to(where, (CHUNK, width)) == iota((CHUNK, width), 0))
        d_place_ref[enc] += dot_last(d_x, chosen)
        wide = jnp.broadcast_to(rows, (CHUNK, width))
        for cut in range(sizes.padded // CHUNK):
            spot = slice(cut * CHUNK, (cut + 1) * CHUNK)
            chosen = hot(wide == iota((CHUNK, width), 0) + cut * CHUNK)
            d_table_ref[:, spot] += dot_last(d_x, chosen)

    for enc in range(2):
        if sizes.keep:

            def kept_spans(turn, carry):
                steps = [turn * UNROLL + u for u in range(UNROLL)]
                ats = [s if enc == 0 else sizes.steps[0] + s for s in steps]
                work(
                    enc,
                    steps,
                    [entry_ref[at, 0:1, :] for at in ats],
                    [kept_ref[at, 0:128, :] for at in ats],
                    [kept_ref[at, 128:129, :] for at in ats],
                )
                return carry

            lax.fori_loop(0, sizes.steps[enc] // UNROLL, kept_spans, 0)

        def more_level(level, carry_level):
            def one_span(step, carry):
                code = pack_span(sizes, enc, step, level, first, raw_ref)[0]
                scaled, rate = gather_span(sizes, enc, code, table_t, place_t)
                work(enc, [step], [code], [scaled], [rate])
                return carry

            return lax.fori_loop(0, sizes.steps[enc], one_span, carry_level)

        lax.fori_loop(begin, levels_ref[0], more_level, 0)

    for step in range(sizes.steps[0]):
        d_query_ref[step * 8 : step * 8 + 8, 0:count_q, :] = low16(d_query_q[step]).reshape(8, count_q, 128)
    d_query_ref[:, count_q:, :] = low16(d_query_p[...])
    for enc in range(2):
        for part, block in enumerate((d_place_ref, d_attn_ref)):
            for cut in range(2):
                slice_ref[enc, 2 * part + cut] = block[enc, :, cut * 128 : (cut + 1) * 128].astype(
                    slice_ref.dtype
                )
    d_vec_ref[...] = jnp.zeros_like(d_vec_ref)
    same = iota((128, 128), 0) == iota((128, 128), 1)
    for enc in range(2):
        for row, acc in enumerate((acc_gain, acc_shift, acc_value)):
            tall = jnp.broadcast_to(jnp.sum(acc[enc], 1, keepdims=True), (128, 128))
            d_vec_ref[enc * 4 + row : enc * 4 + row + 1, :] = jnp.sum(jnp.where(same, tall, 0.0), 0, keepdims=True)


def tokens_backward(sizes, levels, every, query, mixed, lse, grad, kept, entry, table, positions, attention, vectors):
    many = sizes.many
    count_p = sizes.count[1]
    both = sum(sizes.count)
    return local_call(
        functools.partial(backward_kernel, sizes),
        (
            jax.ShapeDtypeStruct((many, both, 128), jnp.bfloat16),
            jax.ShapeDtypeStruct((128, sizes.padded), jnp.float32),
            jax.ShapeDtypeStruct((2, 4, 128, 128), sizes.kind),
            jax.ShapeDtypeStruct((8, 128), jnp.float32),
        ),
        (levels, every, query, mixed, lse, grad, kept, entry, table, positions, attention, vectors),
        token_scratch(sizes)
        + [
            pltpu.VMEM((2, 128, CHUNK), jnp.float32),
            pltpu.VMEM((2, 128, 256), jnp.float32),
            pltpu.VMEM((2, 128, SPAN), jnp.float32),
            pltpu.VMEM((2, 128, SPAN), jnp.float32),
            pltpu.VMEM((2, 128, SPAN), jnp.float32),
            pltpu.VMEM((sizes.steps[0], sizes.queries[0], 128), jnp.float32),
            pltpu.VMEM((many, count_p, 128), jnp.float32),
        ],
        "tokens_backward",
        smem_in=(0,),
    )


def adam(weight, grad, first, second):
    first_new = BETA_ONE * first + (1.0 - BETA_ONE) * grad
    second_new = BETA_TWO * second + (1.0 - BETA_TWO) * grad * grad
    fix_one = 1.0 - BETA_ONE**STEP
    fix_two = 1.0 - BETA_TWO**STEP
    ratio = first_new / fix_one / (jnp.sqrt(second_new / fix_two) + ADAM_EPS)
    return (first_new, second_new, weight - INNER_RATE * (ratio + WEIGHT_DECAY * weight))


def pieces_of(depth):
    blocks = [(1, (enc,)) for enc in range(2)] + [(2, (enc,)) for enc in range(2)]
    blocks += [(3, (enc, side)) for enc in range(2) for side in range(2)]
    return blocks + [(4, ())]


def square_sum(values):
    return jnp.sum(jnp.sum(values * values, 0, keepdims=True), 1, keepdims=True)


def finish_kernel(sizes, *refs):
    many = sizes.many
    count_q, count_p = sizes.count
    depth = sizes.depth
    (query_ref, slice_ref, first_ref, d_table_ref, rows_ref, raw_ref, xa_q, xa_p, d_out, d_ffn, d_mid) = refs[:11]
    place_ref, attn_ref, vec_ref = refs[11:14]
    state = refs[14:34]
    norm_ref, g_word, g_place, g_attn, g_vec = refs[34:39]
    theirs = refs[39:44]
    held = refs[44:64]
    mine = refs[64:69]
    (query_all, slice_all, first_all, scalar_all, land_query, land_slice, own_query, own_slice, tile, table_t) = refs[69:79]
    send, recv, load, pair_send, pair_recv = refs[79:84]
    loads = []
    for index in range(20):
        copy = pltpu.make_async_copy(state[index], held[index], load.at[index])
        copy.start()
        loads.append(copy)
    me = lax.axis_index("dp")
    other = 1 - lax.axis_index("grp")
    barrier = pltpu.get_barrier_semaphore()

    def greet(step, carry):
        peer = lax.rem(me + step, many)
        pl.semaphore_signal(barrier, inc=1, device_id={"dp": peer}, device_id_type=MESH)
        return carry

    lax.fori_loop(1, many, greet, 0)
    pl.semaphore_signal(barrier, inc=1, device_id={"grp": other}, device_id_type=MESH)
    pl.semaphore_wait(barrier, many)
    pairs = [
        (lambda peer: query_ref.at[peer], land_query),
        (lambda peer: slice_ref.at[peer], land_slice),
        (lambda peer: first_ref, first_all),
    ]
    spread_start(many, me, pairs, send, recv, 0)
    land_query[me] = query_ref[me]
    land_slice[me] = slice_ref[me]
    first_all[me] = first_ref[...]
    spread_wait(many, me, pairs, send, recv, 0)
    own_query[...] = low16(jnp.sum(land_query[...].astype(jnp.float32), 0))
    own_slice[...] = jnp.sum(land_slice[...].astype(jnp.float32), 0).astype(own_slice.dtype)
    pairs = [(lambda peer: own_query, query_all), (lambda peer: own_slice, slice_all)]
    spread_start(many, me, pairs, send, recv, 3)
    query_all[me] = own_query[...]
    slice_all[me] = own_slice[...]
    spread_wait(many, me, pairs, send, recv, 3)

    first_sum = jnp.sum(first_all[...], 0)
    g_vec[...] = d_mid[...]
    first = me * depth
    table_t[...] = d_table_ref[...]
    blocks = slice_all[...].astype(jnp.float32).reshape(8, 128, 128)
    rest = jnp.zeros((1, 1), jnp.float32)
    for enc in range(2):
        low, high = (0, count_q) if enc == 0 else (count_q, count_q + count_p)
        number = many * (high - low)
        d_query = query_all[:, low:high, :].reshape(number, 128)
        x = rows_ref[:, low:high, :].reshape(number, 128).astype(jnp.float32) + place_ref[0, enc, 0:1, :]
        center = x - jnp.mean(x, -1, keepdims=True)
        rate = lax.rsqrt(jnp.mean(center * center, -1, keepdims=True) + NORM_EPS)
        scaled = center * rate
        gain = vector_row(vec_ref, enc, 0)
        a_low = low16(scaled * gain + vector_row(vec_ref, enc, 1))
        xa = xa_q if enc == 0 else xa_p
        d_h = xa[...] + dot_last(d_query, low16(attn_ref[0, enc, :, 0:128]))
        d_scaled = d_h * gain
        slope = jnp.mean(d_scaled * scaled, -1, keepdims=True)
        d_x = (d_scaled - jnp.mean(d_scaled, -1, keepdims=True) - scaled * slope) * rate
        g_place[enc, 0:128, :] = jnp.transpose(blocks[enc * 4])
        g_place[enc, 128:256, :] = jnp.transpose(blocks[enc * 4 + 1])
        g_place[enc, 0:1, :] += jnp.sum(d_x, 0, keepdims=True)
        g_attn[enc, :, 0:128] = dot_rows(a_low, d_query)
        g_attn[enc, :, 128:256] = blocks[enc * 4 + 2]
        g_attn[enc, :, 256:384] = blocks[enc * 4 + 3]
        g_attn[enc, :, 384:512] = d_out[enc]
        spot = slice(enc, enc + 1)
        g_vec[0, spot, :] = first_sum[enc * 4 : enc * 4 + 1] + jnp.sum(d_h * scaled, 0, keepdims=True)
        g_vec[1, spot, :] = first_sum[enc * 4 + 1 : enc * 4 + 2] + jnp.sum(d_h, 0, keepdims=True)
        g_vec[2, spot, :] = jnp.sum(d_query.astype(jnp.float32), 0, keepdims=True)
        g_vec[3, spot, :] = first_sum[enc * 4 + 2 : enc * 4 + 3]
        if enc == 0:
            columns = [
                part
                for peer in range(many)
                for part in (
                    raw_ref[peer, RAW_Q : RAW_Q + 16, 0:1].astype(jnp.int32)[0 : count_q // 2],
                    raw_ref[peer, RAW_Q : RAW_Q + 16, 64:65].astype(jnp.int32)[0 : count_q // 2],
                )
            ]
        else:
            columns = [raw_ref[peer, 0:count_p, 0:1].astype(jnp.int32) for peer in range(many)]
        spot = jnp.concatenate(columns, 0) - first
        spot = jnp.where(spot < depth, spot, -1)
        d_low = low16(d_x)
        wide = jnp.broadcast_to(spot, (number, CHUNK))
        for cut in range(sizes.padded // CHUNK):
            chosen = hot(wide == iota((number, CHUNK), 1) + cut * CHUNK)
            table_t[:, cut * CHUNK : (cut + 1) * CHUNK] += dot_rows(d_low, chosen)
        rest += square_sum(g_place[enc]) + square_sum(g_attn[enc])
        rest += square_sum(d_ffn[enc, 0]) + square_sum(d_ffn[enc, 1])
    for cut in range(0, depth, 128):
        top = min(cut + 128, depth)
        g_word[cut:top, :] = jnp.transpose(table_t[:, cut : cut + 128])[0 : top - cut]
    small = jnp.sum(g_vec[...] * g_vec[...], 0)
    rest += jnp.sum(jnp.sum(small, 0, keepdims=True), 1, keepdims=True)
    tile[...] = jnp.broadcast_to(square_sum(table_t[...]), (8, 128))
    pairs = [(lambda peer: tile, scalar_all)]
    spread_start(many, me, pairs, send, recv, 5)
    scalar_all[me] = tile[...]
    for copy in loads:
        copy.wait()
    spread_wait(many, me, pairs, send, recv, 5)
    norm = jnp.sqrt(jnp.sum(scalar_all[...], 0)[0:1, 0:1] + rest)
    norm_ref[...] = jnp.broadcast_to(norm, (8, 128))
    factor = CLIP_LIMIT / jnp.maximum(norm, CLIP_LIMIT)
    grads = (g_word, g_place, g_attn, d_ffn, g_vec)

    def differ(kind, at, rows):
        weight, moment, square, anchor = (held[kind * 4 + j] for j in range(4))
        grad = grads[kind][at + (rows,)] * factor
        inner = adam(weight[(0,) + at + (rows,)], grad, moment[(0,) + at + (rows,)], square[(0,) + at + (rows,)])[2]
        mine[kind][at + (rows,)] = anchor[at + (rows,)] - inner

    size = math.gcd(depth, 128)

    def table_block(step, carry):
        differ(0, (), pl.ds(pl.multiple_of(step * size, size), size))
        return carry

    lax.fori_loop(0, depth // size, table_block, 0)
    ways = []

    def hand(kind):
        copy = pltpu.make_async_remote_copy(
            src_ref=mine[kind],
            dst_ref=theirs[kind],
            send_sem=pair_send.at[kind],
            recv_sem=pair_recv.at[kind],
            device_id={"grp": other},
            device_id_type=MESH,
        )
        copy.start()
        ways.append(copy)

    hand(0)
    for kind in range(1, 5):
        for found, at in pieces_of(depth):
            if found == kind:
                differ(kind, at, slice(0, 14) if kind == 4 else slice(None))
        hand(kind)
    for kind in range(5):
        ways[kind].wait()


    def table_add(step, carry):
        rows = pl.ds(pl.multiple_of(step * size, size), size)
        theirs[0][rows] += mine[0][rows]
        return carry

    lax.fori_loop(0, depth // size, table_add, 0)
    for kind, at in pieces_of(depth):
        theirs[kind][at] += mine[kind][at]


def finish(sizes, query, slices, first, d_table, rows, every, xa_q, xa_p, d_out, d_ffn, d_mid, params, state):
    many = sizes.many
    both = sum(sizes.count)
    inputs = (query, slices, first, d_table, rows, every, xa_q, xa_p, d_out, d_ffn, d_mid) + params
    flat = tuple(state[j][kind] for kind in range(5) for j in range(4))
    shapes = [state[3][kind].shape for kind in range(5)]
    vm = pl.BlockSpec(memory_space=pltpu.VMEM)
    hbm = pl.BlockSpec(memory_space=pl.ANY)
    f32 = jnp.float32
    return pl.pallas_call(
        functools.partial(finish_kernel, sizes),
        out_shape=tuple(
            jax.ShapeDtypeStruct(shape, f32)
            for shape in [(8, 128), shapes[0], shapes[1], shapes[2], (16, 2, 128)] + shapes
        ),
        in_specs=[vm] * len(inputs) + [hbm] * 20,
        out_specs=[vm] * 10,
        scratch_shapes=[pltpu.VMEM(value.shape, f32) for value in flat]
        + [pltpu.VMEM(shape, f32) for shape in shapes]
        + [
            pltpu.VMEM((many, both, 128), jnp.bfloat16),
            pltpu.VMEM((many, sizes.lines, 128), sizes.kind),
            pltpu.VMEM((many, 8, 128), f32),
            pltpu.VMEM((many, 8, 128), f32),
            pltpu.VMEM((many, both, 128), jnp.bfloat16),
            pltpu.VMEM((many, sizes.lines, 128), sizes.kind),
            pltpu.VMEM((both, 128), jnp.bfloat16),
            pltpu.VMEM((sizes.lines, 128), sizes.kind),
            pltpu.VMEM((8, 128), f32),
            pltpu.VMEM((128, sizes.padded), f32),
            pltpu.SemaphoreType.DMA((6, many)),
            pltpu.SemaphoreType.DMA((6, many)),
            pltpu.SemaphoreType.DMA((20,)),
            pltpu.SemaphoreType.DMA((5,)),
            pltpu.SemaphoreType.DMA((5,)),
        ],
        compiler_params=pltpu.CompilerParams(
            collective_id=3, has_side_effects=True, vmem_limit_bytes=VMEM_LIMIT
        ),
        name="finish",
    )(*inputs, *flat)


def outputs_kernel(depth, groups, *refs):
    norm_ref, g_vec = refs[:2]
    ins = refs[2:31]
    outs = refs[31:56]
    held = refs[56:85]
    made = refs[85:110]
    load, store = refs[110:112]
    loads, stores = ([], [])
    for index in range(29):
        copy = pltpu.make_async_copy(ins[index], held[index], load.at[index])
        copy.start()
        loads.append(copy)
    norm = norm_ref[0:1, 0:1]
    factor = CLIP_LIMIT / jnp.maximum(norm, CLIP_LIMIT)
    grads = tuple(held[25:29]) + (g_vec,)

    def work(kind, at, rows):
        moment, square, anchor, outer, summed = (held[kind * 5 + j] for j in range(5))
        first, second, average, momentum, weight = (made[kind * 5 + j] for j in range(5))
        spot = at + (rows,)
        deep = (0,) + spot
        grad = grads[kind][spot] * factor
        first[deep] = BETA_ONE * moment[deep] + (1.0 - BETA_ONE) * grad
        second[deep] = BETA_TWO * square[deep] + (1.0 - BETA_TWO) * grad * grad
        mean = summed[spot] / groups
        speed = OUTER_MU * outer[spot] + mean
        average[spot] = mean
        momentum[spot] = speed
        weight[deep] = anchor[spot] - OUTER_RATE * (mean + OUTER_MU * speed)

    def give(kind):
        for j in range(5):
            index = kind * 5 + j
            copy = pltpu.make_async_copy(made[index], outs[index], store.at[index])
            copy.start()
            stores.append(copy)

    size = math.gcd(depth, 128)

    def table_block(step, carry):
        work(0, (), pl.ds(pl.multiple_of(step * size, size), size))
        return carry

    for kind in range(5):
        for j in range(5):
            loads[kind * 5 + j].wait()
        if kind < 4:
            loads[25 + kind].wait()
        if kind == 0:
            lax.fori_loop(0, depth // size, table_block, 0)
        else:
            for found, at in pieces_of(depth):
                if found == kind:
                    work(kind, at, slice(0, 14) if kind == 4 else slice(None))
        give(kind)
    for copy in stores:
        copy.wait()


def make_outputs(norm, grads, firsts, seconds, anchors, outers, summed, groups):
    kinds = range(5)
    flat = tuple(v for kind in kinds for v in (firsts[kind], seconds[kind], anchors[kind], outers[kind], summed[kind]))
    flat += tuple(grads[:4])
    out = tuple(
        jax.ShapeDtypeStruct(shape, jnp.float32)
        for kind in kinds
        for shape in (firsts[kind].shape, firsts[kind].shape, anchors[kind].shape, anchors[kind].shape, firsts[kind].shape)
    )
    vm = pl.BlockSpec(memory_space=pltpu.VMEM)
    hbm = pl.BlockSpec(memory_space=pl.ANY)
    got = pl.pallas_call(
        functools.partial(outputs_kernel, anchors[0].shape[0], groups),
        out_shape=out,
        in_specs=[vm] * 2 + [hbm] * 29,
        out_specs=[hbm] * 25,
        scratch_shapes=[pltpu.VMEM(v.shape, jnp.float32) for v in flat]
        + [pltpu.VMEM(v.shape, jnp.float32) for v in out]
        + [pltpu.SemaphoreType.DMA((29,)), pltpu.SemaphoreType.DMA((25,))],
        compiler_params=pltpu.CompilerParams(vmem_limit_bytes=VMEM_LIMIT),
        name="make_outputs",
    )(norm, grads[4], *flat)
    return [[got[kind * 5 + j] for kind in kinds] for j in range(5)]


def square_norm(values):
    center = values - jnp.mean(values, -1, keepdims=True)
    rate = lax.rsqrt(jnp.mean(center * center, -1, keepdims=True) + NORM_EPS)
    return center * rate, rate


def norm_back(d_scaled, scaled, rate):
    slope = jnp.mean(d_scaled * scaled, -1, keepdims=True)
    return (d_scaled - jnp.mean(d_scaled, -1, keepdims=True) - scaled * slope) * rate


def total_of(values):
    return jnp.sum(jnp.sum(values, 0, keepdims=True), 1, keepdims=True)


def score_terms(scores, drop, target, weight, count, axis):
    masked = jnp.where(drop, MASKED, scores)
    top = jnp.max(masked, axis, keepdims=True)
    expo = jnp.exp(masked - top)
    total = jnp.sum(expo, axis, keepdims=True)
    picked = jnp.sum(jnp.where(target, scores, 0.0), axis, keepdims=True)
    loss = total_of(weight * (top + jnp.log(total) - picked))
    grad = low16((weight / count) * (expo / total - jnp.where(target, 1.0, 0.0)))
    return grad, loss


GELU_A = math.sqrt(2.0 / math.pi)
GELU_B = 0.044715


def class_kernel(
    sizes,
    rows_ref,
    mixed_ref,
    raw_ref,
    place_ref,
    attn_ref,
    ffn_ref,
    vec_ref,
    grad_ref,
    xa_q,
    xa_p,
    d_out,
    d_ffn,
    d_mid,
    score_ref,
    cls_ref,
    scaled_a,
    rate_a,
    scaled_f,
    rate_f,
    pre_ref,
    act_ref,
    low_ref,
    flag_ref,
):
    many = sizes.many
    counts = sizes.count
    totals = (many * counts[0], many * counts[1])
    chunk = totals[0]
    parts = [(0, 0, 0)] + [(1, at, totals[0] + at) for at in range(0, totals[1], chunk)]

    def held(ref, enc, at):
        each = counts[enc]
        low = 0 if enc == 0 else counts[0]
        return ref[at // each : (at + chunk) // each, low : low + each, :].reshape(chunk, 128)

    def weights(enc):
        return (
            low16(attn_ref[0, enc, :, 384:512]),
            low16(ffn_ref[0, enc, 0]),
            low16(ffn_ref[0, enc, 1]),
        )

    for enc, at, spot in parts:
        w_out, w_up, w_down = weights(enc)
        row = functools.partial(vector_row, vec_ref, enc)
        here = slice(spot, spot + chunk)
        x = held(rows_ref, enc, at).astype(jnp.float32) + place_ref[0, enc, 0:1, :]
        h_embed = norm_rows(x, row(0), row(1))
        scaled, rate = square_norm(h_embed + (dot(held(mixed_ref, enc, at), w_out) + row(4)))
        scaled_a[here, :] = scaled
        rate_a[here, :] = jnp.broadcast_to(rate, (chunk, 128))
        h_attn = scaled * row(5) + row(6)
        h_low = low16(h_attn)
        low_ref[here, :] = h_low
        pre = dot(h_low, w_up) + jnp.concatenate([row(10), row(11), row(12), row(13)], 1)
        pre_ref[here, :] = pre
        act = low16(0.5 * pre * (1.0 + jnp.tanh(GELU_A * (pre + GELU_B * (pre * pre * pre)))))
        act_ref[here, :] = act
        scaled, rate = square_norm(h_attn + (dot_last(act, w_down) + row(7)))
        scaled_f[here, :] = scaled
        rate_f[here, :] = jnp.broadcast_to(rate, (chunk, 128))
        cls_ref[here, :] = low16(scaled * row(8) + row(9))

    every_q = cls_ref[0 : totals[0], :]
    every_p = cls_ref[totals[0] :, :]
    flag_ref[...] = jnp.zeros_like(flag_ref)
    for peer in range(many):
        flag_ref[peer : peer + 1, :] = raw_ref[peer, RAW_Q:RAW_ROWS, :].astype(jnp.float32)[8:9]
    turned = jnp.transpose(flag_ref[...])

    def column(low, each):
        tall = jnp.concatenate([turned[low : low + each]] * many, 0)
        at = iota(tall.shape, 1) == iota(tall.shape, 0) // each
        return jnp.sum(jnp.where(at, tall, 0.0), 1, keepdims=True)

    keys_q = column(0, counts[0])
    valid = column(counts[0], counts[0])
    keys_p = column(2 * counts[0], counts[1])
    hot_q = hot(jnp.broadcast_to(keys_q, (totals[0], 128)) == iota((totals[0], 128), 1).astype(jnp.float32))
    hot_p = hot(jnp.broadcast_to(keys_p, (totals[1], 128)) == iota((totals[1], 128), 1).astype(jnp.float32))
    same = dot_last(hot_q, hot_p) > 0.5
    count = jnp.maximum(total_of(valid), 1.0)
    scale = 128 ** (-0.5)
    scores = dot_last(every_q, every_p) * scale
    index_q = iota(scores.shape, 0)
    index_p = iota(scores.shape, 1)
    target_qp = index_p == 2 * index_q
    target_pq = index_p // 2 == index_q
    grad_qp, loss_qp = score_terms(scores, same & ~target_qp, target_qp, valid, count, 1)
    drop_pq = (same | (jnp.broadcast_to(valid, scores.shape) == 0.0)) & ~target_pq
    weight_p = jnp.sum(jnp.where(target_qp, jnp.broadcast_to(valid, scores.shape), 0.0), 0, keepdims=True)
    grad_pq, loss_pq = score_terms(scores, drop_pq, target_pq, weight_p, count, 0)
    lane = iota((8, 128), 1)
    score_ref[...] = jnp.where(lane == 0, loss_qp + loss_pq, count)
    d_q = (dot(grad_qp, every_p) + dot(grad_pq, every_p)) * scale
    d_p = (dot_rows(grad_pq, every_q) + dot_rows(grad_qp, every_q)) * scale

    d_mid[...] = jnp.zeros_like(d_mid)
    d_out[...] = jnp.zeros_like(d_out)
    d_ffn[...] = jnp.zeros_like(d_ffn)
    for enc, at, spot in parts:
        w_out, w_up, w_down = weights(enc)
        row = functools.partial(vector_row, vec_ref, enc)
        here = slice(spot, spot + chunk)

        def add(index, values):
            d_mid[index, enc : enc + 1, :] += jnp.sum(values, 0, keepdims=True)

        d_cls = d_q if enc == 0 else d_p[at : at + chunk]
        scaled = scaled_f[here, :]
        add(8, d_cls * scaled)
        add(9, d_cls)
        d_x_ffn = norm_back(d_cls * row(8), scaled, rate_f[here, :])
        d_branch = low16(d_x_ffn)
        add(7, d_branch.astype(jnp.float32))
        d_ffn[enc, 1] += dot_rows(d_branch, act_ref[here, :])
        d_act = dot(d_branch, w_down)
        pre = pre_ref[here, :]
        square = pre * pre
        bend = jnp.tanh(GELU_A * (pre + GELU_B * (square * pre)))
        slope = 0.5 * (1.0 + bend) + (0.5 * GELU_A) * pre * (1.0 - bend * bend) * (
            1.0 + (3.0 * GELU_B) * square
        )
        d_pre = low16(slope * d_act)
        up_bias = jnp.sum(d_pre.astype(jnp.float32), 0, keepdims=True)
        for cut in range(4):
            d_mid[10 + cut, enc : enc + 1, :] += up_bias[:, cut * 128 : (cut + 1) * 128]
        d_ffn[enc, 0] += dot_rows(low_ref[here, :], d_pre)
        d_h = d_x_ffn + dot_last(d_pre, w_up)
        scaled = scaled_a[here, :]
        add(5, d_h * scaled)
        add(6, d_h)
        d_x = norm_back(d_h * row(5), scaled, rate_a[here, :])
        if enc == 0:
            xa_q[...] = d_x
        else:
            xa_p[at : at + chunk, :] = d_x
        d_proj = low16(d_x)
        add(4, d_proj.astype(jnp.float32))
        d_out[enc] += dot_rows(held(mixed_ref, enc, at), d_proj)
        d_mixed = low16(dot_last(d_proj, w_out))
        each = counts[enc]
        low = 0 if enc == 0 else counts[0]
        grad_ref[at // each : (at + chunk) // each, low : low + each, :] = d_mixed.reshape(
            chunk // each, each, 128
        )


def class_stage(sizes, rows, mixed, every, positions, attention, feedforward, vectors):
    many = sizes.many
    n_q, n_p = (many * sizes.count[0], many * sizes.count[1])
    both = n_q + n_p
    f32 = jnp.float32
    return local_call(
        functools.partial(class_kernel, sizes),
        (
            jax.ShapeDtypeStruct((many, sum(sizes.count), 128), jnp.bfloat16),
            jax.ShapeDtypeStruct((n_q, 128), f32),
            jax.ShapeDtypeStruct((n_p, 128), f32),
            jax.ShapeDtypeStruct((2, 128, 128), f32),
            jax.ShapeDtypeStruct((2, 2, 128, 512), f32),
            jax.ShapeDtypeStruct((16, 2, 128), f32),
            jax.ShapeDtypeStruct((8, 128), f32),
        ),
        (rows, mixed, every, positions, attention, feedforward, vectors),
        [
            pltpu.VMEM((both, 128), jnp.bfloat16),
            pltpu.VMEM((both, 128), f32),
            pltpu.VMEM((both, 128), f32),
            pltpu.VMEM((both, 128), f32),
            pltpu.VMEM((both, 128), f32),
            pltpu.VMEM((both, 512), f32),
            pltpu.VMEM((both, 512), jnp.bfloat16),
            pltpu.VMEM((both, 128), jnp.bfloat16),
            pltpu.VMEM((128, 128), f32),
        ],
        "class_stage",
    )


def class_stage_large(sizes, rows_all, mixed_all, every, positions, attention, feedforward, vectors):
    many = sizes.many
    count_q, count_p = sizes.count
    counts = sizes.count
    width = rows_all.shape[2]
    flags_all = every[:, RAW_FLAGS, :].astype(jnp.int32)
    keys_q = flags_all[:, :count_q].reshape(-1)
    valid_all = flags_all[:, count_q : 2 * count_q].reshape(-1)
    keys_p = flags_all[:, 2 * count_q : 2 * count_q + count_p].reshape(-1)
    cuts = ((0, count_q), (count_q, count_q + count_p))
    cls, class_kept, mixes = ([], [], [])
    for enc in range(2):
        low, high = cuts[enc]
        rows = rows_all[:, low:high].reshape(-1, width)
        mixed = mixed_all[:, low:high].reshape(-1, width)
        low_cls, kept_cls = class_forward(
            rows, mixed, positions[0, enc], attention[0, enc], feedforward[0, enc], vectors[0, :, enc]
        )
        cls.append(low_cls)
        class_kept.append(kept_cls)
        mixes.append(mixed)
    d_q, d_p, loss_total, count = score_stage(cls[0], cls[1], keys_q, keys_p, valid_all)
    d_cls = (d_q, d_p)
    grads, xas, outs, ffns, mids = ([], [], [], [], [])
    for enc in range(2):
        d_mixed, d_x_attn, d_w_out, d_ffn, rows_mid, d_up_bias = class_backward(
            class_kept[enc], mixes[enc], attention[0, enc], feedforward[0, enc], vectors[0, :, enc], d_cls[enc]
        )
        grads.append(d_mixed.reshape(many, counts[enc], width))
        xas.append(d_x_attn)
        outs.append(d_w_out)
        ffns.append(d_ffn)
        mid = jnp.concatenate([jnp.stack(list(rows_mid)), d_up_bias.reshape(-1, width)])
        mids.append(jnp.pad(mid, ((4, 2), (0, 0))))
    lane = jnp.arange(128)[None, :]
    score = jnp.broadcast_to(jnp.where(lane == 0, loss_total, count), (8, 128))
    return (
        jnp.concatenate(grads, 1),
        xas[0],
        xas[1],
        jnp.stack(outs),
        jnp.stack(ffns),
        jnp.stack(mids, 1),
        score,
    )


def class_forward(rows, mixed, place, attn_w, ffn_w, vec):
    width = rows.shape[1]
    h_embed = layer_norm(rows.astype(jnp.float32) + place[:1], vec[0], vec[1])
    x_attn = h_embed + (dot(mixed, low16(attn_w[:, 3 * width :])) + vec[4])
    h_attn = layer_norm(x_attn, vec[5], vec[6])
    h_low = low16(h_attn)
    pre = dot(h_low, low16(ffn_w[0])) + vec[10:].reshape(-1)
    act = low16(gelu_tanh(pre))
    x_ffn = h_attn + (dot_last(act, low16(ffn_w[1])) + vec[7])
    h_out = layer_norm(x_ffn, vec[8], vec[9])
    return low16(h_out), (x_attn, h_low, pre, act, x_ffn)


def class_backward(kept, mixed, attn_w, ffn_w, vec, d_cls):
    x_attn, h_low, pre, act, x_ffn = kept
    width = x_attn.shape[1]
    unused, out_back = jax.vjp(layer_norm, x_ffn, vec[8], vec[9])
    d_x_ffn, d_gain_two, d_shift_two = out_back(d_cls)
    d_branch = low16(d_x_ffn)
    d_down_bias = jnp.sum(d_branch, 0, dtype=jnp.float32)
    d_down = dot_rows(d_branch, act)
    d_act = dot(d_branch, low16(ffn_w[1]))
    unused, gelu_back = jax.vjp(gelu_tanh, pre)
    d_pre = low16(gelu_back(d_act)[0])
    d_up_bias = jnp.sum(d_pre, 0, dtype=jnp.float32)
    d_up = dot_rows(h_low, d_pre)
    d_h_attn = d_x_ffn + dot_last(d_pre, low16(ffn_w[0]))
    unused, attn_back = jax.vjp(layer_norm, x_attn, vec[5], vec[6])
    d_x_attn, d_gain_one, d_shift_one = attn_back(d_h_attn)
    d_proj = low16(d_x_attn)
    d_out_bias = jnp.sum(d_proj, 0, dtype=jnp.float32)
    d_w_out = dot_rows(mixed, d_proj)
    d_mixed = low16(dot_last(d_proj, low16(attn_w[:, 3 * width :])))
    rows = (d_out_bias, d_gain_one, d_shift_one, d_down_bias, d_gain_two, d_shift_two)
    return d_mixed, d_x_attn, d_w_out, jnp.stack([d_up, d_down]), rows, d_up_bias


def softmax_terms(scores, drop, target, weight, count, axis):
    masked = jnp.where(drop, MASKED, scores)
    top = jnp.max(masked, axis, keepdims=True)
    expo = jnp.exp(masked - top)
    total = jnp.sum(expo, axis, keepdims=True)
    lse = top + jnp.log(total)
    picked = jnp.sum(jnp.where(target, scores, 0.0), axis, keepdims=True)
    loss = jnp.sum(weight * (lse - picked))
    grad = low16((weight / count) * (expo / total - target.astype(jnp.float32)))
    return grad, loss


def score_stage(every_q, every_p, keys_q, keys_p, valid_q):
    count = jnp.maximum(jnp.sum(valid_q).astype(jnp.float32), 1.0)
    scale = every_q.shape[1] ** (-0.5)
    index_q = jnp.arange(every_q.shape[0])[:, None]
    index_p = jnp.arange(every_p.shape[0])[None, :]
    scores = dot_last(every_q, every_p) * scale
    same = keys_q[:, None] == keys_p[None, :]
    target_qp = index_p == 2 * index_q
    valid = valid_q.astype(jnp.float32)[:, None]
    grad_qp, loss_qp = softmax_terms(scores, same & ~target_qp, target_qp, valid, count, 1)
    target_pq = index_p // 2 == index_q
    drop_pq = (same | (valid_q[:, None] == 0)) & ~target_pq
    owner_valid = jnp.repeat(valid_q, 2)
    weight_p = jnp.where(index_p[0] % 2 == 0, owner_valid, 0).astype(jnp.float32)[None, :]
    grad_pq, loss_pq = softmax_terms(scores, drop_pq, target_pq, weight_p, count, 0)
    d_q = (dot(grad_qp, every_p) + dot(grad_pq, every_p)) * scale
    d_p = (dot_rows(grad_pq, every_q) + dot_rows(grad_qp, every_q)) * scale
    return d_q, d_p, loss_qp + loss_pq, count


def body(
    question_ids,
    passage_ids,
    question_lengths,
    passage_lengths,
    question_keys,
    passage_keys,
    question_valid,
    word_table,
    positions,
    attention,
    feedforward,
    vectors,
    word_first,
    positions_first,
    attention_first,
    feedforward_first,
    vectors_first,
    word_second,
    positions_second,
    attention_second,
    feedforward_second,
    vectors_second,
    word_anchor,
    positions_anchor,
    attention_anchor,
    feedforward_anchor,
    vectors_anchor,
    word_outer,
    positions_outer,
    attention_outer,
    feedforward_outer,
    vectors_outer,
):
    many = lax.axis_size("dp")
    count_q = question_ids.shape[0]
    count_p = passage_ids.shape[0]
    table = word_table[0]
    sizes = Sizes(many, count_q, count_p, table.shape[0])
    swap = lambda values: jnp.swapaxes(values, -3, -2)
    vectors, vectors_first, vectors_second, vectors_anchor, vectors_outer = (
        swap(v) for v in (vectors, vectors_first, vectors_second, vectors_anchor, vectors_outer)
    )
    every, class_rows = exchange_rows(
        many,
        question_ids,
        passage_ids,
        question_lengths,
        passage_lengths,
        question_keys,
        question_valid,
        passage_keys,
        table,
    )
    part, lse_part, query, kept, entry, levels = tokens_forward(
        sizes, every, class_rows, table, positions, attention, vectors
    )
    mixed_all, lse_all = exchange_mixed(sizes, part, lse_part)
    stage = class_stage if many * count_q <= 512 else class_stage_large
    grad_all, xa_q, xa_p, d_out, d_ffn, d_mid, score = stage(
        sizes, class_rows, mixed_all, every, positions, attention, feedforward, vectors
    )
    d_query, d_table_t, slices, d_first = tokens_backward(
        sizes, levels, every, query, mixed_all, lse_all, grad_all, kept, entry, table, positions, attention, vectors
    )
    weights = (word_table, positions, attention, feedforward, vectors)
    firsts = (word_first, positions_first, attention_first, feedforward_first, vectors_first)
    seconds = (word_second, positions_second, attention_second, feedforward_second, vectors_second)
    anchors = (word_anchor, positions_anchor, attention_anchor, feedforward_anchor, vectors_anchor)
    outers = (word_outer, positions_outer, attention_outer, feedforward_outer, vectors_outer)
    done = finish(
        sizes,
        d_query,
        slices.reshape(many, sizes.lines, 128),
        d_first,
        d_table_t,
        class_rows,
        every,
        xa_q,
        xa_p,
        d_out,
        d_ffn,
        d_mid,
        (positions, attention, vectors),
        (weights, firsts, seconds, anchors),
    )
    norm = done[0]
    grads = (done[1], done[2], done[3], d_ffn, done[4])
    made = make_outputs(
        norm, grads, firsts, seconds, anchors, outers, done[5:10], lax.axis_size("grp")
    )
    first_new, second_new, averages, outer_next, weight_next = (
        part[:4] + [swap(part[4])] for part in made
    )
    norm = norm[0, 0]
    loss_total = score[0, 0]
    count = score[0, 1]
    return (
        loss_total.reshape(1),
        count.reshape(1),
        norm.reshape(1),
        first_new[0],
        first_new[1],
        first_new[2],
        first_new[3],
        first_new[4],
        second_new[0],
        second_new[1],
        second_new[2],
        second_new[3],
        second_new[4],
        averages[0],
        averages[1],
        averages[2],
        averages[3],
        averages[4],
        outer_next[0],
        outer_next[1],
        outer_next[2],
        outer_next[3],
        outer_next[4],
        weight_next[0],
        weight_next[1],
        weight_next[2],
        weight_next[3],
        weight_next[4],
    )


def solution(mesh):
    placed = (
        P(("grp", "dp"), None),
        P(("grp", "dp"), None),
        P(("grp", "dp")),
        P(("grp", "dp")),
        P(("grp", "dp")),
        P(("grp", "dp")),
        P(("grp", "dp")),
        P("grp", "dp", None),
        P("grp", None, None, None),
        P("grp", None, None, None),
        P("grp", None, None, None, None),
        P("grp", None, None, None),
        P("grp", "dp", None),
        P("grp", None, None, None),
        P("grp", None, None, None),
        P("grp", None, None, None, None),
        P("grp", None, None, None),
        P("grp", "dp", None),
        P("grp", None, None, None),
        P("grp", None, None, None),
        P("grp", None, None, None, None),
        P("grp", None, None, None),
        P("dp", None),
        P(),
        P(),
        P(),
        P(),
        P("dp", None),
        P(),
        P(),
        P(),
        P(),
    )
    return jax.shard_map(
        body,
        mesh=mesh,
        in_specs=placed,
        out_specs=(
            P("grp"),
            P("grp"),
            P("grp"),
            P("grp", "dp", None),
            P("grp", None, None, None),
            P("grp", None, None, None),
            P("grp", None, None, None, None),
            P("grp", None, None, None),
            P("grp", "dp", None),
            P("grp", None, None, None),
            P("grp", None, None, None),
            P("grp", None, None, None, None),
            P("grp", None, None, None),
            P("dp", None),
            P(),
            P(),
            P(),
            P(),
            P("dp", None),
            P(),
            P(),
            P(),
            P(),
            P("grp", "dp", None),
            P("grp", None, None, None),
            P("grp", None, None, None),
            P("grp", None, None, None, None),
            P("grp", None, None, None),
        ),
        check_vma=False,
    )
```

```python
import functools
import math

import jax
import jax.numpy as jnp
from jax import lax
from jax.experimental import pallas as pl
from jax.experimental.pallas import tpu as pltpu
from jax.sharding import PartitionSpec as P

HEAD = 64
STEP = 5


NORM_EPS = 1e-05
MASKED = -1000000000.0
BETA_ONE = 0.9
BETA_TWO = 0.999
INNER_RATE = 0.05
WEIGHT_DECAY = 0.01
ADAM_EPS = 1e-08
CLIP_LIMIT = 0.01
OUTER_RATE = 0.7
OUTER_MU = 0.9
CONTRACT_ROWS = (((0,), (0,)), ((), ()))
CONTRACT_LAST = (((1,), (1,)), ((), ()))


def layer_norm(values, gain, shift):
    center = values - jnp.mean(values, -1, keepdims=True)
    spread = jnp.mean(center * center, -1, keepdims=True)
    return center * lax.rsqrt(spread + NORM_EPS) * gain + shift


def gelu_tanh(values):
    return jax.nn.gelu(values, approximate=True)


def low16(values):
    return values.astype(jnp.bfloat16)


NEG = -1e30
MESH = pl.DeviceIdType.MESH
VMEM_LIMIT = 60 * 1024 * 1024
WAYS = 4
SLOTS = 128
SPAN = WAYS * SLOTS
CHUNK = 256
UNROLL = 4
RAW_Q = 64
RAW_FLAGS = 72
RAW_ROWS = 80


def greet_all(many):
    me = lax.axis_index("dp")
    barrier = pltpu.get_barrier_semaphore()

    def greet(step, carry):
        peer = lax.rem(me + step, many)
        pl.semaphore_signal(barrier, inc=1, device_id={"dp": peer}, device_id_type=MESH)
        return carry

    lax.fori_loop(1, many, greet, 0)
    return me


def enter(many):
    me = greet_all(many)
    pl.semaphore_wait(pltpu.get_barrier_semaphore(), many - 1)
    return me


def copy_to(peer, src, dst, send, recv):
    return pltpu.make_async_remote_copy(
        src_ref=src,
        dst_ref=dst,
        send_sem=send,
        recv_sem=recv,
        device_id={"dp": peer},
        device_id_type=MESH,
    )


def spread_start(many, me, pairs, send, recv, slot):
    def step_start(step, carry):
        peer = lax.rem(me + step, many)
        for index, (source, landing) in enumerate(pairs):
            copy_to(
                peer,
                source(peer),
                landing.at[me],
                send.at[slot + index, peer],
                recv.at[slot + index, me],
            ).start()
        return carry

    lax.fori_loop(1, many, step_start, 0)


def spread_wait(many, me, pairs, send, recv, slot):
    def step_wait(step, carry):
        peer = lax.rem(me + step, many)
        for index, (source, landing) in enumerate(pairs):
            copy = copy_to(
                peer,
                source(peer),
                landing.at[peer],
                send.at[slot + index, peer],
                recv.at[slot + index, peer],
            )
            copy.wait_recv()
            copy.wait_send()
        return carry

    lax.fori_loop(1, many, step_wait, 0)


def dot(left, right):
    return jnp.dot(left, right, preferred_element_type=jnp.float32)


def dot_rows(left, right):
    return lax.dot_general(left, right, CONTRACT_ROWS, preferred_element_type=jnp.float32)


def dot_last(left, right):
    return lax.dot_general(left, right, CONTRACT_LAST, preferred_element_type=jnp.float32)


def iota(shape, axis):
    return lax.broadcasted_iota(jnp.int32, shape, axis)


def hot(mask):
    return jnp.where(mask, 1.0, 0.0).astype(jnp.bfloat16)


def first_kernel(
    sizes,
    question_ref,
    passage_ref,
    length_q,
    length_p,
    key_q,
    valid_q,
    key_p,
    table_ref,
    place_ref,
    every_ref,
    rows_ref,
    kept_ref,
    entry_ref,
    count_ref,
    stage,
    raw,
    ask,
    asks,
    low_ref,
    offer,
    landed,
    own,
    table_t,
    place_t,
    send,
    recv,
):
    many = sizes.many
    count_q, count_p = sizes.count
    each = count_q + count_p
    depth = sizes.depth
    half = count_q // 2
    me = greet_all(many)
    lane = iota((1, 128), 1)
    for seq in range(count_p):
        stop = length_p[seq]
        stage[seq : seq + 1, :] = jnp.where(lane < stop, passage_ref[seq : seq + 1, 0:128], -1)
        stage[count_p + seq : count_p + seq + 1, :] = jnp.where(
            lane + 128 < stop, passage_ref[seq : seq + 1, 128:256], -1
        )
    both = jnp.concatenate([question_ref[0:half, :], question_ref[half:count_q, :]], 1)
    for seq in range(half):
        stop = jnp.where(lane < 64, length_q[seq], length_q[half + seq] + 64)
        stage[RAW_Q + seq : RAW_Q + seq + 1, :] = jnp.where(lane < stop, both[seq : seq + 1], -1)
    flags = jnp.zeros((1, 128), jnp.int32)
    for spot in range(count_q):
        flags = jnp.where(lane == spot, key_q[spot], flags)
        flags = jnp.where(lane == count_q + spot, valid_q[spot], flags)
    for spot in range(count_p):
        flags = jnp.where(lane == 2 * count_q + spot, key_p[spot], flags)
    stage[RAW_FLAGS:RAW_ROWS, :] = jnp.broadcast_to(flags, (8, 128))
    raw[...] = stage[...].astype(jnp.int16)
    heads = jnp.concatenate([question_ref[:, 0:1], passage_ref[:, 0:1]], 0)
    diagonal = iota((each, 128), 0) == iota((each, 128), 1)
    heads = jnp.sum(jnp.where(diagonal, jnp.broadcast_to(heads, (each, 128)), 0), 0, keepdims=True)
    ask[...] = jnp.broadcast_to(heads, (8, 128))
    pl.semaphore_wait(pltpu.get_barrier_semaphore(), many - 1)
    ask_pairs = [(lambda peer: ask, asks)]
    raw_pairs = [(lambda peer: raw, every_ref)]
    spread_start(many, me, ask_pairs, send, recv, 0)
    spread_start(many, me, raw_pairs, send, recv, 1)
    asks[me] = ask[...]
    every_ref[me] = raw[...]
    padded = sizes.padded
    if padded > depth:
        low_ref[...] = jnp.zeros_like(low_ref)
    low_ref[0:depth, :] = low16(table_ref[...])
    first = me * depth
    block = math.gcd(many, 16)
    spread_wait(many, me, ask_pairs, send, recv, 0)

    def pick(step, carry):
        found = []
        for i in range(block):
            line = jnp.broadcast_to(asks[step * block + i][0:1, :].astype(jnp.float32), (each, 128))
            found.append(jnp.sum(jnp.where(diagonal, line, 0.0), 1, keepdims=True))
        place = jnp.concatenate(found, 0).astype(jnp.int32) - first
        spot = jnp.where((place >= 0) & (place < depth), place, -1)
        number = spot.shape[0]
        total = jnp.zeros((number, 128), jnp.float32)
        wide = jnp.broadcast_to(spot, (number, CHUNK))
        for at in range(padded // CHUNK):
            chosen = hot(wide == iota((number, CHUNK), 1) + at * CHUNK)
            total += dot(chosen, low_ref[at * CHUNK : (at + 1) * CHUNK, :])
        for i in range(block):
            offer[step * block + i] = low16(total[i * each : (i + 1) * each])
        return carry

    lax.fori_loop(0, many // block, pick, 0)
    offer_pairs = [(lambda peer: offer.at[peer], landed)]
    spread_start(many, me, offer_pairs, send, recv, 2)
    landed[me] = offer[me]
    if sizes.keep:
        prepare_tokens(sizes, table_ref, place_ref, table_t, place_t)
    spread_wait(many, me, raw_pairs, send, recv, 1)

    def spans_of(enc, count):
        def spans(turn, count):
            steps = [turn * sizes.unroll[enc] + u for u in range(sizes.unroll[enc])]
            packed = [pack_span(sizes, enc, s, 0, first, every_ref) for s in steps]
            found = [gather_span(sizes, enc, part[0], table_t, place_t) for part in packed]
            for part in packed:
                count = jnp.maximum(count, part[1])
            for u, s in enumerate(steps):
                at = s if enc == 0 else sizes.steps[0] + s
                kept_ref[at, 0:128, :] = found[u][0]
                kept_ref[at, 128:129, :] = found[u][1]
                entry_ref[at, 0:1, :] = packed[u][0]
            return count

        return lax.fori_loop(0, sizes.steps[enc] // sizes.unroll[enc], spans, count)

    count = jnp.zeros((8, 128), jnp.float32)
    if sizes.keep:
        count = spans_of(0, count)
    spread_wait(many, me, offer_pairs, send, recv, 2)
    own[...] = low16(jnp.sum(landed[...].astype(jnp.float32), 0))
    row_pairs = [(lambda peer: own, rows_ref)]
    spread_start(many, me, row_pairs, send, recv, 3)
    rows_ref[me] = own[...]
    if sizes.keep:
        count = spans_of(1, count)
    count_ref[...] = count
    spread_wait(many, me, row_pairs, send, recv, 3)


def first_stage(sizes, ids_q, ids_p, length_q, length_p, key_q, valid_q, key_p, table, positions):
    many = sizes.many
    padded = sizes.padded
    both = sum(sizes.count)
    vm = pl.BlockSpec(memory_space=pltpu.VMEM)
    sm = pl.BlockSpec(memory_space=pltpu.SMEM)
    kept = sizes.spans if sizes.keep else 1
    return pl.pallas_call(
        functools.partial(first_kernel, sizes),
        out_shape=(
            jax.ShapeDtypeStruct((many, RAW_ROWS, 128), jnp.int16),
            jax.ShapeDtypeStruct((many, both, 128), jnp.bfloat16),
            jax.ShapeDtypeStruct((kept, 136, SPAN), jnp.float32),
            jax.ShapeDtypeStruct((kept, 8, SPAN), jnp.int32),
            jax.ShapeDtypeStruct((8, 128), jnp.float32),
        ),
        in_specs=[vm, vm, sm, sm, sm, sm, sm, vm, vm],
        out_specs=[vm] * 5,
        scratch_shapes=[
            pltpu.VMEM((RAW_ROWS, 128), jnp.int32),
            pltpu.VMEM((RAW_ROWS, 128), jnp.int16),
            pltpu.VMEM((8, 128), jnp.int32),
            pltpu.VMEM((many, 8, 128), jnp.int32),
            pltpu.VMEM((padded, 128), jnp.bfloat16),
            pltpu.VMEM((many, both, 128), jnp.bfloat16),
            pltpu.VMEM((many, both, 128), jnp.bfloat16),
            pltpu.VMEM((both, 128), jnp.bfloat16),
            pltpu.VMEM((128, padded), jnp.bfloat16),
            pltpu.VMEM((2, 2, 128, CHUNK), jnp.bfloat16),
            pltpu.SemaphoreType.DMA((4, many)),
            pltpu.SemaphoreType.DMA((4, many)),
        ],
        compiler_params=pltpu.CompilerParams(
            collective_id=1, has_side_effects=True, vmem_limit_bytes=VMEM_LIMIT
        ),
        name="first_stage",
    )(ids_q, ids_p, length_q, length_p, key_q, valid_q, key_p, table, positions)


def norm_rows(values, gain, shift):
    center = values - jnp.mean(values, -1, keepdims=True)
    spread = jnp.mean(center * center, -1, keepdims=True)
    return center * lax.rsqrt(spread + NORM_EPS) * gain + shift


def two_heads(values):
    lane = iota(values.shape, 1)
    low = jnp.where(lane < HEAD, values, jnp.zeros_like(values))
    high = jnp.where(lane >= HEAD, values, jnp.zeros_like(values))
    return jnp.concatenate([low, high], 0)


def merge_heads(both):
    half = both.shape[0] // 2
    lane = iota((half, both.shape[1]), 1)
    return jnp.where(lane < HEAD, both[:half], both[half:])


class Sizes:
    def __init__(self, many, count_q, count_p, depth):
        self.many = many
        self.count = (count_q, count_p)
        self.depth = depth
        self.padded = -(-depth // CHUNK) * CHUNK
        self.steps = (many // (2 * WAYS), many)
        self.unroll = tuple(math.gcd(UNROLL, step) for step in self.steps)
        self.spans = self.steps[0] + self.steps[1]
        self.devices = (2 * WAYS, 1)
        self.queries = (2 * WAYS * count_q, count_p)
        self.lines = 1024 // many
        self.kind = jnp.bfloat16 if self.lines % 16 == 0 else jnp.float32
        self.keep = self.spans * 136 * SPAN * 4 <= 8 * 1024 * 1024


def vector_row(vec_ref, enc, row):
    return vec_ref[0, row, enc : enc + 1, :]


def prepare_tokens(sizes, table_ref, place_ref, table_t, place_t):
    depth = sizes.depth
    if sizes.padded > depth:
        table_t[...] = jnp.zeros_like(table_t)
    for cut in range(0, depth, 128):
        top = min(cut + 128, depth)
        piece = table_ref[cut:top, :]
        if top - cut < 128:
            piece = jnp.concatenate([piece, jnp.zeros((128 - (top - cut), 128), jnp.float32)], 0)
        table_t[:, cut : cut + 128] = low16(jnp.transpose(piece))
    for enc in range(2):
        place = place_ref[0, enc]
        for cut in range(0, place.shape[0], 128):
            turned = jnp.transpose(place[cut : cut + 128])
            high = low16(turned)
            place_t[enc, 0, :, cut : cut + 128] = high
            place_t[enc, 1, :, cut : cut + 128] = low16(turned - high.astype(jnp.float32))


def prepare_weights(attn_ref, vec_ref, w_kv, vec_t):
    for enc in range(2):
        for cut in range(2):
            w_kv[enc, cut * 128 : (cut + 1) * 128, :] = low16(
                jnp.transpose(attn_ref[0, enc, :, (cut + 1) * 128 : (cut + 2) * 128])
            )
        rows = [vector_row(vec_ref, enc, row) for row in range(4)]
        rows = jnp.concatenate(rows + [jnp.zeros((124, 128), jnp.float32)], 0)
        vec_t[enc] = jnp.transpose(rows)


def lane_pick(values, lanes):
    return jnp.take_along_axis(values, lanes, axis=1, mode="promise_in_bounds")


def pack_span(sizes, enc, step, level, first, raw_ref):
    if enc == 1:
        ids = raw_ref[step, 0:RAW_Q, :].astype(jnp.int32)
    else:
        ids = jnp.concatenate(
            [
                raw_ref[step * 8 + i, RAW_Q:RAW_ROWS, :].astype(jnp.int32)[0:8]
                for i in range(8)
            ],
            0,
        )
    place = ids - first
    owned = (place >= 0) & (place < sizes.depth)
    flag = hot(owned)
    inside = dot(flag, hot(iota((128, 128), 0) <= iota((128, 128), 1)))
    total = dot(flag, jnp.ones((128, 128), jnp.bfloat16))
    before = dot(hot(iota((64, 64), 1) < iota((64, 64), 0)), low16(total))
    reached = (inside + before).astype(jnp.int32)
    start = before.astype(jnp.int32)
    stop = (before + total).astype(jnp.int32)
    line = iota((64, 128), 0)
    codes = []
    for window in range(WAYS):
        slot = iota((64, 128), 1) + (window * SLOTS + level * SPAN)
        lane = jnp.zeros((64, 128), jnp.int32)
        for jump in (64, 32, 16, 8, 4, 2, 1):
            seen = lane_pick(reached, lane + (jump - 1))
            lane = jnp.where(seen <= slot, lane + jump, lane)
        row = lane_pick(place, lane)
        if enc == 1:
            where = (line >> 5) * 128 + lane
            seq = (line & 31) + 1
        else:
            where = lane & 63
            seq = (line >> 3) * sizes.count[0] + (lane >> 6) * 8 + (line & 7) + 1
        code = (row << 16) + (where << 8) + seq
        code = jnp.where((slot >= start) & (slot < stop), code, 0)
        codes.append(jnp.sum(code, 0, keepdims=True))
    return jnp.concatenate(codes, 1), (before + total)[56:64]


def gather_span(sizes, enc, code, table_t, place_t):
    rows = code >> 16
    where = (code >> 8) & 255
    x = jnp.zeros((128, SPAN), jnp.float32)
    wide = jnp.broadcast_to(rows, (CHUNK, SPAN))
    for cut in range(sizes.padded // CHUNK):
        chosen = hot(wide == iota((CHUNK, SPAN), 0) + cut * CHUNK)
        x += dot(table_t[:, cut * CHUNK : (cut + 1) * CHUNK], chosen)
    chosen = hot(jnp.broadcast_to(where, (CHUNK, SPAN)) == iota((CHUNK, SPAN), 0))
    x += dot(place_t[enc, 0], chosen) + dot(place_t[enc, 1], chosen)
    center = x - jnp.mean(x, 0, keepdims=True)
    rate = lax.rsqrt(jnp.mean(center * center, 0, keepdims=True) + NORM_EPS)
    return center * rate, rate


def project(enc, scaled, vec_t, w_kv):
    a_t = low16(scaled * vec_t[enc, :, 0:1] + vec_t[enc, :, 1:2])
    kv = dot(w_kv[enc], a_t)
    keys_t = low16(kv[:128])
    values_t = low16(kv[128:] + vec_t[enc, :, 3:4])
    return a_t, keys_t, values_t


def own_slots(code, number):
    line = iota((2 * number, SPAN), 0)
    line = jnp.where(line >= number, line - number, line)
    return line == (code & 255) - 1


def forward_kernel(
    sizes,
    raw_ref,
    rows_ref,
    kept_ref,
    entry_ref,
    count_ref,
    table_ref,
    place_ref,
    attn_ref,
    vec_ref,
    out_ref,
    lse_ref,
    query_ref,
    levels_ref,
    table_t,
    place_t,
    w_kv,
    vec_t,
    query_q,
    total_q,
    top_q,
    mass_q,
    total_p,
    top_p,
    mass_p,
):
    first = lax.axis_index("dp") * sizes.depth
    count_q, count_p = sizes.count
    prepare_weights(attn_ref, vec_ref, w_kv, vec_t)
    begin = 1 if sizes.keep else 0
    count = count_ref[...]
    block = math.gcd(sizes.many, 16)
    for enc in range(2):
        low, high = (0, count_q) if enc == 0 else (count_q, count_q + count_p)
        w_q = low16(attn_ref[0, enc, :, 0:128])

        def ask(step, carry):
            spot = pl.ds(step * block, block)
            held = rows_ref[spot, low:high, :].reshape(block * (high - low), 128)
            x = held.astype(jnp.float32) + place_ref[0, enc, 0:1, :]
            h = norm_rows(x, vector_row(vec_ref, enc, 0), vector_row(vec_ref, enc, 1))
            query = low16(dot(low16(h), w_q) + vector_row(vec_ref, enc, 2))
            query_ref[spot, low:high, :] = query.reshape(block, high - low, 128)
            if enc == 0:
                for half in range(block // 8):
                    query_q[step * (block // 8) + half] = query[half * 8 * count_q : (half + 1) * 8 * count_q]
            return carry

        lax.fori_loop(0, sizes.many // block, ask, 0)
    states = ((total_q, top_q, mass_q), (total_p, top_p, mass_p))
    lse_ref[...] = jnp.full_like(lse_ref, NEG)

    def close(enc, step, total, top, mass):
        some = mass > 0.0
        safe = jnp.where(some, mass, 1.0)
        mixed = merge_heads(total / safe)
        lse = jnp.where(some, top + jnp.log(safe), NEG)
        if enc == 1:
            out_ref[step, count_q:, :] = low16(mixed)
            at = iota(lse.shape, 0) == iota(lse.shape, 1)
            lse_ref[step, 0:1, :] = jnp.sum(jnp.where(at, lse, 0.0), 0, keepdims=True)
        else:
            half = lse.shape[0] // 2
            row = iota((count_q, 128), 0)
            lane = iota((count_q, 128), 1)
            for i in range(8):
                spot = slice(i * count_q, (i + 1) * count_q)
                out_ref[step * 8 + i, 0:count_q, :] = low16(mixed[spot])
                line = jnp.where(lane == row, lse[spot], 0.0) + jnp.where(
                    lane == row + count_q, lse[half + i * count_q : half + (i + 1) * count_q], 0.0
                )
                lse_ref[step * 8 + i, 1:2, :] = jnp.sum(line, 0, keepdims=True)

    def attend(enc, steps, codes, scaleds, olds):
        queries = [query_q[s] if enc == 0 else query_ref[s, count_q:, :] for s in steps]
        made = [project(enc, scaled, vec_t, w_kv) for scaled in scaleds]
        scores = [dot(two_heads(query), part[1]) * HEAD ** (-0.5) for query, part in zip(queries, made)]
        news = []
        for u, score in enumerate(scores):
            mine = own_slots(codes[u], queries[u].shape[0])
            score = jnp.where(mine, score, NEG)
            new = jnp.max(score, 1, keepdims=True)
            if olds is not None:
                new = jnp.maximum(olds[u][1][:, 0:1], new)
            expo = jnp.where(mine, jnp.exp(score - new), 0.0)
            total = dot_last(low16(expo), made[u][2])
            mass = jnp.sum(expo, 1, keepdims=True)
            if olds is not None:
                fade = jnp.exp(olds[u][1] - new)
                total = olds[u][0] * fade + total
                mass = olds[u][2] * fade + mass
            wide = (score.shape[0], 128)
            news.append((total, jnp.broadcast_to(new, wide), jnp.broadcast_to(mass, wide)))
        for u, s in enumerate(steps):
            for ref, value in zip(states[enc], news[u]):
                ref[s] = value
        return news

    for enc in range(2):
        if sizes.keep:

            def kept_spans(turn, carry):
                steps = [turn * sizes.unroll[enc] + u for u in range(sizes.unroll[enc])]
                ats = [s if enc == 0 else sizes.steps[0] + s for s in steps]
                news = attend(
                    enc, steps, [entry_ref[at, 0:1, :] for at in ats], [kept_ref[at, 0:128, :] for at in ats], None
                )
                for s, new in zip(steps, news):
                    close(enc, s, *new)
                return carry

            lax.fori_loop(0, sizes.steps[enc] // sizes.unroll[enc], kept_spans, 0)
        else:
            total, top, mass = states[enc]
            total[...] = jnp.zeros_like(total)
            mass[...] = jnp.zeros_like(mass)
            top[...] = jnp.full_like(top, NEG)

    def needed(count):
        return jnp.maximum((jnp.max(count).astype(jnp.int32) + SPAN - 1) // SPAN, 1)

    start = needed(count)
    levels_ref[0] = start

    @pl.when(start > begin)
    def _():
        prepare_tokens(sizes, table_ref, place_ref, table_t, place_t)

        def one_level(state):
            level, unused, count = state
            for enc in range(2):

                def one_span(step, count):
                    code, found = pack_span(sizes, enc, step, level, first, raw_ref)
                    scaled = gather_span(sizes, enc, code, table_t, place_t)[0]
                    attend(enc, [step], [code], [scaled], [tuple(ref[step] for ref in states[enc])])
                    return jnp.maximum(count, found)

                count = lax.fori_loop(0, sizes.steps[enc], one_span, count)
            return level + 1, needed(count), count

        last = lax.while_loop(
            lambda state: state[0] < state[1], one_level, (jnp.int32(begin), start, count)
        )
        levels_ref[0] = last[1]
        for enc in range(2):

            def close_span(step, carry):
                close(enc, step, *(ref[step] for ref in states[enc]))
                return carry

            lax.fori_loop(0, sizes.steps[enc], close_span, 0)


def token_scratch(sizes):
    return [
        pltpu.VMEM((128, sizes.padded), jnp.bfloat16),
        pltpu.VMEM((2, 2, 128, CHUNK), jnp.bfloat16),
        pltpu.VMEM((2, 256, 128), jnp.bfloat16),
        pltpu.VMEM((2, 128, 128), jnp.float32),
    ]


def local_call(kernel, out_shape, inputs, scratch, name, smem_in=(), smem_out=()):
    vm = pl.BlockSpec(memory_space=pltpu.VMEM)
    sm = pl.BlockSpec(memory_space=pltpu.SMEM)
    return pl.pallas_call(
        kernel,
        out_shape=out_shape,
        in_specs=[sm if i in smem_in else vm for i in range(len(inputs))],
        out_specs=[sm if i in smem_out else vm for i in range(len(out_shape))],
        scratch_shapes=scratch,
        compiler_params=pltpu.CompilerParams(vmem_limit_bytes=VMEM_LIMIT),
        name=name,
    )(*inputs)


def tokens_forward(sizes, every, rows, kept, entry, counted, table, positions, attention, vectors):
    many = sizes.many
    both = sum(sizes.count)
    state = []
    for enc in range(2):
        tall = 2 * sizes.queries[enc]
        state += [pltpu.VMEM((sizes.steps[enc], tall, 128), jnp.float32)] * 3
    return local_call(
        functools.partial(forward_kernel, sizes),
        (
            jax.ShapeDtypeStruct((many, both, 128), jnp.bfloat16),
            jax.ShapeDtypeStruct((many, 8, 128), jnp.float32),
            jax.ShapeDtypeStruct((many, both, 128), jnp.bfloat16),
            jax.ShapeDtypeStruct((1,), jnp.int32),
        ),
        (every, rows, kept, entry, counted, table, positions, attention, vectors),
        token_scratch(sizes)
        + [pltpu.VMEM((sizes.steps[0], sizes.queries[0], 128), jnp.bfloat16)]
        + state,
        "tokens_forward",
        smem_out=(3,),
    )


def mix_kernel(
    many, count_q, part_ref, lse_ref, mixed_ref, total_ref, landed, landed_lse, own, own_lse, send, recv
):
    me = enter(many)
    pairs = [
        (lambda peer: part_ref.at[peer], landed),
        (lambda peer: lse_ref.at[peer], landed_lse),
    ]
    spread_start(many, me, pairs, send, recv, 0)
    landed[me] = part_ref[me]
    landed_lse[me] = lse_ref[me]
    spread_wait(many, me, pairs, send, recv, 0)
    parts = landed_lse[...]
    top = jnp.max(parts, 0)
    total = top + jnp.log(jnp.sum(jnp.exp(parts - top[None]), 0))
    own_lse[...] = total
    share = jnp.exp(parts - total[None])
    columns = jnp.transpose(share.reshape(many * 8, 128))
    count_p = part_ref.shape[1] - count_q
    mixed = jnp.zeros((count_q + count_p, 128), jnp.float32)
    lane_q = iota((count_q, 128), 1)
    lane_p = iota((count_p, 128), 1)
    for peer in range(many):
        factor_p = jnp.where(
            lane_p < HEAD,
            columns[0:count_p, peer * 8 : peer * 8 + 1],
            columns[count_p : 2 * count_p, peer * 8 : peer * 8 + 1],
        )
        factor_q = jnp.where(
            lane_q < HEAD,
            columns[0:count_q, peer * 8 + 1 : peer * 8 + 2],
            columns[count_q : 2 * count_q, peer * 8 + 1 : peer * 8 + 2],
        )
        mixed += jnp.concatenate([factor_q, factor_p], 0) * landed[peer].astype(jnp.float32)
    own[...] = low16(mixed)
    pairs = [(lambda peer: own, mixed_ref), (lambda peer: own_lse, total_ref)]
    spread_start(many, me, pairs, send, recv, 2)
    mixed_ref[me] = own[...]
    total_ref[me] = own_lse[...]
    spread_wait(many, me, pairs, send, recv, 2)


def remote_call(kernel, out_shape, inputs, scratch, lanes, many, ident, name):
    return pl.pallas_call(
        kernel,
        out_shape=out_shape,
        in_specs=[pl.BlockSpec(memory_space=pltpu.VMEM)] * len(inputs),
        out_specs=[pl.BlockSpec(memory_space=pltpu.VMEM)] * len(out_shape),
        scratch_shapes=scratch
        + [pltpu.SemaphoreType.DMA((lanes, many)), pltpu.SemaphoreType.DMA((lanes, many))],
        compiler_params=pltpu.CompilerParams(
            collective_id=ident, has_side_effects=True, vmem_limit_bytes=VMEM_LIMIT
        ),
        name=name,
    )(*inputs)


def exchange_mixed(sizes, part, lse):
    many = sizes.many
    both = sum(sizes.count)
    return remote_call(
        functools.partial(mix_kernel, many, sizes.count[0]),
        (
            jax.ShapeDtypeStruct((many, both, 128), jnp.bfloat16),
            jax.ShapeDtypeStruct((many, 8, 128), jnp.float32),
        ),
        (part, lse),
        [
            pltpu.VMEM((many, both, 128), jnp.bfloat16),
            pltpu.VMEM((many, 8, 128), jnp.float32),
            pltpu.VMEM((both, 128), jnp.bfloat16),
            pltpu.VMEM((8, 128), jnp.float32),
        ],
        4,
        many,
        2,
        "exchange_mixed",
    )


def backward_kernel(
    sizes,
    levels_ref,
    raw_ref,
    query_ref,
    mixed_ref,
    lse_ref,
    grad_ref,
    kept_ref,
    entry_ref,
    table_ref,
    place_ref,
    attn_ref,
    vec_ref,
    d_query_ref,
    d_table_ref,
    slice_ref,
    d_vec_ref,
    table_t,
    place_t,
    w_kv,
    vec_t,
    d_place_ref,
    d_attn_ref,
    acc_gain,
    acc_shift,
    acc_value,
    d_query_q,
    d_query_p,
):
    first = lax.axis_index("dp") * sizes.depth
    count_q, count_p = sizes.count
    prepare_weights(attn_ref, vec_ref, w_kv, vec_t)
    begin = 1 if sizes.keep else 0
    again = levels_ref[0] > begin

    @pl.when(again)
    def _():
        prepare_tokens(sizes, table_ref, place_ref, table_t, place_t)

    for ref in (d_table_ref, d_place_ref, d_attn_ref, d_query_q, d_query_p, acc_gain, acc_shift, acc_value):
        ref[...] = jnp.zeros_like(ref)

    def ask_span(enc, step):
        if enc == 0:
            spot = pl.ds(step * 8, 8)
            shape = (8 * count_q, 128)
            found = [ref[spot, 0:count_q, :].reshape(shape) for ref in (query_ref, grad_ref, mixed_ref)]
            lines = [jnp.broadcast_to(lse_ref[step * 8 + i, 1:2, :], (count_q, 128)) for i in range(8)]
            lines = jnp.concatenate(lines, 0)
            row = iota(lines.shape, 0) % count_q
            lane = iota(lines.shape, 1)
            lse = [
                jnp.sum(jnp.where(lane == row + head * count_q, lines, 0.0), 1, keepdims=True)
                for head in range(2)
            ]
            lse = jnp.concatenate(lse, 0)
        else:
            found = [ref[step, count_q:, :] for ref in (query_ref, grad_ref, mixed_ref)]
            lines = jnp.broadcast_to(lse_ref[step, 0:1, :], (2 * count_p, 128))
            lse = jnp.sum(jnp.where(iota(lines.shape, 1) == iota(lines.shape, 0), lines, 0.0), 1, keepdims=True)
        return found + [lse]

    def work(enc, steps, codes, scaleds, rates):
        w_all = low16(attn_ref[0, enc, :, 128:384])
        asked = [ask_span(enc, step) for step in steps]
        made = [project(enc, scaled, vec_t, w_kv) for scaled in scaleds]
        d_queries, d_kvs = ([], [])
        for (query, grad, mixed, lse), code, (a_t, keys_t, values_t) in zip(asked, codes, made):
            both = two_heads(query)
            grads = two_heads(grad)
            base = jnp.sum(
                grads.astype(jnp.float32) * jnp.concatenate([mixed, mixed], 0).astype(jnp.float32),
                1,
                keepdims=True,
            )
            scores = dot(both, keys_t) * HEAD ** (-0.5)
            mine = own_slots(code, query.shape[0])
            probs = jnp.where(mine, jnp.exp(jnp.where(mine, scores, NEG) - lse), 0.0)
            d_probs = dot(grads, values_t)
            d_scores = low16(probs * (d_probs - base))
            d_values = low16(dot_rows(grads, low16(probs)))
            d_keys = low16(dot_rows(both, d_scores) * HEAD ** (-0.5))
            d_queries.append(merge_heads(dot_last(d_scores, keys_t)) * HEAD ** (-0.5))
            d_kvs.append(jnp.concatenate([d_keys, d_values], 0))
        for step, d_query in zip(steps, d_queries):
            if enc == 0:
                d_query_q[step] += d_query
            else:
                d_query_p[step] += d_query
        d_kv = jnp.concatenate(d_kvs, 1)
        a_t = jnp.concatenate([part[0] for part in made], 1)
        scaled = jnp.concatenate(scaleds, 1)
        rate = jnp.concatenate(rates, 1)
        code = jnp.concatenate(codes, 1)
        width = code.shape[1]
        d_attn_ref[enc] += dot_last(a_t, d_kv)
        d_h = dot(w_all, d_kv)
        fold = lambda values: sum(values[:, i * SPAN : (i + 1) * SPAN] for i in range(width // SPAN))
        acc_value[enc] += fold(d_kv[128:].astype(jnp.float32))
        acc_gain[enc] += fold(d_h * scaled)
        acc_shift[enc] += fold(d_h)
        d_scaled = d_h * vec_t[enc, :, 0:1]
        center = d_scaled - jnp.mean(d_scaled, 0, keepdims=True)
        slope = jnp.mean(d_scaled * scaled, 0, keepdims=True)
        d_x = low16((center - scaled * slope) * rate)
        rows = code >> 16
        where = (code >> 8) & 255
        chosen = hot(jnp.broadcast_to(where, (CHUNK, width)) == iota((CHUNK, width), 0))
        d_place_ref[enc] += dot_last(d_x, chosen)
        wide = jnp.broadcast_to(rows, (CHUNK, width))
        for cut in range(sizes.padded // CHUNK):
            spot = slice(cut * CHUNK, (cut + 1) * CHUNK)
            chosen = hot(wide == iota((CHUNK, width), 0) + cut * CHUNK)
            d_table_ref[spot, :] += dot_last(chosen, d_x)

    for enc in range(2):
        if sizes.keep:

            def kept_spans(turn, carry):
                steps = [turn * sizes.unroll[enc] + u for u in range(sizes.unroll[enc])]
                ats = [s if enc == 0 else sizes.steps[0] + s for s in steps]
                work(
                    enc,
                    steps,
                    [entry_ref[at, 0:1, :] for at in ats],
                    [kept_ref[at, 0:128, :] for at in ats],
                    [kept_ref[at, 128:129, :] for at in ats],
                )
                return carry

            lax.fori_loop(0, sizes.steps[enc] // sizes.unroll[enc], kept_spans, 0)

        def more_level(level, carry_level):
            def one_span(step, carry):
                code = pack_span(sizes, enc, step, level, first, raw_ref)[0]
                scaled, rate = gather_span(sizes, enc, code, table_t, place_t)
                work(enc, [step], [code], [scaled], [rate])
                return carry

            return lax.fori_loop(0, sizes.steps[enc], one_span, carry_level)

        lax.fori_loop(begin, levels_ref[0], more_level, 0)

    for step in range(sizes.steps[0]):
        d_query_ref[step * 8 : step * 8 + 8, 0:count_q, :] = low16(d_query_q[step]).reshape(8, count_q, 128)
    d_query_ref[:, count_q:, :] = low16(d_query_p[...])
    for enc in range(2):
        for part, block in enumerate((d_place_ref, d_attn_ref)):
            for cut in range(2):
                slice_ref[enc, 2 * part + cut] = block[enc, :, cut * 128 : (cut + 1) * 128].astype(
                    slice_ref.dtype
                )
    d_vec_ref[...] = jnp.zeros_like(d_vec_ref)
    same = iota((128, 128), 0) == iota((128, 128), 1)
    for enc in range(2):
        for row, acc in enumerate((acc_gain, acc_shift, acc_value)):
            tall = jnp.broadcast_to(jnp.sum(acc[enc], 1, keepdims=True), (128, 128))
            d_vec_ref[enc * 4 + row : enc * 4 + row + 1, :] = jnp.sum(jnp.where(same, tall, 0.0), 0, keepdims=True)


def tokens_backward(sizes, levels, every, query, mixed, lse, grad, kept, entry, table, positions, attention, vectors):
    many = sizes.many
    count_p = sizes.count[1]
    both = sum(sizes.count)
    return local_call(
        functools.partial(backward_kernel, sizes),
        (
            jax.ShapeDtypeStruct((many, both, 128), jnp.bfloat16),
            jax.ShapeDtypeStruct((sizes.padded, 128), jnp.float32),
            jax.ShapeDtypeStruct((2, 4, 128, 128), sizes.kind),
            jax.ShapeDtypeStruct((8, 128), jnp.float32),
        ),
        (levels, every, query, mixed, lse, grad, kept, entry, table, positions, attention, vectors),
        token_scratch(sizes)
        + [
            pltpu.VMEM((2, 128, CHUNK), jnp.float32),
            pltpu.VMEM((2, 128, 256), jnp.float32),
            pltpu.VMEM((2, 128, SPAN), jnp.float32),
            pltpu.VMEM((2, 128, SPAN), jnp.float32),
            pltpu.VMEM((2, 128, SPAN), jnp.float32),
            pltpu.VMEM((sizes.steps[0], sizes.queries[0], 128), jnp.float32),
            pltpu.VMEM((many, count_p, 128), jnp.float32),
        ],
        "tokens_backward",
        smem_in=(0,),
    )


def adam(weight, grad, first, second):
    first_new = BETA_ONE * first + (1.0 - BETA_ONE) * grad
    second_new = BETA_TWO * second + (1.0 - BETA_TWO) * grad * grad
    fix_one = 1.0 - BETA_ONE**STEP
    fix_two = 1.0 - BETA_TWO**STEP
    ratio = first_new / fix_one / (jnp.sqrt(second_new / fix_two) + ADAM_EPS)
    return (first_new, second_new, weight - INNER_RATE * (ratio + WEIGHT_DECAY * weight))


def pieces_of(depth):
    blocks = [(1, (enc,)) for enc in range(2)] + [(2, (enc,)) for enc in range(2)]
    blocks += [(3, (enc, side)) for enc in range(2) for side in range(2)]
    return blocks + [(4, ())]


def square_sum(values):
    return jnp.sum(jnp.sum(values * values, 0, keepdims=True), 1, keepdims=True)


def finish_kernel(sizes, *refs):
    many = sizes.many
    count_q, count_p = sizes.count
    depth = sizes.depth
    (query_ref, slice_ref, first_ref, d_table_ref, rows_ref, raw_ref, xa_q, xa_p, d_out, d_ffn, d_mid) = refs[:11]
    place_ref, attn_ref, vec_ref = refs[11:14]
    state = refs[14:34]
    norm_ref, g_word, g_place, g_attn, g_vec = refs[34:39]
    joined = refs[39:44]
    held = refs[44:64]
    mine = refs[64:69]
    theirs = refs[69:74]
    (query_all, slice_all, first_all, scalar_all, land_query, land_slice, own_query, own_slice, tile, table_t) = refs[74:84]
    send, recv, load, pair_send, pair_recv = refs[84:89]
    loads = []
    for index in range(20):
        copy = pltpu.make_async_copy(state[index], held[index], load.at[index])
        copy.start()
        loads.append(copy)
    me = lax.axis_index("dp")
    other = 1 - lax.axis_index("grp")
    barrier = pltpu.get_barrier_semaphore()

    def greet(step, carry):
        peer = lax.rem(me + step, many)
        pl.semaphore_signal(barrier, inc=1, device_id={"dp": peer}, device_id_type=MESH)
        return carry

    lax.fori_loop(1, many, greet, 0)
    pl.semaphore_signal(barrier, inc=1, device_id={"grp": other}, device_id_type=MESH)
    pl.semaphore_wait(barrier, many)
    query_pairs = [(lambda peer: query_ref.at[peer], land_query)]
    slice_pairs = [(lambda peer: slice_ref.at[peer], land_slice), (lambda peer: first_ref, first_all)]
    spread_start(many, me, query_pairs, send, recv, 0)
    spread_start(many, me, slice_pairs, send, recv, 1)
    land_query[me] = query_ref[me]
    land_slice[me] = slice_ref[me]
    first_all[me] = first_ref[...]
    spread_wait(many, me, query_pairs, send, recv, 0)
    own_query[...] = low16(jnp.sum(land_query[...].astype(jnp.float32), 0))
    query_back = [(lambda peer: own_query, query_all)]
    spread_start(many, me, query_back, send, recv, 3)
    query_all[me] = own_query[...]
    spread_wait(many, me, slice_pairs, send, recv, 1)
    own_slice[...] = jnp.sum(land_slice[...].astype(jnp.float32), 0).astype(own_slice.dtype)
    slice_back = [(lambda peer: own_slice, slice_all)]
    spread_start(many, me, slice_back, send, recv, 4)
    slice_all[me] = own_slice[...]
    spread_wait(many, me, query_back, send, recv, 3)

    first_sum = jnp.sum(first_all[...], 0)
    g_vec[...] = d_mid[...]
    first = me * depth
    table_t[...] = jnp.zeros_like(table_t)
    rest = jnp.zeros((1, 1), jnp.float32)
    places = []
    for enc in range(2):
        low, high = (0, count_q) if enc == 0 else (count_q, count_q + count_p)
        number = many * (high - low)
        d_query = query_all[:, low:high, :].reshape(number, 128)
        x = rows_ref[:, low:high, :].reshape(number, 128).astype(jnp.float32) + place_ref[0, enc, 0:1, :]
        center = x - jnp.mean(x, -1, keepdims=True)
        rate = lax.rsqrt(jnp.mean(center * center, -1, keepdims=True) + NORM_EPS)
        scaled = center * rate
        gain = vector_row(vec_ref, enc, 0)
        a_low = low16(scaled * gain + vector_row(vec_ref, enc, 1))
        xa = xa_q if enc == 0 else xa_p
        d_h = xa[...] + dot_last(d_query, low16(attn_ref[0, enc, :, 0:128]))
        d_scaled = d_h * gain
        slope = jnp.mean(d_scaled * scaled, -1, keepdims=True)
        d_x = (d_scaled - jnp.mean(d_scaled, -1, keepdims=True) - scaled * slope) * rate
        d_place = jnp.sum(d_x, 0, keepdims=True)
        places.append(d_place)
        g_attn[enc, :, 0:128] = dot_rows(a_low, d_query)
        g_attn[enc, :, 384:512] = d_out[enc]
        spot = slice(enc, enc + 1)
        g_vec[0, spot, :] = first_sum[enc * 4 : enc * 4 + 1] + jnp.sum(d_h * scaled, 0, keepdims=True)
        g_vec[1, spot, :] = first_sum[enc * 4 + 1 : enc * 4 + 2] + jnp.sum(d_h, 0, keepdims=True)
        g_vec[2, spot, :] = jnp.sum(d_query.astype(jnp.float32), 0, keepdims=True)
        g_vec[3, spot, :] = first_sum[enc * 4 + 2 : enc * 4 + 3]
        if enc == 0:
            columns = [
                part
                for peer in range(many)
                for part in (
                    raw_ref[peer, RAW_Q : RAW_Q + 16, 0:1].astype(jnp.int32)[0 : count_q // 2],
                    raw_ref[peer, RAW_Q : RAW_Q + 16, 64:65].astype(jnp.int32)[0 : count_q // 2],
                )
            ]
        else:
            columns = [raw_ref[peer, 0:count_p, 0:1].astype(jnp.int32) for peer in range(many)]
        spot = jnp.concatenate(columns, 0) - first
        spot = jnp.where(spot < depth, spot, -1)
        d_low = low16(d_x)
        wide = jnp.broadcast_to(spot, (number, CHUNK))
        for cut in range(sizes.padded // CHUNK):
            chosen = hot(wide == iota((number, CHUNK), 1) + cut * CHUNK)
            table_t[:, cut * CHUNK : (cut + 1) * CHUNK] += dot_rows(d_low, chosen)
        rest += square_sum(d_ffn[enc, 0]) + square_sum(d_ffn[enc, 1])
    for cut in range(0, depth, 128):
        top = min(cut + 128, depth)
        g_word[cut:top, :] = d_table_ref[cut:top, :] + jnp.transpose(table_t[:, cut : cut + 128])[0 : top - cut]
    tile[...] = jnp.broadcast_to(square_sum(g_word[...]), (8, 128))
    pairs = [(lambda peer: tile, scalar_all)]
    spread_start(many, me, pairs, send, recv, 5)
    scalar_all[me] = tile[...]
    small = jnp.sum(g_vec[...] * g_vec[...], 0)
    rest += jnp.sum(jnp.sum(small, 0, keepdims=True), 1, keepdims=True)
    spread_wait(many, me, slice_back, send, recv, 4)
    blocks = slice_all[...].astype(jnp.float32).reshape(8, 128, 128)
    for enc in range(2):
        g_place[enc, 0:128, :] = jnp.transpose(blocks[enc * 4])
        g_place[enc, 128:256, :] = jnp.transpose(blocks[enc * 4 + 1])
        g_place[enc, 0:1, :] += places[enc]
        g_attn[enc, :, 128:256] = blocks[enc * 4 + 2]
        g_attn[enc, :, 256:384] = blocks[enc * 4 + 3]
        rest += square_sum(g_place[enc]) + square_sum(g_attn[enc])
    for copy in loads:
        copy.wait()
    spread_wait(many, me, pairs, send, recv, 5)
    norm = jnp.sqrt(jnp.sum(scalar_all[...], 0)[0:1, 0:1] + rest)
    norm_ref[...] = jnp.broadcast_to(norm, (8, 128))
    factor = CLIP_LIMIT / jnp.maximum(norm, CLIP_LIMIT)
    grads = (g_word, g_place, g_attn, d_ffn, g_vec)

    def differ(kind, at, rows):
        weight, moment, square, anchor = (held[kind * 4 + j] for j in range(4))
        grad = grads[kind][at + (rows,)] * factor
        inner = adam(weight[(0,) + at + (rows,)], grad, moment[(0,) + at + (rows,)], square[(0,) + at + (rows,)])[2]
        mine[kind][at + (rows,)] = (anchor[at + (rows,)] - inner).astype(mine[kind].dtype)

    size = math.gcd(depth, 128)

    def table_block(step, carry):
        differ(0, (), pl.ds(pl.multiple_of(step * size, size), size))
        return carry

    lax.fori_loop(0, depth // size, table_block, 0)
    ways = []

    def hand(kind):
        copy = pltpu.make_async_remote_copy(
            src_ref=mine[kind],
            dst_ref=theirs[kind],
            send_sem=pair_send.at[kind],
            recv_sem=pair_recv.at[kind],
            device_id={"grp": other},
            device_id_type=MESH,
        )
        copy.start()
        ways.append(copy)

    hand(0)
    for kind in range(1, 5):
        for found, at in pieces_of(depth):
            if found == kind:
                differ(kind, at, slice(0, 14) if kind == 4 else slice(None))
        hand(kind)
    def join(kind, spot):
        joined[kind][spot] = mine[kind][spot].astype(jnp.float32) + theirs[kind][spot].astype(jnp.float32)

    def table_add(step, carry):
        join(0, pl.ds(pl.multiple_of(step * size, size), size))
        return carry

    ways[0].wait()
    lax.fori_loop(0, depth // size, table_add, 0)
    for kind in range(1, 5):
        ways[kind].wait()
        for found, at in pieces_of(depth):
            if found == kind:
                join(kind, at if at else slice(None))


def finish(sizes, query, slices, first, d_table, rows, every, xa_q, xa_p, d_out, d_ffn, d_mid, params, state):
    many = sizes.many
    both = sum(sizes.count)
    inputs = (query, slices, first, d_table, rows, every, xa_q, xa_p, d_out, d_ffn, d_mid) + params
    flat = tuple(state[j][kind] for kind in range(5) for j in range(4))
    shapes = [state[3][kind].shape for kind in range(5)]
    vm = pl.BlockSpec(memory_space=pltpu.VMEM)
    hbm = pl.BlockSpec(memory_space=pl.ANY)
    f32 = jnp.float32
    return pl.pallas_call(
        functools.partial(finish_kernel, sizes),
        out_shape=tuple(
            jax.ShapeDtypeStruct(shape, f32)
            for shape in [(8, 128), shapes[0], shapes[1], shapes[2], (16, 2, 128)] + shapes
        ),
        in_specs=[vm] * len(inputs) + [hbm] * 20,
        out_specs=[vm] * 10,
        scratch_shapes=[pltpu.VMEM(value.shape, f32) for value in flat]
        + [pltpu.VMEM(shape, jnp.bfloat16 if kind < 4 else f32) for kind, shape in enumerate(shapes)] * 2
        + [
            pltpu.VMEM((many, both, 128), jnp.bfloat16),
            pltpu.VMEM((many, sizes.lines, 128), sizes.kind),
            pltpu.VMEM((many, 8, 128), f32),
            pltpu.VMEM((many, 8, 128), f32),
            pltpu.VMEM((many, both, 128), jnp.bfloat16),
            pltpu.VMEM((many, sizes.lines, 128), sizes.kind),
            pltpu.VMEM((both, 128), jnp.bfloat16),
            pltpu.VMEM((sizes.lines, 128), sizes.kind),
            pltpu.VMEM((8, 128), f32),
            pltpu.VMEM((128, sizes.padded), f32),
            pltpu.SemaphoreType.DMA((6, many)),
            pltpu.SemaphoreType.DMA((6, many)),
            pltpu.SemaphoreType.DMA((20,)),
            pltpu.SemaphoreType.DMA((5,)),
            pltpu.SemaphoreType.DMA((5,)),
        ],
        compiler_params=pltpu.CompilerParams(
            collective_id=3, has_side_effects=True, vmem_limit_bytes=VMEM_LIMIT
        ),
        name="finish",
    )(*inputs, *flat)


def output_parts(depth):
    rows = depth // 3 if depth % 24 == 0 else depth
    parts = [(0, slice(at, at + rows)) for at in range(0, depth, rows)]
    return parts + [(kind, None) for kind in (3, 2, 1, 4)]


def outputs_kernel(depth, groups, *refs):
    norm_ref, g_vec = refs[:2]
    ins = refs[2:31]
    outs = refs[31:56]
    held = refs[56:85]
    made = refs[85:110]
    load, store = refs[110:112]
    parts = output_parts(depth)
    loads, stores = ([], [])
    for number, (kind, rows) in enumerate(parts):
        group = []
        for j in range(6 if kind < 4 else 5):
            index = kind * 5 + j if j < 5 else 25 + kind
            source, target = (ins[index], held[index])
            if rows is not None:
                lead = (0,) if len(source.shape) == 3 else ()
                source, target = (source.at[lead + (rows,)], target.at[lead + (rows,)])
            copy = pltpu.make_async_copy(source, target, load.at[number, j])
            copy.start()
            group.append(copy)
        loads.append(group)
    norm = norm_ref[0:1, 0:1]
    factor = CLIP_LIMIT / jnp.maximum(norm, CLIP_LIMIT)
    grads = tuple(held[25:29]) + (g_vec,)

    def work(kind, at, rows):
        moment, square, anchor, outer, summed = (held[kind * 5 + j] for j in range(5))
        first, second, average, momentum, weight = (made[kind * 5 + j] for j in range(5))
        spot = at + (rows,)
        deep = (0,) + spot
        grad = grads[kind][spot] * factor
        first[deep] = BETA_ONE * moment[deep] + (1.0 - BETA_ONE) * grad
        second[deep] = BETA_TWO * square[deep] + (1.0 - BETA_TWO) * grad * grad
        mean = summed[spot] / groups
        speed = OUTER_MU * outer[spot] + mean
        average[spot] = mean
        momentum[spot] = speed
        weight[deep] = anchor[spot] - OUTER_RATE * (mean + OUTER_MU * speed)

    for number, (kind, rows) in enumerate(parts):
        for copy in loads[number]:
            copy.wait()
        if kind == 0:
            size = math.gcd(rows.stop - rows.start, 128)

            def table_block(step, carry):
                work(0, (), pl.ds(pl.multiple_of(rows.start + step * size, size), size))
                return carry

            lax.fori_loop(0, (rows.stop - rows.start) // size, table_block, 0)
        else:
            for found, at in pieces_of(depth):
                if found == kind:
                    work(kind, at, slice(0, 14) if kind == 4 else slice(None))
        for j in range(5):
            source, target = (made[kind * 5 + j], outs[kind * 5 + j])
            if rows is not None:
                lead = (0,) if len(source.shape) == 3 else ()
                source, target = (source.at[lead + (rows,)], target.at[lead + (rows,)])
            copy = pltpu.make_async_copy(source, target, store.at[number, j])
            copy.start()
            stores.append(copy)
    for copy in stores:
        copy.wait()


def make_outputs(norm, grads, firsts, seconds, anchors, outers, summed, groups):
    kinds = range(5)
    flat = tuple(v for kind in kinds for v in (firsts[kind], seconds[kind], anchors[kind], outers[kind], summed[kind]))
    flat += tuple(grads[:4])
    out = tuple(
        jax.ShapeDtypeStruct(shape, jnp.float32)
        for kind in kinds
        for shape in (firsts[kind].shape, firsts[kind].shape, anchors[kind].shape, anchors[kind].shape, firsts[kind].shape)
    )
    vm = pl.BlockSpec(memory_space=pltpu.VMEM)
    hbm = pl.BlockSpec(memory_space=pl.ANY)
    got = pl.pallas_call(
        functools.partial(outputs_kernel, anchors[0].shape[0], groups),
        out_shape=out,
        in_specs=[vm] * 2 + [hbm] * 29,
        out_specs=[hbm] * 25,
        scratch_shapes=[pltpu.VMEM(v.shape, jnp.float32) for v in flat]
        + [pltpu.VMEM(v.shape, jnp.float32) for v in out]
        + [pltpu.SemaphoreType.DMA((7, 6)), pltpu.SemaphoreType.DMA((7, 5))],
        compiler_params=pltpu.CompilerParams(vmem_limit_bytes=VMEM_LIMIT),
        name="make_outputs",
    )(norm, grads[4], *flat)
    return [[got[kind * 5 + j] for kind in kinds] for j in range(5)]


def square_norm(values):
    center = values - jnp.mean(values, -1, keepdims=True)
    rate = lax.rsqrt(jnp.mean(center * center, -1, keepdims=True) + NORM_EPS)
    return center * rate, rate


def norm_back(d_scaled, scaled, rate):
    slope = jnp.mean(d_scaled * scaled, -1, keepdims=True)
    return (d_scaled - jnp.mean(d_scaled, -1, keepdims=True) - scaled * slope) * rate


def total_of(values):
    return jnp.sum(jnp.sum(values, 0, keepdims=True), 1, keepdims=True)


def score_terms(scores, drop, target, weight, count, axis):
    masked = jnp.where(drop, MASKED, scores)
    top = jnp.max(masked, axis, keepdims=True)
    expo = jnp.exp(masked - top)
    total = jnp.sum(expo, axis, keepdims=True)
    picked = jnp.sum(jnp.where(target, scores, 0.0), axis, keepdims=True)
    loss = total_of(weight * (top + jnp.log(total) - picked))
    grad = low16((weight / count) * (expo / total - jnp.where(target, 1.0, 0.0)))
    return grad, loss


GELU_A = math.sqrt(2.0 / math.pi)
GELU_B = 0.044715


def class_kernel(
    sizes,
    rows_ref,
    mixed_ref,
    raw_ref,
    place_ref,
    attn_ref,
    ffn_ref,
    vec_ref,
    grad_ref,
    xa_q,
    xa_p,
    d_out,
    d_ffn,
    d_mid,
    score_ref,
    cls_ref,
    scaled_a,
    rate_a,
    scaled_f,
    rate_f,
    pre_ref,
    act_ref,
    low_ref,
    flag_ref,
):
    many = sizes.many
    counts = sizes.count
    totals = (many * counts[0], many * counts[1])
    chunk = totals[0]
    parts = [(0, 0, 0)] + [(1, at, totals[0] + at) for at in range(0, totals[1], chunk)]

    def held(ref, enc, at):
        each = counts[enc]
        low = 0 if enc == 0 else counts[0]
        return ref[at // each : (at + chunk) // each, low : low + each, :].reshape(chunk, 128)

    def weights(enc):
        return (
            low16(attn_ref[0, enc, :, 384:512]),
            low16(ffn_ref[0, enc, 0]),
            low16(ffn_ref[0, enc, 1]),
        )

    for enc, at, spot in parts:
        w_out, w_up, w_down = weights(enc)
        row = functools.partial(vector_row, vec_ref, enc)
        here = slice(spot, spot + chunk)
        x = held(rows_ref, enc, at).astype(jnp.float32) + place_ref[0, enc, 0:1, :]
        h_embed = norm_rows(x, row(0), row(1))
        scaled, rate = square_norm(h_embed + (dot(held(mixed_ref, enc, at), w_out) + row(4)))
        scaled_a[here, :] = scaled
        rate_a[here, :] = jnp.broadcast_to(rate, (chunk, 128))
        h_attn = scaled * row(5) + row(6)
        h_low = low16(h_attn)
        low_ref[here, :] = h_low
        pre = dot(h_low, w_up) + jnp.concatenate([row(10), row(11), row(12), row(13)], 1)
        pre_ref[here, :] = pre
        act = low16(0.5 * pre * (1.0 + jnp.tanh(GELU_A * (pre + GELU_B * (pre * pre * pre)))))
        act_ref[here, :] = act
        scaled, rate = square_norm(h_attn + (dot_last(act, w_down) + row(7)))
        scaled_f[here, :] = scaled
        rate_f[here, :] = jnp.broadcast_to(rate, (chunk, 128))
        cls_ref[here, :] = low16(scaled * row(8) + row(9))

    every_q = cls_ref[0 : totals[0], :]
    every_p = cls_ref[totals[0] :, :]
    flag_ref[...] = jnp.zeros_like(flag_ref)
    for peer in range(many):
        flag_ref[peer : peer + 1, :] = raw_ref[peer, RAW_Q:RAW_ROWS, :].astype(jnp.float32)[8:9]
    turned = jnp.transpose(flag_ref[...])

    def column(low, each):
        tall = jnp.concatenate([turned[low : low + each]] * many, 0)
        at = iota(tall.shape, 1) == iota(tall.shape, 0) // each
        return jnp.sum(jnp.where(at, tall, 0.0), 1, keepdims=True)

    keys_q = column(0, counts[0])
    valid = column(counts[0], counts[0])
    keys_p = column(2 * counts[0], counts[1])
    hot_q = hot(jnp.broadcast_to(keys_q, (totals[0], 128)) == iota((totals[0], 128), 1).astype(jnp.float32))
    hot_p = hot(jnp.broadcast_to(keys_p, (totals[1], 128)) == iota((totals[1], 128), 1).astype(jnp.float32))
    same = dot_last(hot_q, hot_p) > 0.5
    count = jnp.maximum(total_of(valid), 1.0)
    scale = 128 ** (-0.5)
    scores = dot_last(every_q, every_p) * scale
    index_q = iota(scores.shape, 0)
    index_p = iota(scores.shape, 1)
    target_qp = index_p == 2 * index_q
    target_pq = index_p // 2 == index_q
    grad_qp, loss_qp = score_terms(scores, same & ~target_qp, target_qp, valid, count, 1)
    drop_pq = (same | (jnp.broadcast_to(valid, scores.shape) == 0.0)) & ~target_pq
    weight_p = jnp.sum(jnp.where(target_qp, jnp.broadcast_to(valid, scores.shape), 0.0), 0, keepdims=True)
    grad_pq, loss_pq = score_terms(scores, drop_pq, target_pq, weight_p, count, 0)
    lane = iota((8, 128), 1)
    score_ref[...] = jnp.where(lane == 0, loss_qp + loss_pq, count)
    d_q = (dot(grad_qp, every_p) + dot(grad_pq, every_p)) * scale
    d_p = (dot_rows(grad_pq, every_q) + dot_rows(grad_qp, every_q)) * scale

    d_mid[...] = jnp.zeros_like(d_mid)
    d_out[...] = jnp.zeros_like(d_out)
    d_ffn[...] = jnp.zeros_like(d_ffn)
    for enc, at, spot in parts:
        w_out, w_up, w_down = weights(enc)
        row = functools.partial(vector_row, vec_ref, enc)
        here = slice(spot, spot + chunk)

        def add(index, values):
            d_mid[index, enc : enc + 1, :] += jnp.sum(values, 0, keepdims=True)

        d_cls = d_q if enc == 0 else d_p[at : at + chunk]
        scaled = scaled_f[here, :]
        add(8, d_cls * scaled)
        add(9, d_cls)
        d_x_ffn = norm_back(d_cls * row(8), scaled, rate_f[here, :])
        d_branch = low16(d_x_ffn)
        add(7, d_branch.astype(jnp.float32))
        d_ffn[enc, 1] += dot_rows(d_branch, act_ref[here, :])
        d_act = dot(d_branch, w_down)
        pre = pre_ref[here, :]
        square = pre * pre
        bend = jnp.tanh(GELU_A * (pre + GELU_B * (square * pre)))
        slope = 0.5 * (1.0 + bend) + (0.5 * GELU_A) * pre * (1.0 - bend * bend) * (
            1.0 + (3.0 * GELU_B) * square
        )
        d_pre = low16(slope * d_act)
        up_bias = jnp.sum(d_pre.astype(jnp.float32), 0, keepdims=True)
        for cut in range(4):
            d_mid[10 + cut, enc : enc + 1, :] += up_bias[:, cut * 128 : (cut + 1) * 128]
        d_ffn[enc, 0] += dot_rows(low_ref[here, :], d_pre)
        d_h = d_x_ffn + dot_last(d_pre, w_up)
        scaled = scaled_a[here, :]
        add(5, d_h * scaled)
        add(6, d_h)
        d_x = norm_back(d_h * row(5), scaled, rate_a[here, :])
        if enc == 0:
            xa_q[...] = d_x
        else:
            xa_p[at : at + chunk, :] = d_x
        d_proj = low16(d_x)
        add(4, d_proj.astype(jnp.float32))
        d_out[enc] += dot_rows(held(mixed_ref, enc, at), d_proj)
        d_mixed = low16(dot_last(d_proj, w_out))
        each = counts[enc]
        low = 0 if enc == 0 else counts[0]
        grad_ref[at // each : (at + chunk) // each, low : low + each, :] = d_mixed.reshape(
            chunk // each, each, 128
        )


def class_stage(sizes, rows, mixed, every, positions, attention, feedforward, vectors):
    many = sizes.many
    n_q, n_p = (many * sizes.count[0], many * sizes.count[1])
    both = n_q + n_p
    f32 = jnp.float32
    return local_call(
        functools.partial(class_kernel, sizes),
        (
            jax.ShapeDtypeStruct((many, sum(sizes.count), 128), jnp.bfloat16),
            jax.ShapeDtypeStruct((n_q, 128), f32),
            jax.ShapeDtypeStruct((n_p, 128), f32),
            jax.ShapeDtypeStruct((2, 128, 128), f32),
            jax.ShapeDtypeStruct((2, 2, 128, 512), f32),
            jax.ShapeDtypeStruct((16, 2, 128), f32),
            jax.ShapeDtypeStruct((8, 128), f32),
        ),
        (rows, mixed, every, positions, attention, feedforward, vectors),
        [
            pltpu.VMEM((both, 128), jnp.bfloat16),
            pltpu.VMEM((both, 128), f32),
            pltpu.VMEM((both, 128), f32),
            pltpu.VMEM((both, 128), f32),
            pltpu.VMEM((both, 128), f32),
            pltpu.VMEM((both, 512), f32),
            pltpu.VMEM((both, 512), jnp.bfloat16),
            pltpu.VMEM((both, 128), jnp.bfloat16),
            pltpu.VMEM((128, 128), f32),
        ],
        "class_stage",
    )


def class_stage_large(sizes, rows_all, mixed_all, every, positions, attention, feedforward, vectors):
    many = sizes.many
    count_q, count_p = sizes.count
    counts = sizes.count
    width = rows_all.shape[2]
    flags_all = every[:, RAW_FLAGS, :].astype(jnp.int32)
    keys_q = flags_all[:, :count_q].reshape(-1)
    valid_all = flags_all[:, count_q : 2 * count_q].reshape(-1)
    keys_p = flags_all[:, 2 * count_q : 2 * count_q + count_p].reshape(-1)
    cuts = ((0, count_q), (count_q, count_q + count_p))
    cls, class_kept, mixes = ([], [], [])
    for enc in range(2):
        low, high = cuts[enc]
        rows = rows_all[:, low:high].reshape(-1, width)
        mixed = mixed_all[:, low:high].reshape(-1, width)
        low_cls, kept_cls = class_forward(
            rows, mixed, positions[0, enc], attention[0, enc], feedforward[0, enc], vectors[0, :, enc]
        )
        cls.append(low_cls)
        class_kept.append(kept_cls)
        mixes.append(mixed)
    d_q, d_p, loss_total, count = score_stage(cls[0], cls[1], keys_q, keys_p, valid_all)
    d_cls = (d_q, d_p)
    grads, xas, outs, ffns, mids = ([], [], [], [], [])
    for enc in range(2):
        d_mixed, d_x_attn, d_w_out, d_ffn, rows_mid, d_up_bias = class_backward(
            class_kept[enc], mixes[enc], attention[0, enc], feedforward[0, enc], vectors[0, :, enc], d_cls[enc]
        )
        grads.append(d_mixed.reshape(many, counts[enc], width))
        xas.append(d_x_attn)
        outs.append(d_w_out)
        ffns.append(d_ffn)
        mid = jnp.concatenate([jnp.stack(list(rows_mid)), d_up_bias.reshape(-1, width)])
        mids.append(jnp.pad(mid, ((4, 2), (0, 0))))
    lane = jnp.arange(128)[None, :]
    score = jnp.broadcast_to(jnp.where(lane == 0, loss_total, count), (8, 128))
    return (
        jnp.concatenate(grads, 1),
        xas[0],
        xas[1],
        jnp.stack(outs),
        jnp.stack(ffns),
        jnp.stack(mids, 1),
        score,
    )


def class_forward(rows, mixed, place, attn_w, ffn_w, vec):
    width = rows.shape[1]
    h_embed = layer_norm(rows.astype(jnp.float32) + place[:1], vec[0], vec[1])
    x_attn = h_embed + (dot(mixed, low16(attn_w[:, 3 * width :])) + vec[4])
    h_attn = layer_norm(x_attn, vec[5], vec[6])
    h_low = low16(h_attn)
    pre = dot(h_low, low16(ffn_w[0])) + vec[10:].reshape(-1)
    act = low16(gelu_tanh(pre))
    x_ffn = h_attn + (dot_last(act, low16(ffn_w[1])) + vec[7])
    h_out = layer_norm(x_ffn, vec[8], vec[9])
    return low16(h_out), (x_attn, h_low, pre, act, x_ffn)


def class_backward(kept, mixed, attn_w, ffn_w, vec, d_cls):
    x_attn, h_low, pre, act, x_ffn = kept
    width = x_attn.shape[1]
    unused, out_back = jax.vjp(layer_norm, x_ffn, vec[8], vec[9])
    d_x_ffn, d_gain_two, d_shift_two = out_back(d_cls)
    d_branch = low16(d_x_ffn)
    d_down_bias = jnp.sum(d_branch, 0, dtype=jnp.float32)
    d_down = dot_rows(d_branch, act)
    d_act = dot(d_branch, low16(ffn_w[1]))
    unused, gelu_back = jax.vjp(gelu_tanh, pre)
    d_pre = low16(gelu_back(d_act)[0])
    d_up_bias = jnp.sum(d_pre, 0, dtype=jnp.float32)
    d_up = dot_rows(h_low, d_pre)
    d_h_attn = d_x_ffn + dot_last(d_pre, low16(ffn_w[0]))
    unused, attn_back = jax.vjp(layer_norm, x_attn, vec[5], vec[6])
    d_x_attn, d_gain_one, d_shift_one = attn_back(d_h_attn)
    d_proj = low16(d_x_attn)
    d_out_bias = jnp.sum(d_proj, 0, dtype=jnp.float32)
    d_w_out = dot_rows(mixed, d_proj)
    d_mixed = low16(dot_last(d_proj, low16(attn_w[:, 3 * width :])))
    rows = (d_out_bias, d_gain_one, d_shift_one, d_down_bias, d_gain_two, d_shift_two)
    return d_mixed, d_x_attn, d_w_out, jnp.stack([d_up, d_down]), rows, d_up_bias


def softmax_terms(scores, drop, target, weight, count, axis):
    masked = jnp.where(drop, MASKED, scores)
    top = jnp.max(masked, axis, keepdims=True)
    expo = jnp.exp(masked - top)
    total = jnp.sum(expo, axis, keepdims=True)
    lse = top + jnp.log(total)
    picked = jnp.sum(jnp.where(target, scores, 0.0), axis, keepdims=True)
    loss = jnp.sum(weight * (lse - picked))
    grad = low16((weight / count) * (expo / total - target.astype(jnp.float32)))
    return grad, loss


def score_stage(every_q, every_p, keys_q, keys_p, valid_q):
    count = jnp.maximum(jnp.sum(valid_q).astype(jnp.float32), 1.0)
    scale = every_q.shape[1] ** (-0.5)
    index_q = jnp.arange(every_q.shape[0])[:, None]
    index_p = jnp.arange(every_p.shape[0])[None, :]
    scores = dot_last(every_q, every_p) * scale
    same = keys_q[:, None] == keys_p[None, :]
    target_qp = index_p == 2 * index_q
    valid = valid_q.astype(jnp.float32)[:, None]
    grad_qp, loss_qp = softmax_terms(scores, same & ~target_qp, target_qp, valid, count, 1)
    target_pq = index_p // 2 == index_q
    drop_pq = (same | (valid_q[:, None] == 0)) & ~target_pq
    owner_valid = jnp.repeat(valid_q, 2)
    weight_p = jnp.where(index_p[0] % 2 == 0, owner_valid, 0).astype(jnp.float32)[None, :]
    grad_pq, loss_pq = softmax_terms(scores, drop_pq, target_pq, weight_p, count, 0)
    d_q = (dot(grad_qp, every_p) + dot(grad_pq, every_p)) * scale
    d_p = (dot_rows(grad_pq, every_q) + dot_rows(grad_qp, every_q)) * scale
    return d_q, d_p, loss_qp + loss_pq, count


def body(
    question_ids,
    passage_ids,
    question_lengths,
    passage_lengths,
    question_keys,
    passage_keys,
    question_valid,
    word_table,
    positions,
    attention,
    feedforward,
    vectors,
    word_first,
    positions_first,
    attention_first,
    feedforward_first,
    vectors_first,
    word_second,
    positions_second,
    attention_second,
    feedforward_second,
    vectors_second,
    word_anchor,
    positions_anchor,
    attention_anchor,
    feedforward_anchor,
    vectors_anchor,
    word_outer,
    positions_outer,
    attention_outer,
    feedforward_outer,
    vectors_outer,
):
    many = lax.axis_size("dp")
    count_q = question_ids.shape[0]
    count_p = passage_ids.shape[0]
    table = word_table[0]
    sizes = Sizes(many, count_q, count_p, table.shape[0])
    swap = lambda values: jnp.swapaxes(values, -3, -2)
    vectors, vectors_first, vectors_second, vectors_anchor, vectors_outer = (
        swap(v) for v in (vectors, vectors_first, vectors_second, vectors_anchor, vectors_outer)
    )
    every, class_rows, kept, entry, counted = first_stage(
        sizes,
        question_ids,
        passage_ids,
        question_lengths,
        passage_lengths,
        question_keys,
        question_valid,
        passage_keys,
        table,
        positions,
    )
    part, lse_part, query, levels = tokens_forward(
        sizes, every, class_rows, kept, entry, counted, table, positions, attention, vectors
    )
    mixed_all, lse_all = exchange_mixed(sizes, part, lse_part)
    stage = class_stage if many * count_q <= 512 else class_stage_large
    grad_all, xa_q, xa_p, d_out, d_ffn, d_mid, score = stage(
        sizes, class_rows, mixed_all, every, positions, attention, feedforward, vectors
    )
    d_query, d_table_t, slices, d_first = tokens_backward(
        sizes, levels, every, query, mixed_all, lse_all, grad_all, kept, entry, table, positions, attention, vectors
    )
    weights = (word_table, positions, attention, feedforward, vectors)
    firsts = (word_first, positions_first, attention_first, feedforward_first, vectors_first)
    seconds = (word_second, positions_second, attention_second, feedforward_second, vectors_second)
    anchors = (word_anchor, positions_anchor, attention_anchor, feedforward_anchor, vectors_anchor)
    outers = (word_outer, positions_outer, attention_outer, feedforward_outer, vectors_outer)
    done = finish(
        sizes,
        d_query,
        slices.reshape(many, sizes.lines, 128),
        d_first,
        d_table_t,
        class_rows,
        every,
        xa_q,
        xa_p,
        d_out,
        d_ffn,
        d_mid,
        (positions, attention, vectors),
        (weights, firsts, seconds, anchors),
    )
    norm = done[0]
    grads = (done[1], done[2], done[3], d_ffn, done[4])
    made = make_outputs(
        norm, grads, firsts, seconds, anchors, outers, done[5:10], lax.axis_size("grp")
    )
    first_new, second_new, averages, outer_next, weight_next = (
        part[:4] + [swap(part[4])] for part in made
    )
    norm = norm[0, 0]
    loss_total = score[0, 0]
    count = score[0, 1]
    return (
        loss_total.reshape(1),
        count.reshape(1),
        norm.reshape(1),
        first_new[0],
        first_new[1],
        first_new[2],
        first_new[3],
        first_new[4],
        second_new[0],
        second_new[1],
        second_new[2],
        second_new[3],
        second_new[4],
        averages[0],
        averages[1],
        averages[2],
        averages[3],
        averages[4],
        outer_next[0],
        outer_next[1],
        outer_next[2],
        outer_next[3],
        outer_next[4],
        weight_next[0],
        weight_next[1],
        weight_next[2],
        weight_next[3],
        weight_next[4],
    )


def solution(mesh):
    placed = (
        P(("grp", "dp"), None),
        P(("grp", "dp"), None),
        P(("grp", "dp")),
        P(("grp", "dp")),
        P(("grp", "dp")),
        P(("grp", "dp")),
        P(("grp", "dp")),
        P("grp", "dp", None),
        P("grp", None, None, None),
        P("grp", None, None, None),
        P("grp", None, None, None, None),
        P("grp", None, None, None),
        P("grp", "dp", None),
        P("grp", None, None, None),
        P("grp", None, None, None),
        P("grp", None, None, None, None),
        P("grp", None, None, None),
        P("grp", "dp", None),
        P("grp", None, None, None),
        P("grp", None, None, None),
        P("grp", None, None, None, None),
        P("grp", None, None, None),
        P("dp", None),
        P(),
        P(),
        P(),
        P(),
        P("dp", None),
        P(),
        P(),
        P(),
        P(),
    )
    return jax.shard_map(
        body,
        mesh=mesh,
        in_specs=placed,
        out_specs=(
            P("grp"),
            P("grp"),
            P("grp"),
            P("grp", "dp", None),
            P("grp", None, None, None),
            P("grp", None, None, None),
            P("grp", None, None, None, None),
            P("grp", None, None, None),
            P("grp", "dp", None),
            P("grp", None, None, None),
            P("grp", None, None, None),
            P("grp", None, None, None, None),
            P("grp", None, None, None),
            P("dp", None),
            P(),
            P(),
            P(),
            P(),
            P("dp", None),
            P(),
            P(),
            P(),
            P(),
            P("grp", "dp", None),
            P("grp", None, None, None),
            P("grp", None, None, None),
            P("grp", None, None, None, None),
            P("grp", None, None, None),
        ),
        check_vma=False,
    )
```

```python
import functools
import math

import jax
import jax.numpy as jnp
from jax import lax
from jax.experimental import pallas as pl
from jax.experimental.pallas import tpu as pltpu
from jax.sharding import PartitionSpec as P

HEAD = 64
STEP = 5


NORM_EPS = 1e-05
MASKED = -1000000000.0
BETA_ONE = 0.9
BETA_TWO = 0.999
INNER_RATE = 0.05
WEIGHT_DECAY = 0.01
ADAM_EPS = 1e-08
CLIP_LIMIT = 0.01
OUTER_RATE = 0.7
OUTER_MU = 0.9
CONTRACT_ROWS = (((0,), (0,)), ((), ()))
CONTRACT_LAST = (((1,), (1,)), ((), ()))


def layer_norm(values, gain, shift):
    center = values - jnp.mean(values, -1, keepdims=True)
    spread = jnp.mean(center * center, -1, keepdims=True)
    return center * lax.rsqrt(spread + NORM_EPS) * gain + shift


def gelu_tanh(values):
    return jax.nn.gelu(values, approximate=True)


def low16(values):
    return values.astype(jnp.bfloat16)


NEG = -1e30
MESH = pl.DeviceIdType.MESH
VMEM_LIMIT = 60 * 1024 * 1024
WAYS = 4
SLOTS = 128
SPAN = WAYS * SLOTS
CHUNK = 256
UNROLL = 4
RAW_Q = 64
RAW_FLAGS = 72
RAW_ROWS = 80


def greet_all(many):
    me = lax.axis_index("dp")
    barrier = pltpu.get_barrier_semaphore()

    def greet(step, carry):
        peer = lax.rem(me + step, many)
        pl.semaphore_signal(barrier, inc=1, device_id={"dp": peer}, device_id_type=MESH)
        return carry

    lax.fori_loop(1, many, greet, 0)
    return me


def enter(many):
    me = greet_all(many)
    pl.semaphore_wait(pltpu.get_barrier_semaphore(), many - 1)
    return me


def copy_to(peer, src, dst, send, recv):
    return pltpu.make_async_remote_copy(
        src_ref=src,
        dst_ref=dst,
        send_sem=send,
        recv_sem=recv,
        device_id={"dp": peer},
        device_id_type=MESH,
    )


def spread_start(many, me, pairs, send, recv, slot):
    def step_start(step, carry):
        peer = lax.rem(me + step, many)
        for index, (source, landing) in enumerate(pairs):
            copy_to(
                peer,
                source(peer),
                landing.at[me],
                send.at[slot + index, peer],
                recv.at[slot + index, me],
            ).start()
        return carry

    lax.fori_loop(1, many, step_start, 0)


def spread_wait(many, me, pairs, send, recv, slot):
    def step_wait(step, carry):
        peer = lax.rem(me + step, many)
        for index, (source, landing) in enumerate(pairs):
            copy = copy_to(
                peer,
                source(peer),
                landing.at[peer],
                send.at[slot + index, peer],
                recv.at[slot + index, peer],
            )
            copy.wait_recv()
            copy.wait_send()
        return carry

    lax.fori_loop(1, many, step_wait, 0)


def dot(left, right):
    return jnp.dot(left, right, preferred_element_type=jnp.float32)


def dot_rows(left, right):
    return lax.dot_general(left, right, CONTRACT_ROWS, preferred_element_type=jnp.float32)


def dot_last(left, right):
    return lax.dot_general(left, right, CONTRACT_LAST, preferred_element_type=jnp.float32)


def iota(shape, axis):
    return lax.broadcasted_iota(jnp.int32, shape, axis)


def hot(mask):
    return jnp.where(mask, 1.0, 0.0).astype(jnp.bfloat16)


def first_kernel(
    sizes,
    question_ref,
    passage_ref,
    length_q,
    length_p,
    key_q,
    valid_q,
    key_p,
    table_ref,
    place_ref,
    every_ref,
    rows_ref,
    kept_ref,
    entry_ref,
    count_ref,
    stage,
    raw,
    ask,
    asks,
    low_ref,
    offer,
    landed,
    own,
    table_t,
    place_t,
    send,
    recv,
):
    many = sizes.many
    count_q, count_p = sizes.count
    each = count_q + count_p
    depth = sizes.depth
    half = count_q // 2
    me = greet_all(many)
    lane = iota((1, 128), 1)
    for seq in range(count_p):
        stop = length_p[seq]
        stage[seq : seq + 1, :] = jnp.where(lane < stop, passage_ref[seq : seq + 1, 0:128], -1)
        stage[count_p + seq : count_p + seq + 1, :] = jnp.where(
            lane + 128 < stop, passage_ref[seq : seq + 1, 128:256], -1
        )
    both = jnp.concatenate([question_ref[0:half, :], question_ref[half:count_q, :]], 1)
    for seq in range(half):
        stop = jnp.where(lane < 64, length_q[seq], length_q[half + seq] + 64)
        stage[RAW_Q + seq : RAW_Q + seq + 1, :] = jnp.where(lane < stop, both[seq : seq + 1], -1)
    flags = jnp.zeros((1, 128), jnp.int32)
    for spot in range(count_q):
        flags = jnp.where(lane == spot, key_q[spot], flags)
        flags = jnp.where(lane == count_q + spot, valid_q[spot], flags)
    for spot in range(count_p):
        flags = jnp.where(lane == 2 * count_q + spot, key_p[spot], flags)
    stage[RAW_FLAGS:RAW_ROWS, :] = jnp.broadcast_to(flags, (8, 128))
    raw[...] = stage[...].astype(jnp.int16)
    heads = jnp.concatenate([question_ref[:, 0:1], passage_ref[:, 0:1]], 0)
    diagonal = iota((each, 128), 0) == iota((each, 128), 1)
    heads = jnp.sum(jnp.where(diagonal, jnp.broadcast_to(heads, (each, 128)), 0), 0, keepdims=True)
    ask[...] = jnp.broadcast_to(heads, (8, 128))
    pl.semaphore_wait(pltpu.get_barrier_semaphore(), many - 1)
    ask_pairs = [(lambda peer: ask, asks)]
    raw_pairs = [(lambda peer: raw, every_ref)]
    spread_start(many, me, ask_pairs, send, recv, 0)
    spread_start(many, me, raw_pairs, send, recv, 1)
    asks[me] = ask[...]
    every_ref[me] = raw[...]
    padded = sizes.padded
    if padded > depth:
        low_ref[...] = jnp.zeros_like(low_ref)
    low_ref[0:depth, :] = low16(table_ref[...])
    first = me * depth
    block = math.gcd(many, 16)
    spread_wait(many, me, ask_pairs, send, recv, 0)

    def pick(step, carry):
        found = []
        for i in range(block):
            line = jnp.broadcast_to(asks[step * block + i][0:1, :].astype(jnp.float32), (each, 128))
            found.append(jnp.sum(jnp.where(diagonal, line, 0.0), 1, keepdims=True))
        place = jnp.concatenate(found, 0).astype(jnp.int32) - first
        spot = jnp.where((place >= 0) & (place < depth), place, -1)
        number = spot.shape[0]
        total = jnp.zeros((number, 128), jnp.float32)
        wide = jnp.broadcast_to(spot, (number, CHUNK))
        for at in range(padded // CHUNK):
            chosen = hot(wide == iota((number, CHUNK), 1) + at * CHUNK)
            total += dot(chosen, low_ref[at * CHUNK : (at + 1) * CHUNK, :])
        for i in range(block):
            offer[step * block + i] = low16(total[i * each : (i + 1) * each])
        return carry

    lax.fori_loop(0, many // block, pick, 0)
    offer_pairs = [(lambda peer: offer.at[peer], landed)]
    spread_start(many, me, offer_pairs, send, recv, 2)
    landed[me] = offer[me]
    if sizes.keep:
        prepare_tokens(sizes, table_ref, place_ref, table_t, place_t)
    spread_wait(many, me, raw_pairs, send, recv, 1)

    def spans_of(enc, count):
        def spans(turn, count):
            steps = [turn * sizes.unroll[enc] + u for u in range(sizes.unroll[enc])]
            packed = [pack_span(sizes, enc, s, 0, first, every_ref) for s in steps]
            found = [gather_span(sizes, enc, part[0], table_t, place_t) for part in packed]
            for part in packed:
                count = jnp.maximum(count, part[1])
            for u, s in enumerate(steps):
                at = s if enc == 0 else sizes.steps[0] + s
                kept_ref[at, 0:128, :] = found[u][0]
                kept_ref[at, 128:129, :] = found[u][1]
                entry_ref[at, 0:1, :] = packed[u][0]
            return count

        return lax.fori_loop(0, sizes.steps[enc] // sizes.unroll[enc], spans, count)

    count = jnp.zeros((8, 128), jnp.float32)
    if sizes.keep:
        count = spans_of(0, count)
    spread_wait(many, me, offer_pairs, send, recv, 2)
    own[...] = low16(jnp.sum(landed[...].astype(jnp.float32), 0))
    row_pairs = [(lambda peer: own, rows_ref)]
    spread_start(many, me, row_pairs, send, recv, 3)
    rows_ref[me] = own[...]
    if sizes.keep:
        count = spans_of(1, count)
    count_ref[...] = count
    spread_wait(many, me, row_pairs, send, recv, 3)


def first_stage(sizes, ids_q, ids_p, length_q, length_p, key_q, valid_q, key_p, table, positions):
    many = sizes.many
    padded = sizes.padded
    both = sum(sizes.count)
    vm = pl.BlockSpec(memory_space=pltpu.VMEM)
    sm = pl.BlockSpec(memory_space=pltpu.SMEM)
    kept = sizes.spans if sizes.keep else 1
    return pl.pallas_call(
        functools.partial(first_kernel, sizes),
        out_shape=(
            jax.ShapeDtypeStruct((many, RAW_ROWS, 128), jnp.int16),
            jax.ShapeDtypeStruct((many, both, 128), jnp.bfloat16),
            jax.ShapeDtypeStruct((kept, 136, SPAN), jnp.float32),
            jax.ShapeDtypeStruct((kept, 8, SPAN), jnp.int32),
            jax.ShapeDtypeStruct((8, 128), jnp.float32),
        ),
        in_specs=[vm, vm, sm, sm, sm, sm, sm, vm, vm],
        out_specs=[vm] * 5,
        scratch_shapes=[
            pltpu.VMEM((RAW_ROWS, 128), jnp.int32),
            pltpu.VMEM((RAW_ROWS, 128), jnp.int16),
            pltpu.VMEM((8, 128), jnp.int32),
            pltpu.VMEM((many, 8, 128), jnp.int32),
            pltpu.VMEM((padded, 128), jnp.bfloat16),
            pltpu.VMEM((many, both, 128), jnp.bfloat16),
            pltpu.VMEM((many, both, 128), jnp.bfloat16),
            pltpu.VMEM((both, 128), jnp.bfloat16),
            pltpu.VMEM((128, padded), jnp.bfloat16),
            pltpu.VMEM((2, 2, 128, CHUNK), jnp.bfloat16),
            pltpu.SemaphoreType.DMA((4, many)),
            pltpu.SemaphoreType.DMA((4, many)),
        ],
        compiler_params=pltpu.CompilerParams(
            collective_id=1, has_side_effects=True, vmem_limit_bytes=VMEM_LIMIT
        ),
        name="first_stage",
    )(ids_q, ids_p, length_q, length_p, key_q, valid_q, key_p, table, positions)


def norm_rows(values, gain, shift):
    center = values - jnp.mean(values, -1, keepdims=True)
    spread = jnp.mean(center * center, -1, keepdims=True)
    return center * lax.rsqrt(spread + NORM_EPS) * gain + shift


def two_heads(values):
    lane = iota(values.shape, 1)
    low = jnp.where(lane < HEAD, values, jnp.zeros_like(values))
    high = jnp.where(lane >= HEAD, values, jnp.zeros_like(values))
    return jnp.concatenate([low, high], 0)


def merge_heads(both):
    half = both.shape[0] // 2
    lane = iota((half, both.shape[1]), 1)
    return jnp.where(lane < HEAD, both[:half], both[half:])


class Sizes:
    def __init__(self, many, count_q, count_p, depth):
        self.many = many
        self.count = (count_q, count_p)
        self.depth = depth
        self.padded = -(-depth // CHUNK) * CHUNK
        self.steps = (many // (2 * WAYS), many)
        self.unroll = tuple(math.gcd(UNROLL, step) for step in self.steps)
        self.spans = self.steps[0] + self.steps[1]
        self.devices = (2 * WAYS, 1)
        self.queries = (2 * WAYS * count_q, count_p)
        self.lines = 1024 // many
        self.kind = jnp.bfloat16 if self.lines % 16 == 0 else jnp.float32
        self.keep = self.spans * 136 * SPAN * 4 <= 8 * 1024 * 1024


def vector_row(vec_ref, enc, row):
    return vec_ref[0, row, enc : enc + 1, :]


def prepare_tokens(sizes, table_ref, place_ref, table_t, place_t):
    depth = sizes.depth
    if sizes.padded > depth:
        table_t[...] = jnp.zeros_like(table_t)
    for cut in range(0, depth, 128):
        top = min(cut + 128, depth)
        piece = table_ref[cut:top, :]
        if top - cut < 128:
            piece = jnp.concatenate([piece, jnp.zeros((128 - (top - cut), 128), jnp.float32)], 0)
        table_t[:, cut : cut + 128] = low16(jnp.transpose(piece))
    for enc in range(2):
        place = place_ref[0, enc]
        for cut in range(0, place.shape[0], 128):
            turned = jnp.transpose(place[cut : cut + 128])
            high = low16(turned)
            place_t[enc, 0, :, cut : cut + 128] = high
            place_t[enc, 1, :, cut : cut + 128] = low16(turned - high.astype(jnp.float32))


def prepare_weights(attn_ref, vec_ref, w_kv, vec_t):
    for enc in range(2):
        for cut in range(2):
            w_kv[enc, cut * 128 : (cut + 1) * 128, :] = low16(
                jnp.transpose(attn_ref[0, enc, :, (cut + 1) * 128 : (cut + 2) * 128])
            )
        rows = [vector_row(vec_ref, enc, row) for row in range(4)]
        rows = jnp.concatenate(rows + [jnp.zeros((124, 128), jnp.float32)], 0)
        vec_t[enc] = jnp.transpose(rows)


def lane_pick(values, lanes):
    return jnp.take_along_axis(values, lanes, axis=1, mode="promise_in_bounds")


def pack_span(sizes, enc, step, level, first, raw_ref):
    if enc == 1:
        ids = raw_ref[step, 0:RAW_Q, :].astype(jnp.int32)
    else:
        ids = jnp.concatenate(
            [
                raw_ref[step * 8 + i, RAW_Q:RAW_ROWS, :].astype(jnp.int32)[0:8]
                for i in range(8)
            ],
            0,
        )
    place = ids - first
    owned = (place >= 0) & (place < sizes.depth)
    flag = hot(owned)
    inside = dot(flag, hot(iota((128, 128), 0) <= iota((128, 128), 1))).astype(jnp.int32)
    total = dot(flag, jnp.ones((128, 128), jnp.bfloat16))
    before = dot(hot(iota((64, 64), 1) < iota((64, 64), 0)), low16(total))
    start = before.astype(jnp.int32)
    stop = (before + total).astype(jnp.int32)
    line = iota((64, 128), 0)
    turn = iota((64, 128), 1)
    lane = jnp.zeros((64, 128), jnp.int32)
    for jump in (64, 32, 16, 8, 4, 2, 1):
        seen = lane_pick(inside, lane + (jump - 1))
        lane = jnp.where(seen <= turn, lane + jump, lane)
    row = lane_pick(place, lane)
    if enc == 1:
        where = (line >> 5) * 128 + lane
        seq = (line & 31) + 1
    else:
        where = lane & 63
        seq = (line >> 3) * sizes.count[0] + (lane >> 6) * 8 + (line & 7) + 1
    code = lane_pick((row << 16) + (where << 8) + seq, (turn - start) & 127)
    codes = []
    for window in range(WAYS):
        slot = turn + (window * SLOTS + level * SPAN)
        kept = jnp.where((slot >= start) & (slot < stop), code, 0)
        codes.append(jnp.sum(kept, 0, keepdims=True))
    return jnp.concatenate(codes, 1), (before + total)[56:64]


def gather_span(sizes, enc, code, table_t, place_t):
    rows = code >> 16
    where = (code >> 8) & 255
    x = jnp.zeros((128, SPAN), jnp.float32)
    wide = jnp.broadcast_to(rows, (CHUNK, SPAN))
    for cut in range(sizes.padded // CHUNK):
        chosen = hot(wide == iota((CHUNK, SPAN), 0) + cut * CHUNK)
        x += dot(table_t[:, cut * CHUNK : (cut + 1) * CHUNK], chosen)
    chosen = hot(jnp.broadcast_to(where, (CHUNK, SPAN)) == iota((CHUNK, SPAN), 0))
    x += dot(place_t[enc, 0], chosen) + dot(place_t[enc, 1], chosen)
    center = x - jnp.mean(x, 0, keepdims=True)
    rate = lax.rsqrt(jnp.mean(center * center, 0, keepdims=True) + NORM_EPS)
    return center * rate, rate


def project(enc, scaled, vec_t, w_kv):
    a_t = low16(scaled * vec_t[enc, :, 0:1] + vec_t[enc, :, 1:2])
    kv = dot(w_kv[enc], a_t)
    keys_t = low16(kv[:128])
    values_t = low16(kv[128:] + vec_t[enc, :, 3:4])
    return a_t, keys_t, values_t


def own_slots(code, number):
    line = iota((2 * number, SPAN), 0)
    line = jnp.where(line >= number, line - number, line)
    return line == (code & 255) - 1


def forward_kernel(
    sizes,
    raw_ref,
    rows_ref,
    kept_hbm,
    entry_hbm,
    count_ref,
    table_ref,
    place_ref,
    attn_ref,
    vec_ref,
    out_ref,
    lse_ref,
    query_ref,
    levels_ref,
    table_t,
    place_t,
    w_kv,
    vec_t,
    query_q,
    total_q,
    top_q,
    mass_q,
    total_p,
    top_p,
    mass_p,
    kept_ref,
    entry_ref,
    load,
):
    loads = load_kept(sizes, kept_hbm, entry_hbm, kept_ref, entry_ref, load)
    first = lax.axis_index("dp") * sizes.depth
    count_q, count_p = sizes.count
    prepare_weights(attn_ref, vec_ref, w_kv, vec_t)
    begin = 1 if sizes.keep else 0
    count = count_ref[...]
    block = math.gcd(sizes.many, 16)
    for enc in range(2):
        low, high = (0, count_q) if enc == 0 else (count_q, count_q + count_p)
        w_q = low16(attn_ref[0, enc, :, 0:128])

        def ask(step, carry):
            spot = pl.ds(step * block, block)
            held = rows_ref[spot, low:high, :].reshape(block * (high - low), 128)
            x = held.astype(jnp.float32) + place_ref[0, enc, 0:1, :]
            h = norm_rows(x, vector_row(vec_ref, enc, 0), vector_row(vec_ref, enc, 1))
            query = low16(dot(low16(h), w_q) + vector_row(vec_ref, enc, 2))
            query_ref[spot, low:high, :] = query.reshape(block, high - low, 128)
            if enc == 0:
                for half in range(block // 8):
                    query_q[step * (block // 8) + half] = query[half * 8 * count_q : (half + 1) * 8 * count_q]
            return carry

        lax.fori_loop(0, sizes.many // block, ask, 0)
    states = ((total_q, top_q, mass_q), (total_p, top_p, mass_p))
    lse_ref[...] = jnp.full_like(lse_ref, NEG)

    def close(enc, step, total, top, mass):
        some = mass > 0.0
        safe = jnp.where(some, mass, 1.0)
        mixed = merge_heads(total / safe)
        lse = jnp.where(some, top + jnp.log(safe), NEG)
        if enc == 1:
            out_ref[step, count_q:, :] = low16(mixed)
            at = iota(lse.shape, 0) == iota(lse.shape, 1)
            lse_ref[step, 0:1, :] = jnp.sum(jnp.where(at, lse, 0.0), 0, keepdims=True)
        else:
            half = lse.shape[0] // 2
            row = iota((count_q, 128), 0)
            lane = iota((count_q, 128), 1)
            for i in range(8):
                spot = slice(i * count_q, (i + 1) * count_q)
                out_ref[step * 8 + i, 0:count_q, :] = low16(mixed[spot])
                line = jnp.where(lane == row, lse[spot], 0.0) + jnp.where(
                    lane == row + count_q, lse[half + i * count_q : half + (i + 1) * count_q], 0.0
                )
                lse_ref[step * 8 + i, 1:2, :] = jnp.sum(line, 0, keepdims=True)

    def attend(enc, steps, codes, scaleds, olds):
        queries = [query_q[s] if enc == 0 else query_ref[s, count_q:, :] for s in steps]
        made = [project(enc, scaled, vec_t, w_kv) for scaled in scaleds]
        scores = [dot(two_heads(query), part[1]) * HEAD ** (-0.5) for query, part in zip(queries, made)]
        news = []
        for u, score in enumerate(scores):
            mine = own_slots(codes[u], queries[u].shape[0])
            score = jnp.where(mine, score, NEG)
            new = jnp.max(score, 1, keepdims=True)
            if olds is not None:
                new = jnp.maximum(olds[u][1][:, 0:1], new)
            expo = jnp.where(mine, jnp.exp(score - new), 0.0)
            total = dot_last(low16(expo), made[u][2])
            mass = jnp.sum(expo, 1, keepdims=True)
            if olds is not None:
                fade = jnp.exp(olds[u][1] - new)
                total = olds[u][0] * fade + total
                mass = olds[u][2] * fade + mass
            wide = (score.shape[0], 128)
            news.append((total, jnp.broadcast_to(new, wide), jnp.broadcast_to(mass, wide)))
        for u, s in enumerate(steps):
            for ref, value in zip(states[enc], news[u]):
                ref[s] = value
        return news

    for enc in range(2):
        if sizes.keep:
            for copy in loads[2 * enc : 2 * enc + 2]:
                copy.wait()

            def kept_spans(turn, carry):
                steps = [turn * sizes.unroll[enc] + u for u in range(sizes.unroll[enc])]
                ats = [s if enc == 0 else sizes.steps[0] + s for s in steps]
                news = attend(
                    enc, steps, [entry_ref[at, 0:1, :] for at in ats], [kept_ref[at, 0:128, :] for at in ats], None
                )
                for s, new in zip(steps, news):
                    close(enc, s, *new)
                return carry

            lax.fori_loop(0, sizes.steps[enc] // sizes.unroll[enc], kept_spans, 0)
        else:
            total, top, mass = states[enc]
            total[...] = jnp.zeros_like(total)
            mass[...] = jnp.zeros_like(mass)
            top[...] = jnp.full_like(top, NEG)

    def needed(count):
        return jnp.maximum((jnp.max(count).astype(jnp.int32) + SPAN - 1) // SPAN, 1)

    start = needed(count)
    levels_ref[0] = start

    @pl.when(start > begin)
    def _():
        prepare_tokens(sizes, table_ref, place_ref, table_t, place_t)

        def one_level(state):
            level, unused, count = state
            for enc in range(2):

                def one_span(step, count):
                    code, found = pack_span(sizes, enc, step, level, first, raw_ref)
                    scaled = gather_span(sizes, enc, code, table_t, place_t)[0]
                    attend(enc, [step], [code], [scaled], [tuple(ref[step] for ref in states[enc])])
                    return jnp.maximum(count, found)

                count = lax.fori_loop(0, sizes.steps[enc], one_span, count)
            return level + 1, needed(count), count

        if sizes.keep:
            lax.fori_loop(
                begin, start, lambda level, carry: one_level((level, carry, count))[1], jnp.int32(0)
            )
        else:
            last = lax.while_loop(
                lambda state: state[0] < state[1], one_level, (jnp.int32(begin), start, count)
            )
            levels_ref[0] = last[1]
        for enc in range(2):

            def close_span(step, carry):
                close(enc, step, *(ref[step] for ref in states[enc]))
                return carry

            lax.fori_loop(0, sizes.steps[enc], close_span, 0)


def load_kept(sizes, kept_hbm, entry_hbm, kept_ref, entry_ref, load):
    if not sizes.keep:
        return []
    copies = []
    for enc, rows in enumerate((slice(0, sizes.steps[0]), slice(sizes.steps[0], sizes.spans))):
        for j, (source, target) in enumerate(((kept_hbm, kept_ref), (entry_hbm, entry_ref))):
            copy = pltpu.make_async_copy(source.at[rows], target.at[rows], load.at[enc, j])
            copy.start()
            copies.append(copy)
    return copies


def kept_scratch(sizes):
    kept = sizes.spans if sizes.keep else 1
    return [
        pltpu.VMEM((kept, 136, SPAN), jnp.float32),
        pltpu.VMEM((kept, 8, SPAN), jnp.int32),
        pltpu.SemaphoreType.DMA((2, 2)),
    ]


def token_scratch(sizes):
    return [
        pltpu.VMEM((128, sizes.padded), jnp.bfloat16),
        pltpu.VMEM((2, 2, 128, CHUNK), jnp.bfloat16),
        pltpu.VMEM((2, 256, 128), jnp.bfloat16),
        pltpu.VMEM((2, 128, 128), jnp.float32),
    ]


def local_call(kernel, out_shape, inputs, scratch, name, smem_in=(), smem_out=(), any_in=()):
    vm = pl.BlockSpec(memory_space=pltpu.VMEM)
    sm = pl.BlockSpec(memory_space=pltpu.SMEM)
    hbm = pl.BlockSpec(memory_space=pl.ANY)
    return pl.pallas_call(
        kernel,
        out_shape=out_shape,
        in_specs=[sm if i in smem_in else hbm if i in any_in else vm for i in range(len(inputs))],
        out_specs=[sm if i in smem_out else vm for i in range(len(out_shape))],
        scratch_shapes=scratch,
        compiler_params=pltpu.CompilerParams(vmem_limit_bytes=VMEM_LIMIT),
        name=name,
    )(*inputs)


def tokens_forward(sizes, every, rows, kept, entry, counted, table, positions, attention, vectors):
    many = sizes.many
    both = sum(sizes.count)
    state = []
    for enc in range(2):
        tall = 2 * sizes.queries[enc]
        state += [pltpu.VMEM((sizes.steps[enc], tall, 128), jnp.float32)] * 3
    return local_call(
        functools.partial(forward_kernel, sizes),
        (
            jax.ShapeDtypeStruct((many, both, 128), jnp.bfloat16),
            jax.ShapeDtypeStruct((many, 2, 128), jnp.float32),
            jax.ShapeDtypeStruct((many, both, 128), jnp.bfloat16),
            jax.ShapeDtypeStruct((1,), jnp.int32),
        ),
        (every, rows, kept, entry, counted, table, positions, attention, vectors),
        token_scratch(sizes)
        + [pltpu.VMEM((sizes.steps[0], sizes.queries[0], 128), jnp.bfloat16)]
        + state
        + kept_scratch(sizes),
        "tokens_forward",
        smem_out=(3,),
        any_in=(2, 3),
    )


def mix_kernel(
    many, count_q, part_ref, lse_ref, mixed_ref, total_ref, landed, landed_lse, own, own_lse, send, recv
):
    me = enter(many)
    pairs = [
        (lambda peer: part_ref.at[peer], landed),
        (lambda peer: lse_ref.at[peer], landed_lse),
    ]
    spread_start(many, me, pairs, send, recv, 0)
    landed[me] = part_ref[me]
    landed_lse[me] = lse_ref[me]
    spread_wait(many, me, pairs, send, recv, 0)
    parts = landed_lse[...]
    top = jnp.max(parts, 0)
    total = top + jnp.log(jnp.sum(jnp.exp(parts - top[None]), 0))
    own_lse[...] = total
    share = jnp.exp(parts - total[None])
    count_p = part_ref.shape[1] - count_q
    mixed = jnp.zeros((count_q + count_p, 128), jnp.float32)
    for peer in range(many):
        factors = []
        for row, number in ((1, count_q), (0, count_p)):
            wide = (2 * number, 128)
            at = iota(wide, 0) == iota(wide, 1)
            line = jnp.broadcast_to(share[peer][row : row + 1], wide)
            column = jnp.sum(jnp.where(at, line, 0.0), 1, keepdims=True)
            lane = iota((number, 128), 1)
            factors.append(jnp.where(lane < HEAD, column[0:number], column[number:]))
        mixed += jnp.concatenate(factors, 0) * landed[peer].astype(jnp.float32)
    own[...] = low16(mixed)
    pairs = [(lambda peer: own, mixed_ref), (lambda peer: own_lse, total_ref)]
    spread_start(many, me, pairs, send, recv, 2)
    mixed_ref[me] = own[...]
    total_ref[me] = own_lse[...]
    spread_wait(many, me, pairs, send, recv, 2)


def remote_call(kernel, out_shape, inputs, scratch, lanes, many, ident, name):
    return pl.pallas_call(
        kernel,
        out_shape=out_shape,
        in_specs=[pl.BlockSpec(memory_space=pltpu.VMEM)] * len(inputs),
        out_specs=[pl.BlockSpec(memory_space=pltpu.VMEM)] * len(out_shape),
        scratch_shapes=scratch
        + [pltpu.SemaphoreType.DMA((lanes, many)), pltpu.SemaphoreType.DMA((lanes, many))],
        compiler_params=pltpu.CompilerParams(
            collective_id=ident, has_side_effects=True, vmem_limit_bytes=VMEM_LIMIT
        ),
        name=name,
    )(*inputs)


def exchange_mixed(sizes, part, lse):
    many = sizes.many
    both = sum(sizes.count)
    return remote_call(
        functools.partial(mix_kernel, many, sizes.count[0]),
        (
            jax.ShapeDtypeStruct((many, both, 128), jnp.bfloat16),
            jax.ShapeDtypeStruct((many, 2, 128), jnp.float32),
        ),
        (part, lse),
        [
            pltpu.VMEM((many, both, 128), jnp.bfloat16),
            pltpu.VMEM((many, 2, 128), jnp.float32),
            pltpu.VMEM((both, 128), jnp.bfloat16),
            pltpu.VMEM((2, 128), jnp.float32),
        ],
        4,
        many,
        2,
        "exchange_mixed",
    )


def backward_kernel(
    sizes,
    levels_ref,
    raw_ref,
    query_ref,
    mixed_ref,
    lse_ref,
    grad_ref,
    kept_hbm,
    entry_hbm,
    table_ref,
    place_ref,
    attn_ref,
    vec_ref,
    d_query_ref,
    d_table_ref,
    slice_ref,
    table_t,
    place_t,
    w_kv,
    vec_t,
    d_place_ref,
    d_attn_ref,
    acc_gain,
    acc_shift,
    acc_value,
    d_query_q,
    d_query_p,
    kept_ref,
    entry_ref,
    load,
):
    loads = load_kept(sizes, kept_hbm, entry_hbm, kept_ref, entry_ref, load)
    first = lax.axis_index("dp") * sizes.depth
    count_q, count_p = sizes.count
    prepare_weights(attn_ref, vec_ref, w_kv, vec_t)
    begin = 1 if sizes.keep else 0
    again = levels_ref[0] > begin

    @pl.when(again)
    def _():
        prepare_tokens(sizes, table_ref, place_ref, table_t, place_t)

    for ref in (d_table_ref, d_place_ref, d_attn_ref, d_query_q, d_query_p, acc_gain, acc_shift, acc_value):
        ref[...] = jnp.zeros_like(ref)

    def ask_span(enc, step):
        if enc == 0:
            spot = pl.ds(step * 8, 8)
            shape = (8 * count_q, 128)
            found = [ref[spot, 0:count_q, :].reshape(shape) for ref in (query_ref, grad_ref, mixed_ref)]
            lines = [jnp.broadcast_to(lse_ref[step * 8 + i, 1:2, :], (count_q, 128)) for i in range(8)]
            lines = jnp.concatenate(lines, 0)
            row = iota(lines.shape, 0) % count_q
            lane = iota(lines.shape, 1)
            lse = [
                jnp.sum(jnp.where(lane == row + head * count_q, lines, 0.0), 1, keepdims=True)
                for head in range(2)
            ]
            lse = jnp.concatenate(lse, 0)
        else:
            found = [ref[step, count_q:, :] for ref in (query_ref, grad_ref, mixed_ref)]
            lines = jnp.broadcast_to(lse_ref[step, 0:1, :], (2 * count_p, 128))
            lse = jnp.sum(jnp.where(iota(lines.shape, 1) == iota(lines.shape, 0), lines, 0.0), 1, keepdims=True)
        return found + [lse]

    def work(enc, steps, codes, scaleds, rates):
        w_all = low16(attn_ref[0, enc, :, 128:384])
        asked = [ask_span(enc, step) for step in steps]
        made = [project(enc, scaled, vec_t, w_kv) for scaled in scaleds]
        d_queries, d_kvs = ([], [])
        for (query, grad, mixed, lse), code, (a_t, keys_t, values_t) in zip(asked, codes, made):
            both = two_heads(query)
            grads = two_heads(grad)
            base = jnp.sum(
                grads.astype(jnp.float32) * jnp.concatenate([mixed, mixed], 0).astype(jnp.float32),
                1,
                keepdims=True,
            )
            scores = dot(both, keys_t) * HEAD ** (-0.5)
            mine = own_slots(code, query.shape[0])
            probs = jnp.where(mine, jnp.exp(jnp.where(mine, scores, NEG) - lse), 0.0)
            d_probs = dot(grads, values_t)
            d_scores = low16(probs * (d_probs - base))
            d_values = low16(dot_rows(grads, low16(probs)))
            d_keys = low16(dot_rows(both, d_scores) * HEAD ** (-0.5))
            d_queries.append(merge_heads(dot_last(d_scores, keys_t)) * HEAD ** (-0.5))
            d_kvs.append(jnp.concatenate([d_keys, d_values], 0))
        for step, d_query in zip(steps, d_queries):
            if enc == 0:
                d_query_q[step] += d_query
            else:
                d_query_p[step] += d_query
        d_kv = jnp.concatenate(d_kvs, 1)
        a_t = jnp.concatenate([part[0] for part in made], 1)
        scaled = jnp.concatenate(scaleds, 1)
        rate = jnp.concatenate(rates, 1)
        code = jnp.concatenate(codes, 1)
        width = code.shape[1]
        d_attn_ref[enc] += dot_last(a_t, d_kv)
        d_h = dot(w_all, d_kv)
        fold = lambda values: sum(values[:, i * SPAN : (i + 1) * SPAN] for i in range(width // SPAN))
        acc_value[enc] += fold(d_kv[128:].astype(jnp.float32))
        acc_gain[enc] += fold(d_h * scaled)
        acc_shift[enc] += fold(d_h)
        d_scaled = d_h * vec_t[enc, :, 0:1]
        center = d_scaled - jnp.mean(d_scaled, 0, keepdims=True)
        slope = jnp.mean(d_scaled * scaled, 0, keepdims=True)
        d_x = low16((center - scaled * slope) * rate)
        rows = code >> 16
        where = (code >> 8) & 255
        chosen = hot(jnp.broadcast_to(where, (CHUNK, width)) == iota((CHUNK, width), 0))
        d_place_ref[enc] += dot_last(d_x, chosen)
        wide = jnp.broadcast_to(rows, (CHUNK, width))
        for cut in range(sizes.padded // CHUNK):
            spot = slice(cut * CHUNK, (cut + 1) * CHUNK)
            chosen = hot(wide == iota((CHUNK, width), 0) + cut * CHUNK)
            d_table_ref[spot, :] += dot_last(chosen, d_x)

    for enc in range(2):
        if sizes.keep:
            for copy in loads[2 * enc : 2 * enc + 2]:
                copy.wait()

            def kept_spans(turn, carry):
                steps = [turn * sizes.unroll[enc] + u for u in range(sizes.unroll[enc])]
                ats = [s if enc == 0 else sizes.steps[0] + s for s in steps]
                work(
                    enc,
                    steps,
                    [entry_ref[at, 0:1, :] for at in ats],
                    [kept_ref[at, 0:128, :] for at in ats],
                    [kept_ref[at, 128:129, :] for at in ats],
                )
                return carry

            lax.fori_loop(0, sizes.steps[enc] // sizes.unroll[enc], kept_spans, 0)

        def more_level(level, carry_level):
            def one_span(step, carry):
                code = pack_span(sizes, enc, step, level, first, raw_ref)[0]
                scaled, rate = gather_span(sizes, enc, code, table_t, place_t)
                work(enc, [step], [code], [scaled], [rate])
                return carry

            return lax.fori_loop(0, sizes.steps[enc], one_span, carry_level)

        lax.fori_loop(begin, levels_ref[0], more_level, 0)

    for step in range(sizes.steps[0]):
        d_query_ref[step * 8 : step * 8 + 8, 0:count_q, :] = low16(d_query_q[step]).reshape(8, count_q, 128)
    d_query_ref[:, count_q:, :] = low16(d_query_p[...])
    for enc in range(2):
        for part, block in enumerate((d_place_ref, d_attn_ref)):
            for cut in range(2):
                slice_ref[enc, 2 * part + cut] = block[enc, :, cut * 128 : (cut + 1) * 128].astype(
                    slice_ref.dtype
                )
    slice_ref[0, 1] = jnp.zeros_like(slice_ref[0, 1])
    sums = []
    same = iota((128, 128), 0) == iota((128, 128), 1)
    for enc in range(2):
        for row, acc in enumerate((acc_gain, acc_shift, acc_value)):
            tall = jnp.broadcast_to(jnp.sum(acc[enc], 1, keepdims=True), (128, 128))
            sums.append(jnp.sum(jnp.where(same, tall, 0.0), 0, keepdims=True))
    sums = jnp.concatenate(sums + [jnp.zeros((10, 128), jnp.float32)], 0)
    slice_ref[0, 1, 0:16, :] = sums.astype(slice_ref.dtype)


def tokens_backward(sizes, levels, every, query, mixed, lse, grad, kept, entry, table, positions, attention, vectors):
    many = sizes.many
    count_p = sizes.count[1]
    both = sum(sizes.count)
    return local_call(
        functools.partial(backward_kernel, sizes),
        (
            jax.ShapeDtypeStruct((many, both, 128), jnp.bfloat16),
            jax.ShapeDtypeStruct((sizes.padded, 128), jnp.float32),
            jax.ShapeDtypeStruct((2, 4, 128, 128), sizes.kind),
        ),
        (levels, every, query, mixed, lse, grad, kept, entry, table, positions, attention, vectors),
        token_scratch(sizes)
        + [
            pltpu.VMEM((2, 128, CHUNK), jnp.float32),
            pltpu.VMEM((2, 128, 256), jnp.float32),
            pltpu.VMEM((2, 128, SPAN), jnp.float32),
            pltpu.VMEM((2, 128, SPAN), jnp.float32),
            pltpu.VMEM((2, 128, SPAN), jnp.float32),
            pltpu.VMEM((sizes.steps[0], sizes.queries[0], 128), jnp.float32),
            pltpu.VMEM((many, count_p, 128), jnp.float32),
        ]
        + kept_scratch(sizes),
        "tokens_backward",
        smem_in=(0,),
        any_in=(6, 7),
    )


def adam(weight, grad, first, second):
    first_new = BETA_ONE * first + (1.0 - BETA_ONE) * grad
    second_new = BETA_TWO * second + (1.0 - BETA_TWO) * grad * grad
    fix_one = 1.0 - BETA_ONE**STEP
    fix_two = 1.0 - BETA_TWO**STEP
    ratio = first_new / fix_one / (jnp.sqrt(second_new / fix_two) + ADAM_EPS)
    return (first_new, second_new, weight - INNER_RATE * (ratio + WEIGHT_DECAY * weight))


def pieces_of(depth):
    blocks = [(1, (enc,)) for enc in range(2)] + [(2, (enc,)) for enc in range(2)]
    blocks += [(3, (enc, side)) for enc in range(2) for side in range(2)]
    return blocks + [(4, ())]


def square_sum(values):
    return jnp.sum(jnp.sum(values * values, 0, keepdims=True), 1, keepdims=True)


def finish_kernel(sizes, *refs):
    many = sizes.many
    count_q, count_p = sizes.count
    depth = sizes.depth
    (query_ref, slice_ref, d_table_ref, rows_ref, raw_ref, xa_q, xa_p, d_out, d_ffn, d_mid) = refs[:10]
    place_ref, attn_ref, vec_ref = refs[10:13]
    state = refs[13:33]
    norm_ref, g_word, g_place, g_attn, g_vec = refs[33:38]
    joined = refs[38:43]
    held = refs[43:63]
    mine = refs[63:68]
    theirs = refs[68:73]
    (query_all, slice_all, scalar_all, land_query, land_slice, own_query, own_slice, tile, table_t) = refs[73:82]
    send, recv, load, pair_send, pair_recv = refs[82:87]
    loads = []
    for index in range(20):
        copy = pltpu.make_async_copy(state[index], held[index], load.at[index])
        copy.start()
        loads.append(copy)
    me = lax.axis_index("dp")
    other = 1 - lax.axis_index("grp")
    barrier = pltpu.get_barrier_semaphore()

    def greet(step, carry):
        peer = lax.rem(me + step, many)
        pl.semaphore_signal(barrier, inc=1, device_id={"dp": peer}, device_id_type=MESH)
        return carry

    lax.fori_loop(1, many, greet, 0)
    pl.semaphore_signal(barrier, inc=1, device_id={"grp": other}, device_id_type=MESH)
    pl.semaphore_wait(barrier, many)
    query_pairs = [(lambda peer: query_ref.at[peer], land_query)]
    slice_pairs = [(lambda peer: slice_ref.at[peer], land_slice)]
    spread_start(many, me, query_pairs, send, recv, 0)
    spread_start(many, me, slice_pairs, send, recv, 1)
    land_query[me] = query_ref[me]
    land_slice[me] = slice_ref[me]
    spread_wait(many, me, query_pairs, send, recv, 0)
    own_query[...] = low16(jnp.sum(land_query[...].astype(jnp.float32), 0))
    query_back = [(lambda peer: own_query, query_all)]
    spread_start(many, me, query_back, send, recv, 3)
    query_all[me] = own_query[...]
    spread_wait(many, me, slice_pairs, send, recv, 1)
    own_slice[...] = jnp.sum(land_slice[...].astype(jnp.float32), 0).astype(own_slice.dtype)
    slice_back = [(lambda peer: own_slice, slice_all)]
    spread_start(many, me, slice_back, send, recv, 4)
    slice_all[me] = own_slice[...]
    spread_wait(many, me, query_back, send, recv, 3)

    g_vec[...] = d_mid[...]
    tops = []
    first = me * depth
    table_t[...] = jnp.zeros_like(table_t)
    rest = jnp.zeros((1, 1), jnp.float32)
    places = []
    for enc in range(2):
        low, high = (0, count_q) if enc == 0 else (count_q, count_q + count_p)
        number = many * (high - low)
        d_query = query_all[:, low:high, :].reshape(number, 128)
        x = rows_ref[:, low:high, :].reshape(number, 128).astype(jnp.float32) + place_ref[0, enc, 0:1, :]
        center = x - jnp.mean(x, -1, keepdims=True)
        rate = lax.rsqrt(jnp.mean(center * center, -1, keepdims=True) + NORM_EPS)
        scaled = center * rate
        gain = vector_row(vec_ref, enc, 0)
        a_low = low16(scaled * gain + vector_row(vec_ref, enc, 1))
        xa = xa_q if enc == 0 else xa_p
        d_h = xa[...] + dot_last(d_query, low16(attn_ref[0, enc, :, 0:128]))
        d_scaled = d_h * gain
        slope = jnp.mean(d_scaled * scaled, -1, keepdims=True)
        d_x = (d_scaled - jnp.mean(d_scaled, -1, keepdims=True) - scaled * slope) * rate
        d_place = jnp.sum(d_x, 0, keepdims=True)
        places.append(d_place)
        g_attn[enc, :, 0:128] = dot_rows(a_low, d_query)
        g_attn[enc, :, 384:512] = d_out[enc]
        spot = slice(enc, enc + 1)
        g_vec[2, spot, :] = jnp.sum(d_query.astype(jnp.float32), 0, keepdims=True)
        tops.append((jnp.sum(d_h * scaled, 0, keepdims=True), jnp.sum(d_h, 0, keepdims=True)))
        if enc == 0:
            columns = [
                part
                for peer in range(many)
                for part in (
                    raw_ref[peer, RAW_Q : RAW_Q + 16, 0:1].astype(jnp.int32)[0 : count_q // 2],
                    raw_ref[peer, RAW_Q : RAW_Q + 16, 64:65].astype(jnp.int32)[0 : count_q // 2],
                )
            ]
        else:
            columns = [raw_ref[peer, 0:count_p, 0:1].astype(jnp.int32) for peer in range(many)]
        spot = jnp.concatenate(columns, 0) - first
        spot = jnp.where(spot < depth, spot, -1)
        d_low = low16(d_x)
        wide = jnp.broadcast_to(spot, (number, CHUNK))
        for cut in range(sizes.padded // CHUNK):
            chosen = hot(wide == iota((number, CHUNK), 1) + cut * CHUNK)
            table_t[:, cut * CHUNK : (cut + 1) * CHUNK] += dot_rows(d_low, chosen)
        rest += square_sum(d_ffn[enc, 0]) + square_sum(d_ffn[enc, 1])
    for cut in range(0, depth, 128):
        top = min(cut + 128, depth)
        g_word[cut:top, :] = d_table_ref[cut:top, :] + jnp.transpose(table_t[:, cut : cut + 128])[0 : top - cut]
    tile[...] = jnp.broadcast_to(square_sum(g_word[...]), (8, 128))
    pairs = [(lambda peer: tile, scalar_all)]
    spread_start(many, me, pairs, send, recv, 5)
    scalar_all[me] = tile[...]
    spread_wait(many, me, slice_back, send, recv, 4)
    blocks = slice_all[...].astype(jnp.float32).reshape(8, 128, 128)
    for enc in range(2):
        spot = slice(enc, enc + 1)
        g_vec[0, spot, :] = blocks[1][enc * 3 : enc * 3 + 1] + tops[enc][0]
        g_vec[1, spot, :] = blocks[1][enc * 3 + 1 : enc * 3 + 2] + tops[enc][1]
        g_vec[3, spot, :] = blocks[1][enc * 3 + 2 : enc * 3 + 3]
        g_place[enc, 0:128, :] = jnp.transpose(blocks[enc * 4])
        if enc == 0:
            g_place[enc, 128:256, :] = jnp.zeros((128, 128), jnp.float32)
        else:
            g_place[enc, 128:256, :] = jnp.transpose(blocks[enc * 4 + 1])
        g_place[enc, 0:1, :] += places[enc]
        g_attn[enc, :, 128:256] = blocks[enc * 4 + 2]
        g_attn[enc, :, 256:384] = blocks[enc * 4 + 3]
        rest += square_sum(g_place[enc]) + square_sum(g_attn[enc])
    small = jnp.sum(g_vec[...] * g_vec[...], 0)
    rest += jnp.sum(jnp.sum(small, 0, keepdims=True), 1, keepdims=True)
    for copy in loads:
        copy.wait()
    spread_wait(many, me, pairs, send, recv, 5)
    norm = jnp.sqrt(jnp.sum(scalar_all[...], 0)[0:1, 0:1] + rest)
    norm_ref[...] = jnp.broadcast_to(norm, (8, 128))
    factor = CLIP_LIMIT / jnp.maximum(norm, CLIP_LIMIT)
    grads = (g_word, g_place, g_attn, d_ffn, g_vec)

    def differ(kind, at, rows):
        weight, moment, square, anchor = (held[kind * 4 + j] for j in range(4))
        grad = grads[kind][at + (rows,)] * factor
        inner = adam(weight[(0,) + at + (rows,)], grad, moment[(0,) + at + (rows,)], square[(0,) + at + (rows,)])[2]
        mine[kind][at + (rows,)] = (anchor[at + (rows,)] - inner).astype(mine[kind].dtype)

    size = math.gcd(depth, 128)

    def table_block(step, carry):
        differ(0, (), pl.ds(pl.multiple_of(step * size, size), size))
        return carry

    lax.fori_loop(0, depth // size, table_block, 0)
    ways = []

    def hand(kind):
        copy = pltpu.make_async_remote_copy(
            src_ref=mine[kind],
            dst_ref=theirs[kind],
            send_sem=pair_send.at[kind],
            recv_sem=pair_recv.at[kind],
            device_id={"grp": other},
            device_id_type=MESH,
        )
        copy.start()
        ways.append(copy)

    hand(0)
    for kind in range(1, 5):
        for found, at in pieces_of(depth):
            if found == kind:
                differ(kind, at, slice(0, 14) if kind == 4 else slice(None))
        hand(kind)
    def join(kind, spot):
        joined[kind][spot] = mine[kind][spot].astype(jnp.float32) + theirs[kind][spot].astype(jnp.float32)

    def table_add(step, carry):
        join(0, pl.ds(pl.multiple_of(step * size, size), size))
        return carry

    ways[0].wait()
    lax.fori_loop(0, depth // size, table_add, 0)
    for kind in range(1, 5):
        ways[kind].wait()
        for found, at in pieces_of(depth):
            if found == kind:
                join(kind, at if at else slice(None))


def finish(sizes, query, slices, d_table, rows, every, xa_q, xa_p, d_out, d_ffn, d_mid, params, state):
    many = sizes.many
    both = sum(sizes.count)
    inputs = (query, slices, d_table, rows, every, xa_q, xa_p, d_out, d_ffn, d_mid) + params
    flat = tuple(state[j][kind] for kind in range(5) for j in range(4))
    shapes = [state[3][kind].shape for kind in range(5)]
    vm = pl.BlockSpec(memory_space=pltpu.VMEM)
    hbm = pl.BlockSpec(memory_space=pl.ANY)
    f32 = jnp.float32
    return pl.pallas_call(
        functools.partial(finish_kernel, sizes),
        out_shape=tuple(
            jax.ShapeDtypeStruct(shape, f32)
            for shape in [(8, 128), shapes[0], shapes[1], shapes[2], (16, 2, 128)] + shapes
        ),
        in_specs=[vm] * len(inputs) + [hbm] * 20,
        out_specs=[vm] * 10,
        scratch_shapes=[pltpu.VMEM(value.shape, f32) for value in flat]
        + [pltpu.VMEM(shape, jnp.bfloat16 if kind < 4 else f32) for kind, shape in enumerate(shapes)] * 2
        + [
            pltpu.VMEM((many, both, 128), jnp.bfloat16),
            pltpu.VMEM((many, sizes.lines, 128), sizes.kind),
            pltpu.VMEM((many, 8, 128), f32),
            pltpu.VMEM((many, both, 128), jnp.bfloat16),
            pltpu.VMEM((many, sizes.lines, 128), sizes.kind),
            pltpu.VMEM((both, 128), jnp.bfloat16),
            pltpu.VMEM((sizes.lines, 128), sizes.kind),
            pltpu.VMEM((8, 128), f32),
            pltpu.VMEM((128, sizes.padded), f32),
            pltpu.SemaphoreType.DMA((6, many)),
            pltpu.SemaphoreType.DMA((6, many)),
            pltpu.SemaphoreType.DMA((20,)),
            pltpu.SemaphoreType.DMA((5,)),
            pltpu.SemaphoreType.DMA((5,)),
        ],
        compiler_params=pltpu.CompilerParams(
            collective_id=3, has_side_effects=True, vmem_limit_bytes=VMEM_LIMIT
        ),
        name="finish",
    )(*inputs, *flat)


def output_parts(depth):
    rows = depth // 3 if depth % 24 == 0 else depth
    parts = [(0, slice(at, at + rows)) for at in range(0, depth, rows)]
    return parts + [(kind, None) for kind in (3, 2, 1, 4)]


def outputs_kernel(depth, groups, *refs):
    norm_ref, g_vec = refs[:2]
    ins = refs[2:31]
    outs = refs[31:56]
    total_ref = refs[56]
    held = refs[57:86]
    made = refs[86:111]
    load, store = refs[111:113]
    parts = output_parts(depth)
    loads, stores = ([], [])
    for number, (kind, rows) in enumerate(parts):
        group = []
        for j in range(6 if kind < 4 else 5):
            index = kind * 5 + j if j < 5 else 25 + kind
            source, target = (ins[index], held[index])
            if rows is not None:
                lead = (0,) if len(source.shape) == 3 else ()
                source, target = (source.at[lead + (rows,)], target.at[lead + (rows,)])
            copy = pltpu.make_async_copy(source, target, load.at[number, j])
            copy.start()
            group.append(copy)
        loads.append(group)
    total_ref[0] = jnp.max(norm_ref[...])
    norm = norm_ref[0:1, 0:1]
    factor = CLIP_LIMIT / jnp.maximum(norm, CLIP_LIMIT)
    grads = tuple(held[25:29]) + (g_vec,)

    def work(kind, at, rows):
        moment, square, anchor, outer, summed = (held[kind * 5 + j] for j in range(5))
        first, second, average, momentum, weight = (made[kind * 5 + j] for j in range(5))
        spot = at + (rows,)
        deep = (0,) + spot
        grad = grads[kind][spot] * factor
        first[deep] = BETA_ONE * moment[deep] + (1.0 - BETA_ONE) * grad
        second[deep] = BETA_TWO * square[deep] + (1.0 - BETA_TWO) * grad * grad
        mean = summed[spot] / groups
        speed = OUTER_MU * outer[spot] + mean
        average[spot] = mean
        momentum[spot] = speed
        weight[deep] = anchor[spot] - OUTER_RATE * (mean + OUTER_MU * speed)

    for number, (kind, rows) in enumerate(parts):
        for copy in loads[number]:
            copy.wait()
        if kind == 0:
            size = math.gcd(rows.stop - rows.start, 128)

            def table_block(step, carry):
                work(0, (), pl.ds(pl.multiple_of(rows.start + step * size, size), size))
                return carry

            lax.fori_loop(0, (rows.stop - rows.start) // size, table_block, 0)
        else:
            for found, at in pieces_of(depth):
                if found == kind:
                    work(kind, at, slice(0, 14) if kind == 4 else slice(None))
        for j in range(5):
            source, target = (made[kind * 5 + j], outs[kind * 5 + j])
            if rows is not None:
                lead = (0,) if len(source.shape) == 3 else ()
                source, target = (source.at[lead + (rows,)], target.at[lead + (rows,)])
            copy = pltpu.make_async_copy(source, target, store.at[number, j])
            copy.start()
            stores.append(copy)
    for copy in stores:
        copy.wait()


def make_outputs(norm, grads, firsts, seconds, anchors, outers, summed, groups):
    kinds = range(5)
    flat = tuple(v for kind in kinds for v in (firsts[kind], seconds[kind], anchors[kind], outers[kind], summed[kind]))
    flat += tuple(grads[:4])
    out = tuple(
        jax.ShapeDtypeStruct(shape, jnp.float32)
        for kind in kinds
        for shape in (firsts[kind].shape, firsts[kind].shape, anchors[kind].shape, anchors[kind].shape, firsts[kind].shape)
    )
    vm = pl.BlockSpec(memory_space=pltpu.VMEM)
    hbm = pl.BlockSpec(memory_space=pl.ANY)
    got = pl.pallas_call(
        functools.partial(outputs_kernel, anchors[0].shape[0], groups),
        out_shape=out + (jax.ShapeDtypeStruct((1,), jnp.float32),),
        in_specs=[vm] * 2 + [hbm] * 29,
        out_specs=[hbm] * 25 + [pl.BlockSpec(memory_space=pltpu.SMEM)],
        scratch_shapes=[pltpu.VMEM(v.shape, jnp.float32) for v in flat]
        + [pltpu.VMEM(v.shape, jnp.float32) for v in out]
        + [pltpu.SemaphoreType.DMA((7, 6)), pltpu.SemaphoreType.DMA((7, 5))],
        compiler_params=pltpu.CompilerParams(vmem_limit_bytes=VMEM_LIMIT),
        name="make_outputs",
    )(norm, grads[4], *flat)
    return [[got[kind * 5 + j] for kind in kinds] for j in range(5)], got[25]


def square_norm(values):
    center = values - jnp.mean(values, -1, keepdims=True)
    rate = lax.rsqrt(jnp.mean(center * center, -1, keepdims=True) + NORM_EPS)
    return center * rate, rate


def norm_back(d_scaled, scaled, rate):
    slope = jnp.mean(d_scaled * scaled, -1, keepdims=True)
    return (d_scaled - jnp.mean(d_scaled, -1, keepdims=True) - scaled * slope) * rate


def total_of(values):
    return jnp.sum(jnp.sum(values, 0, keepdims=True), 1, keepdims=True)


def score_terms(scores, drop, target, weight, count, axis):
    masked = jnp.where(drop, MASKED, scores)
    top = jnp.max(masked, axis, keepdims=True)
    expo = jnp.exp(masked - top)
    total = jnp.sum(expo, axis, keepdims=True)
    picked = jnp.sum(jnp.where(target, scores, 0.0), axis, keepdims=True)
    loss = total_of(weight * (top + jnp.log(total) - picked))
    grad = low16((weight / count) * (expo / total - jnp.where(target, 1.0, 0.0)))
    return grad, loss


GELU_A = math.sqrt(2.0 / math.pi)
GELU_B = 0.044715


def class_kernel(
    sizes,
    rows_ref,
    mixed_ref,
    raw_ref,
    place_ref,
    attn_ref,
    ffn_ref,
    vec_ref,
    grad_ref,
    xa_q,
    xa_p,
    d_out,
    d_ffn,
    d_mid,
    loss_ref,
    count_ref,
    cls_ref,
    scaled_a,
    rate_a,
    scaled_f,
    rate_f,
    pre_ref,
    act_ref,
    low_ref,
    flag_ref,
):
    many = sizes.many
    counts = sizes.count
    totals = (many * counts[0], many * counts[1])
    chunk = totals[0]
    parts = [(0, 0, 0)] + [(1, at, totals[0] + at) for at in range(0, totals[1], chunk)]

    def held(ref, enc, at):
        each = counts[enc]
        low = 0 if enc == 0 else counts[0]
        return ref[at // each : (at + chunk) // each, low : low + each, :].reshape(chunk, 128)

    def weights(enc):
        return (
            low16(attn_ref[0, enc, :, 384:512]),
            low16(ffn_ref[0, enc, 0]),
            low16(ffn_ref[0, enc, 1]),
        )

    for enc, at, spot in parts:
        w_out, w_up, w_down = weights(enc)
        row = functools.partial(vector_row, vec_ref, enc)
        here = slice(spot, spot + chunk)
        x = held(rows_ref, enc, at).astype(jnp.float32) + place_ref[0, enc, 0:1, :]
        h_embed = norm_rows(x, row(0), row(1))
        scaled, rate = square_norm(h_embed + (dot(held(mixed_ref, enc, at), w_out) + row(4)))
        scaled_a[here, :] = scaled
        rate_a[here, :] = jnp.broadcast_to(rate, (chunk, 128))
        h_attn = scaled * row(5) + row(6)
        h_low = low16(h_attn)
        low_ref[here, :] = h_low
        pre = dot(h_low, w_up) + jnp.concatenate([row(10), row(11), row(12), row(13)], 1)
        pre_ref[here, :] = pre
        act = low16(0.5 * pre * (1.0 + jnp.tanh(GELU_A * (pre + GELU_B * (pre * pre * pre)))))
        act_ref[here, :] = act
        scaled, rate = square_norm(h_attn + (dot_last(act, w_down) + row(7)))
        scaled_f[here, :] = scaled
        rate_f[here, :] = jnp.broadcast_to(rate, (chunk, 128))
        cls_ref[here, :] = low16(scaled * row(8) + row(9))

    every_q = cls_ref[0 : totals[0], :]
    every_p = cls_ref[totals[0] :, :]
    flag_ref[...] = jnp.zeros_like(flag_ref)
    for peer in range(many):
        flag_ref[peer : peer + 1, :] = raw_ref[peer, RAW_Q:RAW_ROWS, :].astype(jnp.float32)[8:9]
    turned = jnp.transpose(flag_ref[...])

    def column(low, each):
        tall = jnp.concatenate([turned[low : low + each]] * many, 0)
        at = iota(tall.shape, 1) == iota(tall.shape, 0) // each
        return jnp.sum(jnp.where(at, tall, 0.0), 1, keepdims=True)

    keys_q = column(0, counts[0])
    valid = column(counts[0], counts[0])
    keys_p = column(2 * counts[0], counts[1])
    hot_q = hot(jnp.broadcast_to(keys_q, (totals[0], 128)) == iota((totals[0], 128), 1).astype(jnp.float32))
    hot_p = hot(jnp.broadcast_to(keys_p, (totals[1], 128)) == iota((totals[1], 128), 1).astype(jnp.float32))
    same = dot_last(hot_q, hot_p) > 0.5
    count = jnp.maximum(total_of(valid), 1.0)
    scale = 128 ** (-0.5)
    scores = dot_last(every_q, every_p) * scale
    index_q = iota(scores.shape, 0)
    index_p = iota(scores.shape, 1)
    target_qp = index_p == 2 * index_q
    target_pq = index_p // 2 == index_q
    grad_qp, loss_qp = score_terms(scores, same & ~target_qp, target_qp, valid, count, 1)
    drop_pq = (same | (jnp.broadcast_to(valid, scores.shape) == 0.0)) & ~target_pq
    weight_p = jnp.sum(jnp.where(target_qp, jnp.broadcast_to(valid, scores.shape), 0.0), 0, keepdims=True)
    grad_pq, loss_pq = score_terms(scores, drop_pq, target_pq, weight_p, count, 0)
    loss_ref[0] = jnp.max(loss_qp + loss_pq)
    count_ref[0] = jnp.max(count)
    d_q = (dot(grad_qp, every_p) + dot(grad_pq, every_p)) * scale
    d_p = (dot_rows(grad_pq, every_q) + dot_rows(grad_qp, every_q)) * scale

    d_mid[...] = jnp.zeros_like(d_mid)
    d_out[...] = jnp.zeros_like(d_out)
    d_ffn[...] = jnp.zeros_like(d_ffn)
    for enc, at, spot in parts:
        w_out, w_up, w_down = weights(enc)
        row = functools.partial(vector_row, vec_ref, enc)
        here = slice(spot, spot + chunk)

        def add(index, values):
            d_mid[index, enc : enc + 1, :] += jnp.sum(values, 0, keepdims=True)

        d_cls = d_q if enc == 0 else d_p[at : at + chunk]
        scaled = scaled_f[here, :]
        add(8, d_cls * scaled)
        add(9, d_cls)
        d_x_ffn = norm_back(d_cls * row(8), scaled, rate_f[here, :])
        d_branch = low16(d_x_ffn)
        add(7, d_branch.astype(jnp.float32))
        d_ffn[enc, 1] += dot_rows(d_branch, act_ref[here, :])
        d_act = dot(d_branch, w_down)
        pre = pre_ref[here, :]
        square = pre * pre
        bend = jnp.tanh(GELU_A * (pre + GELU_B * (square * pre)))
        slope = 0.5 * (1.0 + bend) + (0.5 * GELU_A) * pre * (1.0 - bend * bend) * (
            1.0 + (3.0 * GELU_B) * square
        )
        d_pre = low16(slope * d_act)
        up_bias = jnp.sum(d_pre.astype(jnp.float32), 0, keepdims=True)
        for cut in range(4):
            d_mid[10 + cut, enc : enc + 1, :] += up_bias[:, cut * 128 : (cut + 1) * 128]
        d_ffn[enc, 0] += dot_rows(low_ref[here, :], d_pre)
        d_h = d_x_ffn + dot_last(d_pre, w_up)
        scaled = scaled_a[here, :]
        add(5, d_h * scaled)
        add(6, d_h)
        d_x = norm_back(d_h * row(5), scaled, rate_a[here, :])
        if enc == 0:
            xa_q[...] = d_x
        else:
            xa_p[at : at + chunk, :] = d_x
        d_proj = low16(d_x)
        add(4, d_proj.astype(jnp.float32))
        d_out[enc] += dot_rows(held(mixed_ref, enc, at), d_proj)
        d_mixed = low16(dot_last(d_proj, w_out))
        each = counts[enc]
        low = 0 if enc == 0 else counts[0]
        grad_ref[at // each : (at + chunk) // each, low : low + each, :] = d_mixed.reshape(
            chunk // each, each, 128
        )


def class_stage(sizes, rows, mixed, every, positions, attention, feedforward, vectors):
    many = sizes.many
    n_q, n_p = (many * sizes.count[0], many * sizes.count[1])
    both = n_q + n_p
    f32 = jnp.float32
    return local_call(
        functools.partial(class_kernel, sizes),
        (
            jax.ShapeDtypeStruct((many, sum(sizes.count), 128), jnp.bfloat16),
            jax.ShapeDtypeStruct((n_q, 128), f32),
            jax.ShapeDtypeStruct((n_p, 128), f32),
            jax.ShapeDtypeStruct((2, 128, 128), f32),
            jax.ShapeDtypeStruct((2, 2, 128, 512), f32),
            jax.ShapeDtypeStruct((16, 2, 128), f32),
            jax.ShapeDtypeStruct((1,), f32),
            jax.ShapeDtypeStruct((1,), f32),
        ),
        (rows, mixed, every, positions, attention, feedforward, vectors),
        [
            pltpu.VMEM((both, 128), jnp.bfloat16),
            pltpu.VMEM((both, 128), f32),
            pltpu.VMEM((both, 128), f32),
            pltpu.VMEM((both, 128), f32),
            pltpu.VMEM((both, 128), f32),
            pltpu.VMEM((both, 512), f32),
            pltpu.VMEM((both, 512), jnp.bfloat16),
            pltpu.VMEM((both, 128), jnp.bfloat16),
            pltpu.VMEM((128, 128), f32),
        ],
        "class_stage",
        smem_out=(6, 7),
    )


def class_stage_large(sizes, rows_all, mixed_all, every, positions, attention, feedforward, vectors):
    many = sizes.many
    count_q, count_p = sizes.count
    counts = sizes.count
    width = rows_all.shape[2]
    flags_all = every[:, RAW_FLAGS, :].astype(jnp.int32)
    keys_q = flags_all[:, :count_q].reshape(-1)
    valid_all = flags_all[:, count_q : 2 * count_q].reshape(-1)
    keys_p = flags_all[:, 2 * count_q : 2 * count_q + count_p].reshape(-1)
    cuts = ((0, count_q), (count_q, count_q + count_p))
    cls, class_kept, mixes = ([], [], [])
    for enc in range(2):
        low, high = cuts[enc]
        rows = rows_all[:, low:high].reshape(-1, width)
        mixed = mixed_all[:, low:high].reshape(-1, width)
        low_cls, kept_cls = class_forward(
            rows, mixed, positions[0, enc], attention[0, enc], feedforward[0, enc], vectors[0, :, enc]
        )
        cls.append(low_cls)
        class_kept.append(kept_cls)
        mixes.append(mixed)
    d_q, d_p, loss_total, count = score_stage(cls[0], cls[1], keys_q, keys_p, valid_all)
    d_cls = (d_q, d_p)
    grads, xas, outs, ffns, mids = ([], [], [], [], [])
    for enc in range(2):
        d_mixed, d_x_attn, d_w_out, d_ffn, rows_mid, d_up_bias = class_backward(
            class_kept[enc], mixes[enc], attention[0, enc], feedforward[0, enc], vectors[0, :, enc], d_cls[enc]
        )
        grads.append(d_mixed.reshape(many, counts[enc], width))
        xas.append(d_x_attn)
        outs.append(d_w_out)
        ffns.append(d_ffn)
        mid = jnp.concatenate([jnp.stack(list(rows_mid)), d_up_bias.reshape(-1, width)])
        mids.append(jnp.pad(mid, ((4, 2), (0, 0))))
    return (
        jnp.concatenate(grads, 1),
        xas[0],
        xas[1],
        jnp.stack(outs),
        jnp.stack(ffns),
        jnp.stack(mids, 1),
        loss_total.reshape(1),
        count.reshape(1),
    )


def class_forward(rows, mixed, place, attn_w, ffn_w, vec):
    width = rows.shape[1]
    h_embed = layer_norm(rows.astype(jnp.float32) + place[:1], vec[0], vec[1])
    x_attn = h_embed + (dot(mixed, low16(attn_w[:, 3 * width :])) + vec[4])
    h_attn = layer_norm(x_attn, vec[5], vec[6])
    h_low = low16(h_attn)
    pre = dot(h_low, low16(ffn_w[0])) + vec[10:].reshape(-1)
    act = low16(gelu_tanh(pre))
    x_ffn = h_attn + (dot_last(act, low16(ffn_w[1])) + vec[7])
    h_out = layer_norm(x_ffn, vec[8], vec[9])
    return low16(h_out), (x_attn, h_low, pre, act, x_ffn)


def class_backward(kept, mixed, attn_w, ffn_w, vec, d_cls):
    x_attn, h_low, pre, act, x_ffn = kept
    width = x_attn.shape[1]
    unused, out_back = jax.vjp(layer_norm, x_ffn, vec[8], vec[9])
    d_x_ffn, d_gain_two, d_shift_two = out_back(d_cls)
    d_branch = low16(d_x_ffn)
    d_down_bias = jnp.sum(d_branch, 0, dtype=jnp.float32)
    d_down = dot_rows(d_branch, act)
    d_act = dot(d_branch, low16(ffn_w[1]))
    unused, gelu_back = jax.vjp(gelu_tanh, pre)
    d_pre = low16(gelu_back(d_act)[0])
    d_up_bias = jnp.sum(d_pre, 0, dtype=jnp.float32)
    d_up = dot_rows(h_low, d_pre)
    d_h_attn = d_x_ffn + dot_last(d_pre, low16(ffn_w[0]))
    unused, attn_back = jax.vjp(layer_norm, x_attn, vec[5], vec[6])
    d_x_attn, d_gain_one, d_shift_one = attn_back(d_h_attn)
    d_proj = low16(d_x_attn)
    d_out_bias = jnp.sum(d_proj, 0, dtype=jnp.float32)
    d_w_out = dot_rows(mixed, d_proj)
    d_mixed = low16(dot_last(d_proj, low16(attn_w[:, 3 * width :])))
    rows = (d_out_bias, d_gain_one, d_shift_one, d_down_bias, d_gain_two, d_shift_two)
    return d_mixed, d_x_attn, d_w_out, jnp.stack([d_up, d_down]), rows, d_up_bias


def softmax_terms(scores, drop, target, weight, count, axis):
    masked = jnp.where(drop, MASKED, scores)
    top = jnp.max(masked, axis, keepdims=True)
    expo = jnp.exp(masked - top)
    total = jnp.sum(expo, axis, keepdims=True)
    lse = top + jnp.log(total)
    picked = jnp.sum(jnp.where(target, scores, 0.0), axis, keepdims=True)
    loss = jnp.sum(weight * (lse - picked))
    grad = low16((weight / count) * (expo / total - target.astype(jnp.float32)))
    return grad, loss


def score_stage(every_q, every_p, keys_q, keys_p, valid_q):
    count = jnp.maximum(jnp.sum(valid_q).astype(jnp.float32), 1.0)
    scale = every_q.shape[1] ** (-0.5)
    index_q = jnp.arange(every_q.shape[0])[:, None]
    index_p = jnp.arange(every_p.shape[0])[None, :]
    scores = dot_last(every_q, every_p) * scale
    same = keys_q[:, None] == keys_p[None, :]
    target_qp = index_p == 2 * index_q
    valid = valid_q.astype(jnp.float32)[:, None]
    grad_qp, loss_qp = softmax_terms(scores, same & ~target_qp, target_qp, valid, count, 1)
    target_pq = index_p // 2 == index_q
    drop_pq = (same | (valid_q[:, None] == 0)) & ~target_pq
    owner_valid = jnp.repeat(valid_q, 2)
    weight_p = jnp.where(index_p[0] % 2 == 0, owner_valid, 0).astype(jnp.float32)[None, :]
    grad_pq, loss_pq = softmax_terms(scores, drop_pq, target_pq, weight_p, count, 0)
    d_q = (dot(grad_qp, every_p) + dot(grad_pq, every_p)) * scale
    d_p = (dot_rows(grad_pq, every_q) + dot_rows(grad_qp, every_q)) * scale
    return d_q, d_p, loss_qp + loss_pq, count


def body(
    question_ids,
    passage_ids,
    question_lengths,
    passage_lengths,
    question_keys,
    passage_keys,
    question_valid,
    word_table,
    positions,
    attention,
    feedforward,
    vectors,
    word_first,
    positions_first,
    attention_first,
    feedforward_first,
    vectors_first,
    word_second,
    positions_second,
    attention_second,
    feedforward_second,
    vectors_second,
    word_anchor,
    positions_anchor,
    attention_anchor,
    feedforward_anchor,
    vectors_anchor,
    word_outer,
    positions_outer,
    attention_outer,
    feedforward_outer,
    vectors_outer,
):
    many = lax.axis_size("dp")
    count_q = question_ids.shape[0]
    count_p = passage_ids.shape[0]
    table = word_table[0]
    sizes = Sizes(many, count_q, count_p, table.shape[0])
    swap = lambda values: jnp.swapaxes(values, -3, -2)
    vectors, vectors_first, vectors_second, vectors_anchor, vectors_outer = (
        swap(v) for v in (vectors, vectors_first, vectors_second, vectors_anchor, vectors_outer)
    )
    every, class_rows, kept, entry, counted = first_stage(
        sizes,
        question_ids,
        passage_ids,
        question_lengths,
        passage_lengths,
        question_keys,
        question_valid,
        passage_keys,
        table,
        positions,
    )
    part, lse_part, query, levels = tokens_forward(
        sizes, every, class_rows, kept, entry, counted, table, positions, attention, vectors
    )
    mixed_all, lse_all = exchange_mixed(sizes, part, lse_part)
    stage = class_stage if many * count_q <= 512 else class_stage_large
    grad_all, xa_q, xa_p, d_out, d_ffn, d_mid, loss_total, count = stage(
        sizes, class_rows, mixed_all, every, positions, attention, feedforward, vectors
    )
    d_query, d_table, slices = tokens_backward(
        sizes, levels, every, query, mixed_all, lse_all, grad_all, kept, entry, table, positions, attention, vectors
    )
    weights = (word_table, positions, attention, feedforward, vectors)
    firsts = (word_first, positions_first, attention_first, feedforward_first, vectors_first)
    seconds = (word_second, positions_second, attention_second, feedforward_second, vectors_second)
    anchors = (word_anchor, positions_anchor, attention_anchor, feedforward_anchor, vectors_anchor)
    outers = (word_outer, positions_outer, attention_outer, feedforward_outer, vectors_outer)
    done = finish(
        sizes,
        d_query,
        slices.reshape(many, sizes.lines, 128),
        d_table,
        class_rows,
        every,
        xa_q,
        xa_p,
        d_out,
        d_ffn,
        d_mid,
        (positions, attention, vectors),
        (weights, firsts, seconds, anchors),
    )
    norm = done[0]
    grads = (done[1], done[2], done[3], d_ffn, done[4])
    made, norm = make_outputs(
        norm, grads, firsts, seconds, anchors, outers, done[5:10], lax.axis_size("grp")
    )
    first_new, second_new, averages, outer_next, weight_next = (
        part[:4] + [swap(part[4])] for part in made
    )
    return (
        loss_total.reshape(1),
        count.reshape(1),
        norm.reshape(1),
        first_new[0],
        first_new[1],
        first_new[2],
        first_new[3],
        first_new[4],
        second_new[0],
        second_new[1],
        second_new[2],
        second_new[3],
        second_new[4],
        averages[0],
        averages[1],
        averages[2],
        averages[3],
        averages[4],
        outer_next[0],
        outer_next[1],
        outer_next[2],
        outer_next[3],
        outer_next[4],
        weight_next[0],
        weight_next[1],
        weight_next[2],
        weight_next[3],
        weight_next[4],
    )


def solution(mesh):
    placed = (
        P(("grp", "dp"), None),
        P(("grp", "dp"), None),
        P(("grp", "dp")),
        P(("grp", "dp")),
        P(("grp", "dp")),
        P(("grp", "dp")),
        P(("grp", "dp")),
        P("grp", "dp", None),
        P("grp", None, None, None),
        P("grp", None, None, None),
        P("grp", None, None, None, None),
        P("grp", None, None, None),
        P("grp", "dp", None),
        P("grp", None, None, None),
        P("grp", None, None, None),
        P("grp", None, None, None, None),
        P("grp", None, None, None),
        P("grp", "dp", None),
        P("grp", None, None, None),
        P("grp", None, None, None),
        P("grp", None, None, None, None),
        P("grp", None, None, None),
        P("dp", None),
        P(),
        P(),
        P(),
        P(),
        P("dp", None),
        P(),
        P(),
        P(),
        P(),
    )
    return jax.shard_map(
        body,
        mesh=mesh,
        in_specs=placed,
        out_specs=(
            P("grp"),
            P("grp"),
            P("grp"),
            P("grp", "dp", None),
            P("grp", None, None, None),
            P("grp", None, None, None),
            P("grp", None, None, None, None),
            P("grp", None, None, None),
            P("grp", "dp", None),
            P("grp", None, None, None),
            P("grp", None, None, None),
            P("grp", None, None, None, None),
            P("grp", None, None, None),
            P("dp", None),
            P(),
            P(),
            P(),
            P(),
            P("dp", None),
            P(),
            P(),
            P(),
            P(),
            P("grp", "dp", None),
            P("grp", None, None, None),
            P("grp", None, None, None),
            P("grp", None, None, None, None),
            P("grp", None, None, None),
        ),
        check_vma=False,
    )
```

```python
import functools
import math

import jax
import jax.numpy as jnp
from jax import lax
from jax.experimental import pallas as pl
from jax.experimental.pallas import tpu as pltpu
from jax.sharding import PartitionSpec as P

HEAD = 64
STEP = 5


NORM_EPS = 1e-05
MASKED = -1000000000.0
BETA_ONE = 0.9
BETA_TWO = 0.999
INNER_RATE = 0.05
WEIGHT_DECAY = 0.01
ADAM_EPS = 1e-08
CLIP_LIMIT = 0.01
OUTER_RATE = 0.7
OUTER_MU = 0.9
CONTRACT_ROWS = (((0,), (0,)), ((), ()))
CONTRACT_LAST = (((1,), (1,)), ((), ()))


def layer_norm(values, gain, shift):
    center = values - jnp.mean(values, -1, keepdims=True)
    spread = jnp.mean(center * center, -1, keepdims=True)
    return center * lax.rsqrt(spread + NORM_EPS) * gain + shift


def gelu_tanh(values):
    return jax.nn.gelu(values, approximate=True)


def low16(values):
    return values.astype(jnp.bfloat16)


NEG = -1e30
MESH = pl.DeviceIdType.MESH
VMEM_LIMIT = 60 * 1024 * 1024
WAYS = 4
SLOTS = 128
SPAN = WAYS * SLOTS
CHUNK = 256
UNROLL = 4
RAW_Q = 64
RAW_FLAGS = 72
RAW_ROWS = 80


def greet_all(many):
    me = lax.axis_index("dp")
    barrier = pltpu.get_barrier_semaphore()

    def greet(step, carry):
        peer = lax.rem(me + step, many)
        pl.semaphore_signal(barrier, inc=1, device_id={"dp": peer}, device_id_type=MESH)
        return carry

    lax.fori_loop(1, many, greet, 0)
    return me


def enter(many):
    me = greet_all(many)
    pl.semaphore_wait(pltpu.get_barrier_semaphore(), many - 1)
    return me


def copy_to(peer, src, dst, send, recv):
    return pltpu.make_async_remote_copy(
        src_ref=src,
        dst_ref=dst,
        send_sem=send,
        recv_sem=recv,
        device_id={"dp": peer},
        device_id_type=MESH,
    )


def spread_start(many, me, pairs, send, recv, slot):
    def step_start(step, carry):
        peer = lax.rem(me + step, many)
        for index, (source, landing) in enumerate(pairs):
            copy_to(
                peer,
                source(peer),
                landing.at[me],
                send.at[slot + index, peer],
                recv.at[slot + index, me],
            ).start()
        return carry

    lax.fori_loop(1, many, step_start, 0)


def spread_wait(many, me, pairs, send, recv, slot):
    def step_wait(step, carry):
        peer = lax.rem(me + step, many)
        for index, (source, landing) in enumerate(pairs):
            copy = copy_to(
                peer,
                source(peer),
                landing.at[peer],
                send.at[slot + index, peer],
                recv.at[slot + index, peer],
            )
            copy.wait_recv()
            copy.wait_send()
        return carry

    lax.fori_loop(1, many, step_wait, 0)


def dot(left, right):
    return jnp.dot(left, right, preferred_element_type=jnp.float32)


def dot_rows(left, right):
    return lax.dot_general(left, right, CONTRACT_ROWS, preferred_element_type=jnp.float32)


def dot_last(left, right):
    return lax.dot_general(left, right, CONTRACT_LAST, preferred_element_type=jnp.float32)


def iota(shape, axis):
    return lax.broadcasted_iota(jnp.int32, shape, axis)


def hot(mask):
    return jnp.where(mask, 1.0, 0.0).astype(jnp.bfloat16)


def first_kernel(
    sizes,
    question_ref,
    passage_ref,
    length_q,
    length_p,
    key_q,
    valid_q,
    key_p,
    table_ref,
    place_ref,
    every_ref,
    rows_ref,
    kept_ref,
    entry_ref,
    count_ref,
    stage,
    raw,
    ask,
    asks,
    low_ref,
    offer,
    landed,
    own,
    table_t,
    place_t,
    send,
    recv,
):
    many = sizes.many
    count_q, count_p = sizes.count
    each = count_q + count_p
    depth = sizes.depth
    half = count_q // 2
    me = greet_all(many)
    lane = iota((1, 128), 1)
    for seq in range(count_p):
        stop = length_p[seq]
        stage[seq : seq + 1, :] = jnp.where(lane < stop, passage_ref[seq : seq + 1, 0:128], -1)
        stage[count_p + seq : count_p + seq + 1, :] = jnp.where(
            lane + 128 < stop, passage_ref[seq : seq + 1, 128:256], -1
        )
    both = jnp.concatenate([question_ref[0:half, :], question_ref[half:count_q, :]], 1)
    for seq in range(half):
        stop = jnp.where(lane < 64, length_q[seq], length_q[half + seq] + 64)
        stage[RAW_Q + seq : RAW_Q + seq + 1, :] = jnp.where(lane < stop, both[seq : seq + 1], -1)
    flags = jnp.zeros((1, 128), jnp.int32)
    for spot in range(count_q):
        flags = jnp.where(lane == spot, key_q[spot], flags)
        flags = jnp.where(lane == count_q + spot, valid_q[spot], flags)
    for spot in range(count_p):
        flags = jnp.where(lane == 2 * count_q + spot, key_p[spot], flags)
    stage[RAW_FLAGS:RAW_ROWS, :] = jnp.broadcast_to(flags, (8, 128))
    raw[...] = stage[...].astype(jnp.int16)
    heads = jnp.concatenate([question_ref[:, 0:1], passage_ref[:, 0:1]], 0)
    diagonal = iota((each, 128), 0) == iota((each, 128), 1)
    heads = jnp.sum(jnp.where(diagonal, jnp.broadcast_to(heads, (each, 128)), 0), 0, keepdims=True)
    ask[...] = jnp.broadcast_to(heads, (8, 128))
    pl.semaphore_wait(pltpu.get_barrier_semaphore(), many - 1)
    ask_pairs = [(lambda peer: ask, asks)]
    raw_pairs = [(lambda peer: raw, every_ref)]
    spread_start(many, me, ask_pairs, send, recv, 0)
    spread_start(many, me, raw_pairs, send, recv, 1)
    asks[me] = ask[...]
    every_ref[me] = raw[...]
    padded = sizes.padded
    if padded > depth:
        low_ref[...] = jnp.zeros_like(low_ref)
    low_ref[0:depth, :] = low16(table_ref[...])
    first = me * depth
    block = math.gcd(many, 16)
    spread_wait(many, me, ask_pairs, send, recv, 0)

    def pick(step, carry):
        found = []
        for i in range(block):
            line = jnp.broadcast_to(asks[step * block + i][0:1, :].astype(jnp.float32), (each, 128))
            found.append(jnp.sum(jnp.where(diagonal, line, 0.0), 1, keepdims=True))
        place = jnp.concatenate(found, 0).astype(jnp.int32) - first
        spot = jnp.where((place >= 0) & (place < depth), place, -1)
        number = spot.shape[0]
        total = jnp.zeros((number, 128), jnp.float32)
        wide = jnp.broadcast_to(spot, (number, CHUNK))
        for at in range(padded // CHUNK):
            chosen = hot(wide == iota((number, CHUNK), 1) + at * CHUNK)
            total += dot(chosen, low_ref[at * CHUNK : (at + 1) * CHUNK, :])
        for i in range(block):
            offer[step * block + i] = low16(total[i * each : (i + 1) * each])
        return carry

    lax.fori_loop(0, many // block, pick, 0)
    offer_pairs = [(lambda peer: offer.at[peer], landed)]
    spread_start(many, me, offer_pairs, send, recv, 2)
    landed[me] = offer[me]
    if sizes.keep:
        prepare_tokens(sizes, table_ref, place_ref, table_t, place_t)
    spread_wait(many, me, raw_pairs, send, recv, 1)

    def spans_of(enc, count):
        def spans(turn, count):
            steps = [turn * sizes.unroll[enc] + u for u in range(sizes.unroll[enc])]
            packed = [pack_span(sizes, enc, s, 0, first, every_ref) for s in steps]
            found = [gather_span(sizes, enc, part[0], table_t, place_t) for part in packed]
            for part in packed:
                count = jnp.maximum(count, part[1])
            for u, s in enumerate(steps):
                at = s if enc == 0 else sizes.steps[0] + s
                kept_ref[at, 0:128, :] = found[u][0]
                kept_ref[at, 128:129, :] = found[u][1]
                entry_ref[at, 0:1, :] = packed[u][0]
            return count

        return lax.fori_loop(0, sizes.steps[enc] // sizes.unroll[enc], spans, count)

    count = jnp.zeros((8, 128), jnp.float32)
    if sizes.keep:
        count = spans_of(0, count)
    spread_wait(many, me, offer_pairs, send, recv, 2)
    own[...] = low16(jnp.sum(landed[...].astype(jnp.float32), 0))
    row_pairs = [(lambda peer: own, rows_ref)]
    spread_start(many, me, row_pairs, send, recv, 3)
    rows_ref[me] = own[...]
    if sizes.keep:
        count = spans_of(1, count)
    count_ref[...] = count
    spread_wait(many, me, row_pairs, send, recv, 3)


def first_stage(sizes, ids_q, ids_p, length_q, length_p, key_q, valid_q, key_p, table, positions):
    many = sizes.many
    padded = sizes.padded
    both = sum(sizes.count)
    vm = pl.BlockSpec(memory_space=pltpu.VMEM)
    sm = pl.BlockSpec(memory_space=pltpu.SMEM)
    kept = sizes.spans if sizes.keep else 1
    return pl.pallas_call(
        functools.partial(first_kernel, sizes),
        out_shape=(
            jax.ShapeDtypeStruct((many, RAW_ROWS, 128), jnp.int16),
            jax.ShapeDtypeStruct((many, both, 128), jnp.bfloat16),
            jax.ShapeDtypeStruct((kept, 136, SPAN), jnp.float32),
            jax.ShapeDtypeStruct((kept, 8, SPAN), jnp.int32),
            jax.ShapeDtypeStruct((8, 128), jnp.float32),
        ),
        in_specs=[vm, vm, sm, sm, sm, sm, sm, vm, vm],
        out_specs=[vm] * 5,
        scratch_shapes=[
            pltpu.VMEM((RAW_ROWS, 128), jnp.int32),
            pltpu.VMEM((RAW_ROWS, 128), jnp.int16),
            pltpu.VMEM((8, 128), jnp.int32),
            pltpu.VMEM((many, 8, 128), jnp.int32),
            pltpu.VMEM((padded, 128), jnp.bfloat16),
            pltpu.VMEM((many, both, 128), jnp.bfloat16),
            pltpu.VMEM((many, both, 128), jnp.bfloat16),
            pltpu.VMEM((both, 128), jnp.bfloat16),
            pltpu.VMEM((128, padded), jnp.bfloat16),
            pltpu.VMEM((2, 2, 128, CHUNK), jnp.bfloat16),
            pltpu.SemaphoreType.DMA((4, many)),
            pltpu.SemaphoreType.DMA((4, many)),
        ],
        compiler_params=pltpu.CompilerParams(
            collective_id=1, has_side_effects=True, vmem_limit_bytes=VMEM_LIMIT
        ),
        name="first_stage",
    )(ids_q, ids_p, length_q, length_p, key_q, valid_q, key_p, table, positions)


def norm_rows(values, gain, shift):
    center = values - jnp.mean(values, -1, keepdims=True)
    spread = jnp.mean(center * center, -1, keepdims=True)
    return center * lax.rsqrt(spread + NORM_EPS) * gain + shift


def two_heads(values):
    lane = iota(values.shape, 1)
    low = jnp.where(lane < HEAD, values, jnp.zeros_like(values))
    high = jnp.where(lane >= HEAD, values, jnp.zeros_like(values))
    return jnp.concatenate([low, high], 0)


def merge_heads(both):
    half = both.shape[0] // 2
    lane = iota((half, both.shape[1]), 1)
    return jnp.where(lane < HEAD, both[:half], both[half:])


class Sizes:
    def __init__(self, many, count_q, count_p, depth):
        self.many = many
        self.count = (count_q, count_p)
        self.depth = depth
        self.padded = -(-depth // CHUNK) * CHUNK
        self.steps = (many // (2 * WAYS), many)
        self.unroll = tuple(math.gcd(UNROLL, step) for step in self.steps)
        self.spans = self.steps[0] + self.steps[1]
        self.devices = (2 * WAYS, 1)
        self.queries = (2 * WAYS * count_q, count_p)
        self.lines = 1024 // many
        self.kind = jnp.bfloat16 if self.lines % 16 == 0 else jnp.float32
        self.keep = self.spans * 136 * SPAN * 4 <= 8 * 1024 * 1024


def vector_row(vec_ref, enc, row):
    return vec_ref[0, row, enc : enc + 1, :]


def prepare_tokens(sizes, table_ref, place_ref, table_t, place_t):
    depth = sizes.depth
    if sizes.padded > depth:
        table_t[...] = jnp.zeros_like(table_t)

    def turn(step, carry):
        spot = pl.ds(pl.multiple_of(step * 128, 128), 128)
        table_t[:, spot] = low16(jnp.transpose(table_ref[spot, :]))
        return carry

    whole = depth // 128
    lax.fori_loop(0, whole, turn, 0)
    rest = depth - whole * 128
    if rest:
        piece = jnp.concatenate([table_ref[whole * 128 :, :], jnp.zeros((128 - rest, 128), jnp.float32)], 0)
        table_t[:, whole * 128 : (whole + 1) * 128] = low16(jnp.transpose(piece))

    def turn_place(step, carry):
        enc, cut = (step // 2, step % 2)
        spot = pl.ds(pl.multiple_of(cut * 128, 128), 128)
        turned = jnp.transpose(place_ref[0, enc, spot, :])
        high = low16(turned)
        place_t[enc, 0, :, spot] = high
        place_t[enc, 1, :, spot] = low16(turned - high.astype(jnp.float32))
        return carry

    lax.fori_loop(0, 4, turn_place, 0)


def prepare_weights(attn_ref, vec_ref, w_kv, vec_t):
    for enc in range(2):
        for cut in range(2):
            w_kv[enc, cut * 128 : (cut + 1) * 128, :] = low16(
                jnp.transpose(attn_ref[0, enc, :, (cut + 1) * 128 : (cut + 2) * 128])
            )
        rows = [vector_row(vec_ref, enc, row) for row in range(4)]
        rows = jnp.concatenate(rows + [jnp.zeros((124, 128), jnp.float32)], 0)
        vec_t[enc] = jnp.transpose(rows)


def lane_pick(values, lanes):
    return jnp.take_along_axis(values, lanes, axis=1, mode="promise_in_bounds")


def pack_span(sizes, enc, step, level, first, raw_ref):
    if enc == 1:
        ids = raw_ref[step, 0:RAW_Q, :].astype(jnp.int32)
    else:
        ids = jnp.concatenate(
            [
                raw_ref[step * 8 + i, RAW_Q:RAW_ROWS, :].astype(jnp.int32)[0:8]
                for i in range(8)
            ],
            0,
        )
    place = ids - first
    owned = (place >= 0) & (place < sizes.depth)
    flag = hot(owned)
    inside = dot(flag, hot(iota((128, 128), 0) <= iota((128, 128), 1))).astype(jnp.int32)
    total = dot(flag, jnp.ones((128, 128), jnp.bfloat16))
    before = dot(hot(iota((64, 64), 1) < iota((64, 64), 0)), low16(total))
    start = before.astype(jnp.int32)
    stop = (before + total).astype(jnp.int32)
    line = iota((64, 128), 0)
    turn = iota((64, 128), 1)
    lane = jnp.zeros((64, 128), jnp.int32)
    for jump in (64, 32, 16, 8, 4, 2, 1):
        seen = lane_pick(inside, lane + (jump - 1))
        lane = jnp.where(seen <= turn, lane + jump, lane)
    row = lane_pick(place, lane)
    if enc == 1:
        where = (line >> 5) * 128 + lane
        seq = (line & 31) + 1
    else:
        where = lane & 63
        seq = (line >> 3) * sizes.count[0] + (lane >> 6) * 8 + (line & 7) + 1
    code = lane_pick((row << 16) + (where << 8) + seq, (turn - start) & 127)
    codes = []
    for window in range(WAYS):
        slot = turn + (window * SLOTS + level * SPAN)
        kept = jnp.where((slot >= start) & (slot < stop), code, 0)
        codes.append(jnp.sum(kept, 0, keepdims=True))
    return jnp.concatenate(codes, 1), (before + total)[56:64]


def gather_span(sizes, enc, code, table_t, place_t, short=False):
    rows = code >> 16
    where = (code >> 8) & 255
    x = jnp.zeros((128, SPAN), jnp.float32)
    wide = jnp.broadcast_to(rows, (CHUNK, SPAN))

    def add(cut, x):
        spot = pl.ds(pl.multiple_of(cut * CHUNK, CHUNK), CHUNK)
        return x + dot(table_t[:, spot], hot(wide == iota((CHUNK, SPAN), 0) + cut * CHUNK))

    x = lax.fori_loop(0, sizes.padded // CHUNK, add, x, unroll=not short)
    chosen = hot(jnp.broadcast_to(where, (CHUNK, SPAN)) == iota((CHUNK, SPAN), 0))
    x += dot(place_t[enc, 0], chosen) + dot(place_t[enc, 1], chosen)
    center = x - jnp.mean(x, 0, keepdims=True)
    rate = lax.rsqrt(jnp.mean(center * center, 0, keepdims=True) + NORM_EPS)
    return center * rate, rate


def project(enc, scaled, vec_t, w_kv):
    a_t = low16(scaled * vec_t[enc, :, 0:1] + vec_t[enc, :, 1:2])
    kv = dot(w_kv[enc], a_t)
    keys_t = low16(kv[:128])
    values_t = low16(kv[128:] + vec_t[enc, :, 3:4])
    return a_t, keys_t, values_t


def own_slots(code, number):
    line = iota((2 * number, SPAN), 0)
    line = jnp.where(line >= number, line - number, line)
    return line == (code & 255) - 1


def forward_kernel(
    sizes,
    raw_ref,
    rows_ref,
    kept_hbm,
    entry_hbm,
    count_ref,
    table_ref,
    place_ref,
    attn_ref,
    vec_ref,
    out_ref,
    lse_ref,
    query_ref,
    levels_ref,
    table_t,
    place_t,
    w_kv,
    vec_t,
    query_q,
    total_q,
    top_q,
    mass_q,
    total_p,
    top_p,
    mass_p,
    kept_ref,
    entry_ref,
    load,
):
    loads = load_kept(sizes, kept_hbm, entry_hbm, kept_ref, entry_ref, load)
    first = lax.axis_index("dp") * sizes.depth
    count_q, count_p = sizes.count
    prepare_weights(attn_ref, vec_ref, w_kv, vec_t)
    begin = 1 if sizes.keep else 0
    count = count_ref[...]
    block = math.gcd(sizes.many, 16)
    for enc in range(2):
        low, high = (0, count_q) if enc == 0 else (count_q, count_q + count_p)
        w_q = low16(attn_ref[0, enc, :, 0:128])

        def ask(step, carry):
            spot = pl.ds(step * block, block)
            held = rows_ref[spot, low:high, :].reshape(block * (high - low), 128)
            x = held.astype(jnp.float32) + place_ref[0, enc, 0:1, :]
            h = norm_rows(x, vector_row(vec_ref, enc, 0), vector_row(vec_ref, enc, 1))
            query = low16(dot(low16(h), w_q) + vector_row(vec_ref, enc, 2))
            query_ref[spot, low:high, :] = query.reshape(block, high - low, 128)
            if enc == 0:
                for half in range(block // 8):
                    query_q[step * (block // 8) + half] = query[half * 8 * count_q : (half + 1) * 8 * count_q]
            return carry

        lax.fori_loop(0, sizes.many // block, ask, 0)
    states = ((total_q, top_q, mass_q), (total_p, top_p, mass_p))
    lse_ref[...] = jnp.full_like(lse_ref, NEG)

    def close(enc, step, total, top, mass):
        some = mass > 0.0
        safe = jnp.where(some, mass, 1.0)
        mixed = merge_heads(total / safe)
        lse = jnp.where(some, top + jnp.log(safe), NEG)
        if enc == 1:
            out_ref[step, count_q:, :] = low16(mixed)
            at = iota(lse.shape, 0) == iota(lse.shape, 1)
            lse_ref[step, 0:1, :] = jnp.sum(jnp.where(at, lse, 0.0), 0, keepdims=True)
        else:
            half = lse.shape[0] // 2
            row = iota((count_q, 128), 0)
            lane = iota((count_q, 128), 1)
            for i in range(8):
                spot = slice(i * count_q, (i + 1) * count_q)
                out_ref[step * 8 + i, 0:count_q, :] = low16(mixed[spot])
                line = jnp.where(lane == row, lse[spot], 0.0) + jnp.where(
                    lane == row + count_q, lse[half + i * count_q : half + (i + 1) * count_q], 0.0
                )
                lse_ref[step * 8 + i, 1:2, :] = jnp.sum(line, 0, keepdims=True)

    def attend(enc, steps, codes, scaleds, olds):
        queries = [query_q[s] if enc == 0 else query_ref[s, count_q:, :] for s in steps]
        made = [project(enc, scaled, vec_t, w_kv) for scaled in scaleds]
        scores = [dot(two_heads(query), part[1]) * HEAD ** (-0.5) for query, part in zip(queries, made)]
        news = []
        for u, score in enumerate(scores):
            mine = own_slots(codes[u], queries[u].shape[0])
            score = jnp.where(mine, score, NEG)
            new = jnp.max(score, 1, keepdims=True)
            if olds is not None:
                new = jnp.maximum(olds[u][1][:, 0:1], new)
            expo = jnp.where(mine, jnp.exp(score - new), 0.0)
            total = dot_last(low16(expo), made[u][2])
            mass = jnp.sum(expo, 1, keepdims=True)
            if olds is not None:
                fade = jnp.exp(olds[u][1] - new)
                total = olds[u][0] * fade + total
                mass = olds[u][2] * fade + mass
            wide = (score.shape[0], 128)
            news.append((total, jnp.broadcast_to(new, wide), jnp.broadcast_to(mass, wide)))
        for u, s in enumerate(steps):
            for ref, value in zip(states[enc], news[u]):
                ref[s] = value
        return news

    for enc in range(2):
        if sizes.keep:
            for copy in loads[2 * enc : 2 * enc + 2]:
                copy.wait()

            def kept_spans(turn, carry):
                steps = [turn * sizes.unroll[enc] + u for u in range(sizes.unroll[enc])]
                ats = [s if enc == 0 else sizes.steps[0] + s for s in steps]
                news = attend(
                    enc, steps, [entry_ref[at, 0:1, :] for at in ats], [kept_ref[at, 0:128, :] for at in ats], None
                )
                for s, new in zip(steps, news):
                    close(enc, s, *new)
                return carry

            lax.fori_loop(0, sizes.steps[enc] // sizes.unroll[enc], kept_spans, 0)
        else:
            total, top, mass = states[enc]
            total[...] = jnp.zeros_like(total)
            mass[...] = jnp.zeros_like(mass)
            top[...] = jnp.full_like(top, NEG)

    def needed(count):
        return jnp.maximum((jnp.max(count).astype(jnp.int32) + SPAN - 1) // SPAN, 1)

    start = needed(count)
    levels_ref[0] = start

    @pl.when(start > begin)
    def _():
        prepare_tokens(sizes, table_ref, place_ref, table_t, place_t)

        def one_level(state):
            level, unused, count = state
            for enc in range(2):

                def one_span(step, count):
                    code, found = pack_span(sizes, enc, step, level, first, raw_ref)
                    scaled = gather_span(sizes, enc, code, table_t, place_t, True)[0]
                    attend(enc, [step], [code], [scaled], [tuple(ref[step] for ref in states[enc])])
                    return jnp.maximum(count, found)

                count = lax.fori_loop(0, sizes.steps[enc], one_span, count)
            return level + 1, needed(count), count

        if sizes.keep:
            lax.fori_loop(
                begin, start, lambda level, carry: one_level((level, carry, count))[1], jnp.int32(0)
            )
        else:
            last = lax.while_loop(
                lambda state: state[0] < state[1], one_level, (jnp.int32(begin), start, count)
            )
            levels_ref[0] = last[1]
        for enc in range(2):

            def close_span(step, carry):
                close(enc, step, *(ref[step] for ref in states[enc]))
                return carry

            lax.fori_loop(0, sizes.steps[enc], close_span, 0)


def load_kept(sizes, kept_hbm, entry_hbm, kept_ref, entry_ref, load):
    if not sizes.keep:
        return []
    copies = []
    for enc, rows in enumerate((slice(0, sizes.steps[0]), slice(sizes.steps[0], sizes.spans))):
        for j, (source, target) in enumerate(((kept_hbm, kept_ref), (entry_hbm, entry_ref))):
            copy = pltpu.make_async_copy(source.at[rows], target.at[rows], load.at[enc, j])
            copy.start()
            copies.append(copy)
    return copies


def kept_scratch(sizes):
    kept = sizes.spans if sizes.keep else 1
    return [
        pltpu.VMEM((kept, 136, SPAN), jnp.float32),
        pltpu.VMEM((kept, 8, SPAN), jnp.int32),
        pltpu.SemaphoreType.DMA((2, 2)),
    ]


def token_scratch(sizes):
    return [
        pltpu.VMEM((128, sizes.padded), jnp.bfloat16),
        pltpu.VMEM((2, 2, 128, CHUNK), jnp.bfloat16),
        pltpu.VMEM((2, 256, 128), jnp.bfloat16),
        pltpu.VMEM((2, 128, 128), jnp.float32),
    ]


def local_call(kernel, out_shape, inputs, scratch, name, smem_in=(), smem_out=(), any_in=()):
    vm = pl.BlockSpec(memory_space=pltpu.VMEM)
    sm = pl.BlockSpec(memory_space=pltpu.SMEM)
    hbm = pl.BlockSpec(memory_space=pl.ANY)
    return pl.pallas_call(
        kernel,
        out_shape=out_shape,
        in_specs=[sm if i in smem_in else hbm if i in any_in else vm for i in range(len(inputs))],
        out_specs=[sm if i in smem_out else vm for i in range(len(out_shape))],
        scratch_shapes=scratch,
        compiler_params=pltpu.CompilerParams(vmem_limit_bytes=VMEM_LIMIT),
        name=name,
    )(*inputs)


def tokens_forward(sizes, every, rows, kept, entry, counted, table, positions, attention, vectors):
    many = sizes.many
    both = sum(sizes.count)
    state = []
    for enc in range(2):
        tall = 2 * sizes.queries[enc]
        state += [pltpu.VMEM((sizes.steps[enc], tall, 128), jnp.float32)] * 3
    return local_call(
        functools.partial(forward_kernel, sizes),
        (
            jax.ShapeDtypeStruct((many, both, 128), jnp.bfloat16),
            jax.ShapeDtypeStruct((many, 2, 128), jnp.float32),
            jax.ShapeDtypeStruct((many, both, 128), jnp.bfloat16),
            jax.ShapeDtypeStruct((1,), jnp.int32),
        ),
        (every, rows, kept, entry, counted, table, positions, attention, vectors),
        token_scratch(sizes)
        + [pltpu.VMEM((sizes.steps[0], sizes.queries[0], 128), jnp.bfloat16)]
        + state
        + kept_scratch(sizes),
        "tokens_forward",
        smem_out=(3,),
        any_in=(2, 3),
    )


def mix_kernel(
    many, count_q, part_ref, lse_ref, mixed_ref, total_ref, landed, landed_lse, own, own_lse, send, recv
):
    me = enter(many)
    pairs = [
        (lambda peer: part_ref.at[peer], landed),
        (lambda peer: lse_ref.at[peer], landed_lse),
    ]
    spread_start(many, me, pairs, send, recv, 0)
    landed[me] = part_ref[me]
    landed_lse[me] = lse_ref[me]
    spread_wait(many, me, pairs, send, recv, 0)
    parts = landed_lse[...]
    top = jnp.max(parts, 0)
    total = top + jnp.log(jnp.sum(jnp.exp(parts - top[None]), 0))
    own_lse[...] = total
    share = jnp.exp(parts - total[None])
    count_p = part_ref.shape[1] - count_q
    mixed = jnp.zeros((count_q + count_p, 128), jnp.float32)
    for peer in range(many):
        factors = []
        for row, number in ((1, count_q), (0, count_p)):
            wide = (2 * number, 128)
            at = iota(wide, 0) == iota(wide, 1)
            line = jnp.broadcast_to(share[peer][row : row + 1], wide)
            column = jnp.sum(jnp.where(at, line, 0.0), 1, keepdims=True)
            lane = iota((number, 128), 1)
            factors.append(jnp.where(lane < HEAD, column[0:number], column[number:]))
        mixed += jnp.concatenate(factors, 0) * landed[peer].astype(jnp.float32)
    own[...] = low16(mixed)
    pairs = [(lambda peer: own, mixed_ref), (lambda peer: own_lse, total_ref)]
    spread_start(many, me, pairs, send, recv, 2)
    mixed_ref[me] = own[...]
    total_ref[me] = own_lse[...]
    spread_wait(many, me, pairs, send, recv, 2)


def remote_call(kernel, out_shape, inputs, scratch, lanes, many, ident, name):
    return pl.pallas_call(
        kernel,
        out_shape=out_shape,
        in_specs=[pl.BlockSpec(memory_space=pltpu.VMEM)] * len(inputs),
        out_specs=[pl.BlockSpec(memory_space=pltpu.VMEM)] * len(out_shape),
        scratch_shapes=scratch
        + [pltpu.SemaphoreType.DMA((lanes, many)), pltpu.SemaphoreType.DMA((lanes, many))],
        compiler_params=pltpu.CompilerParams(
            collective_id=ident, has_side_effects=True, vmem_limit_bytes=VMEM_LIMIT
        ),
        name=name,
    )(*inputs)


def exchange_mixed(sizes, part, lse):
    many = sizes.many
    both = sum(sizes.count)
    return remote_call(
        functools.partial(mix_kernel, many, sizes.count[0]),
        (
            jax.ShapeDtypeStruct((many, both, 128), jnp.bfloat16),
            jax.ShapeDtypeStruct((many, 2, 128), jnp.float32),
        ),
        (part, lse),
        [
            pltpu.VMEM((many, both, 128), jnp.bfloat16),
            pltpu.VMEM((many, 2, 128), jnp.float32),
            pltpu.VMEM((both, 128), jnp.bfloat16),
            pltpu.VMEM((2, 128), jnp.float32),
        ],
        4,
        many,
        2,
        "exchange_mixed",
    )


def backward_kernel(
    sizes,
    levels_ref,
    raw_ref,
    query_ref,
    mixed_ref,
    lse_ref,
    grad_ref,
    kept_hbm,
    entry_hbm,
    table_ref,
    place_ref,
    attn_ref,
    vec_ref,
    d_query_ref,
    d_table_ref,
    slice_ref,
    table_t,
    place_t,
    w_kv,
    vec_t,
    d_place_ref,
    d_attn_ref,
    acc_gain,
    acc_shift,
    acc_value,
    d_query_q,
    d_query_p,
    kept_ref,
    entry_ref,
    load,
):
    loads = load_kept(sizes, kept_hbm, entry_hbm, kept_ref, entry_ref, load)
    first = lax.axis_index("dp") * sizes.depth
    count_q, count_p = sizes.count
    prepare_weights(attn_ref, vec_ref, w_kv, vec_t)
    begin = 1 if sizes.keep else 0
    again = levels_ref[0] > begin

    @pl.when(again)
    def _():
        prepare_tokens(sizes, table_ref, place_ref, table_t, place_t)

    for ref in (d_table_ref, d_place_ref, d_attn_ref, d_query_q, d_query_p, acc_gain, acc_shift, acc_value):
        ref[...] = jnp.zeros_like(ref)

    def ask_span(enc, step):
        if enc == 0:
            spot = pl.ds(step * 8, 8)
            shape = (8 * count_q, 128)
            found = [ref[spot, 0:count_q, :].reshape(shape) for ref in (query_ref, grad_ref, mixed_ref)]
            lines = [jnp.broadcast_to(lse_ref[step * 8 + i, 1:2, :], (count_q, 128)) for i in range(8)]
            lines = jnp.concatenate(lines, 0)
            row = iota(lines.shape, 0) % count_q
            lane = iota(lines.shape, 1)
            lse = [
                jnp.sum(jnp.where(lane == row + head * count_q, lines, 0.0), 1, keepdims=True)
                for head in range(2)
            ]
            lse = jnp.concatenate(lse, 0)
        else:
            found = [ref[step, count_q:, :] for ref in (query_ref, grad_ref, mixed_ref)]
            lines = jnp.broadcast_to(lse_ref[step, 0:1, :], (2 * count_p, 128))
            lse = jnp.sum(jnp.where(iota(lines.shape, 1) == iota(lines.shape, 0), lines, 0.0), 1, keepdims=True)
        return found + [lse]

    def work(enc, steps, codes, scaleds, rates, short=False):
        w_all = low16(attn_ref[0, enc, :, 128:384])
        asked = [ask_span(enc, step) for step in steps]
        made = [project(enc, scaled, vec_t, w_kv) for scaled in scaleds]
        d_queries, d_kvs = ([], [])
        for (query, grad, mixed, lse), code, (a_t, keys_t, values_t) in zip(asked, codes, made):
            both = two_heads(query)
            grads = two_heads(grad)
            base = jnp.sum(
                grads.astype(jnp.float32) * jnp.concatenate([mixed, mixed], 0).astype(jnp.float32),
                1,
                keepdims=True,
            )
            scores = dot(both, keys_t) * HEAD ** (-0.5)
            mine = own_slots(code, query.shape[0])
            probs = jnp.where(mine, jnp.exp(jnp.where(mine, scores, NEG) - lse), 0.0)
            d_probs = dot(grads, values_t)
            d_scores = low16(probs * (d_probs - base))
            d_values = low16(dot_rows(grads, low16(probs)))
            d_keys = low16(dot_rows(both, d_scores) * HEAD ** (-0.5))
            d_queries.append(merge_heads(dot_last(d_scores, keys_t)) * HEAD ** (-0.5))
            d_kvs.append(jnp.concatenate([d_keys, d_values], 0))
        for step, d_query in zip(steps, d_queries):
            if enc == 0:
                d_query_q[step] += d_query
            else:
                d_query_p[step] += d_query
        d_kv = jnp.concatenate(d_kvs, 1)
        a_t = jnp.concatenate([part[0] for part in made], 1)
        scaled = jnp.concatenate(scaleds, 1)
        rate = jnp.concatenate(rates, 1)
        code = jnp.concatenate(codes, 1)
        width = code.shape[1]
        d_attn_ref[enc] += dot_last(a_t, d_kv)
        d_h = dot(w_all, d_kv)
        fold = lambda values: sum(values[:, i * SPAN : (i + 1) * SPAN] for i in range(width // SPAN))
        acc_value[enc] += fold(d_kv[128:].astype(jnp.float32))
        acc_gain[enc] += fold(d_h * scaled)
        acc_shift[enc] += fold(d_h)
        d_scaled = d_h * vec_t[enc, :, 0:1]
        center = d_scaled - jnp.mean(d_scaled, 0, keepdims=True)
        slope = jnp.mean(d_scaled * scaled, 0, keepdims=True)
        d_x = low16((center - scaled * slope) * rate)
        rows = code >> 16
        where = (code >> 8) & 255
        chosen = hot(jnp.broadcast_to(where, (CHUNK, width)) == iota((CHUNK, width), 0))
        d_place_ref[enc] += dot_last(d_x, chosen)
        wide = jnp.broadcast_to(rows, (CHUNK, width))

        def add(cut, carry):
            spot = pl.ds(pl.multiple_of(cut * CHUNK, CHUNK), CHUNK)
            chosen = hot(wide == iota((CHUNK, width), 0) + cut * CHUNK)
            d_table_ref[spot, :] += dot_last(chosen, d_x)
            return carry

        lax.fori_loop(0, sizes.padded // CHUNK, add, 0, unroll=not short)

    for enc in range(2):
        if sizes.keep:
            for copy in loads[2 * enc : 2 * enc + 2]:
                copy.wait()

            def kept_spans(turn, carry):
                steps = [turn * sizes.unroll[enc] + u for u in range(sizes.unroll[enc])]
                ats = [s if enc == 0 else sizes.steps[0] + s for s in steps]
                work(
                    enc,
                    steps,
                    [entry_ref[at, 0:1, :] for at in ats],
                    [kept_ref[at, 0:128, :] for at in ats],
                    [kept_ref[at, 128:129, :] for at in ats],
                )
                return carry

            lax.fori_loop(0, sizes.steps[enc] // sizes.unroll[enc], kept_spans, 0)

        def more_level(level, carry_level):
            def one_span(step, carry):
                code = pack_span(sizes, enc, step, level, first, raw_ref)[0]
                scaled, rate = gather_span(sizes, enc, code, table_t, place_t, True)
                work(enc, [step], [code], [scaled], [rate], True)
                return carry

            return lax.fori_loop(0, sizes.steps[enc], one_span, carry_level)

        lax.fori_loop(begin, levels_ref[0], more_level, 0)

    for step in range(sizes.steps[0]):
        d_query_ref[step * 8 : step * 8 + 8, 0:count_q, :] = low16(d_query_q[step]).reshape(8, count_q, 128)
    d_query_ref[:, count_q:, :] = low16(d_query_p[...])
    for enc in range(2):
        for part, block in enumerate((d_place_ref, d_attn_ref)):
            for cut in range(2):
                slice_ref[enc, 2 * part + cut] = block[enc, :, cut * 128 : (cut + 1) * 128].astype(
                    slice_ref.dtype
                )
    slice_ref[0, 1] = jnp.zeros_like(slice_ref[0, 1])
    sums = []
    same = iota((128, 128), 0) == iota((128, 128), 1)
    for enc in range(2):
        for row, acc in enumerate((acc_gain, acc_shift, acc_value)):
            tall = jnp.broadcast_to(jnp.sum(acc[enc], 1, keepdims=True), (128, 128))
            sums.append(jnp.sum(jnp.where(same, tall, 0.0), 0, keepdims=True))
    sums = jnp.concatenate(sums + [jnp.zeros((10, 128), jnp.float32)], 0)
    slice_ref[0, 1, 0:16, :] = sums.astype(slice_ref.dtype)


def tokens_backward(sizes, levels, every, query, mixed, lse, grad, kept, entry, table, positions, attention, vectors):
    many = sizes.many
    count_p = sizes.count[1]
    both = sum(sizes.count)
    return local_call(
        functools.partial(backward_kernel, sizes),
        (
            jax.ShapeDtypeStruct((many, both, 128), jnp.bfloat16),
            jax.ShapeDtypeStruct((sizes.padded, 128), jnp.float32),
            jax.ShapeDtypeStruct((2, 4, 128, 128), sizes.kind),
        ),
        (levels, every, query, mixed, lse, grad, kept, entry, table, positions, attention, vectors),
        token_scratch(sizes)
        + [
            pltpu.VMEM((2, 128, CHUNK), jnp.float32),
            pltpu.VMEM((2, 128, 256), jnp.float32),
            pltpu.VMEM((2, 128, SPAN), jnp.float32),
            pltpu.VMEM((2, 128, SPAN), jnp.float32),
            pltpu.VMEM((2, 128, SPAN), jnp.float32),
            pltpu.VMEM((sizes.steps[0], sizes.queries[0], 128), jnp.float32),
            pltpu.VMEM((many, count_p, 128), jnp.float32),
        ]
        + kept_scratch(sizes),
        "tokens_backward",
        smem_in=(0,),
        any_in=(6, 7),
    )


def adam(weight, grad, first, second):
    first_new = BETA_ONE * first + (1.0 - BETA_ONE) * grad
    second_new = BETA_TWO * second + (1.0 - BETA_TWO) * grad * grad
    fix_one = 1.0 - BETA_ONE**STEP
    fix_two = 1.0 - BETA_TWO**STEP
    ratio = first_new / fix_one / (jnp.sqrt(second_new / fix_two) + ADAM_EPS)
    return (first_new, second_new, weight - INNER_RATE * (ratio + WEIGHT_DECAY * weight))


def pieces_of(depth):
    blocks = [(1, (enc,)) for enc in range(2)] + [(2, (enc,)) for enc in range(2)]
    blocks += [(3, (enc, side)) for enc in range(2) for side in range(2)]
    return blocks + [(4, ())]


def square_sum(values):
    return jnp.sum(jnp.sum(values * values, 0, keepdims=True), 1, keepdims=True)


def finish_kernel(sizes, *refs):
    many = sizes.many
    count_q, count_p = sizes.count
    depth = sizes.depth
    (query_ref, slice_ref, d_table_ref, rows_ref, raw_ref, xa_q, xa_p, d_out, d_ffn, d_mid) = refs[:10]
    place_ref, attn_ref, vec_ref = refs[10:13]
    state = refs[13:33]
    norm_ref, g_word, g_place, g_attn, g_vec = refs[33:38]
    joined = refs[38:43]
    held = refs[43:63]
    mine = refs[63:68]
    theirs = refs[68:73]
    (query_all, slice_all, scalar_all, land_query, land_slice, own_query, own_slice, tile, table_t) = refs[73:82]
    send, recv, load, pair_send, pair_recv = refs[82:87]
    loads = []
    for index in range(20):
        copy = pltpu.make_async_copy(state[index], held[index], load.at[index])
        copy.start()
        loads.append(copy)
    me = lax.axis_index("dp")
    other = 1 - lax.axis_index("grp")
    barrier = pltpu.get_barrier_semaphore()

    def greet(step, carry):
        peer = lax.rem(me + step, many)
        pl.semaphore_signal(barrier, inc=1, device_id={"dp": peer}, device_id_type=MESH)
        return carry

    lax.fori_loop(1, many, greet, 0)
    pl.semaphore_signal(barrier, inc=1, device_id={"grp": other}, device_id_type=MESH)
    pl.semaphore_wait(barrier, many)
    query_pairs = [(lambda peer: query_ref.at[peer], land_query)]
    slice_pairs = [(lambda peer: slice_ref.at[peer], land_slice)]
    spread_start(many, me, query_pairs, send, recv, 0)
    spread_start(many, me, slice_pairs, send, recv, 1)
    land_query[me] = query_ref[me]
    land_slice[me] = slice_ref[me]
    spread_wait(many, me, query_pairs, send, recv, 0)
    own_query[...] = low16(jnp.sum(land_query[...].astype(jnp.float32), 0))
    query_back = [(lambda peer: own_query, query_all)]
    spread_start(many, me, query_back, send, recv, 3)
    query_all[me] = own_query[...]
    spread_wait(many, me, slice_pairs, send, recv, 1)
    own_slice[...] = jnp.sum(land_slice[...].astype(jnp.float32), 0).astype(own_slice.dtype)
    slice_back = [(lambda peer: own_slice, slice_all)]
    spread_start(many, me, slice_back, send, recv, 4)
    slice_all[me] = own_slice[...]
    spread_wait(many, me, query_back, send, recv, 3)

    g_vec[...] = d_mid[...]
    tops = []
    first = me * depth
    table_t[...] = jnp.zeros_like(table_t)
    rest = jnp.zeros((1, 1), jnp.float32)
    places = []
    for enc in range(2):
        low, high = (0, count_q) if enc == 0 else (count_q, count_q + count_p)
        number = many * (high - low)
        d_query = query_all[:, low:high, :].reshape(number, 128)
        x = rows_ref[:, low:high, :].reshape(number, 128).astype(jnp.float32) + place_ref[0, enc, 0:1, :]
        center = x - jnp.mean(x, -1, keepdims=True)
        rate = lax.rsqrt(jnp.mean(center * center, -1, keepdims=True) + NORM_EPS)
        scaled = center * rate
        gain = vector_row(vec_ref, enc, 0)
        a_low = low16(scaled * gain + vector_row(vec_ref, enc, 1))
        xa = xa_q if enc == 0 else xa_p
        d_h = xa[...] + dot_last(d_query, low16(attn_ref[0, enc, :, 0:128]))
        d_scaled = d_h * gain
        slope = jnp.mean(d_scaled * scaled, -1, keepdims=True)
        d_x = (d_scaled - jnp.mean(d_scaled, -1, keepdims=True) - scaled * slope) * rate
        d_place = jnp.sum(d_x, 0, keepdims=True)
        places.append(d_place)
        g_attn[enc, :, 0:128] = dot_rows(a_low, d_query)
        g_attn[enc, :, 384:512] = d_out[enc]
        spot = slice(enc, enc + 1)
        g_vec[2, spot, :] = jnp.sum(d_query.astype(jnp.float32), 0, keepdims=True)
        tops.append((jnp.sum(d_h * scaled, 0, keepdims=True), jnp.sum(d_h, 0, keepdims=True)))
        if enc == 0:
            columns = [
                part
                for peer in range(many)
                for part in (
                    raw_ref[peer, RAW_Q : RAW_Q + 16, 0:1].astype(jnp.int32)[0 : count_q // 2],
                    raw_ref[peer, RAW_Q : RAW_Q + 16, 64:65].astype(jnp.int32)[0 : count_q // 2],
                )
            ]
        else:
            columns = [raw_ref[peer, 0:count_p, 0:1].astype(jnp.int32) for peer in range(many)]
        spot = jnp.concatenate(columns, 0) - first
        spot = jnp.where(spot < depth, spot, -1)
        d_low = low16(d_x)
        wide = jnp.broadcast_to(spot, (number, CHUNK))
        for cut in range(sizes.padded // CHUNK):
            chosen = hot(wide == iota((number, CHUNK), 1) + cut * CHUNK)
            table_t[:, cut * CHUNK : (cut + 1) * CHUNK] += dot_rows(d_low, chosen)
        rest += square_sum(d_ffn[enc, 0]) + square_sum(d_ffn[enc, 1])
    for cut in range(0, depth, 128):
        top = min(cut + 128, depth)
        g_word[cut:top, :] = d_table_ref[cut:top, :] + jnp.transpose(table_t[:, cut : cut + 128])[0 : top - cut]
    tile[...] = jnp.broadcast_to(square_sum(g_word[...]), (8, 128))
    pairs = [(lambda peer: tile, scalar_all)]
    spread_start(many, me, pairs, send, recv, 5)
    scalar_all[me] = tile[...]
    spread_wait(many, me, slice_back, send, recv, 4)
    blocks = slice_all[...].astype(jnp.float32).reshape(8, 128, 128)
    for enc in range(2):
        spot = slice(enc, enc + 1)
        g_vec[0, spot, :] = blocks[1][enc * 3 : enc * 3 + 1] + tops[enc][0]
        g_vec[1, spot, :] = blocks[1][enc * 3 + 1 : enc * 3 + 2] + tops[enc][1]
        g_vec[3, spot, :] = blocks[1][enc * 3 + 2 : enc * 3 + 3]
        g_place[enc, 0:128, :] = jnp.transpose(blocks[enc * 4])
        if enc == 0:
            g_place[enc, 128:256, :] = jnp.zeros((128, 128), jnp.float32)
        else:
            g_place[enc, 128:256, :] = jnp.transpose(blocks[enc * 4 + 1])
        g_place[enc, 0:1, :] += places[enc]
        g_attn[enc, :, 128:256] = blocks[enc * 4 + 2]
        g_attn[enc, :, 256:384] = blocks[enc * 4 + 3]
        rest += square_sum(g_place[enc]) + square_sum(g_attn[enc])
    small = jnp.sum(g_vec[...] * g_vec[...], 0)
    rest += jnp.sum(jnp.sum(small, 0, keepdims=True), 1, keepdims=True)
    for copy in loads:
        copy.wait()
    spread_wait(many, me, pairs, send, recv, 5)
    norm = jnp.sqrt(jnp.sum(scalar_all[...], 0)[0:1, 0:1] + rest)
    norm_ref[...] = jnp.broadcast_to(norm, (8, 128))
    factor = CLIP_LIMIT / jnp.maximum(norm, CLIP_LIMIT)
    grads = (g_word, g_place, g_attn, d_ffn, g_vec)

    def differ(kind, at, rows):
        weight, moment, square, anchor = (held[kind * 4 + j] for j in range(4))
        grad = grads[kind][at + (rows,)] * factor
        inner = adam(weight[(0,) + at + (rows,)], grad, moment[(0,) + at + (rows,)], square[(0,) + at + (rows,)])[2]
        mine[kind][at + (rows,)] = (anchor[at + (rows,)] - inner).astype(mine[kind].dtype)

    size = math.gcd(depth, 128)

    def table_block(step, carry):
        differ(0, (), pl.ds(pl.multiple_of(step * size, size), size))
        return carry

    lax.fori_loop(0, depth // size, table_block, 0)
    ways = []

    def hand(kind):
        copy = pltpu.make_async_remote_copy(
            src_ref=mine[kind],
            dst_ref=theirs[kind],
            send_sem=pair_send.at[kind],
            recv_sem=pair_recv.at[kind],
            device_id={"grp": other},
            device_id_type=MESH,
        )
        copy.start()
        ways.append(copy)

    hand(0)
    for kind in range(1, 5):
        for found, at in pieces_of(depth):
            if found == kind:
                differ(kind, at, slice(0, 14) if kind == 4 else slice(None))
        hand(kind)
    def join(kind, spot):
        joined[kind][spot] = mine[kind][spot].astype(jnp.float32) + theirs[kind][spot].astype(jnp.float32)

    def table_add(step, carry):
        join(0, pl.ds(pl.multiple_of(step * size, size), size))
        return carry

    ways[0].wait()
    lax.fori_loop(0, depth // size, table_add, 0)
    for kind in range(1, 5):
        ways[kind].wait()
        for found, at in pieces_of(depth):
            if found == kind:
                join(kind, at if at else slice(None))


def finish(sizes, query, slices, d_table, rows, every, xa_q, xa_p, d_out, d_ffn, d_mid, params, state):
    many = sizes.many
    both = sum(sizes.count)
    inputs = (query, slices, d_table, rows, every, xa_q, xa_p, d_out, d_ffn, d_mid) + params
    flat = tuple(state[j][kind] for kind in range(5) for j in range(4))
    shapes = [state[3][kind].shape for kind in range(5)]
    vm = pl.BlockSpec(memory_space=pltpu.VMEM)
    hbm = pl.BlockSpec(memory_space=pl.ANY)
    f32 = jnp.float32
    return pl.pallas_call(
        functools.partial(finish_kernel, sizes),
        out_shape=tuple(
            jax.ShapeDtypeStruct(shape, f32)
            for shape in [(8, 128), shapes[0], shapes[1], shapes[2], (16, 2, 128)] + shapes
        ),
        in_specs=[vm] * len(inputs) + [hbm] * 20,
        out_specs=[vm] * 10,
        scratch_shapes=[pltpu.VMEM(value.shape, f32) for value in flat]
        + [pltpu.VMEM(shape, jnp.bfloat16 if kind < 4 else f32) for kind, shape in enumerate(shapes)] * 2
        + [
            pltpu.VMEM((many, both, 128), jnp.bfloat16),
            pltpu.VMEM((many, sizes.lines, 128), sizes.kind),
            pltpu.VMEM((many, 8, 128), f32),
            pltpu.VMEM((many, both, 128), jnp.bfloat16),
            pltpu.VMEM((many, sizes.lines, 128), sizes.kind),
            pltpu.VMEM((both, 128), jnp.bfloat16),
            pltpu.VMEM((sizes.lines, 128), sizes.kind),
            pltpu.VMEM((8, 128), f32),
            pltpu.VMEM((128, sizes.padded), f32),
            pltpu.SemaphoreType.DMA((6, many)),
            pltpu.SemaphoreType.DMA((6, many)),
            pltpu.SemaphoreType.DMA((20,)),
            pltpu.SemaphoreType.DMA((5,)),
            pltpu.SemaphoreType.DMA((5,)),
        ],
        compiler_params=pltpu.CompilerParams(
            collective_id=3, has_side_effects=True, vmem_limit_bytes=VMEM_LIMIT
        ),
        name="finish",
    )(*inputs, *flat)


def output_parts(depth):
    rows = depth // 3 if depth % 24 == 0 else depth
    parts = [(0, slice(at, at + rows)) for at in range(0, depth, rows)]
    return parts + [(kind, None) for kind in (3, 2, 1, 4)]


def outputs_kernel(depth, groups, *refs):
    norm_ref, g_vec = refs[:2]
    ins = refs[2:31]
    outs = refs[31:56]
    total_ref = refs[56]
    held = refs[57:86]
    made = refs[86:111]
    load, store = refs[111:113]
    parts = output_parts(depth)
    loads, stores = ([], [])
    for number, (kind, rows) in enumerate(parts):
        group = []
        for j in range(6 if kind < 4 else 5):
            index = kind * 5 + j if j < 5 else 25 + kind
            source, target = (ins[index], held[index])
            if rows is not None:
                lead = (0,) if len(source.shape) == 3 else ()
                source, target = (source.at[lead + (rows,)], target.at[lead + (rows,)])
            copy = pltpu.make_async_copy(source, target, load.at[number, j])
            copy.start()
            group.append(copy)
        loads.append(group)
    total_ref[0] = jnp.max(norm_ref[...])
    norm = norm_ref[0:1, 0:1]
    factor = CLIP_LIMIT / jnp.maximum(norm, CLIP_LIMIT)
    grads = tuple(held[25:29]) + (g_vec,)

    def work(kind, at, rows):
        moment, square, anchor, outer, summed = (held[kind * 5 + j] for j in range(5))
        first, second, average, momentum, weight = (made[kind * 5 + j] for j in range(5))
        spot = at + (rows,)
        deep = (0,) + spot
        grad = grads[kind][spot] * factor
        first[deep] = BETA_ONE * moment[deep] + (1.0 - BETA_ONE) * grad
        second[deep] = BETA_TWO * square[deep] + (1.0 - BETA_TWO) * grad * grad
        mean = summed[spot] / groups
        speed = OUTER_MU * outer[spot] + mean
        average[spot] = mean
        momentum[spot] = speed
        weight[deep] = anchor[spot] - OUTER_RATE * (mean + OUTER_MU * speed)

    for number, (kind, rows) in enumerate(parts):
        for copy in loads[number]:
            copy.wait()
        if kind == 0:
            size = math.gcd(rows.stop - rows.start, 128)

            def table_block(step, carry):
                work(0, (), pl.ds(pl.multiple_of(rows.start + step * size, size), size))
                return carry

            lax.fori_loop(0, (rows.stop - rows.start) // size, table_block, 0)
        else:
            for found, at in pieces_of(depth):
                if found == kind:
                    work(kind, at, slice(0, 14) if kind == 4 else slice(None))
        for j in range(5):
            source, target = (made[kind * 5 + j], outs[kind * 5 + j])
            if rows is not None:
                lead = (0,) if len(source.shape) == 3 else ()
                source, target = (source.at[lead + (rows,)], target.at[lead + (rows,)])
            copy = pltpu.make_async_copy(source, target, store.at[number, j])
            copy.start()
            stores.append(copy)
    for copy in stores:
        copy.wait()


def make_outputs(norm, grads, firsts, seconds, anchors, outers, summed, groups):
    kinds = range(5)
    flat = tuple(v for kind in kinds for v in (firsts[kind], seconds[kind], anchors[kind], outers[kind], summed[kind]))
    flat += tuple(grads[:4])
    out = tuple(
        jax.ShapeDtypeStruct(shape, jnp.float32)
        for kind in kinds
        for shape in (firsts[kind].shape, firsts[kind].shape, anchors[kind].shape, anchors[kind].shape, firsts[kind].shape)
    )
    vm = pl.BlockSpec(memory_space=pltpu.VMEM)
    hbm = pl.BlockSpec(memory_space=pl.ANY)
    got = pl.pallas_call(
        functools.partial(outputs_kernel, anchors[0].shape[0], groups),
        out_shape=out + (jax.ShapeDtypeStruct((1,), jnp.float32),),
        in_specs=[vm] * 2 + [hbm] * 29,
        out_specs=[hbm] * 25 + [pl.BlockSpec(memory_space=pltpu.SMEM)],
        scratch_shapes=[pltpu.VMEM(v.shape, jnp.float32) for v in flat]
        + [pltpu.VMEM(v.shape, jnp.float32) for v in out]
        + [pltpu.SemaphoreType.DMA((7, 6)), pltpu.SemaphoreType.DMA((7, 5))],
        compiler_params=pltpu.CompilerParams(vmem_limit_bytes=VMEM_LIMIT),
        name="make_outputs",
    )(norm, grads[4], *flat)
    return [[got[kind * 5 + j] for kind in kinds] for j in range(5)], got[25]


def square_norm(values):
    center = values - jnp.mean(values, -1, keepdims=True)
    rate = lax.rsqrt(jnp.mean(center * center, -1, keepdims=True) + NORM_EPS)
    return center * rate, rate


def norm_back(d_scaled, scaled, rate):
    slope = jnp.mean(d_scaled * scaled, -1, keepdims=True)
    return (d_scaled - jnp.mean(d_scaled, -1, keepdims=True) - scaled * slope) * rate


def total_of(values):
    return jnp.sum(jnp.sum(values, 0, keepdims=True), 1, keepdims=True)


def score_terms(scores, drop, target, weight, count, axis):
    masked = jnp.where(drop, MASKED, scores)
    top = jnp.max(masked, axis, keepdims=True)
    expo = jnp.exp(masked - top)
    total = jnp.sum(expo, axis, keepdims=True)
    picked = jnp.sum(jnp.where(target, scores, 0.0), axis, keepdims=True)
    loss = total_of(weight * (top + jnp.log(total) - picked))
    grad = low16((weight / count) * (expo / total - jnp.where(target, 1.0, 0.0)))
    return grad, loss


GELU_A = math.sqrt(2.0 / math.pi)
GELU_B = 0.044715


def class_kernel(
    sizes,
    rows_ref,
    mixed_ref,
    raw_ref,
    place_ref,
    attn_ref,
    ffn_ref,
    vec_ref,
    grad_ref,
    xa_q,
    xa_p,
    d_out,
    d_ffn,
    d_mid,
    loss_ref,
    count_ref,
    cls_ref,
    scaled_a,
    rate_a,
    scaled_f,
    rate_f,
    pre_ref,
    act_ref,
    low_ref,
    flag_ref,
):
    many = sizes.many
    counts = sizes.count
    totals = (many * counts[0], many * counts[1])
    chunk = totals[0]
    parts = [(0, 0, 0)] + [(1, at, totals[0] + at) for at in range(0, totals[1], chunk)]

    def held(ref, enc, at):
        each = counts[enc]
        low = 0 if enc == 0 else counts[0]
        return ref[at // each : (at + chunk) // each, low : low + each, :].reshape(chunk, 128)

    def weights(enc):
        return (
            low16(attn_ref[0, enc, :, 384:512]),
            low16(ffn_ref[0, enc, 0]),
            low16(ffn_ref[0, enc, 1]),
        )

    for enc, at, spot in parts:
        w_out, w_up, w_down = weights(enc)
        row = functools.partial(vector_row, vec_ref, enc)
        here = slice(spot, spot + chunk)
        x = held(rows_ref, enc, at).astype(jnp.float32) + place_ref[0, enc, 0:1, :]
        h_embed = norm_rows(x, row(0), row(1))
        scaled, rate = square_norm(h_embed + (dot(held(mixed_ref, enc, at), w_out) + row(4)))
        scaled_a[here, :] = scaled
        rate_a[here, :] = jnp.broadcast_to(rate, (chunk, 128))
        h_attn = scaled * row(5) + row(6)
        h_low = low16(h_attn)
        low_ref[here, :] = h_low
        pre = dot(h_low, w_up) + jnp.concatenate([row(10), row(11), row(12), row(13)], 1)
        pre_ref[here, :] = pre
        act = low16(0.5 * pre * (1.0 + jnp.tanh(GELU_A * (pre + GELU_B * (pre * pre * pre)))))
        act_ref[here, :] = act
        scaled, rate = square_norm(h_attn + (dot_last(act, w_down) + row(7)))
        scaled_f[here, :] = scaled
        rate_f[here, :] = jnp.broadcast_to(rate, (chunk, 128))
        cls_ref[here, :] = low16(scaled * row(8) + row(9))

    every_q = cls_ref[0 : totals[0], :]
    every_p = cls_ref[totals[0] :, :]
    flag_ref[...] = jnp.zeros_like(flag_ref)
    for peer in range(many):
        flag_ref[peer : peer + 1, :] = raw_ref[peer, RAW_Q:RAW_ROWS, :].astype(jnp.float32)[8:9]
    turned = jnp.transpose(flag_ref[...])

    def column(low, each):
        tall = jnp.concatenate([turned[low : low + each]] * many, 0)
        at = iota(tall.shape, 1) == iota(tall.shape, 0) // each
        return jnp.sum(jnp.where(at, tall, 0.0), 1, keepdims=True)

    keys_q = column(0, counts[0])
    valid = column(counts[0], counts[0])
    keys_p = column(2 * counts[0], counts[1])
    hot_q = hot(jnp.broadcast_to(keys_q, (totals[0], 128)) == iota((totals[0], 128), 1).astype(jnp.float32))
    hot_p = hot(jnp.broadcast_to(keys_p, (totals[1], 128)) == iota((totals[1], 128), 1).astype(jnp.float32))
    same = dot_last(hot_q, hot_p) > 0.5
    count = jnp.maximum(total_of(valid), 1.0)
    scale = 128 ** (-0.5)
    scores = dot_last(every_q, every_p) * scale
    index_q = iota(scores.shape, 0)
    index_p = iota(scores.shape, 1)
    target_qp = index_p == 2 * index_q
    target_pq = index_p // 2 == index_q
    grad_qp, loss_qp = score_terms(scores, same & ~target_qp, target_qp, valid, count, 1)
    drop_pq = (same | (jnp.broadcast_to(valid, scores.shape) == 0.0)) & ~target_pq
    weight_p = jnp.sum(jnp.where(target_qp, jnp.broadcast_to(valid, scores.shape), 0.0), 0, keepdims=True)
    grad_pq, loss_pq = score_terms(scores, drop_pq, target_pq, weight_p, count, 0)
    loss_ref[0] = jnp.max(loss_qp + loss_pq)
    count_ref[0] = jnp.max(count)
    d_q = (dot(grad_qp, every_p) + dot(grad_pq, every_p)) * scale
    d_p = (dot_rows(grad_pq, every_q) + dot_rows(grad_qp, every_q)) * scale

    d_mid[...] = jnp.zeros_like(d_mid)
    d_out[...] = jnp.zeros_like(d_out)
    d_ffn[...] = jnp.zeros_like(d_ffn)
    for enc, at, spot in parts:
        w_out, w_up, w_down = weights(enc)
        row = functools.partial(vector_row, vec_ref, enc)
        here = slice(spot, spot + chunk)

        def add(index, values):
            d_mid[index, enc : enc + 1, :] += jnp.sum(values, 0, keepdims=True)

        d_cls = d_q if enc == 0 else d_p[at : at + chunk]
        scaled = scaled_f[here, :]
        add(8, d_cls * scaled)
        add(9, d_cls)
        d_x_ffn = norm_back(d_cls * row(8), scaled, rate_f[here, :])
        d_branch = low16(d_x_ffn)
        add(7, d_branch.astype(jnp.float32))
        d_ffn[enc, 1] += dot_rows(d_branch, act_ref[here, :])
        d_act = dot(d_branch, w_down)
        pre = pre_ref[here, :]
        square = pre * pre
        bend = jnp.tanh(GELU_A * (pre + GELU_B * (square * pre)))
        slope = 0.5 * (1.0 + bend) + (0.5 * GELU_A) * pre * (1.0 - bend * bend) * (
            1.0 + (3.0 * GELU_B) * square
        )
        d_pre = low16(slope * d_act)
        up_bias = jnp.sum(d_pre.astype(jnp.float32), 0, keepdims=True)
        for cut in range(4):
            d_mid[10 + cut, enc : enc + 1, :] += up_bias[:, cut * 128 : (cut + 1) * 128]
        d_ffn[enc, 0] += dot_rows(low_ref[here, :], d_pre)
        d_h = d_x_ffn + dot_last(d_pre, w_up)
        scaled = scaled_a[here, :]
        add(5, d_h * scaled)
        add(6, d_h)
        d_x = norm_back(d_h * row(5), scaled, rate_a[here, :])
        if enc == 0:
            xa_q[...] = d_x
        else:
            xa_p[at : at + chunk, :] = d_x
        d_proj = low16(d_x)
        add(4, d_proj.astype(jnp.float32))
        d_out[enc] += dot_rows(held(mixed_ref, enc, at), d_proj)
        d_mixed = low16(dot_last(d_proj, w_out))
        each = counts[enc]
        low = 0 if enc == 0 else counts[0]
        grad_ref[at // each : (at + chunk) // each, low : low + each, :] = d_mixed.reshape(
            chunk // each, each, 128
        )


def class_stage(sizes, rows, mixed, every, positions, attention, feedforward, vectors):
    many = sizes.many
    n_q, n_p = (many * sizes.count[0], many * sizes.count[1])
    both = n_q + n_p
    f32 = jnp.float32
    return local_call(
        functools.partial(class_kernel, sizes),
        (
            jax.ShapeDtypeStruct((many, sum(sizes.count), 128), jnp.bfloat16),
            jax.ShapeDtypeStruct((n_q, 128), f32),
            jax.ShapeDtypeStruct((n_p, 128), f32),
            jax.ShapeDtypeStruct((2, 128, 128), f32),
            jax.ShapeDtypeStruct((2, 2, 128, 512), f32),
            jax.ShapeDtypeStruct((16, 2, 128), f32),
            jax.ShapeDtypeStruct((1,), f32),
            jax.ShapeDtypeStruct((1,), f32),
        ),
        (rows, mixed, every, positions, attention, feedforward, vectors),
        [
            pltpu.VMEM((both, 128), jnp.bfloat16),
            pltpu.VMEM((both, 128), f32),
            pltpu.VMEM((both, 128), f32),
            pltpu.VMEM((both, 128), f32),
            pltpu.VMEM((both, 128), f32),
            pltpu.VMEM((both, 512), f32),
            pltpu.VMEM((both, 512), jnp.bfloat16),
            pltpu.VMEM((both, 128), jnp.bfloat16),
            pltpu.VMEM((128, 128), f32),
        ],
        "class_stage",
        smem_out=(6, 7),
    )


def class_stage_large(sizes, rows_all, mixed_all, every, positions, attention, feedforward, vectors):
    many = sizes.many
    count_q, count_p = sizes.count
    counts = sizes.count
    width = rows_all.shape[2]
    flags_all = every[:, RAW_FLAGS, :].astype(jnp.int32)
    keys_q = flags_all[:, :count_q].reshape(-1)
    valid_all = flags_all[:, count_q : 2 * count_q].reshape(-1)
    keys_p = flags_all[:, 2 * count_q : 2 * count_q + count_p].reshape(-1)
    cuts = ((0, count_q), (count_q, count_q + count_p))
    cls, class_kept, mixes = ([], [], [])
    for enc in range(2):
        low, high = cuts[enc]
        rows = rows_all[:, low:high].reshape(-1, width)
        mixed = mixed_all[:, low:high].reshape(-1, width)
        low_cls, kept_cls = class_forward(
            rows, mixed, positions[0, enc], attention[0, enc], feedforward[0, enc], vectors[0, :, enc]
        )
        cls.append(low_cls)
        class_kept.append(kept_cls)
        mixes.append(mixed)
    d_q, d_p, loss_total, count = score_stage(cls[0], cls[1], keys_q, keys_p, valid_all)
    d_cls = (d_q, d_p)
    grads, xas, outs, ffns, mids = ([], [], [], [], [])
    for enc in range(2):
        d_mixed, d_x_attn, d_w_out, d_ffn, rows_mid, d_up_bias = class_backward(
            class_kept[enc], mixes[enc], attention[0, enc], feedforward[0, enc], vectors[0, :, enc], d_cls[enc]
        )
        grads.append(d_mixed.reshape(many, counts[enc], width))
        xas.append(d_x_attn)
        outs.append(d_w_out)
        ffns.append(d_ffn)
        mid = jnp.concatenate([jnp.stack(list(rows_mid)), d_up_bias.reshape(-1, width)])
        mids.append(jnp.pad(mid, ((4, 2), (0, 0))))
    return (
        jnp.concatenate(grads, 1),
        xas[0],
        xas[1],
        jnp.stack(outs),
        jnp.stack(ffns),
        jnp.stack(mids, 1),
        loss_total.reshape(1),
        count.reshape(1),
    )


def class_forward(rows, mixed, place, attn_w, ffn_w, vec):
    width = rows.shape[1]
    h_embed = layer_norm(rows.astype(jnp.float32) + place[:1], vec[0], vec[1])
    x_attn = h_embed + (dot(mixed, low16(attn_w[:, 3 * width :])) + vec[4])
    h_attn = layer_norm(x_attn, vec[5], vec[6])
    h_low = low16(h_attn)
    pre = dot(h_low, low16(ffn_w[0])) + vec[10:].reshape(-1)
    act = low16(gelu_tanh(pre))
    x_ffn = h_attn + (dot_last(act, low16(ffn_w[1])) + vec[7])
    h_out = layer_norm(x_ffn, vec[8], vec[9])
    return low16(h_out), (x_attn, h_low, pre, act, x_ffn)


def class_backward(kept, mixed, attn_w, ffn_w, vec, d_cls):
    x_attn, h_low, pre, act, x_ffn = kept
    width = x_attn.shape[1]
    unused, out_back = jax.vjp(layer_norm, x_ffn, vec[8], vec[9])
    d_x_ffn, d_gain_two, d_shift_two = out_back(d_cls)
    d_branch = low16(d_x_ffn)
    d_down_bias = jnp.sum(d_branch, 0, dtype=jnp.float32)
    d_down = dot_rows(d_branch, act)
    d_act = dot(d_branch, low16(ffn_w[1]))
    unused, gelu_back = jax.vjp(gelu_tanh, pre)
    d_pre = low16(gelu_back(d_act)[0])
    d_up_bias = jnp.sum(d_pre, 0, dtype=jnp.float32)
    d_up = dot_rows(h_low, d_pre)
    d_h_attn = d_x_ffn + dot_last(d_pre, low16(ffn_w[0]))
    unused, attn_back = jax.vjp(layer_norm, x_attn, vec[5], vec[6])
    d_x_attn, d_gain_one, d_shift_one = attn_back(d_h_attn)
    d_proj = low16(d_x_attn)
    d_out_bias = jnp.sum(d_proj, 0, dtype=jnp.float32)
    d_w_out = dot_rows(mixed, d_proj)
    d_mixed = low16(dot_last(d_proj, low16(attn_w[:, 3 * width :])))
    rows = (d_out_bias, d_gain_one, d_shift_one, d_down_bias, d_gain_two, d_shift_two)
    return d_mixed, d_x_attn, d_w_out, jnp.stack([d_up, d_down]), rows, d_up_bias


def softmax_terms(scores, drop, target, weight, count, axis):
    masked = jnp.where(drop, MASKED, scores)
    top = jnp.max(masked, axis, keepdims=True)
    expo = jnp.exp(masked - top)
    total = jnp.sum(expo, axis, keepdims=True)
    lse = top + jnp.log(total)
    picked = jnp.sum(jnp.where(target, scores, 0.0), axis, keepdims=True)
    loss = jnp.sum(weight * (lse - picked))
    grad = low16((weight / count) * (expo / total - target.astype(jnp.float32)))
    return grad, loss


def score_stage(every_q, every_p, keys_q, keys_p, valid_q):
    count = jnp.maximum(jnp.sum(valid_q).astype(jnp.float32), 1.0)
    scale = every_q.shape[1] ** (-0.5)
    index_q = jnp.arange(every_q.shape[0])[:, None]
    index_p = jnp.arange(every_p.shape[0])[None, :]
    scores = dot_last(every_q, every_p) * scale
    same = keys_q[:, None] == keys_p[None, :]
    target_qp = index_p == 2 * index_q
    valid = valid_q.astype(jnp.float32)[:, None]
    grad_qp, loss_qp = softmax_terms(scores, same & ~target_qp, target_qp, valid, count, 1)
    target_pq = index_p // 2 == index_q
    drop_pq = (same | (valid_q[:, None] == 0)) & ~target_pq
    owner_valid = jnp.repeat(valid_q, 2)
    weight_p = jnp.where(index_p[0] % 2 == 0, owner_valid, 0).astype(jnp.float32)[None, :]
    grad_pq, loss_pq = softmax_terms(scores, drop_pq, target_pq, weight_p, count, 0)
    d_q = (dot(grad_qp, every_p) + dot(grad_pq, every_p)) * scale
    d_p = (dot_rows(grad_pq, every_q) + dot_rows(grad_qp, every_q)) * scale
    return d_q, d_p, loss_qp + loss_pq, count


def body(
    question_ids,
    passage_ids,
    question_lengths,
    passage_lengths,
    question_keys,
    passage_keys,
    question_valid,
    word_table,
    positions,
    attention,
    feedforward,
    vectors,
    word_first,
    positions_first,
    attention_first,
    feedforward_first,
    vectors_first,
    word_second,
    positions_second,
    attention_second,
    feedforward_second,
    vectors_second,
    word_anchor,
    positions_anchor,
    attention_anchor,
    feedforward_anchor,
    vectors_anchor,
    word_outer,
    positions_outer,
    attention_outer,
    feedforward_outer,
    vectors_outer,
):
    many = lax.axis_size("dp")
    count_q = question_ids.shape[0]
    count_p = passage_ids.shape[0]
    table = word_table[0]
    sizes = Sizes(many, count_q, count_p, table.shape[0])
    swap = lambda values: jnp.swapaxes(values, -3, -2)
    vectors, vectors_first, vectors_second, vectors_anchor, vectors_outer = (
        swap(v) for v in (vectors, vectors_first, vectors_second, vectors_anchor, vectors_outer)
    )
    every, class_rows, kept, entry, counted = first_stage(
        sizes,
        question_ids,
        passage_ids,
        question_lengths,
        passage_lengths,
        question_keys,
        question_valid,
        passage_keys,
        table,
        positions,
    )
    part, lse_part, query, levels = tokens_forward(
        sizes, every, class_rows, kept, entry, counted, table, positions, attention, vectors
    )
    mixed_all, lse_all = exchange_mixed(sizes, part, lse_part)
    stage = class_stage if many * count_q <= 512 else class_stage_large
    grad_all, xa_q, xa_p, d_out, d_ffn, d_mid, loss_total, count = stage(
        sizes, class_rows, mixed_all, every, positions, attention, feedforward, vectors
    )
    d_query, d_table, slices = tokens_backward(
        sizes, levels, every, query, mixed_all, lse_all, grad_all, kept, entry, table, positions, attention, vectors
    )
    weights = (word_table, positions, attention, feedforward, vectors)
    firsts = (word_first, positions_first, attention_first, feedforward_first, vectors_first)
    seconds = (word_second, positions_second, attention_second, feedforward_second, vectors_second)
    anchors = (word_anchor, positions_anchor, attention_anchor, feedforward_anchor, vectors_anchor)
    outers = (word_outer, positions_outer, attention_outer, feedforward_outer, vectors_outer)
    done = finish(
        sizes,
        d_query,
        slices.reshape(many, sizes.lines, 128),
        d_table,
        class_rows,
        every,
        xa_q,
        xa_p,
        d_out,
        d_ffn,
        d_mid,
        (positions, attention, vectors),
        (weights, firsts, seconds, anchors),
    )
    norm = done[0]
    grads = (done[1], done[2], done[3], d_ffn, done[4])
    made, norm = make_outputs(
        norm, grads, firsts, seconds, anchors, outers, done[5:10], lax.axis_size("grp")
    )
    first_new, second_new, averages, outer_next, weight_next = (
        part[:4] + [swap(part[4])] for part in made
    )
    return (
        loss_total.reshape(1),
        count.reshape(1),
        norm.reshape(1),
        first_new[0],
        first_new[1],
        first_new[2],
        first_new[3],
        first_new[4],
        second_new[0],
        second_new[1],
        second_new[2],
        second_new[3],
        second_new[4],
        averages[0],
        averages[1],
        averages[2],
        averages[3],
        averages[4],
        outer_next[0],
        outer_next[1],
        outer_next[2],
        outer_next[3],
        outer_next[4],
        weight_next[0],
        weight_next[1],
        weight_next[2],
        weight_next[3],
        weight_next[4],
    )


def solution(mesh):
    placed = (
        P(("grp", "dp"), None),
        P(("grp", "dp"), None),
        P(("grp", "dp")),
        P(("grp", "dp")),
        P(("grp", "dp")),
        P(("grp", "dp")),
        P(("grp", "dp")),
        P("grp", "dp", None),
        P("grp", None, None, None),
        P("grp", None, None, None),
        P("grp", None, None, None, None),
        P("grp", None, None, None),
        P("grp", "dp", None),
        P("grp", None, None, None),
        P("grp", None, None, None),
        P("grp", None, None, None, None),
        P("grp", None, None, None),
        P("grp", "dp", None),
        P("grp", None, None, None),
        P("grp", None, None, None),
        P("grp", None, None, None, None),
        P("grp", None, None, None),
        P("dp", None),
        P(),
        P(),
        P(),
        P(),
        P("dp", None),
        P(),
        P(),
        P(),
        P(),
    )
    return jax.shard_map(
        body,
        mesh=mesh,
        in_specs=placed,
        out_specs=(
            P("grp"),
            P("grp"),
            P("grp"),
            P("grp", "dp", None),
            P("grp", None, None, None),
            P("grp", None, None, None),
            P("grp", None, None, None, None),
            P("grp", None, None, None),
            P("grp", "dp", None),
            P("grp", None, None, None),
            P("grp", None, None, None),
            P("grp", None, None, None, None),
            P("grp", None, None, None),
            P("dp", None),
            P(),
            P(),
            P(),
            P(),
            P("dp", None),
            P(),
            P(),
            P(),
            P(),
            P("grp", "dp", None),
            P("grp", None, None, None),
            P("grp", None, None, None),
            P("grp", None, None, None, None),
            P("grp", None, None, None),
        ),
        check_vma=False,
    )
```

```python
import functools
import math

import jax
import jax.numpy as jnp
from jax import lax
from jax.experimental import pallas as pl
from jax.experimental.pallas import tpu as pltpu
from jax.sharding import PartitionSpec as P

HEAD = 64
STEP = 5


NORM_EPS = 1e-05
MASKED = -1000000000.0
BETA_ONE = 0.9
BETA_TWO = 0.999
INNER_RATE = 0.05
WEIGHT_DECAY = 0.01
ADAM_EPS = 1e-08
CLIP_LIMIT = 0.01
OUTER_RATE = 0.7
OUTER_MU = 0.9
CONTRACT_ROWS = (((0,), (0,)), ((), ()))
CONTRACT_LAST = (((1,), (1,)), ((), ()))


def layer_norm(values, gain, shift):
    center = values - jnp.mean(values, -1, keepdims=True)
    spread = jnp.mean(center * center, -1, keepdims=True)
    return center * lax.rsqrt(spread + NORM_EPS) * gain + shift


def gelu_tanh(values):
    return jax.nn.gelu(values, approximate=True)


def low16(values):
    return values.astype(jnp.bfloat16)


NEG = -1e30
MESH = pl.DeviceIdType.MESH
VMEM_LIMIT = 60 * 1024 * 1024
WAYS = 4
SLOTS = 128
SPAN = WAYS * SLOTS
CHUNK = 256
UNROLL = 4
RAW_Q = 64
RAW_FLAGS = 72
RAW_ROWS = 80


def greet_all(many):
    me = lax.axis_index("dp")
    barrier = pltpu.get_barrier_semaphore()

    def greet(step, carry):
        peer = lax.rem(me + step, many)
        pl.semaphore_signal(barrier, inc=1, device_id={"dp": peer}, device_id_type=MESH)
        return carry

    lax.fori_loop(1, many, greet, 0)
    return me


def enter(many):
    me = greet_all(many)
    pl.semaphore_wait(pltpu.get_barrier_semaphore(), many - 1)
    return me


def copy_to(peer, src, dst, send, recv):
    return pltpu.make_async_remote_copy(
        src_ref=src,
        dst_ref=dst,
        send_sem=send,
        recv_sem=recv,
        device_id={"dp": peer},
        device_id_type=MESH,
    )


def spread_start(many, me, pairs, send, recv, slot):
    def step_start(step, carry):
        peer = lax.rem(me + step, many)
        for index, (source, landing) in enumerate(pairs):
            copy_to(
                peer,
                source(peer),
                landing.at[me],
                send.at[slot + index, peer],
                recv.at[slot + index, me],
            ).start()
        return carry

    lax.fori_loop(1, many, step_start, 0)


def spread_wait(many, me, pairs, send, recv, slot):
    def step_wait(step, carry):
        peer = lax.rem(me + step, many)
        for index, (source, landing) in enumerate(pairs):
            copy = copy_to(
                peer,
                source(peer),
                landing.at[peer],
                send.at[slot + index, peer],
                recv.at[slot + index, peer],
            )
            copy.wait_recv()
            copy.wait_send()
        return carry

    lax.fori_loop(1, many, step_wait, 0)


NEAR = 4


def place_of(many, me, far, near):
    row = lax.rem(me // NEAR + far, many // NEAR)
    return row * NEAR + lax.rem(lax.rem(me, NEAR) + near, NEAR)


def relay_start(many, me, source, landing, send, recv, slot):
    for near in range(NEAR):
        count = many // NEAR if near == 0 else 1

        def one(far, carry):
            peer = place_of(many, me, far, near)
            copy_to(peer, source, landing.at[me], send.at[slot, peer], recv.at[slot, me]).start()
            return carry

        lax.fori_loop(1 if near == 0 else 0, count, one, 0)


def relay_pass(many, me, source, landing, send, recv, slot):
    def one(far, carry):
        block = place_of(many, me, far, 0)
        copy_to(block, source, landing.at[block], send.at[slot, block], recv.at[slot, block]).wait_recv()
        for near in range(1, NEAR):
            peer = place_of(many, me, 0, near)
            key = place_of(many, me, far, near)
            copy_to(peer, landing.at[block], landing.at[block], send.at[slot, key], recv.at[slot, block]).start()
        return carry

    lax.fori_loop(1, many // NEAR, one, 0)


def relay_wait(many, me, source, landing, send, recv, slot):
    def one(far, carry):
        for near in range(NEAR):
            key = place_of(many, me, far, near)
            copy = copy_to(key, source, landing.at[key], send.at[slot, key], recv.at[slot, key])

            @pl.when((far > 0) | (near > 0))
            def _():
                copy.wait_send()

            if near > 0:
                copy.wait_recv()
        return carry

    lax.fori_loop(0, many // NEAR, one, 0)


def fold_start(many, me, blocks, landing, send, recv, slot):
    def one(row, carry):
        for near in range(1, NEAR):
            peer = place_of(many, me, 0, near)
            target = row * NEAR + lax.rem(peer, NEAR)
            copy_to(
                peer,
                blocks.at[target],
                landing.at[row * NEAR + lax.rem(me, NEAR)],
                send.at[slot, target],
                recv.at[slot, row * NEAR + lax.rem(me, NEAR)],
            ).start()
        mine = row * NEAR + lax.rem(me, NEAR)
        landing[mine] = blocks[mine]
        return carry

    lax.fori_loop(0, many // NEAR, one, 0)


def fold_pass(many, me, blocks, landing, halves, second, send, recv, slot, later):
    def one(row, carry):
        for near in range(1, NEAR):
            key = row * NEAR + lax.rem(place_of(many, me, 0, near), NEAR)
            copy = copy_to(
                place_of(many, me, 0, near), blocks.at[key], landing.at[key], send.at[slot, key], recv.at[slot, key]
            )
            copy.wait_recv()
            copy.wait_send()
        return carry

    lax.fori_loop(0, many // NEAR, one, 0)

    def two(far, carry):
        peer = place_of(many, me, far, 0)
        row = peer // NEAR
        total = landing[row * NEAR].astype(jnp.float32)
        for near in range(1, NEAR):
            total += landing[row * NEAR + near].astype(jnp.float32)
        halves[row] = total.astype(halves.dtype)

        @pl.when(far > 0)
        def _():
            copy_to(peer, halves.at[row], second.at[me // NEAR], send.at[later, row], recv.at[later, me // NEAR]).start()

        @pl.when(far == 0)
        def _():
            second[row] = halves[row]

        return carry

    lax.fori_loop(0, many // NEAR, two, 0)


def fold_wait(many, me, halves, second, send, recv, later):
    def one(far, carry):
        peer = place_of(many, me, far, 0)
        row = peer // NEAR
        copy = copy_to(peer, halves.at[row], second.at[row], send.at[later, row], recv.at[later, row])
        copy.wait_recv()
        copy.wait_send()
        return carry

    lax.fori_loop(1, many // NEAR, one, 0)
    return jnp.sum(second[...].astype(jnp.float32), 0)


def dot(left, right):
    return jnp.dot(left, right, preferred_element_type=jnp.float32)


def dot_rows(left, right):
    return lax.dot_general(left, right, CONTRACT_ROWS, preferred_element_type=jnp.float32)


def dot_last(left, right):
    return lax.dot_general(left, right, CONTRACT_LAST, preferred_element_type=jnp.float32)


def iota(shape, axis):
    return lax.broadcasted_iota(jnp.int32, shape, axis)


def hot(mask):
    return jnp.where(mask, 1.0, 0.0).astype(jnp.bfloat16)


def first_kernel(
    sizes,
    question_ref,
    passage_ref,
    length_q,
    length_p,
    key_q,
    valid_q,
    key_p,
    table_ref,
    place_ref,
    every_ref,
    rows_ref,
    kept_ref,
    entry_ref,
    count_ref,
    stage,
    raw,
    ask,
    asks,
    low_ref,
    offer,
    landed,
    own,
    table_t,
    place_t,
    send,
    recv,
):
    many = sizes.many
    count_q, count_p = sizes.count
    each = count_q + count_p
    depth = sizes.depth
    half = count_q // 2
    me = greet_all(many)
    lane = iota((1, 128), 1)
    for seq in range(count_p):
        stop = length_p[seq]
        stage[seq : seq + 1, :] = jnp.where(lane < stop, passage_ref[seq : seq + 1, 0:128], -1)
        stage[count_p + seq : count_p + seq + 1, :] = jnp.where(
            lane + 128 < stop, passage_ref[seq : seq + 1, 128:256], -1
        )
    both = jnp.concatenate([question_ref[0:half, :], question_ref[half:count_q, :]], 1)
    for seq in range(half):
        stop = jnp.where(lane < 64, length_q[seq], length_q[half + seq] + 64)
        stage[RAW_Q + seq : RAW_Q + seq + 1, :] = jnp.where(lane < stop, both[seq : seq + 1], -1)
    flags = jnp.zeros((1, 128), jnp.int32)
    for spot in range(count_q):
        flags = jnp.where(lane == spot, key_q[spot], flags)
        flags = jnp.where(lane == count_q + spot, valid_q[spot], flags)
    for spot in range(count_p):
        flags = jnp.where(lane == 2 * count_q + spot, key_p[spot], flags)
    stage[RAW_FLAGS:RAW_ROWS, :] = jnp.broadcast_to(flags, (8, 128))
    raw[...] = stage[...].astype(jnp.int16)
    heads = jnp.concatenate([question_ref[:, 0:1], passage_ref[:, 0:1]], 0)
    diagonal = iota((each, 128), 0) == iota((each, 128), 1)
    heads = jnp.sum(jnp.where(diagonal, jnp.broadcast_to(heads, (each, 128)), 0), 0, keepdims=True)
    ask[...] = jnp.broadcast_to(heads, (8, 128))
    pl.semaphore_wait(pltpu.get_barrier_semaphore(), many - 1)
    ask_pairs = [(lambda peer: ask, asks)]
    raw_pairs = [(lambda peer: raw, every_ref)]
    spread_start(many, me, ask_pairs, send, recv, 0)
    spread_start(many, me, raw_pairs, send, recv, 1)
    asks[me] = ask[...]
    every_ref[me] = raw[...]
    padded = sizes.padded
    if padded > depth:
        low_ref[...] = jnp.zeros_like(low_ref)
    low_ref[0:depth, :] = low16(table_ref[...])
    first = me * depth
    block = math.gcd(many, 16)
    spread_wait(many, me, ask_pairs, send, recv, 0)

    def pick(step, carry):
        found = []
        for i in range(block):
            line = jnp.broadcast_to(asks[step * block + i][0:1, :].astype(jnp.float32), (each, 128))
            found.append(jnp.sum(jnp.where(diagonal, line, 0.0), 1, keepdims=True))
        place = jnp.concatenate(found, 0).astype(jnp.int32) - first
        spot = jnp.where((place >= 0) & (place < depth), place, -1)
        number = spot.shape[0]
        total = jnp.zeros((number, 128), jnp.float32)
        wide = jnp.broadcast_to(spot, (number, CHUNK))
        for at in range(padded // CHUNK):
            chosen = hot(wide == iota((number, CHUNK), 1) + at * CHUNK)
            total += dot(chosen, low_ref[at * CHUNK : (at + 1) * CHUNK, :])
        for i in range(block):
            offer[step * block + i] = low16(total[i * each : (i + 1) * each])
        return carry

    lax.fori_loop(0, many // block, pick, 0)
    offer_pairs = [(lambda peer: offer.at[peer], landed)]
    spread_start(many, me, offer_pairs, send, recv, 2)
    landed[me] = offer[me]
    if sizes.keep:
        prepare_tokens(sizes, table_ref, place_ref, table_t, place_t)
    spread_wait(many, me, raw_pairs, send, recv, 1)

    row_pairs = [(lambda peer: own, rows_ref)]

    def send_rows():
        spread_wait(many, me, offer_pairs, send, recv, 2)
        own[...] = low16(jnp.sum(landed[...].astype(jnp.float32), 0))
        spread_start(many, me, row_pairs, send, recv, 3)
        rows_ref[me] = own[...]

    def spans_of(enc, count):
        def spans(turn, count):
            if enc == 1:
                pl.when(turn == 1)(send_rows)
            steps = [turn * sizes.unroll[enc] + u for u in range(sizes.unroll[enc])]
            packed = [pack_span(sizes, enc, s, 0, first, every_ref) for s in steps]
            found = [gather_span(sizes, enc, part[0], table_t, place_t) for part in packed]
            for part in packed:
                count = jnp.maximum(count, part[1])
            for u, s in enumerate(steps):
                at = s if enc == 0 else sizes.steps[0] + s
                kept_ref[at, 0:128, :] = found[u][0]
                kept_ref[at, 128:129, :] = found[u][1]
                entry_ref[at, 0:1, :] = packed[u][0]
            return count

        return lax.fori_loop(0, sizes.steps[enc] // sizes.unroll[enc], spans, count)

    count = jnp.zeros((8, 128), jnp.float32)
    if sizes.keep:
        count = spans_of(1, spans_of(0, count))
    else:
        send_rows()
    count_ref[...] = count
    spread_wait(many, me, row_pairs, send, recv, 3)


def first_stage(sizes, ids_q, ids_p, length_q, length_p, key_q, valid_q, key_p, table, positions):
    many = sizes.many
    padded = sizes.padded
    both = sum(sizes.count)
    vm = pl.BlockSpec(memory_space=pltpu.VMEM)
    sm = pl.BlockSpec(memory_space=pltpu.SMEM)
    kept = sizes.spans if sizes.keep else 1
    return pl.pallas_call(
        functools.partial(first_kernel, sizes),
        out_shape=(
            jax.ShapeDtypeStruct((many, RAW_ROWS, 128), jnp.int16),
            jax.ShapeDtypeStruct((many, both, 128), jnp.bfloat16),
            jax.ShapeDtypeStruct((kept, 136, SPAN), jnp.float32),
            jax.ShapeDtypeStruct((kept, 8, SPAN), jnp.int32),
            jax.ShapeDtypeStruct((8, 128), jnp.float32),
        ),
        in_specs=[vm, vm, sm, sm, sm, sm, sm, vm, vm],
        out_specs=[vm] * 5,
        scratch_shapes=[
            pltpu.VMEM((RAW_ROWS, 128), jnp.int32),
            pltpu.VMEM((RAW_ROWS, 128), jnp.int16),
            pltpu.VMEM((8, 128), jnp.int32),
            pltpu.VMEM((many, 8, 128), jnp.int32),
            pltpu.VMEM((padded, 128), jnp.bfloat16),
            pltpu.VMEM((many, both, 128), jnp.bfloat16),
            pltpu.VMEM((many, both, 128), jnp.bfloat16),
            pltpu.VMEM((both, 128), jnp.bfloat16),
            pltpu.VMEM((128, padded), jnp.bfloat16),
            pltpu.VMEM((2, 2, 128, CHUNK), jnp.bfloat16),
            pltpu.SemaphoreType.DMA((4, many)),
            pltpu.SemaphoreType.DMA((4, many)),
        ],
        compiler_params=pltpu.CompilerParams(
            collective_id=1, has_side_effects=True, vmem_limit_bytes=VMEM_LIMIT
        ),
        name="first_stage",
    )(ids_q, ids_p, length_q, length_p, key_q, valid_q, key_p, table, positions)


def norm_rows(values, gain, shift):
    center = values - jnp.mean(values, -1, keepdims=True)
    spread = jnp.mean(center * center, -1, keepdims=True)
    return center * lax.rsqrt(spread + NORM_EPS) * gain + shift


def two_heads(values):
    lane = iota(values.shape, 1)
    low = jnp.where(lane < HEAD, values, jnp.zeros_like(values))
    high = jnp.where(lane >= HEAD, values, jnp.zeros_like(values))
    return jnp.concatenate([low, high], 0)


def merge_heads(both):
    half = both.shape[0] // 2
    lane = iota((half, both.shape[1]), 1)
    return jnp.where(lane < HEAD, both[:half], both[half:])


class Sizes:
    def __init__(self, many, count_q, count_p, depth):
        self.many = many
        self.count = (count_q, count_p)
        self.depth = depth
        self.padded = -(-depth // CHUNK) * CHUNK
        self.steps = (many // (2 * WAYS), many)
        self.unroll = tuple(math.gcd(UNROLL, step) for step in self.steps)
        self.spans = self.steps[0] + self.steps[1]
        self.devices = (2 * WAYS, 1)
        self.queries = (2 * WAYS * count_q, count_p)
        assert self.steps[1] // self.unroll[1] > 1
        self.lines = 1024 // many
        self.kind = jnp.bfloat16 if self.lines % 16 == 0 else jnp.float32
        self.keep = self.spans * 136 * SPAN * 4 <= 8 * 1024 * 1024


def vector_row(vec_ref, enc, row):
    return vec_ref[0, row, enc : enc + 1, :]


def prepare_tokens(sizes, table_ref, place_ref, table_t, place_t):
    depth = sizes.depth
    if sizes.padded > depth:
        table_t[...] = jnp.zeros_like(table_t)

    def turn(step, carry):
        spot = pl.ds(pl.multiple_of(step * 128, 128), 128)
        table_t[:, spot] = low16(jnp.transpose(table_ref[spot, :]))
        return carry

    whole = depth // 128
    lax.fori_loop(0, whole, turn, 0)
    rest = depth - whole * 128
    if rest:
        piece = jnp.concatenate([table_ref[whole * 128 :, :], jnp.zeros((128 - rest, 128), jnp.float32)], 0)
        table_t[:, whole * 128 : (whole + 1) * 128] = low16(jnp.transpose(piece))

    def turn_place(step, carry):
        enc, cut = (step // 2, step % 2)
        spot = pl.ds(pl.multiple_of(cut * 128, 128), 128)
        turned = jnp.transpose(place_ref[0, enc, spot, :])
        high = low16(turned)
        place_t[enc, 0, :, spot] = high
        place_t[enc, 1, :, spot] = low16(turned - high.astype(jnp.float32))
        return carry

    lax.fori_loop(0, 4, turn_place, 0)


def prepare_weights(attn_ref, vec_ref, w_kv, vec_t):
    for enc in range(2):
        for cut in range(2):
            w_kv[enc, cut * 128 : (cut + 1) * 128, :] = low16(
                jnp.transpose(attn_ref[0, enc, :, (cut + 1) * 128 : (cut + 2) * 128])
            )
        rows = [vector_row(vec_ref, enc, row) for row in range(4)]
        rows = jnp.concatenate(rows + [jnp.zeros((124, 128), jnp.float32)], 0)
        vec_t[enc] = jnp.transpose(rows)


def lane_pick(values, lanes):
    return jnp.take_along_axis(values, lanes, axis=1, mode="promise_in_bounds")


def pack_span(sizes, enc, step, level, first, raw_ref):
    if enc == 1:
        ids = raw_ref[step, 0:RAW_Q, :].astype(jnp.int32)
    else:
        ids = jnp.concatenate(
            [
                raw_ref[step * 8 + i, RAW_Q:RAW_ROWS, :].astype(jnp.int32)[0:8]
                for i in range(8)
            ],
            0,
        )
    place = ids - first
    owned = (place >= 0) & (place < sizes.depth)
    flag = hot(owned)
    inside = dot(flag, hot(iota((128, 128), 0) <= iota((128, 128), 1))).astype(jnp.int32)
    total = dot(flag, jnp.ones((128, 128), jnp.bfloat16))
    before = dot(hot(iota((64, 64), 1) < iota((64, 64), 0)), low16(total))
    start = before.astype(jnp.int32)
    stop = (before + total).astype(jnp.int32)
    line = iota((64, 128), 0)
    turn = iota((64, 128), 1)
    lane = jnp.zeros((64, 128), jnp.int32)
    for jump in (64, 32, 16, 8, 4, 2, 1):
        seen = lane_pick(inside, lane + (jump - 1))
        lane = jnp.where(seen <= turn, lane + jump, lane)
    row = lane_pick(place, lane)
    if enc == 1:
        where = (line >> 5) * 128 + lane
        seq = (line & 31) + 1
    else:
        where = lane & 63
        seq = (line >> 3) * sizes.count[0] + (lane >> 6) * 8 + (line & 7) + 1
    code = lane_pick((row << 16) + (where << 8) + seq, (turn - start) & 127)
    codes = []
    for window in range(WAYS):
        slot = turn + (window * SLOTS + level * SPAN)
        kept = jnp.where((slot >= start) & (slot < stop), code, 0)
        codes.append(jnp.sum(kept, 0, keepdims=True))
    return jnp.concatenate(codes, 1), (before + total)[56:64]


def gather_span(sizes, enc, code, table_t, place_t, short=False):
    rows = code >> 16
    where = (code >> 8) & 255
    x = jnp.zeros((128, SPAN), jnp.float32)
    wide = jnp.broadcast_to(rows, (CHUNK, SPAN))

    def add(cut, x):
        spot = pl.ds(pl.multiple_of(cut * CHUNK, CHUNK), CHUNK)
        return x + dot(table_t[:, spot], hot(wide == iota((CHUNK, SPAN), 0) + cut * CHUNK))

    x = lax.fori_loop(0, sizes.padded // CHUNK, add, x, unroll=not short)
    chosen = hot(jnp.broadcast_to(where, (CHUNK, SPAN)) == iota((CHUNK, SPAN), 0))
    x += dot(place_t[enc, 0], chosen) + dot(place_t[enc, 1], chosen)
    center = x - jnp.mean(x, 0, keepdims=True)
    rate = lax.rsqrt(jnp.mean(center * center, 0, keepdims=True) + NORM_EPS)
    return center * rate, rate


def project(enc, scaled, vec_t, w_kv):
    a_t = low16(scaled * vec_t[enc, :, 0:1] + vec_t[enc, :, 1:2])
    kv = dot(w_kv[enc], a_t)
    keys_t = low16(kv[:128])
    values_t = low16(kv[128:] + vec_t[enc, :, 3:4])
    return a_t, keys_t, values_t


def own_slots(code, number):
    line = iota((2 * number, SPAN), 0)
    line = jnp.where(line >= number, line - number, line)
    return line == (code & 255) - 1


def forward_kernel(
    sizes,
    raw_ref,
    rows_ref,
    kept_hbm,
    entry_hbm,
    count_ref,
    table_ref,
    place_ref,
    attn_ref,
    vec_ref,
    out_ref,
    lse_ref,
    query_ref,
    levels_ref,
    table_t,
    place_t,
    w_kv,
    vec_t,
    query_q,
    total_q,
    top_q,
    mass_q,
    total_p,
    top_p,
    mass_p,
    kept_ref,
    entry_ref,
    load,
):
    loads = load_kept(sizes, kept_hbm, entry_hbm, kept_ref, entry_ref, load)
    first = lax.axis_index("dp") * sizes.depth
    count_q, count_p = sizes.count
    prepare_weights(attn_ref, vec_ref, w_kv, vec_t)
    begin = 1 if sizes.keep else 0
    count = count_ref[...]
    block = math.gcd(sizes.many, 16)
    for enc in range(2):
        low, high = (0, count_q) if enc == 0 else (count_q, count_q + count_p)
        w_q = low16(attn_ref[0, enc, :, 0:128])

        def ask(step, carry):
            spot = pl.ds(step * block, block)
            held = rows_ref[spot, low:high, :].reshape(block * (high - low), 128)
            x = held.astype(jnp.float32) + place_ref[0, enc, 0:1, :]
            h = norm_rows(x, vector_row(vec_ref, enc, 0), vector_row(vec_ref, enc, 1))
            query = low16(dot(low16(h), w_q) + vector_row(vec_ref, enc, 2))
            query_ref[spot, low:high, :] = query.reshape(block, high - low, 128)
            if enc == 0:
                for half in range(block // 8):
                    query_q[step * (block // 8) + half] = query[half * 8 * count_q : (half + 1) * 8 * count_q]
            return carry

        lax.fori_loop(0, sizes.many // block, ask, 0)
    states = ((total_q, top_q, mass_q), (total_p, top_p, mass_p))
    lse_ref[...] = jnp.full_like(lse_ref, NEG)

    def close(enc, step, total, top, mass):
        some = mass > 0.0
        safe = jnp.where(some, mass, 1.0)
        mixed = merge_heads(total / safe)
        lse = jnp.where(some, top + jnp.log(safe), NEG)
        if enc == 1:
            out_ref[step, count_q:, :] = low16(mixed)
            at = iota(lse.shape, 0) == iota(lse.shape, 1)
            lse_ref[step, 0:1, :] = jnp.sum(jnp.where(at, lse, 0.0), 0, keepdims=True)
        else:
            half = lse.shape[0] // 2
            row = iota((count_q, 128), 0)
            lane = iota((count_q, 128), 1)
            for i in range(8):
                spot = slice(i * count_q, (i + 1) * count_q)
                out_ref[step * 8 + i, 0:count_q, :] = low16(mixed[spot])
                line = jnp.where(lane == row, lse[spot], 0.0) + jnp.where(
                    lane == row + count_q, lse[half + i * count_q : half + (i + 1) * count_q], 0.0
                )
                lse_ref[step * 8 + i, 1:2, :] = jnp.sum(line, 0, keepdims=True)

    def attend(enc, steps, codes, scaleds, olds):
        queries = [query_q[s] if enc == 0 else query_ref[s, count_q:, :] for s in steps]
        made = [project(enc, scaled, vec_t, w_kv) for scaled in scaleds]
        scores = [dot(two_heads(query), part[1]) * HEAD ** (-0.5) for query, part in zip(queries, made)]
        news = []
        for u, score in enumerate(scores):
            mine = own_slots(codes[u], queries[u].shape[0])
            score = jnp.where(mine, score, NEG)
            new = jnp.max(score, 1, keepdims=True)
            if olds is not None:
                new = jnp.maximum(olds[u][1][:, 0:1], new)
            expo = jnp.where(mine, jnp.exp(score - new), 0.0)
            total = dot_last(low16(expo), made[u][2])
            mass = jnp.sum(expo, 1, keepdims=True)
            if olds is not None:
                fade = jnp.exp(olds[u][1] - new)
                total = olds[u][0] * fade + total
                mass = olds[u][2] * fade + mass
            wide = (score.shape[0], 128)
            news.append((total, jnp.broadcast_to(new, wide), jnp.broadcast_to(mass, wide)))
        for u, s in enumerate(steps):
            for ref, value in zip(states[enc], news[u]):
                ref[s] = value
        return news

    for enc in range(2):
        if sizes.keep:
            for copy in loads[2 * enc : 2 * enc + 2]:
                copy.wait()

            def kept_spans(turn, carry):
                steps = [turn * sizes.unroll[enc] + u for u in range(sizes.unroll[enc])]
                ats = [s if enc == 0 else sizes.steps[0] + s for s in steps]
                news = attend(
                    enc, steps, [entry_ref[at, 0:1, :] for at in ats], [kept_ref[at, 0:128, :] for at in ats], None
                )
                for s, new in zip(steps, news):
                    close(enc, s, *new)
                return carry

            lax.fori_loop(0, sizes.steps[enc] // sizes.unroll[enc], kept_spans, 0)
        else:
            total, top, mass = states[enc]
            total[...] = jnp.zeros_like(total)
            mass[...] = jnp.zeros_like(mass)
            top[...] = jnp.full_like(top, NEG)

    def needed(count):
        return jnp.maximum((jnp.max(count).astype(jnp.int32) + SPAN - 1) // SPAN, 1)

    start = needed(count)
    levels_ref[0] = start

    @pl.when(start > begin)
    def _():
        prepare_tokens(sizes, table_ref, place_ref, table_t, place_t)

        def one_level(state):
            level, unused, count = state
            for enc in range(2):

                def one_span(step, count):
                    code, found = pack_span(sizes, enc, step, level, first, raw_ref)
                    scaled = gather_span(sizes, enc, code, table_t, place_t, True)[0]
                    attend(enc, [step], [code], [scaled], [tuple(ref[step] for ref in states[enc])])
                    return jnp.maximum(count, found)

                count = lax.fori_loop(0, sizes.steps[enc], one_span, count)
            return level + 1, needed(count), count

        if sizes.keep:
            lax.fori_loop(
                begin, start, lambda level, carry: one_level((level, carry, count))[1], jnp.int32(0)
            )
        else:
            last = lax.while_loop(
                lambda state: state[0] < state[1], one_level, (jnp.int32(begin), start, count)
            )
            levels_ref[0] = last[1]
        for enc in range(2):

            def close_span(step, carry):
                close(enc, step, *(ref[step] for ref in states[enc]))
                return carry

            lax.fori_loop(0, sizes.steps[enc], close_span, 0)


def load_kept(sizes, kept_hbm, entry_hbm, kept_ref, entry_ref, load):
    if not sizes.keep:
        return []
    copies = []
    for enc, rows in enumerate((slice(0, sizes.steps[0]), slice(sizes.steps[0], sizes.spans))):
        for j, (source, target) in enumerate(((kept_hbm, kept_ref), (entry_hbm, entry_ref))):
            copy = pltpu.make_async_copy(source.at[rows], target.at[rows], load.at[enc, j])
            copy.start()
            copies.append(copy)
    return copies


def kept_scratch(sizes):
    kept = sizes.spans if sizes.keep else 1
    return [
        pltpu.VMEM((kept, 136, SPAN), jnp.float32),
        pltpu.VMEM((kept, 8, SPAN), jnp.int32),
        pltpu.SemaphoreType.DMA((2, 2)),
    ]


def token_scratch(sizes):
    return [
        pltpu.VMEM((128, sizes.padded), jnp.bfloat16),
        pltpu.VMEM((2, 2, 128, CHUNK), jnp.bfloat16),
        pltpu.VMEM((2, 256, 128), jnp.bfloat16),
        pltpu.VMEM((2, 128, 128), jnp.float32),
    ]


def local_call(kernel, out_shape, inputs, scratch, name, smem_in=(), smem_out=(), any_in=()):
    vm = pl.BlockSpec(memory_space=pltpu.VMEM)
    sm = pl.BlockSpec(memory_space=pltpu.SMEM)
    hbm = pl.BlockSpec(memory_space=pl.ANY)
    return pl.pallas_call(
        kernel,
        out_shape=out_shape,
        in_specs=[sm if i in smem_in else hbm if i in any_in else vm for i in range(len(inputs))],
        out_specs=[sm if i in smem_out else vm for i in range(len(out_shape))],
        scratch_shapes=scratch,
        compiler_params=pltpu.CompilerParams(vmem_limit_bytes=VMEM_LIMIT),
        name=name,
    )(*inputs)


def tokens_forward(sizes, every, rows, kept, entry, counted, table, positions, attention, vectors):
    many = sizes.many
    both = sum(sizes.count)
    state = []
    for enc in range(2):
        tall = 2 * sizes.queries[enc]
        state += [pltpu.VMEM((sizes.steps[enc], tall, 128), jnp.float32)] * 3
    return local_call(
        functools.partial(forward_kernel, sizes),
        (
            jax.ShapeDtypeStruct((many, both, 128), jnp.bfloat16),
            jax.ShapeDtypeStruct((many, 2, 128), jnp.float32),
            jax.ShapeDtypeStruct((many, both, 128), jnp.bfloat16),
            jax.ShapeDtypeStruct((1,), jnp.int32),
        ),
        (every, rows, kept, entry, counted, table, positions, attention, vectors),
        token_scratch(sizes)
        + [pltpu.VMEM((sizes.steps[0], sizes.queries[0], 128), jnp.bfloat16)]
        + state
        + kept_scratch(sizes),
        "tokens_forward",
        smem_out=(3,),
        any_in=(2, 3),
    )


def mix_kernel(
    many, count_q, part_ref, lse_ref, mixed_ref, total_ref, landed, landed_lse, own, own_lse, send, recv
):
    me = enter(many)
    pairs = [
        (lambda peer: part_ref.at[peer], landed),
        (lambda peer: lse_ref.at[peer], landed_lse),
    ]
    spread_start(many, me, pairs, send, recv, 0)
    landed[me] = part_ref[me]
    landed_lse[me] = lse_ref[me]
    spread_wait(many, me, pairs, send, recv, 0)
    parts = landed_lse[...]
    top = jnp.max(parts, 0)
    total = top + jnp.log(jnp.sum(jnp.exp(parts - top[None]), 0))
    own_lse[...] = total
    share = jnp.exp(parts - total[None])
    count_p = part_ref.shape[1] - count_q
    mixed = jnp.zeros((count_q + count_p, 128), jnp.float32)
    for peer in range(many):
        factors = []
        for row, number in ((1, count_q), (0, count_p)):
            wide = (2 * number, 128)
            at = iota(wide, 0) == iota(wide, 1)
            line = jnp.broadcast_to(share[peer][row : row + 1], wide)
            column = jnp.sum(jnp.where(at, line, 0.0), 1, keepdims=True)
            lane = iota((number, 128), 1)
            factors.append(jnp.where(lane < HEAD, column[0:number], column[number:]))
        mixed += jnp.concatenate(factors, 0) * landed[peer].astype(jnp.float32)
    own[...] = low16(mixed)
    pairs = [(lambda peer: own, mixed_ref), (lambda peer: own_lse, total_ref)]
    spread_start(many, me, pairs, send, recv, 2)
    mixed_ref[me] = own[...]
    total_ref[me] = own_lse[...]
    spread_wait(many, me, pairs, send, recv, 2)


def remote_call(kernel, out_shape, inputs, scratch, lanes, many, ident, name):
    return pl.pallas_call(
        kernel,
        out_shape=out_shape,
        in_specs=[pl.BlockSpec(memory_space=pltpu.VMEM)] * len(inputs),
        out_specs=[pl.BlockSpec(memory_space=pltpu.VMEM)] * len(out_shape),
        scratch_shapes=scratch
        + [pltpu.SemaphoreType.DMA((lanes, many)), pltpu.SemaphoreType.DMA((lanes, many))],
        compiler_params=pltpu.CompilerParams(
            collective_id=ident, has_side_effects=True, vmem_limit_bytes=VMEM_LIMIT
        ),
        name=name,
    )(*inputs)


def exchange_mixed(sizes, part, lse):
    many = sizes.many
    both = sum(sizes.count)
    return remote_call(
        functools.partial(mix_kernel, many, sizes.count[0]),
        (
            jax.ShapeDtypeStruct((many, both, 128), jnp.bfloat16),
            jax.ShapeDtypeStruct((many, 2, 128), jnp.float32),
        ),
        (part, lse),
        [
            pltpu.VMEM((many, both, 128), jnp.bfloat16),
            pltpu.VMEM((many, 2, 128), jnp.float32),
            pltpu.VMEM((both, 128), jnp.bfloat16),
            pltpu.VMEM((2, 128), jnp.float32),
        ],
        4,
        many,
        2,
        "exchange_mixed",
    )


def backward_kernel(
    sizes,
    levels_ref,
    raw_ref,
    query_ref,
    mixed_ref,
    lse_ref,
    grad_ref,
    kept_hbm,
    entry_hbm,
    table_ref,
    place_ref,
    attn_ref,
    vec_ref,
    d_query_ref,
    d_table_ref,
    slice_ref,
    table_t,
    place_t,
    w_kv,
    vec_t,
    d_place_ref,
    d_attn_ref,
    acc_gain,
    acc_shift,
    acc_value,
    d_query_q,
    d_query_p,
    kept_ref,
    entry_ref,
    load,
):
    loads = load_kept(sizes, kept_hbm, entry_hbm, kept_ref, entry_ref, load)
    first = lax.axis_index("dp") * sizes.depth
    count_q, count_p = sizes.count
    prepare_weights(attn_ref, vec_ref, w_kv, vec_t)
    begin = 1 if sizes.keep else 0
    again = levels_ref[0] > begin

    @pl.when(again)
    def _():
        prepare_tokens(sizes, table_ref, place_ref, table_t, place_t)

    for ref in (d_table_ref, d_place_ref, d_attn_ref, d_query_q, d_query_p, acc_gain, acc_shift, acc_value):
        ref[...] = jnp.zeros_like(ref)

    def ask_span(enc, step):
        if enc == 0:
            spot = pl.ds(step * 8, 8)
            shape = (8 * count_q, 128)
            found = [ref[spot, 0:count_q, :].reshape(shape) for ref in (query_ref, grad_ref, mixed_ref)]
            lines = [jnp.broadcast_to(lse_ref[step * 8 + i, 1:2, :], (count_q, 128)) for i in range(8)]
            lines = jnp.concatenate(lines, 0)
            row = iota(lines.shape, 0) % count_q
            lane = iota(lines.shape, 1)
            lse = [
                jnp.sum(jnp.where(lane == row + head * count_q, lines, 0.0), 1, keepdims=True)
                for head in range(2)
            ]
            lse = jnp.concatenate(lse, 0)
        else:
            found = [ref[step, count_q:, :] for ref in (query_ref, grad_ref, mixed_ref)]
            lines = jnp.broadcast_to(lse_ref[step, 0:1, :], (2 * count_p, 128))
            lse = jnp.sum(jnp.where(iota(lines.shape, 1) == iota(lines.shape, 0), lines, 0.0), 1, keepdims=True)
        return found + [lse]

    def work(enc, steps, codes, scaleds, rates, short=False):
        w_all = low16(attn_ref[0, enc, :, 128:384])
        asked = [ask_span(enc, step) for step in steps]
        made = [project(enc, scaled, vec_t, w_kv) for scaled in scaleds]
        d_queries, d_kvs = ([], [])
        for (query, grad, mixed, lse), code, (a_t, keys_t, values_t) in zip(asked, codes, made):
            both = two_heads(query)
            grads = two_heads(grad)
            base = jnp.sum(
                grads.astype(jnp.float32) * jnp.concatenate([mixed, mixed], 0).astype(jnp.float32),
                1,
                keepdims=True,
            )
            scores = dot(both, keys_t) * HEAD ** (-0.5)
            mine = own_slots(code, query.shape[0])
            probs = jnp.where(mine, jnp.exp(jnp.where(mine, scores, NEG) - lse), 0.0)
            d_probs = dot(grads, values_t)
            d_scores = low16(probs * (d_probs - base))
            d_values = low16(dot_rows(grads, low16(probs)))
            d_keys = low16(dot_rows(both, d_scores) * HEAD ** (-0.5))
            d_queries.append(merge_heads(dot_last(d_scores, keys_t)) * HEAD ** (-0.5))
            d_kvs.append(jnp.concatenate([d_keys, d_values], 0))
        for step, d_query in zip(steps, d_queries):
            if enc == 0:
                d_query_q[step] += d_query
            else:
                d_query_p[step] += d_query
        d_kv = jnp.concatenate(d_kvs, 1)
        a_t = jnp.concatenate([part[0] for part in made], 1)
        scaled = jnp.concatenate(scaleds, 1)
        rate = jnp.concatenate(rates, 1)
        code = jnp.concatenate(codes, 1)
        width = code.shape[1]
        d_attn_ref[enc] += dot_last(a_t, d_kv)
        d_h = dot(w_all, d_kv)
        fold = lambda values: sum(values[:, i * SPAN : (i + 1) * SPAN] for i in range(width // SPAN))
        acc_value[enc] += fold(d_kv[128:].astype(jnp.float32))
        acc_gain[enc] += fold(d_h * scaled)
        acc_shift[enc] += fold(d_h)
        d_scaled = d_h * vec_t[enc, :, 0:1]
        center = d_scaled - jnp.mean(d_scaled, 0, keepdims=True)
        slope = jnp.mean(d_scaled * scaled, 0, keepdims=True)
        d_x = low16((center - scaled * slope) * rate)
        rows = code >> 16
        where = (code >> 8) & 255
        chosen = hot(jnp.broadcast_to(where, (CHUNK, width)) == iota((CHUNK, width), 0))
        d_place_ref[enc] += dot_last(d_x, chosen)
        wide = jnp.broadcast_to(rows, (CHUNK, width))

        def add(cut, carry):
            spot = pl.ds(pl.multiple_of(cut * CHUNK, CHUNK), CHUNK)
            chosen = hot(wide == iota((CHUNK, width), 0) + cut * CHUNK)
            d_table_ref[spot, :] += dot_last(chosen, d_x)
            return carry

        lax.fori_loop(0, sizes.padded // CHUNK, add, 0, unroll=not short)

    for enc in range(2):
        if sizes.keep:
            for copy in loads[2 * enc : 2 * enc + 2]:
                copy.wait()

            def kept_spans(turn, carry):
                steps = [turn * sizes.unroll[enc] + u for u in range(sizes.unroll[enc])]
                ats = [s if enc == 0 else sizes.steps[0] + s for s in steps]
                work(
                    enc,
                    steps,
                    [entry_ref[at, 0:1, :] for at in ats],
                    [kept_ref[at, 0:128, :] for at in ats],
                    [kept_ref[at, 128:129, :] for at in ats],
                )
                return carry

            lax.fori_loop(0, sizes.steps[enc] // sizes.unroll[enc], kept_spans, 0)

        def more_level(level, carry_level):
            def one_span(step, carry):
                code = pack_span(sizes, enc, step, level, first, raw_ref)[0]
                scaled, rate = gather_span(sizes, enc, code, table_t, place_t, True)
                work(enc, [step], [code], [scaled], [rate], True)
                return carry

            return lax.fori_loop(0, sizes.steps[enc], one_span, carry_level)

        lax.fori_loop(begin, levels_ref[0], more_level, 0)

    for step in range(sizes.steps[0]):
        d_query_ref[step * 8 : step * 8 + 8, 0:count_q, :] = low16(d_query_q[step]).reshape(8, count_q, 128)
    d_query_ref[:, count_q:, :] = low16(d_query_p[...])
    for enc in range(2):
        for part, block in enumerate((d_place_ref, d_attn_ref)):
            for cut in range(2):
                slice_ref[enc, 2 * part + cut] = block[enc, :, cut * 128 : (cut + 1) * 128].astype(
                    slice_ref.dtype
                )
    slice_ref[0, 1] = jnp.zeros_like(slice_ref[0, 1])
    sums = []
    same = iota((128, 128), 0) == iota((128, 128), 1)
    for enc in range(2):
        for row, acc in enumerate((acc_gain, acc_shift, acc_value)):
            tall = jnp.broadcast_to(jnp.sum(acc[enc], 1, keepdims=True), (128, 128))
            sums.append(jnp.sum(jnp.where(same, tall, 0.0), 0, keepdims=True))
    sums = jnp.concatenate(sums + [jnp.zeros((10, 128), jnp.float32)], 0)
    slice_ref[0, 1, 0:16, :] = sums.astype(slice_ref.dtype)


def tokens_backward(sizes, levels, every, query, mixed, lse, grad, kept, entry, table, positions, attention, vectors):
    many = sizes.many
    count_p = sizes.count[1]
    both = sum(sizes.count)
    return local_call(
        functools.partial(backward_kernel, sizes),
        (
            jax.ShapeDtypeStruct((many, both, 128), jnp.bfloat16),
            jax.ShapeDtypeStruct((sizes.padded, 128), jnp.float32),
            jax.ShapeDtypeStruct((2, 4, 128, 128), sizes.kind),
        ),
        (levels, every, query, mixed, lse, grad, kept, entry, table, positions, attention, vectors),
        token_scratch(sizes)
        + [
            pltpu.VMEM((2, 128, CHUNK), jnp.float32),
            pltpu.VMEM((2, 128, 256), jnp.float32),
            pltpu.VMEM((2, 128, SPAN), jnp.float32),
            pltpu.VMEM((2, 128, SPAN), jnp.float32),
            pltpu.VMEM((2, 128, SPAN), jnp.float32),
            pltpu.VMEM((sizes.steps[0], sizes.queries[0], 128), jnp.float32),
            pltpu.VMEM((many, count_p, 128), jnp.float32),
        ]
        + kept_scratch(sizes),
        "tokens_backward",
        smem_in=(0,),
        any_in=(6, 7),
    )


def adam(weight, grad, first, second):
    first_new = BETA_ONE * first + (1.0 - BETA_ONE) * grad
    second_new = BETA_TWO * second + (1.0 - BETA_TWO) * grad * grad
    fix_one = 1.0 - BETA_ONE**STEP
    fix_two = 1.0 - BETA_TWO**STEP
    ratio = first_new / fix_one / (jnp.sqrt(second_new / fix_two) + ADAM_EPS)
    return (first_new, second_new, weight - INNER_RATE * (ratio + WEIGHT_DECAY * weight))


def pieces_of(depth):
    blocks = [(1, (enc,)) for enc in range(2)] + [(2, (enc,)) for enc in range(2)]
    blocks += [(3, (enc, side)) for enc in range(2) for side in range(2)]
    return blocks + [(4, ())]


def square_sum(values):
    return jnp.sum(jnp.sum(values * values, 0, keepdims=True), 1, keepdims=True)


def finish_kernel(sizes, *refs):
    many = sizes.many
    count_q, count_p = sizes.count
    depth = sizes.depth
    (query_ref, slice_ref, d_table_ref, rows_ref, raw_ref, xa_q, xa_p, d_out, d_ffn, d_mid) = refs[:10]
    place_ref, attn_ref, vec_ref = refs[10:13]
    state = refs[13:33]
    norm_ref, g_word, g_place, g_attn, g_vec = refs[33:38]
    joined = refs[38:43]
    held = refs[43:63]
    mine = refs[63:68]
    theirs = refs[68:73]
    (query_all, slice_all, scalar_all, land_query, land_slice, own_query, own_slice, tile, table_t) = refs[73:82]
    half_query, far_query, half_slice, far_slice = refs[82:86]
    send, recv, load, pair_send, pair_recv = refs[86:91]
    loads = []
    for index in range(20):
        copy = pltpu.make_async_copy(state[index], held[index], load.at[index])
        copy.start()
        loads.append(copy)
    me = lax.axis_index("dp")
    other = 1 - lax.axis_index("grp")
    barrier = pltpu.get_barrier_semaphore()

    def greet(step, carry):
        peer = lax.rem(me + step, many)
        pl.semaphore_signal(barrier, inc=1, device_id={"dp": peer}, device_id_type=MESH)
        return carry

    lax.fori_loop(1, many, greet, 0)
    pl.semaphore_signal(barrier, inc=1, device_id={"grp": other}, device_id_type=MESH)
    pl.semaphore_wait(barrier, many)
    fold_start(many, me, query_ref, land_query, send, recv, 0)
    fold_start(many, me, slice_ref, land_slice, send, recv, 1)
    fold_pass(many, me, query_ref, land_query, half_query, far_query, send, recv, 0, 6)
    fold_pass(many, me, slice_ref, land_slice, half_slice, far_slice, send, recv, 1, 7)
    own_query[...] = low16(fold_wait(many, me, half_query, far_query, send, recv, 6))
    relay_start(many, me, own_query, query_all, send, recv, 3)
    query_all[me] = own_query[...]
    own_slice[...] = fold_wait(many, me, half_slice, far_slice, send, recv, 7).astype(own_slice.dtype)
    relay_start(many, me, own_slice, slice_all, send, recv, 4)
    slice_all[me] = own_slice[...]
    relay_pass(many, me, own_query, query_all, send, recv, 3)
    relay_pass(many, me, own_slice, slice_all, send, recv, 4)
    relay_wait(many, me, own_query, query_all, send, recv, 3)

    g_vec[...] = d_mid[...]
    tops = []
    first = me * depth
    table_t[...] = jnp.zeros_like(table_t)
    rest = jnp.zeros((1, 1), jnp.float32)
    places = []
    for enc in range(2):
        low, high = (0, count_q) if enc == 0 else (count_q, count_q + count_p)
        number = many * (high - low)
        d_query = query_all[:, low:high, :].reshape(number, 128)
        x = rows_ref[:, low:high, :].reshape(number, 128).astype(jnp.float32) + place_ref[0, enc, 0:1, :]
        center = x - jnp.mean(x, -1, keepdims=True)
        rate = lax.rsqrt(jnp.mean(center * center, -1, keepdims=True) + NORM_EPS)
        scaled = center * rate
        gain = vector_row(vec_ref, enc, 0)
        a_low = low16(scaled * gain + vector_row(vec_ref, enc, 1))
        xa = xa_q if enc == 0 else xa_p
        d_h = xa[...] + dot_last(d_query, low16(attn_ref[0, enc, :, 0:128]))
        d_scaled = d_h * gain
        slope = jnp.mean(d_scaled * scaled, -1, keepdims=True)
        d_x = (d_scaled - jnp.mean(d_scaled, -1, keepdims=True) - scaled * slope) * rate
        d_place = jnp.sum(d_x, 0, keepdims=True)
        places.append(d_place)
        g_attn[enc, :, 0:128] = dot_rows(a_low, d_query)
        g_attn[enc, :, 384:512] = d_out[enc]
        spot = slice(enc, enc + 1)
        g_vec[2, spot, :] = jnp.sum(d_query.astype(jnp.float32), 0, keepdims=True)
        tops.append((jnp.sum(d_h * scaled, 0, keepdims=True), jnp.sum(d_h, 0, keepdims=True)))
        if enc == 0:
            columns = [
                part
                for peer in range(many)
                for part in (
                    raw_ref[peer, RAW_Q : RAW_Q + 16, 0:1].astype(jnp.int32)[0 : count_q // 2],
                    raw_ref[peer, RAW_Q : RAW_Q + 16, 64:65].astype(jnp.int32)[0 : count_q // 2],
                )
            ]
        else:
            columns = [raw_ref[peer, 0:count_p, 0:1].astype(jnp.int32) for peer in range(many)]
        spot = jnp.concatenate(columns, 0) - first
        spot = jnp.where(spot < depth, spot, -1)
        d_low = low16(d_x)
        wide = jnp.broadcast_to(spot, (number, CHUNK))
        for cut in range(sizes.padded // CHUNK):
            chosen = hot(wide == iota((number, CHUNK), 1) + cut * CHUNK)
            table_t[:, cut * CHUNK : (cut + 1) * CHUNK] += dot_rows(d_low, chosen)
        rest += square_sum(d_ffn[enc, 0]) + square_sum(d_ffn[enc, 1])
    for cut in range(0, depth, 128):
        top = min(cut + 128, depth)
        g_word[cut:top, :] = d_table_ref[cut:top, :] + jnp.transpose(table_t[:, cut : cut + 128])[0 : top - cut]
    tile[...] = jnp.broadcast_to(square_sum(g_word[...]), (8, 128))
    pairs = [(lambda peer: tile, scalar_all)]
    spread_start(many, me, pairs, send, recv, 5)
    scalar_all[me] = tile[...]
    relay_wait(many, me, own_slice, slice_all, send, recv, 4)
    blocks = slice_all[...].astype(jnp.float32).reshape(8, 128, 128)
    for enc in range(2):
        spot = slice(enc, enc + 1)
        g_vec[0, spot, :] = blocks[1][enc * 3 : enc * 3 + 1] + tops[enc][0]
        g_vec[1, spot, :] = blocks[1][enc * 3 + 1 : enc * 3 + 2] + tops[enc][1]
        g_vec[3, spot, :] = blocks[1][enc * 3 + 2 : enc * 3 + 3]
        g_place[enc, 0:128, :] = jnp.transpose(blocks[enc * 4])
        if enc == 0:
            g_place[enc, 128:256, :] = jnp.zeros((128, 128), jnp.float32)
        else:
            g_place[enc, 128:256, :] = jnp.transpose(blocks[enc * 4 + 1])
        g_place[enc, 0:1, :] += places[enc]
        g_attn[enc, :, 128:256] = blocks[enc * 4 + 2]
        g_attn[enc, :, 256:384] = blocks[enc * 4 + 3]
        rest += square_sum(g_place[enc]) + square_sum(g_attn[enc])
    small = jnp.sum(g_vec[...] * g_vec[...], 0)
    rest += jnp.sum(jnp.sum(small, 0, keepdims=True), 1, keepdims=True)
    for copy in loads:
        copy.wait()
    spread_wait(many, me, pairs, send, recv, 5)
    norm = jnp.sqrt(jnp.sum(scalar_all[...], 0)[0:1, 0:1] + rest)
    norm_ref[...] = jnp.broadcast_to(norm, (8, 128))
    factor = CLIP_LIMIT / jnp.maximum(norm, CLIP_LIMIT)
    grads = (g_word, g_place, g_attn, d_ffn, g_vec)

    def differ(kind, at, rows):
        weight, moment, square, anchor = (held[kind * 4 + j] for j in range(4))
        grad = grads[kind][at + (rows,)] * factor
        inner = adam(weight[(0,) + at + (rows,)], grad, moment[(0,) + at + (rows,)], square[(0,) + at + (rows,)])[2]
        mine[kind][at + (rows,)] = (anchor[at + (rows,)] - inner).astype(mine[kind].dtype)

    size = math.gcd(depth, 128)

    def table_block(step, carry):
        differ(0, (), pl.ds(pl.multiple_of(step * size, size), size))
        return carry

    lax.fori_loop(0, depth // size, table_block, 0)
    ways = []

    def hand(kind):
        copy = pltpu.make_async_remote_copy(
            src_ref=mine[kind],
            dst_ref=theirs[kind],
            send_sem=pair_send.at[kind],
            recv_sem=pair_recv.at[kind],
            device_id={"grp": other},
            device_id_type=MESH,
        )
        copy.start()
        ways.append(copy)

    hand(0)
    for kind in range(1, 5):
        for found, at in pieces_of(depth):
            if found == kind:
                differ(kind, at, slice(0, 14) if kind == 4 else slice(None))
        hand(kind)
    def join(kind, spot):
        joined[kind][spot] = mine[kind][spot].astype(jnp.float32) + theirs[kind][spot].astype(jnp.float32)

    def table_add(step, carry):
        join(0, pl.ds(pl.multiple_of(step * size, size), size))
        return carry

    ways[0].wait()
    lax.fori_loop(0, depth // size, table_add, 0)
    for kind in range(1, 5):
        ways[kind].wait()
        for found, at in pieces_of(depth):
            if found == kind:
                join(kind, at if at else slice(None))


def finish(sizes, query, slices, d_table, rows, every, xa_q, xa_p, d_out, d_ffn, d_mid, params, state):
    many = sizes.many
    both = sum(sizes.count)
    inputs = (query, slices, d_table, rows, every, xa_q, xa_p, d_out, d_ffn, d_mid) + params
    flat = tuple(state[j][kind] for kind in range(5) for j in range(4))
    shapes = [state[3][kind].shape for kind in range(5)]
    vm = pl.BlockSpec(memory_space=pltpu.VMEM)
    hbm = pl.BlockSpec(memory_space=pl.ANY)
    f32 = jnp.float32
    return pl.pallas_call(
        functools.partial(finish_kernel, sizes),
        out_shape=tuple(
            jax.ShapeDtypeStruct(shape, f32)
            for shape in [(8, 128), shapes[0], shapes[1], shapes[2], (16, 2, 128)] + shapes
        ),
        in_specs=[vm] * len(inputs) + [hbm] * 20,
        out_specs=[vm] * 10,
        scratch_shapes=[pltpu.VMEM(value.shape, f32) for value in flat]
        + [pltpu.VMEM(shape, jnp.bfloat16 if kind < 4 else f32) for kind, shape in enumerate(shapes)] * 2
        + [
            pltpu.VMEM((many, both, 128), jnp.bfloat16),
            pltpu.VMEM((many, sizes.lines, 128), sizes.kind),
            pltpu.VMEM((many, 8, 128), f32),
            pltpu.VMEM((many, both, 128), jnp.bfloat16),
            pltpu.VMEM((many, sizes.lines, 128), sizes.kind),
            pltpu.VMEM((both, 128), jnp.bfloat16),
            pltpu.VMEM((sizes.lines, 128), sizes.kind),
            pltpu.VMEM((8, 128), f32),
            pltpu.VMEM((128, sizes.padded), f32),
            pltpu.VMEM((many // NEAR, both, 128), jnp.bfloat16),
            pltpu.VMEM((many // NEAR, both, 128), jnp.bfloat16),
            pltpu.VMEM((many // NEAR, sizes.lines, 128), sizes.kind),
            pltpu.VMEM((many // NEAR, sizes.lines, 128), sizes.kind),
            pltpu.SemaphoreType.DMA((8, many)),
            pltpu.SemaphoreType.DMA((8, many)),
            pltpu.SemaphoreType.DMA((20,)),
            pltpu.SemaphoreType.DMA((5,)),
            pltpu.SemaphoreType.DMA((5,)),
        ],
        compiler_params=pltpu.CompilerParams(
            collective_id=3, has_side_effects=True, vmem_limit_bytes=VMEM_LIMIT
        ),
        name="finish",
    )(*inputs, *flat)


def output_parts(depth):
    rows = depth // 3 if depth % 24 == 0 else depth
    parts = [(0, slice(at, at + rows)) for at in range(0, depth, rows)]
    return parts + [(kind, None) for kind in (3, 2, 1, 4)]


def outputs_kernel(depth, groups, *refs):
    norm_ref, g_vec = refs[:2]
    ins = refs[2:31]
    outs = refs[31:56]
    total_ref = refs[56]
    held = refs[57:86]
    made = refs[86:111]
    load, store = refs[111:113]
    parts = output_parts(depth)
    loads, stores = ([], [])
    for number, (kind, rows) in enumerate(parts):
        group = []
        for j in range(6 if kind < 4 else 5):
            index = kind * 5 + j if j < 5 else 25 + kind
            source, target = (ins[index], held[index])
            if rows is not None:
                lead = (0,) if len(source.shape) == 3 else ()
                source, target = (source.at[lead + (rows,)], target.at[lead + (rows,)])
            copy = pltpu.make_async_copy(source, target, load.at[number, j])
            copy.start()
            group.append(copy)
        loads.append(group)
    total_ref[0] = jnp.max(norm_ref[...])
    norm = norm_ref[0:1, 0:1]
    factor = CLIP_LIMIT / jnp.maximum(norm, CLIP_LIMIT)
    grads = tuple(held[25:29]) + (g_vec,)

    def work(kind, at, rows):
        moment, square, anchor, outer, summed = (held[kind * 5 + j] for j in range(5))
        first, second, average, momentum, weight = (made[kind * 5 + j] for j in range(5))
        spot = at + (rows,)
        deep = (0,) + spot
        grad = grads[kind][spot] * factor
        first[deep] = BETA_ONE * moment[deep] + (1.0 - BETA_ONE) * grad
        second[deep] = BETA_TWO * square[deep] + (1.0 - BETA_TWO) * grad * grad
        mean = summed[spot] / groups
        speed = OUTER_MU * outer[spot] + mean
        average[spot] = mean
        momentum[spot] = speed
        weight[deep] = anchor[spot] - OUTER_RATE * (mean + OUTER_MU * speed)

    for number, (kind, rows) in enumerate(parts):
        for copy in loads[number]:
            copy.wait()
        if kind == 0:
            size = math.gcd(rows.stop - rows.start, 128)

            def table_block(step, carry):
                work(0, (), pl.ds(pl.multiple_of(rows.start + step * size, size), size))
                return carry

            lax.fori_loop(0, (rows.stop - rows.start) // size, table_block, 0)
        else:
            for found, at in pieces_of(depth):
                if found == kind:
                    work(kind, at, slice(0, 14) if kind == 4 else slice(None))
        for j in range(5):
            source, target = (made[kind * 5 + j], outs[kind * 5 + j])
            if rows is not None:
                lead = (0,) if len(source.shape) == 3 else ()
                source, target = (source.at[lead + (rows,)], target.at[lead + (rows,)])
            copy = pltpu.make_async_copy(source, target, store.at[number, j])
            copy.start()
            stores.append(copy)
    for copy in stores:
        copy.wait()


def make_outputs(norm, grads, firsts, seconds, anchors, outers, summed, groups):
    kinds = range(5)
    flat = tuple(v for kind in kinds for v in (firsts[kind], seconds[kind], anchors[kind], outers[kind], summed[kind]))
    flat += tuple(grads[:4])
    out = tuple(
        jax.ShapeDtypeStruct(shape, jnp.float32)
        for kind in kinds
        for shape in (firsts[kind].shape, firsts[kind].shape, anchors[kind].shape, anchors[kind].shape, firsts[kind].shape)
    )
    vm = pl.BlockSpec(memory_space=pltpu.VMEM)
    hbm = pl.BlockSpec(memory_space=pl.ANY)
    got = pl.pallas_call(
        functools.partial(outputs_kernel, anchors[0].shape[0], groups),
        out_shape=out + (jax.ShapeDtypeStruct((1,), jnp.float32),),
        in_specs=[vm] * 2 + [hbm] * 29,
        out_specs=[hbm] * 25 + [pl.BlockSpec(memory_space=pltpu.SMEM)],
        scratch_shapes=[pltpu.VMEM(v.shape, jnp.float32) for v in flat]
        + [pltpu.VMEM(v.shape, jnp.float32) for v in out]
        + [pltpu.SemaphoreType.DMA((7, 6)), pltpu.SemaphoreType.DMA((7, 5))],
        compiler_params=pltpu.CompilerParams(vmem_limit_bytes=VMEM_LIMIT),
        name="make_outputs",
    )(norm, grads[4], *flat)
    return [[got[kind * 5 + j] for kind in kinds] for j in range(5)], got[25]


def square_norm(values):
    center = values - jnp.mean(values, -1, keepdims=True)
    rate = lax.rsqrt(jnp.mean(center * center, -1, keepdims=True) + NORM_EPS)
    return center * rate, rate


def norm_back(d_scaled, scaled, rate):
    slope = jnp.mean(d_scaled * scaled, -1, keepdims=True)
    return (d_scaled - jnp.mean(d_scaled, -1, keepdims=True) - scaled * slope) * rate


def total_of(values):
    return jnp.sum(jnp.sum(values, 0, keepdims=True), 1, keepdims=True)


def score_terms(scores, drop, target, weight, count, axis):
    masked = jnp.where(drop, MASKED, scores)
    top = jnp.max(masked, axis, keepdims=True)
    expo = jnp.exp(masked - top)
    total = jnp.sum(expo, axis, keepdims=True)
    picked = jnp.sum(jnp.where(target, scores, 0.0), axis, keepdims=True)
    loss = total_of(weight * (top + jnp.log(total) - picked))
    grad = low16((weight / count) * (expo / total - jnp.where(target, 1.0, 0.0)))
    return grad, loss


GELU_A = math.sqrt(2.0 / math.pi)
GELU_B = 0.044715


def class_kernel(
    sizes,
    rows_ref,
    mixed_ref,
    raw_ref,
    place_ref,
    attn_ref,
    ffn_ref,
    vec_ref,
    grad_ref,
    xa_q,
    xa_p,
    d_out,
    d_ffn,
    d_mid,
    loss_ref,
    count_ref,
    cls_ref,
    scaled_a,
    rate_a,
    scaled_f,
    rate_f,
    pre_ref,
    act_ref,
    low_ref,
    flag_ref,
):
    many = sizes.many
    counts = sizes.count
    totals = (many * counts[0], many * counts[1])
    chunk = totals[0]
    parts = [(0, 0, 0)] + [(1, at, totals[0] + at) for at in range(0, totals[1], chunk)]

    def held(ref, enc, at):
        each = counts[enc]
        low = 0 if enc == 0 else counts[0]
        return ref[at // each : (at + chunk) // each, low : low + each, :].reshape(chunk, 128)

    def weights(enc):
        return (
            low16(attn_ref[0, enc, :, 384:512]),
            low16(ffn_ref[0, enc, 0]),
            low16(ffn_ref[0, enc, 1]),
        )

    for enc, at, spot in parts:
        w_out, w_up, w_down = weights(enc)
        row = functools.partial(vector_row, vec_ref, enc)
        here = slice(spot, spot + chunk)
        x = held(rows_ref, enc, at).astype(jnp.float32) + place_ref[0, enc, 0:1, :]
        h_embed = norm_rows(x, row(0), row(1))
        scaled, rate = square_norm(h_embed + (dot(held(mixed_ref, enc, at), w_out) + row(4)))
        scaled_a[here, :] = scaled
        rate_a[here, :] = jnp.broadcast_to(rate, (chunk, 128))
        h_attn = scaled * row(5) + row(6)
        h_low = low16(h_attn)
        low_ref[here, :] = h_low
        pre = dot(h_low, w_up) + jnp.concatenate([row(10), row(11), row(12), row(13)], 1)
        pre_ref[here, :] = pre
        act = low16(0.5 * pre * (1.0 + jnp.tanh(GELU_A * (pre + GELU_B * (pre * pre * pre)))))
        act_ref[here, :] = act
        scaled, rate = square_norm(h_attn + (dot_last(act, w_down) + row(7)))
        scaled_f[here, :] = scaled
        rate_f[here, :] = jnp.broadcast_to(rate, (chunk, 128))
        cls_ref[here, :] = low16(scaled * row(8) + row(9))

    every_q = cls_ref[0 : totals[0], :]
    every_p = cls_ref[totals[0] :, :]
    flag_ref[...] = jnp.zeros_like(flag_ref)
    for peer in range(many):
        flag_ref[peer : peer + 1, :] = raw_ref[peer, RAW_Q:RAW_ROWS, :].astype(jnp.float32)[8:9]
    turned = jnp.transpose(flag_ref[...])

    def column(low, each):
        tall = jnp.concatenate([turned[low : low + each]] * many, 0)
        at = iota(tall.shape, 1) == iota(tall.shape, 0) // each
        return jnp.sum(jnp.where(at, tall, 0.0), 1, keepdims=True)

    keys_q = column(0, counts[0])
    valid = column(counts[0], counts[0])
    keys_p = column(2 * counts[0], counts[1])
    hot_q = hot(jnp.broadcast_to(keys_q, (totals[0], 128)) == iota((totals[0], 128), 1).astype(jnp.float32))
    hot_p = hot(jnp.broadcast_to(keys_p, (totals[1], 128)) == iota((totals[1], 128), 1).astype(jnp.float32))
    same = dot_last(hot_q, hot_p) > 0.5
    count = jnp.maximum(total_of(valid), 1.0)
    scale = 128 ** (-0.5)
    scores = dot_last(every_q, every_p) * scale
    index_q = iota(scores.shape, 0)
    index_p = iota(scores.shape, 1)
    target_qp = index_p == 2 * index_q
    target_pq = index_p // 2 == index_q
    grad_qp, loss_qp = score_terms(scores, same & ~target_qp, target_qp, valid, count, 1)
    drop_pq = (same | (jnp.broadcast_to(valid, scores.shape) == 0.0)) & ~target_pq
    weight_p = jnp.sum(jnp.where(target_qp, jnp.broadcast_to(valid, scores.shape), 0.0), 0, keepdims=True)
    grad_pq, loss_pq = score_terms(scores, drop_pq, target_pq, weight_p, count, 0)
    loss_ref[0] = jnp.max(loss_qp + loss_pq)
    count_ref[0] = jnp.max(count)
    d_q = (dot(grad_qp, every_p) + dot(grad_pq, every_p)) * scale
    d_p = (dot_rows(grad_pq, every_q) + dot_rows(grad_qp, every_q)) * scale

    d_mid[...] = jnp.zeros_like(d_mid)
    d_out[...] = jnp.zeros_like(d_out)
    d_ffn[...] = jnp.zeros_like(d_ffn)
    for enc, at, spot in parts:
        w_out, w_up, w_down = weights(enc)
        row = functools.partial(vector_row, vec_ref, enc)
        here = slice(spot, spot + chunk)

        def add(index, values):
            d_mid[index, enc : enc + 1, :] += jnp.sum(values, 0, keepdims=True)

        d_cls = d_q if enc == 0 else d_p[at : at + chunk]
        scaled = scaled_f[here, :]
        add(8, d_cls * scaled)
        add(9, d_cls)
        d_x_ffn = norm_back(d_cls * row(8), scaled, rate_f[here, :])
        d_branch = low16(d_x_ffn)
        add(7, d_branch.astype(jnp.float32))
        d_ffn[enc, 1] += dot_rows(d_branch, act_ref[here, :])
        d_act = dot(d_branch, w_down)
        pre = pre_ref[here, :]
        square = pre * pre
        bend = jnp.tanh(GELU_A * (pre + GELU_B * (square * pre)))
        slope = 0.5 * (1.0 + bend) + (0.5 * GELU_A) * pre * (1.0 - bend * bend) * (
            1.0 + (3.0 * GELU_B) * square
        )
        d_pre = low16(slope * d_act)
        up_bias = jnp.sum(d_pre.astype(jnp.float32), 0, keepdims=True)
        for cut in range(4):
            d_mid[10 + cut, enc : enc + 1, :] += up_bias[:, cut * 128 : (cut + 1) * 128]
        d_ffn[enc, 0] += dot_rows(low_ref[here, :], d_pre)
        d_h = d_x_ffn + dot_last(d_pre, w_up)
        scaled = scaled_a[here, :]
        add(5, d_h * scaled)
        add(6, d_h)
        d_x = norm_back(d_h * row(5), scaled, rate_a[here, :])
        if enc == 0:
            xa_q[...] = d_x
        else:
            xa_p[at : at + chunk, :] = d_x
        d_proj = low16(d_x)
        add(4, d_proj.astype(jnp.float32))
        d_out[enc] += dot_rows(held(mixed_ref, enc, at), d_proj)
        d_mixed = low16(dot_last(d_proj, w_out))
        each = counts[enc]
        low = 0 if enc == 0 else counts[0]
        grad_ref[at // each : (at + chunk) // each, low : low + each, :] = d_mixed.reshape(
            chunk // each, each, 128
        )


def class_stage(sizes, rows, mixed, every, positions, attention, feedforward, vectors):
    many = sizes.many
    n_q, n_p = (many * sizes.count[0], many * sizes.count[1])
    both = n_q + n_p
    f32 = jnp.float32
    return local_call(
        functools.partial(class_kernel, sizes),
        (
            jax.ShapeDtypeStruct((many, sum(sizes.count), 128), jnp.bfloat16),
            jax.ShapeDtypeStruct((n_q, 128), f32),
            jax.ShapeDtypeStruct((n_p, 128), f32),
            jax.ShapeDtypeStruct((2, 128, 128), f32),
            jax.ShapeDtypeStruct((2, 2, 128, 512), f32),
            jax.ShapeDtypeStruct((16, 2, 128), f32),
            jax.ShapeDtypeStruct((1,), f32),
            jax.ShapeDtypeStruct((1,), f32),
        ),
        (rows, mixed, every, positions, attention, feedforward, vectors),
        [
            pltpu.VMEM((both, 128), jnp.bfloat16),
            pltpu.VMEM((both, 128), f32),
            pltpu.VMEM((both, 128), f32),
            pltpu.VMEM((both, 128), f32),
            pltpu.VMEM((both, 128), f32),
            pltpu.VMEM((both, 512), f32),
            pltpu.VMEM((both, 512), jnp.bfloat16),
            pltpu.VMEM((both, 128), jnp.bfloat16),
            pltpu.VMEM((128, 128), f32),
        ],
        "class_stage",
        smem_out=(6, 7),
    )


def class_stage_large(sizes, rows_all, mixed_all, every, positions, attention, feedforward, vectors):
    many = sizes.many
    count_q, count_p = sizes.count
    counts = sizes.count
    width = rows_all.shape[2]
    flags_all = every[:, RAW_FLAGS, :].astype(jnp.int32)
    keys_q = flags_all[:, :count_q].reshape(-1)
    valid_all = flags_all[:, count_q : 2 * count_q].reshape(-1)
    keys_p = flags_all[:, 2 * count_q : 2 * count_q + count_p].reshape(-1)
    cuts = ((0, count_q), (count_q, count_q + count_p))
    cls, class_kept, mixes = ([], [], [])
    for enc in range(2):
        low, high = cuts[enc]
        rows = rows_all[:, low:high].reshape(-1, width)
        mixed = mixed_all[:, low:high].reshape(-1, width)
        low_cls, kept_cls = class_forward(
            rows, mixed, positions[0, enc], attention[0, enc], feedforward[0, enc], vectors[0, :, enc]
        )
        cls.append(low_cls)
        class_kept.append(kept_cls)
        mixes.append(mixed)
    d_q, d_p, loss_total, count = score_stage(cls[0], cls[1], keys_q, keys_p, valid_all)
    d_cls = (d_q, d_p)
    grads, xas, outs, ffns, mids = ([], [], [], [], [])
    for enc in range(2):
        d_mixed, d_x_attn, d_w_out, d_ffn, rows_mid, d_up_bias = class_backward(
            class_kept[enc], mixes[enc], attention[0, enc], feedforward[0, enc], vectors[0, :, enc], d_cls[enc]
        )
        grads.append(d_mixed.reshape(many, counts[enc], width))
        xas.append(d_x_attn)
        outs.append(d_w_out)
        ffns.append(d_ffn)
        mid = jnp.concatenate([jnp.stack(list(rows_mid)), d_up_bias.reshape(-1, width)])
        mids.append(jnp.pad(mid, ((4, 2), (0, 0))))
    return (
        jnp.concatenate(grads, 1),
        xas[0],
        xas[1],
        jnp.stack(outs),
        jnp.stack(ffns),
        jnp.stack(mids, 1),
        loss_total.reshape(1),
        count.reshape(1),
    )


def class_forward(rows, mixed, place, attn_w, ffn_w, vec):
    width = rows.shape[1]
    h_embed = layer_norm(rows.astype(jnp.float32) + place[:1], vec[0], vec[1])
    x_attn = h_embed + (dot(mixed, low16(attn_w[:, 3 * width :])) + vec[4])
    h_attn = layer_norm(x_attn, vec[5], vec[6])
    h_low = low16(h_attn)
    pre = dot(h_low, low16(ffn_w[0])) + vec[10:].reshape(-1)
    act = low16(gelu_tanh(pre))
    x_ffn = h_attn + (dot_last(act, low16(ffn_w[1])) + vec[7])
    h_out = layer_norm(x_ffn, vec[8], vec[9])
    return low16(h_out), (x_attn, h_low, pre, act, x_ffn)


def class_backward(kept, mixed, attn_w, ffn_w, vec, d_cls):
    x_attn, h_low, pre, act, x_ffn = kept
    width = x_attn.shape[1]
    unused, out_back = jax.vjp(layer_norm, x_ffn, vec[8], vec[9])
    d_x_ffn, d_gain_two, d_shift_two = out_back(d_cls)
    d_branch = low16(d_x_ffn)
    d_down_bias = jnp.sum(d_branch, 0, dtype=jnp.float32)
    d_down = dot_rows(d_branch, act)
    d_act = dot(d_branch, low16(ffn_w[1]))
    unused, gelu_back = jax.vjp(gelu_tanh, pre)
    d_pre = low16(gelu_back(d_act)[0])
    d_up_bias = jnp.sum(d_pre, 0, dtype=jnp.float32)
    d_up = dot_rows(h_low, d_pre)
    d_h_attn = d_x_ffn + dot_last(d_pre, low16(ffn_w[0]))
    unused, attn_back = jax.vjp(layer_norm, x_attn, vec[5], vec[6])
    d_x_attn, d_gain_one, d_shift_one = attn_back(d_h_attn)
    d_proj = low16(d_x_attn)
    d_out_bias = jnp.sum(d_proj, 0, dtype=jnp.float32)
    d_w_out = dot_rows(mixed, d_proj)
    d_mixed = low16(dot_last(d_proj, low16(attn_w[:, 3 * width :])))
    rows = (d_out_bias, d_gain_one, d_shift_one, d_down_bias, d_gain_two, d_shift_two)
    return d_mixed, d_x_attn, d_w_out, jnp.stack([d_up, d_down]), rows, d_up_bias


def softmax_terms(scores, drop, target, weight, count, axis):
    masked = jnp.where(drop, MASKED, scores)
    top = jnp.max(masked, axis, keepdims=True)
    expo = jnp.exp(masked - top)
    total = jnp.sum(expo, axis, keepdims=True)
    lse = top + jnp.log(total)
    picked = jnp.sum(jnp.where(target, scores, 0.0), axis, keepdims=True)
    loss = jnp.sum(weight * (lse - picked))
    grad = low16((weight / count) * (expo / total - target.astype(jnp.float32)))
    return grad, loss


def score_stage(every_q, every_p, keys_q, keys_p, valid_q):
    count = jnp.maximum(jnp.sum(valid_q).astype(jnp.float32), 1.0)
    scale = every_q.shape[1] ** (-0.5)
    index_q = jnp.arange(every_q.shape[0])[:, None]
    index_p = jnp.arange(every_p.shape[0])[None, :]
    scores = dot_last(every_q, every_p) * scale
    same = keys_q[:, None] == keys_p[None, :]
    target_qp = index_p == 2 * index_q
    valid = valid_q.astype(jnp.float32)[:, None]
    grad_qp, loss_qp = softmax_terms(scores, same & ~target_qp, target_qp, valid, count, 1)
    target_pq = index_p // 2 == index_q
    drop_pq = (same | (valid_q[:, None] == 0)) & ~target_pq
    owner_valid = jnp.repeat(valid_q, 2)
    weight_p = jnp.where(index_p[0] % 2 == 0, owner_valid, 0).astype(jnp.float32)[None, :]
    grad_pq, loss_pq = softmax_terms(scores, drop_pq, target_pq, weight_p, count, 0)
    d_q = (dot(grad_qp, every_p) + dot(grad_pq, every_p)) * scale
    d_p = (dot_rows(grad_pq, every_q) + dot_rows(grad_qp, every_q)) * scale
    return d_q, d_p, loss_qp + loss_pq, count


def body(
    question_ids,
    passage_ids,
    question_lengths,
    passage_lengths,
    question_keys,
    passage_keys,
    question_valid,
    word_table,
    positions,
    attention,
    feedforward,
    vectors,
    word_first,
    positions_first,
    attention_first,
    feedforward_first,
    vectors_first,
    word_second,
    positions_second,
    attention_second,
    feedforward_second,
    vectors_second,
    word_anchor,
    positions_anchor,
    attention_anchor,
    feedforward_anchor,
    vectors_anchor,
    word_outer,
    positions_outer,
    attention_outer,
    feedforward_outer,
    vectors_outer,
):
    many = lax.axis_size("dp")
    count_q = question_ids.shape[0]
    count_p = passage_ids.shape[0]
    table = word_table[0]
    sizes = Sizes(many, count_q, count_p, table.shape[0])
    swap = lambda values: jnp.swapaxes(values, -3, -2)
    vectors, vectors_first, vectors_second, vectors_anchor, vectors_outer = (
        swap(v) for v in (vectors, vectors_first, vectors_second, vectors_anchor, vectors_outer)
    )
    every, class_rows, kept, entry, counted = first_stage(
        sizes,
        question_ids,
        passage_ids,
        question_lengths,
        passage_lengths,
        question_keys,
        question_valid,
        passage_keys,
        table,
        positions,
    )
    part, lse_part, query, levels = tokens_forward(
        sizes, every, class_rows, kept, entry, counted, table, positions, attention, vectors
    )
    mixed_all, lse_all = exchange_mixed(sizes, part, lse_part)
    stage = class_stage if many * count_q <= 512 else class_stage_large
    grad_all, xa_q, xa_p, d_out, d_ffn, d_mid, loss_total, count = stage(
        sizes, class_rows, mixed_all, every, positions, attention, feedforward, vectors
    )
    d_query, d_table, slices = tokens_backward(
        sizes, levels, every, query, mixed_all, lse_all, grad_all, kept, entry, table, positions, attention, vectors
    )
    weights = (word_table, positions, attention, feedforward, vectors)
    firsts = (word_first, positions_first, attention_first, feedforward_first, vectors_first)
    seconds = (word_second, positions_second, attention_second, feedforward_second, vectors_second)
    anchors = (word_anchor, positions_anchor, attention_anchor, feedforward_anchor, vectors_anchor)
    outers = (word_outer, positions_outer, attention_outer, feedforward_outer, vectors_outer)
    done = finish(
        sizes,
        d_query,
        slices.reshape(many, sizes.lines, 128),
        d_table,
        class_rows,
        every,
        xa_q,
        xa_p,
        d_out,
        d_ffn,
        d_mid,
        (positions, attention, vectors),
        (weights, firsts, seconds, anchors),
    )
    norm = done[0]
    grads = (done[1], done[2], done[3], d_ffn, done[4])
    made, norm = make_outputs(
        norm, grads, firsts, seconds, anchors, outers, done[5:10], lax.axis_size("grp")
    )
    first_new, second_new, averages, outer_next, weight_next = (
        part[:4] + [swap(part[4])] for part in made
    )
    return (
        loss_total.reshape(1),
        count.reshape(1),
        norm.reshape(1),
        first_new[0],
        first_new[1],
        first_new[2],
        first_new[3],
        first_new[4],
        second_new[0],
        second_new[1],
        second_new[2],
        second_new[3],
        second_new[4],
        averages[0],
        averages[1],
        averages[2],
        averages[3],
        averages[4],
        outer_next[0],
        outer_next[1],
        outer_next[2],
        outer_next[3],
        outer_next[4],
        weight_next[0],
        weight_next[1],
        weight_next[2],
        weight_next[3],
        weight_next[4],
    )


def solution(mesh):
    placed = (
        P(("grp", "dp"), None),
        P(("grp", "dp"), None),
        P(("grp", "dp")),
        P(("grp", "dp")),
        P(("grp", "dp")),
        P(("grp", "dp")),
        P(("grp", "dp")),
        P("grp", "dp", None),
        P("grp", None, None, None),
        P("grp", None, None, None),
        P("grp", None, None, None, None),
        P("grp", None, None, None),
        P("grp", "dp", None),
        P("grp", None, None, None),
        P("grp", None, None, None),
        P("grp", None, None, None, None),
        P("grp", None, None, None),
        P("grp", "dp", None),
        P("grp", None, None, None),
        P("grp", None, None, None),
        P("grp", None, None, None, None),
        P("grp", None, None, None),
        P("dp", None),
        P(),
        P(),
        P(),
        P(),
        P("dp", None),
        P(),
        P(),
        P(),
        P(),
    )
    return jax.shard_map(
        body,
        mesh=mesh,
        in_specs=placed,
        out_specs=(
            P("grp"),
            P("grp"),
            P("grp"),
            P("grp", "dp", None),
            P("grp", None, None, None),
            P("grp", None, None, None),
            P("grp", None, None, None, None),
            P("grp", None, None, None),
            P("grp", "dp", None),
            P("grp", None, None, None),
            P("grp", None, None, None),
            P("grp", None, None, None, None),
            P("grp", None, None, None),
            P("dp", None),
            P(),
            P(),
            P(),
            P(),
            P("dp", None),
            P(),
            P(),
            P(),
            P(),
            P("grp", "dp", None),
            P("grp", None, None, None),
            P("grp", None, None, None),
            P("grp", None, None, None, None),
            P("grp", None, None, None),
        ),
        check_vma=False,
    )
```

```python
import functools
import math

import jax
import jax.numpy as jnp
from jax import lax
from jax.experimental import pallas as pl
from jax.experimental.pallas import tpu as pltpu
from jax.sharding import PartitionSpec as P

HEAD = 64
STEP = 5


NORM_EPS = 1e-05
MASKED = -1000000000.0
BETA_ONE = 0.9
BETA_TWO = 0.999
INNER_RATE = 0.05
WEIGHT_DECAY = 0.01
ADAM_EPS = 1e-08
CLIP_LIMIT = 0.01
OUTER_RATE = 0.7
OUTER_MU = 0.9
CONTRACT_ROWS = (((0,), (0,)), ((), ()))
CONTRACT_LAST = (((1,), (1,)), ((), ()))


def layer_norm(values, gain, shift):
    center = values - jnp.mean(values, -1, keepdims=True)
    spread = jnp.mean(center * center, -1, keepdims=True)
    return center * lax.rsqrt(spread + NORM_EPS) * gain + shift


def gelu_tanh(values):
    return jax.nn.gelu(values, approximate=True)


def low16(values):
    return values.astype(jnp.bfloat16)


NEG = -1e30
MESH = pl.DeviceIdType.MESH
VMEM_LIMIT = 60 * 1024 * 1024
WAYS = 4
SLOTS = 128
SPAN = WAYS * SLOTS
CHUNK = 256
UNROLL = 4
RAW_Q = 64
RAW_FLAGS = 72
RAW_ROWS = 80


def greet_all(many):
    me = lax.axis_index("dp")
    barrier = pltpu.get_barrier_semaphore()

    def greet(step, carry):
        peer = lax.rem(me + step, many)
        pl.semaphore_signal(barrier, inc=1, device_id={"dp": peer}, device_id_type=MESH)
        return carry

    lax.fori_loop(1, many, greet, 0)
    return me


def enter(many):
    me = greet_all(many)
    pl.semaphore_wait(pltpu.get_barrier_semaphore(), many - 1)
    return me


def copy_to(peer, src, dst, send, recv):
    return pltpu.make_async_remote_copy(
        src_ref=src,
        dst_ref=dst,
        send_sem=send,
        recv_sem=recv,
        device_id={"dp": peer},
        device_id_type=MESH,
    )


def spread_start(many, me, pairs, send, recv, slot):
    def step_start(step, carry):
        peer = lax.rem(me + step, many)
        for index, (source, landing) in enumerate(pairs):
            copy_to(
                peer,
                source(peer),
                landing.at[me],
                send.at[slot + index, peer],
                recv.at[slot + index, me],
            ).start()
        return carry

    lax.fori_loop(1, many, step_start, 0)


def spread_wait(many, me, pairs, send, recv, slot):
    def step_wait(step, carry):
        peer = lax.rem(me + step, many)
        for index, (source, landing) in enumerate(pairs):
            copy = copy_to(
                peer,
                source(peer),
                landing.at[peer],
                send.at[slot + index, peer],
                recv.at[slot + index, peer],
            )
            copy.wait_recv()
            copy.wait_send()
        return carry

    lax.fori_loop(1, many, step_wait, 0)


NEAR = 4


def place_of(many, me, far, near):
    row = lax.rem(me // NEAR + far, many // NEAR)
    return row * NEAR + lax.rem(lax.rem(me, NEAR) + near, NEAR)


def relay_start(many, me, source, landing, send, recv, slot):
    for near in range(NEAR):
        count = many // NEAR if near == 0 else 1

        def one(far, carry):
            peer = place_of(many, me, far, near)
            copy_to(peer, source, landing.at[me], send.at[slot, peer], recv.at[slot, me]).start()
            return carry

        lax.fori_loop(1 if near == 0 else 0, count, one, 0)


def relay_pass(many, me, source, landing, send, recv, slot):
    def one(far, carry):
        block = place_of(many, me, far, 0)
        copy_to(block, source, landing.at[block], send.at[slot, block], recv.at[slot, block]).wait_recv()
        for near in range(1, NEAR):
            peer = place_of(many, me, 0, near)
            key = place_of(many, me, far, near)
            copy_to(peer, landing.at[block], landing.at[block], send.at[slot, key], recv.at[slot, block]).start()
        return carry

    lax.fori_loop(1, many // NEAR, one, 0)


def relay_wait(many, me, source, landing, send, recv, slot):
    def one(far, carry):
        for near in range(NEAR):
            key = place_of(many, me, far, near)
            copy = copy_to(key, source, landing.at[key], send.at[slot, key], recv.at[slot, key])

            @pl.when((far > 0) | (near > 0))
            def _():
                copy.wait_send()

            if near > 0:
                copy.wait_recv()
        return carry

    lax.fori_loop(0, many // NEAR, one, 0)


def fold_start(many, me, blocks, landing, send, recv, slot):
    def one(row, carry):
        for near in range(1, NEAR):
            peer = place_of(many, me, 0, near)
            target = row * NEAR + lax.rem(peer, NEAR)
            copy_to(
                peer,
                blocks.at[target],
                landing.at[row * NEAR + lax.rem(me, NEAR)],
                send.at[slot, target],
                recv.at[slot, row * NEAR + lax.rem(me, NEAR)],
            ).start()
        mine = row * NEAR + lax.rem(me, NEAR)
        landing[mine] = blocks[mine]
        return carry

    lax.fori_loop(0, many // NEAR, one, 0)


def fold_pass(many, me, blocks, landing, halves, second, send, recv, slot, later):
    def one(row, carry):
        for near in range(1, NEAR):
            key = row * NEAR + lax.rem(place_of(many, me, 0, near), NEAR)
            copy = copy_to(
                place_of(many, me, 0, near), blocks.at[key], landing.at[key], send.at[slot, key], recv.at[slot, key]
            )
            copy.wait_recv()
            copy.wait_send()
        return carry

    lax.fori_loop(0, many // NEAR, one, 0)

    def two(far, carry):
        peer = place_of(many, me, far, 0)
        row = peer // NEAR
        total = landing[row * NEAR].astype(jnp.float32)
        for near in range(1, NEAR):
            total += landing[row * NEAR + near].astype(jnp.float32)
        halves[row] = total.astype(halves.dtype)

        @pl.when(far > 0)
        def _():
            copy_to(peer, halves.at[row], second.at[me // NEAR], send.at[later, row], recv.at[later, me // NEAR]).start()

        @pl.when(far == 0)
        def _():
            second[row] = halves[row]

        return carry

    lax.fori_loop(0, many // NEAR, two, 0)


def fold_wait(many, me, halves, second, send, recv, later):
    def one(far, carry):
        peer = place_of(many, me, far, 0)
        row = peer // NEAR
        copy = copy_to(peer, halves.at[row], second.at[row], send.at[later, row], recv.at[later, row])
        copy.wait_recv()
        copy.wait_send()
        return carry

    lax.fori_loop(1, many // NEAR, one, 0)
    return jnp.sum(second[...].astype(jnp.float32), 0)


def dot(left, right):
    return jnp.dot(left, right, preferred_element_type=jnp.float32)


def dot_rows(left, right):
    return lax.dot_general(left, right, CONTRACT_ROWS, preferred_element_type=jnp.float32)


def dot_last(left, right):
    return lax.dot_general(left, right, CONTRACT_LAST, preferred_element_type=jnp.float32)


def iota(shape, axis):
    return lax.broadcasted_iota(jnp.int32, shape, axis)


def hot(mask):
    return jnp.where(mask, 1.0, 0.0).astype(jnp.bfloat16)


def first_kernel(
    sizes,
    question_ref,
    passage_ref,
    length_q,
    length_p,
    key_q,
    valid_q,
    key_p,
    table_ref,
    place_ref,
    every_ref,
    rows_ref,
    kept_ref,
    entry_ref,
    count_ref,
    stage,
    raw,
    ask,
    asks,
    low_ref,
    offer,
    landed,
    own,
    table_t,
    place_t,
    send,
    recv,
):
    many = sizes.many
    count_q, count_p = sizes.count
    each = count_q + count_p
    depth = sizes.depth
    half = count_q // 2
    me = greet_all(many)
    lane = iota((1, 128), 1)
    for seq in range(count_p):
        stop = length_p[seq]
        stage[seq : seq + 1, :] = jnp.where(lane < stop, passage_ref[seq : seq + 1, 0:128], -1)
        stage[count_p + seq : count_p + seq + 1, :] = jnp.where(
            lane + 128 < stop, passage_ref[seq : seq + 1, 128:256], -1
        )
    both = jnp.concatenate([question_ref[0:half, :], question_ref[half:count_q, :]], 1)
    for seq in range(half):
        stop = jnp.where(lane < 64, length_q[seq], length_q[half + seq] + 64)
        stage[RAW_Q + seq : RAW_Q + seq + 1, :] = jnp.where(lane < stop, both[seq : seq + 1], -1)
    flags = jnp.zeros((1, 128), jnp.int32)
    for spot in range(count_q):
        flags = jnp.where(lane == spot, key_q[spot], flags)
        flags = jnp.where(lane == count_q + spot, valid_q[spot], flags)
    for spot in range(count_p):
        flags = jnp.where(lane == 2 * count_q + spot, key_p[spot], flags)
    stage[RAW_FLAGS:RAW_ROWS, :] = jnp.broadcast_to(flags, (8, 128))
    raw[...] = stage[...].astype(jnp.int16)
    heads = jnp.concatenate([question_ref[:, 0:1], passage_ref[:, 0:1]], 0)
    diagonal = iota((each, 128), 0) == iota((each, 128), 1)
    heads = jnp.sum(jnp.where(diagonal, jnp.broadcast_to(heads, (each, 128)), 0), 0, keepdims=True)
    ask[...] = jnp.broadcast_to(heads, (8, 128))
    pl.semaphore_wait(pltpu.get_barrier_semaphore(), many - 1)
    ask_pairs = [(lambda peer: ask, asks)]
    spread_start(many, me, ask_pairs, send, recv, 0)
    relay_start(many, me, raw, every_ref, send, recv, 1)
    asks[me] = ask[...]
    every_ref[me] = raw[...]
    padded = sizes.padded
    if padded > depth:
        low_ref[...] = jnp.zeros_like(low_ref)
    low_ref[0:depth, :] = low16(table_ref[...])
    first = me * depth
    block = math.gcd(many, 16)
    spread_wait(many, me, ask_pairs, send, recv, 0)
    relay_pass(many, me, raw, every_ref, send, recv, 1)

    def pick(step, carry):
        found = []
        for i in range(block):
            line = jnp.broadcast_to(asks[step * block + i][0:1, :].astype(jnp.float32), (each, 128))
            found.append(jnp.sum(jnp.where(diagonal, line, 0.0), 1, keepdims=True))
        place = jnp.concatenate(found, 0).astype(jnp.int32) - first
        spot = jnp.where((place >= 0) & (place < depth), place, -1)
        number = spot.shape[0]
        total = jnp.zeros((number, 128), jnp.float32)
        wide = jnp.broadcast_to(spot, (number, CHUNK))
        for at in range(padded // CHUNK):
            chosen = hot(wide == iota((number, CHUNK), 1) + at * CHUNK)
            total += dot(chosen, low_ref[at * CHUNK : (at + 1) * CHUNK, :])
        for i in range(block):
            offer[step * block + i] = low16(total[i * each : (i + 1) * each])
        return carry

    lax.fori_loop(0, many // block, pick, 0)
    offer_pairs = [(lambda peer: offer.at[peer], landed)]
    spread_start(many, me, offer_pairs, send, recv, 2)
    landed[me] = offer[me]
    if sizes.keep:
        prepare_tokens(sizes, table_ref, place_ref, table_t, place_t)
    relay_wait(many, me, raw, every_ref, send, recv, 1)

    row_pairs = [(lambda peer: own, rows_ref)]

    def send_rows():
        spread_wait(many, me, offer_pairs, send, recv, 2)
        own[...] = low16(jnp.sum(landed[...].astype(jnp.float32), 0))
        spread_start(many, me, row_pairs, send, recv, 3)
        rows_ref[me] = own[...]

    def spans_of(enc, count):
        def spans(turn, count):
            if enc == 1:
                pl.when(turn == 1)(send_rows)
            steps = [turn * sizes.unroll[enc] + u for u in range(sizes.unroll[enc])]
            packed = [pack_span(sizes, enc, s, 0, first, every_ref) for s in steps]
            found = [gather_span(sizes, enc, part[0], table_t, place_t) for part in packed]
            for part in packed:
                count = jnp.maximum(count, part[1])
            for u, s in enumerate(steps):
                at = s if enc == 0 else sizes.steps[0] + s
                kept_ref[at, 0:128, :] = found[u][0]
                kept_ref[at, 128:129, :] = found[u][1]
                entry_ref[at, 0:1, :] = packed[u][0]
            return count

        return lax.fori_loop(0, sizes.steps[enc] // sizes.unroll[enc], spans, count)

    count = jnp.zeros((8, 128), jnp.float32)
    if sizes.keep:
        count = spans_of(1, spans_of(0, count))
    else:
        send_rows()
    count_ref[...] = count
    spread_wait(many, me, row_pairs, send, recv, 3)


def first_stage(sizes, ids_q, ids_p, length_q, length_p, key_q, valid_q, key_p, table, positions):
    many = sizes.many
    padded = sizes.padded
    both = sum(sizes.count)
    vm = pl.BlockSpec(memory_space=pltpu.VMEM)
    sm = pl.BlockSpec(memory_space=pltpu.SMEM)
    kept = sizes.spans if sizes.keep else 1
    return pl.pallas_call(
        functools.partial(first_kernel, sizes),
        out_shape=(
            jax.ShapeDtypeStruct((many, RAW_ROWS, 128), jnp.int16),
            jax.ShapeDtypeStruct((many, both, 128), jnp.bfloat16),
            jax.ShapeDtypeStruct((kept, 136, SPAN), jnp.float32),
            jax.ShapeDtypeStruct((kept, 8, SPAN), jnp.int32),
            jax.ShapeDtypeStruct((8, 128), jnp.float32),
        ),
        in_specs=[vm, vm, sm, sm, sm, sm, sm, vm, vm],
        out_specs=[vm] * 5,
        scratch_shapes=[
            pltpu.VMEM((RAW_ROWS, 128), jnp.int32),
            pltpu.VMEM((RAW_ROWS, 128), jnp.int16),
            pltpu.VMEM((8, 128), jnp.int32),
            pltpu.VMEM((many, 8, 128), jnp.int32),
            pltpu.VMEM((padded, 128), jnp.bfloat16),
            pltpu.VMEM((many, both, 128), jnp.bfloat16),
            pltpu.VMEM((many, both, 128), jnp.bfloat16),
            pltpu.VMEM((both, 128), jnp.bfloat16),
            pltpu.VMEM((128, padded), jnp.bfloat16),
            pltpu.VMEM((2, 2, 128, CHUNK), jnp.bfloat16),
            pltpu.SemaphoreType.DMA((4, many)),
            pltpu.SemaphoreType.DMA((4, many)),
        ],
        compiler_params=pltpu.CompilerParams(
            collective_id=1, has_side_effects=True, vmem_limit_bytes=VMEM_LIMIT
        ),
        name="first_stage",
    )(ids_q, ids_p, length_q, length_p, key_q, valid_q, key_p, table, positions)


def norm_rows(values, gain, shift):
    center = values - jnp.mean(values, -1, keepdims=True)
    spread = jnp.mean(center * center, -1, keepdims=True)
    return center * lax.rsqrt(spread + NORM_EPS) * gain + shift


def two_heads(values):
    lane = iota(values.shape, 1)
    low = jnp.where(lane < HEAD, values, jnp.zeros_like(values))
    high = jnp.where(lane >= HEAD, values, jnp.zeros_like(values))
    return jnp.concatenate([low, high], 0)


def merge_heads(both):
    half = both.shape[0] // 2
    lane = iota((half, both.shape[1]), 1)
    return jnp.where(lane < HEAD, both[:half], both[half:])


class Sizes:
    def __init__(self, many, count_q, count_p, depth):
        self.many = many
        self.count = (count_q, count_p)
        self.depth = depth
        self.padded = -(-depth // CHUNK) * CHUNK
        self.steps = (many // (2 * WAYS), many)
        self.unroll = tuple(math.gcd(UNROLL, step) for step in self.steps)
        self.spans = self.steps[0] + self.steps[1]
        self.devices = (2 * WAYS, 1)
        self.queries = (2 * WAYS * count_q, count_p)
        assert self.steps[1] // self.unroll[1] > 1
        self.lines = 1024 // many
        self.kind = jnp.bfloat16 if self.lines % 16 == 0 else jnp.float32
        self.keep = self.spans * 136 * SPAN * 4 <= 8 * 1024 * 1024


def vector_row(vec_ref, enc, row):
    return vec_ref[0, row, enc : enc + 1, :]


def prepare_tokens(sizes, table_ref, place_ref, table_t, place_t):
    depth = sizes.depth
    if sizes.padded > depth:
        table_t[...] = jnp.zeros_like(table_t)

    def turn(step, carry):
        spot = pl.ds(pl.multiple_of(step * 128, 128), 128)
        table_t[:, spot] = low16(jnp.transpose(table_ref[spot, :]))
        return carry

    whole = depth // 128
    lax.fori_loop(0, whole, turn, 0)
    rest = depth - whole * 128
    if rest:
        piece = jnp.concatenate([table_ref[whole * 128 :, :], jnp.zeros((128 - rest, 128), jnp.float32)], 0)
        table_t[:, whole * 128 : (whole + 1) * 128] = low16(jnp.transpose(piece))

    def turn_place(step, carry):
        enc, cut = (step // 2, step % 2)
        spot = pl.ds(pl.multiple_of(cut * 128, 128), 128)
        turned = jnp.transpose(place_ref[0, enc, spot, :])
        high = low16(turned)
        place_t[enc, 0, :, spot] = high
        place_t[enc, 1, :, spot] = low16(turned - high.astype(jnp.float32))
        return carry

    lax.fori_loop(0, 4, turn_place, 0)


def prepare_weights(attn_ref, vec_ref, w_kv, vec_t):
    for enc in range(2):
        for cut in range(2):
            w_kv[enc, cut * 128 : (cut + 1) * 128, :] = low16(
                jnp.transpose(attn_ref[0, enc, :, (cut + 1) * 128 : (cut + 2) * 128])
            )
        rows = [vector_row(vec_ref, enc, row) for row in range(4)]
        rows = jnp.concatenate(rows + [jnp.zeros((124, 128), jnp.float32)], 0)
        vec_t[enc] = jnp.transpose(rows)


def lane_pick(values, lanes):
    return jnp.take_along_axis(values, lanes, axis=1, mode="promise_in_bounds")


def pack_span(sizes, enc, step, level, first, raw_ref):
    if enc == 1:
        ids = raw_ref[step, 0:RAW_Q, :].astype(jnp.int32)
    else:
        ids = jnp.concatenate(
            [
                raw_ref[step * 8 + i, RAW_Q:RAW_ROWS, :].astype(jnp.int32)[0:8]
                for i in range(8)
            ],
            0,
        )
    place = ids - first
    owned = (place >= 0) & (place < sizes.depth)
    flag = hot(owned)
    inside = dot(flag, hot(iota((128, 128), 0) <= iota((128, 128), 1))).astype(jnp.int32)
    total = dot(flag, jnp.ones((128, 128), jnp.bfloat16))
    before = dot(hot(iota((64, 64), 1) < iota((64, 64), 0)), low16(total))
    start = before.astype(jnp.int32)
    stop = (before + total).astype(jnp.int32)
    line = iota((64, 128), 0)
    turn = iota((64, 128), 1)
    lane = jnp.zeros((64, 128), jnp.int32)
    for jump in (64, 32, 16, 8, 4, 2, 1):
        seen = lane_pick(inside, lane + (jump - 1))
        lane = jnp.where(seen <= turn, lane + jump, lane)
    row = lane_pick(place, lane)
    if enc == 1:
        where = (line >> 5) * 128 + lane
        seq = (line & 31) + 1
    else:
        where = lane & 63
        seq = (line >> 3) * sizes.count[0] + (lane >> 6) * 8 + (line & 7) + 1
    code = lane_pick((row << 16) + (where << 8) + seq, (turn - start) & 127)
    codes = []
    for window in range(WAYS):
        slot = turn + (window * SLOTS + level * SPAN)
        kept = jnp.where((slot >= start) & (slot < stop), code, 0)
        codes.append(jnp.sum(kept, 0, keepdims=True))
    return jnp.concatenate(codes, 1), (before + total)[56:64]


def gather_span(sizes, enc, code, table_t, place_t, short=False):
    rows = code >> 16
    where = (code >> 8) & 255
    x = jnp.zeros((128, SPAN), jnp.float32)
    wide = jnp.broadcast_to(rows, (CHUNK, SPAN))

    def add(cut, x):
        spot = pl.ds(pl.multiple_of(cut * CHUNK, CHUNK), CHUNK)
        return x + dot(table_t[:, spot], hot(wide == iota((CHUNK, SPAN), 0) + cut * CHUNK))

    x = lax.fori_loop(0, sizes.padded // CHUNK, add, x, unroll=not short)
    chosen = hot(jnp.broadcast_to(where, (CHUNK, SPAN)) == iota((CHUNK, SPAN), 0))
    x += dot(place_t[enc, 0], chosen) + dot(place_t[enc, 1], chosen)
    center = x - jnp.mean(x, 0, keepdims=True)
    rate = lax.rsqrt(jnp.mean(center * center, 0, keepdims=True) + NORM_EPS)
    return center * rate, rate


def project(enc, scaled, vec_t, w_kv):
    a_t = low16(scaled * vec_t[enc, :, 0:1] + vec_t[enc, :, 1:2])
    kv = dot(w_kv[enc], a_t)
    keys_t = low16(kv[:128])
    values_t = low16(kv[128:] + vec_t[enc, :, 3:4])
    return a_t, keys_t, values_t


def own_slots(code, number):
    line = iota((2 * number, SPAN), 0)
    line = jnp.where(line >= number, line - number, line)
    return line == (code & 255) - 1


def forward_kernel(
    sizes,
    raw_ref,
    rows_ref,
    kept_hbm,
    entry_hbm,
    count_ref,
    table_ref,
    place_ref,
    attn_ref,
    vec_ref,
    out_ref,
    lse_ref,
    query_ref,
    levels_ref,
    table_t,
    place_t,
    w_kv,
    vec_t,
    query_q,
    total_q,
    top_q,
    mass_q,
    total_p,
    top_p,
    mass_p,
    kept_ref,
    entry_ref,
    load,
):
    loads = load_kept(sizes, kept_hbm, entry_hbm, kept_ref, entry_ref, load)
    first = lax.axis_index("dp") * sizes.depth
    count_q, count_p = sizes.count
    prepare_weights(attn_ref, vec_ref, w_kv, vec_t)
    begin = 1 if sizes.keep else 0
    count = count_ref[...]
    block = math.gcd(sizes.many, 16)
    for enc in range(2):
        low, high = (0, count_q) if enc == 0 else (count_q, count_q + count_p)
        w_q = low16(attn_ref[0, enc, :, 0:128])

        def ask(step, carry):
            spot = pl.ds(step * block, block)
            held = rows_ref[spot, low:high, :].reshape(block * (high - low), 128)
            x = held.astype(jnp.float32) + place_ref[0, enc, 0:1, :]
            h = norm_rows(x, vector_row(vec_ref, enc, 0), vector_row(vec_ref, enc, 1))
            query = low16(dot(low16(h), w_q) + vector_row(vec_ref, enc, 2))
            query_ref[spot, low:high, :] = query.reshape(block, high - low, 128)
            if enc == 0:
                for half in range(block // 8):
                    query_q[step * (block // 8) + half] = query[half * 8 * count_q : (half + 1) * 8 * count_q]
            return carry

        lax.fori_loop(0, sizes.many // block, ask, 0)
    states = ((total_q, top_q, mass_q), (total_p, top_p, mass_p))
    lse_ref[...] = jnp.full_like(lse_ref, NEG)

    def close(enc, step, total, top, mass):
        some = mass > 0.0
        safe = jnp.where(some, mass, 1.0)
        mixed = merge_heads(total / safe)
        lse = jnp.where(some, top + jnp.log(safe), NEG)
        if enc == 1:
            out_ref[step, count_q:, :] = low16(mixed)
            at = iota(lse.shape, 0) == iota(lse.shape, 1)
            lse_ref[step, 0:1, :] = jnp.sum(jnp.where(at, lse, 0.0), 0, keepdims=True)
        else:
            half = lse.shape[0] // 2
            row = iota((count_q, 128), 0)
            lane = iota((count_q, 128), 1)
            for i in range(8):
                spot = slice(i * count_q, (i + 1) * count_q)
                out_ref[step * 8 + i, 0:count_q, :] = low16(mixed[spot])
                line = jnp.where(lane == row, lse[spot], 0.0) + jnp.where(
                    lane == row + count_q, lse[half + i * count_q : half + (i + 1) * count_q], 0.0
                )
                lse_ref[step * 8 + i, 1:2, :] = jnp.sum(line, 0, keepdims=True)

    def attend(enc, steps, codes, scaleds, olds):
        queries = [query_q[s] if enc == 0 else query_ref[s, count_q:, :] for s in steps]
        made = [project(enc, scaled, vec_t, w_kv) for scaled in scaleds]
        scores = [dot(two_heads(query), part[1]) * HEAD ** (-0.5) for query, part in zip(queries, made)]
        news = []
        for u, score in enumerate(scores):
            mine = own_slots(codes[u], queries[u].shape[0])
            score = jnp.where(mine, score, NEG)
            new = jnp.max(score, 1, keepdims=True)
            if olds is not None:
                new = jnp.maximum(olds[u][1][:, 0:1], new)
            expo = jnp.where(mine, jnp.exp(score - new), 0.0)
            total = dot_last(low16(expo), made[u][2])
            mass = jnp.sum(expo, 1, keepdims=True)
            if olds is not None:
                fade = jnp.exp(olds[u][1] - new)
                total = olds[u][0] * fade + total
                mass = olds[u][2] * fade + mass
            wide = (score.shape[0], 128)
            news.append((total, jnp.broadcast_to(new, wide), jnp.broadcast_to(mass, wide)))
        for u, s in enumerate(steps):
            for ref, value in zip(states[enc], news[u]):
                ref[s] = value
        return news

    for enc in range(2):
        if sizes.keep:
            for copy in loads[2 * enc : 2 * enc + 2]:
                copy.wait()

            def kept_spans(turn, carry):
                steps = [turn * sizes.unroll[enc] + u for u in range(sizes.unroll[enc])]
                ats = [s if enc == 0 else sizes.steps[0] + s for s in steps]
                news = attend(
                    enc, steps, [entry_ref[at, 0:1, :] for at in ats], [kept_ref[at, 0:128, :] for at in ats], None
                )
                for s, new in zip(steps, news):
                    close(enc, s, *new)
                return carry

            lax.fori_loop(0, sizes.steps[enc] // sizes.unroll[enc], kept_spans, 0)
        else:
            total, top, mass = states[enc]
            total[...] = jnp.zeros_like(total)
            mass[...] = jnp.zeros_like(mass)
            top[...] = jnp.full_like(top, NEG)

    def needed(count):
        return jnp.maximum((jnp.max(count).astype(jnp.int32) + SPAN - 1) // SPAN, 1)

    start = needed(count)
    levels_ref[0] = start

    @pl.when(start > begin)
    def _():
        prepare_tokens(sizes, table_ref, place_ref, table_t, place_t)

        def one_level(state):
            level, unused, count = state
            for enc in range(2):

                def one_span(step, count):
                    code, found = pack_span(sizes, enc, step, level, first, raw_ref)
                    scaled = gather_span(sizes, enc, code, table_t, place_t, True)[0]
                    attend(enc, [step], [code], [scaled], [tuple(ref[step] for ref in states[enc])])
                    return jnp.maximum(count, found)

                count = lax.fori_loop(0, sizes.steps[enc], one_span, count)
            return level + 1, needed(count), count

        if sizes.keep:
            lax.fori_loop(
                begin, start, lambda level, carry: one_level((level, carry, count))[1], jnp.int32(0)
            )
        else:
            last = lax.while_loop(
                lambda state: state[0] < state[1], one_level, (jnp.int32(begin), start, count)
            )
            levels_ref[0] = last[1]
        for enc in range(2):

            def close_span(step, carry):
                close(enc, step, *(ref[step] for ref in states[enc]))
                return carry

            lax.fori_loop(0, sizes.steps[enc], close_span, 0)


def load_kept(sizes, kept_hbm, entry_hbm, kept_ref, entry_ref, load):
    if not sizes.keep:
        return []
    copies = []
    for enc, rows in enumerate((slice(0, sizes.steps[0]), slice(sizes.steps[0], sizes.spans))):
        for j, (source, target) in enumerate(((kept_hbm, kept_ref), (entry_hbm, entry_ref))):
            copy = pltpu.make_async_copy(source.at[rows], target.at[rows], load.at[enc, j])
            copy.start()
            copies.append(copy)
    return copies


def kept_scratch(sizes):
    kept = sizes.spans if sizes.keep else 1
    return [
        pltpu.VMEM((kept, 136, SPAN), jnp.float32),
        pltpu.VMEM((kept, 8, SPAN), jnp.int32),
        pltpu.SemaphoreType.DMA((2, 2)),
    ]


def token_scratch(sizes):
    return [
        pltpu.VMEM((128, sizes.padded), jnp.bfloat16),
        pltpu.VMEM((2, 2, 128, CHUNK), jnp.bfloat16),
        pltpu.VMEM((2, 256, 128), jnp.bfloat16),
        pltpu.VMEM((2, 128, 128), jnp.float32),
    ]


def local_call(kernel, out_shape, inputs, scratch, name, smem_in=(), smem_out=(), any_in=()):
    vm = pl.BlockSpec(memory_space=pltpu.VMEM)
    sm = pl.BlockSpec(memory_space=pltpu.SMEM)
    hbm = pl.BlockSpec(memory_space=pl.ANY)
    return pl.pallas_call(
        kernel,
        out_shape=out_shape,
        in_specs=[sm if i in smem_in else hbm if i in any_in else vm for i in range(len(inputs))],
        out_specs=[sm if i in smem_out else vm for i in range(len(out_shape))],
        scratch_shapes=scratch,
        compiler_params=pltpu.CompilerParams(vmem_limit_bytes=VMEM_LIMIT),
        name=name,
    )(*inputs)


def tokens_forward(sizes, every, rows, kept, entry, counted, table, positions, attention, vectors):
    many = sizes.many
    both = sum(sizes.count)
    state = []
    for enc in range(2):
        tall = 2 * sizes.queries[enc]
        state += [pltpu.VMEM((sizes.steps[enc], tall, 128), jnp.float32)] * 3
    return local_call(
        functools.partial(forward_kernel, sizes),
        (
            jax.ShapeDtypeStruct((many, both, 128), jnp.bfloat16),
            jax.ShapeDtypeStruct((many, 2, 128), jnp.float32),
            jax.ShapeDtypeStruct((many, both, 128), jnp.bfloat16),
            jax.ShapeDtypeStruct((1,), jnp.int32),
        ),
        (every, rows, kept, entry, counted, table, positions, attention, vectors),
        token_scratch(sizes)
        + [pltpu.VMEM((sizes.steps[0], sizes.queries[0], 128), jnp.bfloat16)]
        + state
        + kept_scratch(sizes),
        "tokens_forward",
        smem_out=(3,),
        any_in=(2, 3),
    )


def mix_kernel(
    many, count_q, part_ref, lse_ref, mixed_ref, total_ref, landed, landed_lse, own, own_lse, send, recv
):
    me = enter(many)
    pairs = [
        (lambda peer: part_ref.at[peer], landed),
        (lambda peer: lse_ref.at[peer], landed_lse),
    ]
    spread_start(many, me, pairs, send, recv, 0)
    landed[me] = part_ref[me]
    landed_lse[me] = lse_ref[me]
    spread_wait(many, me, pairs, send, recv, 0)
    parts = landed_lse[...]
    top = jnp.max(parts, 0)
    total = top + jnp.log(jnp.sum(jnp.exp(parts - top[None]), 0))
    own_lse[...] = total
    share = jnp.exp(parts - total[None])
    count_p = part_ref.shape[1] - count_q
    mixed = jnp.zeros((count_q + count_p, 128), jnp.float32)
    for peer in range(many):
        factors = []
        for row, number in ((1, count_q), (0, count_p)):
            wide = (2 * number, 128)
            at = iota(wide, 0) == iota(wide, 1)
            line = jnp.broadcast_to(share[peer][row : row + 1], wide)
            column = jnp.sum(jnp.where(at, line, 0.0), 1, keepdims=True)
            lane = iota((number, 128), 1)
            factors.append(jnp.where(lane < HEAD, column[0:number], column[number:]))
        mixed += jnp.concatenate(factors, 0) * landed[peer].astype(jnp.float32)
    own[...] = low16(mixed)
    pairs = [(lambda peer: own, mixed_ref), (lambda peer: own_lse, total_ref)]
    spread_start(many, me, pairs, send, recv, 2)
    mixed_ref[me] = own[...]
    total_ref[me] = own_lse[...]
    spread_wait(many, me, pairs, send, recv, 2)


def remote_call(kernel, out_shape, inputs, scratch, lanes, many, ident, name):
    return pl.pallas_call(
        kernel,
        out_shape=out_shape,
        in_specs=[pl.BlockSpec(memory_space=pltpu.VMEM)] * len(inputs),
        out_specs=[pl.BlockSpec(memory_space=pltpu.VMEM)] * len(out_shape),
        scratch_shapes=scratch
        + [pltpu.SemaphoreType.DMA((lanes, many)), pltpu.SemaphoreType.DMA((lanes, many))],
        compiler_params=pltpu.CompilerParams(
            collective_id=ident, has_side_effects=True, vmem_limit_bytes=VMEM_LIMIT
        ),
        name=name,
    )(*inputs)


def exchange_mixed(sizes, part, lse):
    many = sizes.many
    both = sum(sizes.count)
    return remote_call(
        functools.partial(mix_kernel, many, sizes.count[0]),
        (
            jax.ShapeDtypeStruct((many, both, 128), jnp.bfloat16),
            jax.ShapeDtypeStruct((many, 2, 128), jnp.float32),
        ),
        (part, lse),
        [
            pltpu.VMEM((many, both, 128), jnp.bfloat16),
            pltpu.VMEM((many, 2, 128), jnp.float32),
            pltpu.VMEM((both, 128), jnp.bfloat16),
            pltpu.VMEM((2, 128), jnp.float32),
        ],
        4,
        many,
        2,
        "exchange_mixed",
    )


def backward_kernel(
    sizes,
    levels_ref,
    raw_ref,
    query_ref,
    mixed_ref,
    lse_ref,
    grad_ref,
    kept_hbm,
    entry_hbm,
    table_ref,
    place_ref,
    attn_ref,
    vec_ref,
    d_query_ref,
    d_table_ref,
    slice_ref,
    table_t,
    place_t,
    w_kv,
    vec_t,
    d_place_ref,
    d_attn_ref,
    acc_gain,
    acc_shift,
    acc_value,
    d_query_q,
    d_query_p,
    kept_ref,
    entry_ref,
    load,
):
    loads = load_kept(sizes, kept_hbm, entry_hbm, kept_ref, entry_ref, load)
    first = lax.axis_index("dp") * sizes.depth
    count_q, count_p = sizes.count
    prepare_weights(attn_ref, vec_ref, w_kv, vec_t)
    begin = 1 if sizes.keep else 0
    again = levels_ref[0] > begin

    @pl.when(again)
    def _():
        prepare_tokens(sizes, table_ref, place_ref, table_t, place_t)

    for ref in (d_table_ref, d_place_ref, d_attn_ref, d_query_q, d_query_p, acc_gain, acc_shift, acc_value):
        ref[...] = jnp.zeros_like(ref)

    def ask_span(enc, step):
        if enc == 0:
            spot = pl.ds(step * 8, 8)
            shape = (8 * count_q, 128)
            found = [ref[spot, 0:count_q, :].reshape(shape) for ref in (query_ref, grad_ref, mixed_ref)]
            lines = [jnp.broadcast_to(lse_ref[step * 8 + i, 1:2, :], (count_q, 128)) for i in range(8)]
            lines = jnp.concatenate(lines, 0)
            row = iota(lines.shape, 0) % count_q
            lane = iota(lines.shape, 1)
            lse = [
                jnp.sum(jnp.where(lane == row + head * count_q, lines, 0.0), 1, keepdims=True)
                for head in range(2)
            ]
            lse = jnp.concatenate(lse, 0)
        else:
            found = [ref[step, count_q:, :] for ref in (query_ref, grad_ref, mixed_ref)]
            lines = jnp.broadcast_to(lse_ref[step, 0:1, :], (2 * count_p, 128))
            lse = jnp.sum(jnp.where(iota(lines.shape, 1) == iota(lines.shape, 0), lines, 0.0), 1, keepdims=True)
        return found + [lse]

    def work(enc, steps, codes, scaleds, rates, short=False):
        w_all = low16(attn_ref[0, enc, :, 128:384])
        asked = [ask_span(enc, step) for step in steps]
        made = [project(enc, scaled, vec_t, w_kv) for scaled in scaleds]
        d_queries, d_kvs = ([], [])
        for (query, grad, mixed, lse), code, (a_t, keys_t, values_t) in zip(asked, codes, made):
            both = two_heads(query)
            grads = two_heads(grad)
            base = jnp.sum(
                grads.astype(jnp.float32) * jnp.concatenate([mixed, mixed], 0).astype(jnp.float32),
                1,
                keepdims=True,
            )
            scores = dot(both, keys_t) * HEAD ** (-0.5)
            mine = own_slots(code, query.shape[0])
            probs = jnp.where(mine, jnp.exp(jnp.where(mine, scores, NEG) - lse), 0.0)
            d_probs = dot(grads, values_t)
            d_scores = low16(probs * (d_probs - base))
            d_values = low16(dot_rows(grads, low16(probs)))
            d_keys = low16(dot_rows(both, d_scores) * HEAD ** (-0.5))
            d_queries.append(merge_heads(dot_last(d_scores, keys_t)) * HEAD ** (-0.5))
            d_kvs.append(jnp.concatenate([d_keys, d_values], 0))
        for step, d_query in zip(steps, d_queries):
            if enc == 0:
                d_query_q[step] += d_query
            else:
                d_query_p[step] += d_query
        d_kv = jnp.concatenate(d_kvs, 1)
        a_t = jnp.concatenate([part[0] for part in made], 1)
        scaled = jnp.concatenate(scaleds, 1)
        rate = jnp.concatenate(rates, 1)
        code = jnp.concatenate(codes, 1)
        width = code.shape[1]
        d_attn_ref[enc] += dot_last(a_t, d_kv)
        d_h = dot(w_all, d_kv)
        fold = lambda values: sum(values[:, i * SPAN : (i + 1) * SPAN] for i in range(width // SPAN))
        acc_value[enc] += fold(d_kv[128:].astype(jnp.float32))
        acc_gain[enc] += fold(d_h * scaled)
        acc_shift[enc] += fold(d_h)
        d_scaled = d_h * vec_t[enc, :, 0:1]
        center = d_scaled - jnp.mean(d_scaled, 0, keepdims=True)
        slope = jnp.mean(d_scaled * scaled, 0, keepdims=True)
        d_x = low16((center - scaled * slope) * rate)
        rows = code >> 16
        where = (code >> 8) & 255
        chosen = hot(jnp.broadcast_to(where, (CHUNK, width)) == iota((CHUNK, width), 0))
        d_place_ref[enc] += dot_last(d_x, chosen)
        wide = jnp.broadcast_to(rows, (CHUNK, width))

        def add(cut, carry):
            spot = pl.ds(pl.multiple_of(cut * CHUNK, CHUNK), CHUNK)
            chosen = hot(wide == iota((CHUNK, width), 0) + cut * CHUNK)
            d_table_ref[spot, :] += dot_last(chosen, d_x)
            return carry

        lax.fori_loop(0, sizes.padded // CHUNK, add, 0, unroll=not short)

    for enc in range(2):
        if sizes.keep:
            for copy in loads[2 * enc : 2 * enc + 2]:
                copy.wait()

            def kept_spans(turn, carry):
                steps = [turn * sizes.unroll[enc] + u for u in range(sizes.unroll[enc])]
                ats = [s if enc == 0 else sizes.steps[0] + s for s in steps]
                work(
                    enc,
                    steps,
                    [entry_ref[at, 0:1, :] for at in ats],
                    [kept_ref[at, 0:128, :] for at in ats],
                    [kept_ref[at, 128:129, :] for at in ats],
                )
                return carry

            lax.fori_loop(0, sizes.steps[enc] // sizes.unroll[enc], kept_spans, 0)

        def more_level(level, carry_level):
            def one_span(step, carry):
                code = pack_span(sizes, enc, step, level, first, raw_ref)[0]
                scaled, rate = gather_span(sizes, enc, code, table_t, place_t, True)
                work(enc, [step], [code], [scaled], [rate], True)
                return carry

            return lax.fori_loop(0, sizes.steps[enc], one_span, carry_level)

        lax.fori_loop(begin, levels_ref[0], more_level, 0)

    for step in range(sizes.steps[0]):
        d_query_ref[step * 8 : step * 8 + 8, 0:count_q, :] = low16(d_query_q[step]).reshape(8, count_q, 128)
    d_query_ref[:, count_q:, :] = low16(d_query_p[...])
    for enc in range(2):
        for part, block in enumerate((d_place_ref, d_attn_ref)):
            for cut in range(2):
                slice_ref[enc, 2 * part + cut] = block[enc, :, cut * 128 : (cut + 1) * 128].astype(
                    slice_ref.dtype
                )
    slice_ref[0, 1] = jnp.zeros_like(slice_ref[0, 1])
    sums = []
    same = iota((128, 128), 0) == iota((128, 128), 1)
    for enc in range(2):
        for row, acc in enumerate((acc_gain, acc_shift, acc_value)):
            tall = jnp.broadcast_to(jnp.sum(acc[enc], 1, keepdims=True), (128, 128))
            sums.append(jnp.sum(jnp.where(same, tall, 0.0), 0, keepdims=True))
    sums = jnp.concatenate(sums + [jnp.zeros((10, 128), jnp.float32)], 0)
    slice_ref[0, 1, 0:16, :] = sums.astype(slice_ref.dtype)


def tokens_backward(sizes, levels, every, query, mixed, lse, grad, kept, entry, table, positions, attention, vectors):
    many = sizes.many
    count_p = sizes.count[1]
    both = sum(sizes.count)
    return local_call(
        functools.partial(backward_kernel, sizes),
        (
            jax.ShapeDtypeStruct((many, both, 128), jnp.bfloat16),
            jax.ShapeDtypeStruct((sizes.padded, 128), jnp.float32),
            jax.ShapeDtypeStruct((2, 4, 128, 128), sizes.kind),
        ),
        (levels, every, query, mixed, lse, grad, kept, entry, table, positions, attention, vectors),
        token_scratch(sizes)
        + [
            pltpu.VMEM((2, 128, CHUNK), jnp.float32),
            pltpu.VMEM((2, 128, 256), jnp.float32),
            pltpu.VMEM((2, 128, SPAN), jnp.float32),
            pltpu.VMEM((2, 128, SPAN), jnp.float32),
            pltpu.VMEM((2, 128, SPAN), jnp.float32),
            pltpu.VMEM((sizes.steps[0], sizes.queries[0], 128), jnp.float32),
            pltpu.VMEM((many, count_p, 128), jnp.float32),
        ]
        + kept_scratch(sizes),
        "tokens_backward",
        smem_in=(0,),
        any_in=(6, 7),
    )


def adam(weight, grad, first, second):
    first_new = BETA_ONE * first + (1.0 - BETA_ONE) * grad
    second_new = BETA_TWO * second + (1.0 - BETA_TWO) * grad * grad
    fix_one = 1.0 - BETA_ONE**STEP
    fix_two = 1.0 - BETA_TWO**STEP
    ratio = first_new / fix_one / (jnp.sqrt(second_new / fix_two) + ADAM_EPS)
    return (first_new, second_new, weight - INNER_RATE * (ratio + WEIGHT_DECAY * weight))


def pieces_of(depth):
    blocks = [(1, (enc,)) for enc in range(2)] + [(2, (enc,)) for enc in range(2)]
    blocks += [(3, (enc, side)) for enc in range(2) for side in range(2)]
    return blocks + [(4, ())]


def square_sum(values):
    return jnp.sum(jnp.sum(values * values, 0, keepdims=True), 1, keepdims=True)


def finish_kernel(sizes, *refs):
    many = sizes.many
    count_q, count_p = sizes.count
    depth = sizes.depth
    (query_ref, slice_ref, d_table_ref, rows_ref, raw_ref, xa_q, xa_p, d_out, d_ffn, d_mid) = refs[:10]
    place_ref, attn_ref, vec_ref = refs[10:13]
    state = refs[13:33]
    norm_ref, g_word, g_place, g_attn, g_vec = refs[33:38]
    joined = refs[38:43]
    held = refs[43:63]
    mine = refs[63:68]
    theirs = refs[68:73]
    (query_all, slice_all, scalar_all, land_query, land_slice, own_query, own_slice, tile, table_t) = refs[73:82]
    half_query, far_query, half_slice, far_slice = refs[82:86]
    send, recv, load, pair_send, pair_recv = refs[86:91]
    loads = []
    for index in range(20):
        copy = pltpu.make_async_copy(state[index], held[index], load.at[index])
        copy.start()
        loads.append(copy)
    me = lax.axis_index("dp")
    other = 1 - lax.axis_index("grp")
    barrier = pltpu.get_barrier_semaphore()

    def greet(step, carry):
        peer = lax.rem(me + step, many)
        pl.semaphore_signal(barrier, inc=1, device_id={"dp": peer}, device_id_type=MESH)
        return carry

    lax.fori_loop(1, many, greet, 0)
    pl.semaphore_signal(barrier, inc=1, device_id={"grp": other}, device_id_type=MESH)
    pl.semaphore_wait(barrier, many)
    fold_start(many, me, query_ref, land_query, send, recv, 0)
    fold_start(many, me, slice_ref, land_slice, send, recv, 1)
    fold_pass(many, me, query_ref, land_query, half_query, far_query, send, recv, 0, 6)
    fold_pass(many, me, slice_ref, land_slice, half_slice, far_slice, send, recv, 1, 7)
    own_query[...] = low16(fold_wait(many, me, half_query, far_query, send, recv, 6))
    relay_start(many, me, own_query, query_all, send, recv, 3)
    query_all[me] = own_query[...]
    own_slice[...] = fold_wait(many, me, half_slice, far_slice, send, recv, 7).astype(own_slice.dtype)
    relay_start(many, me, own_slice, slice_all, send, recv, 4)
    slice_all[me] = own_slice[...]
    relay_pass(many, me, own_query, query_all, send, recv, 3)
    relay_pass(many, me, own_slice, slice_all, send, recv, 4)
    relay_wait(many, me, own_query, query_all, send, recv, 3)

    g_vec[...] = d_mid[...]
    tops = []
    first = me * depth
    table_t[...] = jnp.zeros_like(table_t)
    rest = jnp.zeros((1, 1), jnp.float32)
    places = []
    for enc in range(2):
        low, high = (0, count_q) if enc == 0 else (count_q, count_q + count_p)
        number = many * (high - low)
        d_query = query_all[:, low:high, :].reshape(number, 128)
        x = rows_ref[:, low:high, :].reshape(number, 128).astype(jnp.float32) + place_ref[0, enc, 0:1, :]
        center = x - jnp.mean(x, -1, keepdims=True)
        rate = lax.rsqrt(jnp.mean(center * center, -1, keepdims=True) + NORM_EPS)
        scaled = center * rate
        gain = vector_row(vec_ref, enc, 0)
        a_low = low16(scaled * gain + vector_row(vec_ref, enc, 1))
        xa = xa_q if enc == 0 else xa_p
        d_h = xa[...] + dot_last(d_query, low16(attn_ref[0, enc, :, 0:128]))
        d_scaled = d_h * gain
        slope = jnp.mean(d_scaled * scaled, -1, keepdims=True)
        d_x = (d_scaled - jnp.mean(d_scaled, -1, keepdims=True) - scaled * slope) * rate
        d_place = jnp.sum(d_x, 0, keepdims=True)
        places.append(d_place)
        g_attn[enc, :, 0:128] = dot_rows(a_low, d_query)
        g_attn[enc, :, 384:512] = d_out[enc]
        spot = slice(enc, enc + 1)
        g_vec[2, spot, :] = jnp.sum(d_query.astype(jnp.float32), 0, keepdims=True)
        tops.append((jnp.sum(d_h * scaled, 0, keepdims=True), jnp.sum(d_h, 0, keepdims=True)))
        if enc == 0:
            columns = [
                part
                for peer in range(many)
                for part in (
                    raw_ref[peer, RAW_Q : RAW_Q + 16, 0:1].astype(jnp.int32)[0 : count_q // 2],
                    raw_ref[peer, RAW_Q : RAW_Q + 16, 64:65].astype(jnp.int32)[0 : count_q // 2],
                )
            ]
        else:
            columns = [raw_ref[peer, 0:count_p, 0:1].astype(jnp.int32) for peer in range(many)]
        spot = jnp.concatenate(columns, 0) - first
        spot = jnp.where(spot < depth, spot, -1)
        d_low = low16(d_x)
        wide = jnp.broadcast_to(spot, (number, CHUNK))
        for cut in range(sizes.padded // CHUNK):
            chosen = hot(wide == iota((number, CHUNK), 1) + cut * CHUNK)
            table_t[:, cut * CHUNK : (cut + 1) * CHUNK] += dot_rows(d_low, chosen)
        rest += square_sum(d_ffn[enc, 0]) + square_sum(d_ffn[enc, 1])
    for cut in range(0, depth, 128):
        top = min(cut + 128, depth)
        g_word[cut:top, :] = d_table_ref[cut:top, :] + jnp.transpose(table_t[:, cut : cut + 128])[0 : top - cut]
    tile[...] = jnp.broadcast_to(square_sum(g_word[...]), (8, 128))
    pairs = [(lambda peer: tile, scalar_all)]
    spread_start(many, me, pairs, send, recv, 5)
    scalar_all[me] = tile[...]
    relay_wait(many, me, own_slice, slice_all, send, recv, 4)
    blocks = slice_all[...].astype(jnp.float32).reshape(8, 128, 128)
    for enc in range(2):
        spot = slice(enc, enc + 1)
        g_vec[0, spot, :] = blocks[1][enc * 3 : enc * 3 + 1] + tops[enc][0]
        g_vec[1, spot, :] = blocks[1][enc * 3 + 1 : enc * 3 + 2] + tops[enc][1]
        g_vec[3, spot, :] = blocks[1][enc * 3 + 2 : enc * 3 + 3]
        g_place[enc, 0:128, :] = jnp.transpose(blocks[enc * 4])
        if enc == 0:
            g_place[enc, 128:256, :] = jnp.zeros((128, 128), jnp.float32)
        else:
            g_place[enc, 128:256, :] = jnp.transpose(blocks[enc * 4 + 1])
        g_place[enc, 0:1, :] += places[enc]
        g_attn[enc, :, 128:256] = blocks[enc * 4 + 2]
        g_attn[enc, :, 256:384] = blocks[enc * 4 + 3]
        rest += square_sum(g_place[enc]) + square_sum(g_attn[enc])
    small = jnp.sum(g_vec[...] * g_vec[...], 0)
    rest += jnp.sum(jnp.sum(small, 0, keepdims=True), 1, keepdims=True)
    for copy in loads:
        copy.wait()
    spread_wait(many, me, pairs, send, recv, 5)
    norm = jnp.sqrt(jnp.sum(scalar_all[...], 0)[0:1, 0:1] + rest)
    norm_ref[...] = jnp.broadcast_to(norm, (8, 128))
    factor = CLIP_LIMIT / jnp.maximum(norm, CLIP_LIMIT)
    grads = (g_word, g_place, g_attn, d_ffn, g_vec)

    def differ(kind, at, rows):
        weight, moment, square, anchor = (held[kind * 4 + j] for j in range(4))
        grad = grads[kind][at + (rows,)] * factor
        inner = adam(weight[(0,) + at + (rows,)], grad, moment[(0,) + at + (rows,)], square[(0,) + at + (rows,)])[2]
        mine[kind][at + (rows,)] = (anchor[at + (rows,)] - inner).astype(mine[kind].dtype)

    size = math.gcd(depth, 128)

    def table_block(step, carry):
        differ(0, (), pl.ds(pl.multiple_of(step * size, size), size))
        return carry

    lax.fori_loop(0, depth // size, table_block, 0)
    ways = []

    def hand(kind):
        copy = pltpu.make_async_remote_copy(
            src_ref=mine[kind],
            dst_ref=theirs[kind],
            send_sem=pair_send.at[kind],
            recv_sem=pair_recv.at[kind],
            device_id={"grp": other},
            device_id_type=MESH,
        )
        copy.start()
        ways.append(copy)

    hand(0)
    for kind in range(1, 5):
        for found, at in pieces_of(depth):
            if found == kind:
                differ(kind, at, slice(0, 14) if kind == 4 else slice(None))
        hand(kind)
    def join(kind, spot):
        joined[kind][spot] = mine[kind][spot].astype(jnp.float32) + theirs[kind][spot].astype(jnp.float32)

    def table_add(step, carry):
        join(0, pl.ds(pl.multiple_of(step * size, size), size))
        return carry

    ways[0].wait()
    lax.fori_loop(0, depth // size, table_add, 0)
    for kind in range(1, 5):
        ways[kind].wait()
        for found, at in pieces_of(depth):
            if found == kind:
                join(kind, at if at else slice(None))


def finish(sizes, query, slices, d_table, rows, every, xa_q, xa_p, d_out, d_ffn, d_mid, params, state):
    many = sizes.many
    both = sum(sizes.count)
    inputs = (query, slices, d_table, rows, every, xa_q, xa_p, d_out, d_ffn, d_mid) + params
    flat = tuple(state[j][kind] for kind in range(5) for j in range(4))
    shapes = [state[3][kind].shape for kind in range(5)]
    vm = pl.BlockSpec(memory_space=pltpu.VMEM)
    hbm = pl.BlockSpec(memory_space=pl.ANY)
    f32 = jnp.float32
    return pl.pallas_call(
        functools.partial(finish_kernel, sizes),
        out_shape=tuple(
            jax.ShapeDtypeStruct(shape, f32)
            for shape in [(8, 128), shapes[0], shapes[1], shapes[2], (16, 2, 128)] + shapes
        ),
        in_specs=[vm] * len(inputs) + [hbm] * 20,
        out_specs=[vm] * 10,
        scratch_shapes=[pltpu.VMEM(value.shape, f32) for value in flat]
        + [pltpu.VMEM(shape, jnp.bfloat16 if kind < 4 else f32) for kind, shape in enumerate(shapes)] * 2
        + [
            pltpu.VMEM((many, both, 128), jnp.bfloat16),
            pltpu.VMEM((many, sizes.lines, 128), sizes.kind),
            pltpu.VMEM((many, 8, 128), f32),
            pltpu.VMEM((many, both, 128), jnp.bfloat16),
            pltpu.VMEM((many, sizes.lines, 128), sizes.kind),
            pltpu.VMEM((both, 128), jnp.bfloat16),
            pltpu.VMEM((sizes.lines, 128), sizes.kind),
            pltpu.VMEM((8, 128), f32),
            pltpu.VMEM((128, sizes.padded), f32),
            pltpu.VMEM((many // NEAR, both, 128), jnp.bfloat16),
            pltpu.VMEM((many // NEAR, both, 128), jnp.bfloat16),
            pltpu.VMEM((many // NEAR, sizes.lines, 128), sizes.kind),
            pltpu.VMEM((many // NEAR, sizes.lines, 128), sizes.kind),
            pltpu.SemaphoreType.DMA((8, many)),
            pltpu.SemaphoreType.DMA((8, many)),
            pltpu.SemaphoreType.DMA((20,)),
            pltpu.SemaphoreType.DMA((5,)),
            pltpu.SemaphoreType.DMA((5,)),
        ],
        compiler_params=pltpu.CompilerParams(
            collective_id=3, has_side_effects=True, vmem_limit_bytes=VMEM_LIMIT
        ),
        name="finish",
    )(*inputs, *flat)


def output_parts(depth):
    rows = depth // 3 if depth % 24 == 0 else depth
    parts = [(0, slice(at, at + rows)) for at in range(0, depth, rows)]
    return parts + [(kind, None) for kind in (3, 2, 1, 4)]


def outputs_kernel(depth, groups, *refs):
    norm_ref, g_vec = refs[:2]
    ins = refs[2:31]
    outs = refs[31:56]
    total_ref = refs[56]
    held = refs[57:86]
    made = refs[86:111]
    load, store = refs[111:113]
    parts = output_parts(depth)
    loads, stores = ([], [])
    for number, (kind, rows) in enumerate(parts):
        group = []
        for j in range(6 if kind < 4 else 5):
            index = kind * 5 + j if j < 5 else 25 + kind
            source, target = (ins[index], held[index])
            if rows is not None:
                lead = (0,) if len(source.shape) == 3 else ()
                source, target = (source.at[lead + (rows,)], target.at[lead + (rows,)])
            copy = pltpu.make_async_copy(source, target, load.at[number, j])
            copy.start()
            group.append(copy)
        loads.append(group)
    total_ref[0] = jnp.max(norm_ref[...])
    norm = norm_ref[0:1, 0:1]
    factor = CLIP_LIMIT / jnp.maximum(norm, CLIP_LIMIT)
    grads = tuple(held[25:29]) + (g_vec,)

    def work(kind, at, rows):
        moment, square, anchor, outer, summed = (held[kind * 5 + j] for j in range(5))
        first, second, average, momentum, weight = (made[kind * 5 + j] for j in range(5))
        spot = at + (rows,)
        deep = (0,) + spot
        grad = grads[kind][spot] * factor
        first[deep] = BETA_ONE * moment[deep] + (1.0 - BETA_ONE) * grad
        second[deep] = BETA_TWO * square[deep] + (1.0 - BETA_TWO) * grad * grad
        mean = summed[spot] / groups
        speed = OUTER_MU * outer[spot] + mean
        average[spot] = mean
        momentum[spot] = speed
        weight[deep] = anchor[spot] - OUTER_RATE * (mean + OUTER_MU * speed)

    for number, (kind, rows) in enumerate(parts):
        for copy in loads[number]:
            copy.wait()
        if kind == 0:
            size = math.gcd(rows.stop - rows.start, 128)

            def table_block(step, carry):
                work(0, (), pl.ds(pl.multiple_of(rows.start + step * size, size), size))
                return carry

            lax.fori_loop(0, (rows.stop - rows.start) // size, table_block, 0)
        else:
            for found, at in pieces_of(depth):
                if found == kind:
                    work(kind, at, slice(0, 14) if kind == 4 else slice(None))
        for j in range(5):
            source, target = (made[kind * 5 + j], outs[kind * 5 + j])
            if rows is not None:
                lead = (0,) if len(source.shape) == 3 else ()
                source, target = (source.at[lead + (rows,)], target.at[lead + (rows,)])
            copy = pltpu.make_async_copy(source, target, store.at[number, j])
            copy.start()
            stores.append(copy)
    for copy in stores:
        copy.wait()


def make_outputs(norm, grads, firsts, seconds, anchors, outers, summed, groups):
    kinds = range(5)
    flat = tuple(v for kind in kinds for v in (firsts[kind], seconds[kind], anchors[kind], outers[kind], summed[kind]))
    flat += tuple(grads[:4])
    out = tuple(
        jax.ShapeDtypeStruct(shape, jnp.float32)
        for kind in kinds
        for shape in (firsts[kind].shape, firsts[kind].shape, anchors[kind].shape, anchors[kind].shape, firsts[kind].shape)
    )
    vm = pl.BlockSpec(memory_space=pltpu.VMEM)
    hbm = pl.BlockSpec(memory_space=pl.ANY)
    got = pl.pallas_call(
        functools.partial(outputs_kernel, anchors[0].shape[0], groups),
        out_shape=out + (jax.ShapeDtypeStruct((1,), jnp.float32),),
        in_specs=[vm] * 2 + [hbm] * 29,
        out_specs=[hbm] * 25 + [pl.BlockSpec(memory_space=pltpu.SMEM)],
        scratch_shapes=[pltpu.VMEM(v.shape, jnp.float32) for v in flat]
        + [pltpu.VMEM(v.shape, jnp.float32) for v in out]
        + [pltpu.SemaphoreType.DMA((7, 6)), pltpu.SemaphoreType.DMA((7, 5))],
        compiler_params=pltpu.CompilerParams(vmem_limit_bytes=VMEM_LIMIT),
        name="make_outputs",
    )(norm, grads[4], *flat)
    return [[got[kind * 5 + j] for kind in kinds] for j in range(5)], got[25]


def square_norm(values):
    center = values - jnp.mean(values, -1, keepdims=True)
    rate = lax.rsqrt(jnp.mean(center * center, -1, keepdims=True) + NORM_EPS)
    return center * rate, rate


def norm_back(d_scaled, scaled, rate):
    slope = jnp.mean(d_scaled * scaled, -1, keepdims=True)
    return (d_scaled - jnp.mean(d_scaled, -1, keepdims=True) - scaled * slope) * rate


def total_of(values):
    return jnp.sum(jnp.sum(values, 0, keepdims=True), 1, keepdims=True)


def score_terms(scores, drop, target, weight, count, axis):
    masked = jnp.where(drop, MASKED, scores)
    top = jnp.max(masked, axis, keepdims=True)
    expo = jnp.exp(masked - top)
    total = jnp.sum(expo, axis, keepdims=True)
    picked = jnp.sum(jnp.where(target, scores, 0.0), axis, keepdims=True)
    loss = total_of(weight * (top + jnp.log(total) - picked))
    grad = low16((weight / count) * (expo / total - jnp.where(target, 1.0, 0.0)))
    return grad, loss


GELU_A = math.sqrt(2.0 / math.pi)
GELU_B = 0.044715


def class_kernel(
    sizes,
    rows_ref,
    mixed_ref,
    raw_ref,
    place_ref,
    attn_ref,
    ffn_ref,
    vec_ref,
    grad_ref,
    xa_q,
    xa_p,
    d_out,
    d_ffn,
    d_mid,
    loss_ref,
    count_ref,
    cls_ref,
    scaled_a,
    rate_a,
    scaled_f,
    rate_f,
    pre_ref,
    act_ref,
    low_ref,
    flag_ref,
):
    many = sizes.many
    counts = sizes.count
    totals = (many * counts[0], many * counts[1])
    chunk = totals[0]
    parts = [(0, 0, 0)] + [(1, at, totals[0] + at) for at in range(0, totals[1], chunk)]

    def held(ref, enc, at):
        each = counts[enc]
        low = 0 if enc == 0 else counts[0]
        return ref[at // each : (at + chunk) // each, low : low + each, :].reshape(chunk, 128)

    def weights(enc):
        return (
            low16(attn_ref[0, enc, :, 384:512]),
            low16(ffn_ref[0, enc, 0]),
            low16(ffn_ref[0, enc, 1]),
        )

    for enc, at, spot in parts:
        w_out, w_up, w_down = weights(enc)
        row = functools.partial(vector_row, vec_ref, enc)
        here = slice(spot, spot + chunk)
        x = held(rows_ref, enc, at).astype(jnp.float32) + place_ref[0, enc, 0:1, :]
        h_embed = norm_rows(x, row(0), row(1))
        scaled, rate = square_norm(h_embed + (dot(held(mixed_ref, enc, at), w_out) + row(4)))
        scaled_a[here, :] = scaled
        rate_a[here, :] = jnp.broadcast_to(rate, (chunk, 128))
        h_attn = scaled * row(5) + row(6)
        h_low = low16(h_attn)
        low_ref[here, :] = h_low
        pre = dot(h_low, w_up) + jnp.concatenate([row(10), row(11), row(12), row(13)], 1)
        pre_ref[here, :] = pre
        act = low16(0.5 * pre * (1.0 + jnp.tanh(GELU_A * (pre + GELU_B * (pre * pre * pre)))))
        act_ref[here, :] = act
        scaled, rate = square_norm(h_attn + (dot_last(act, w_down) + row(7)))
        scaled_f[here, :] = scaled
        rate_f[here, :] = jnp.broadcast_to(rate, (chunk, 128))
        cls_ref[here, :] = low16(scaled * row(8) + row(9))

    every_q = cls_ref[0 : totals[0], :]
    every_p = cls_ref[totals[0] :, :]
    flag_ref[...] = jnp.zeros_like(flag_ref)
    for peer in range(many):
        flag_ref[peer : peer + 1, :] = raw_ref[peer, RAW_Q:RAW_ROWS, :].astype(jnp.float32)[8:9]
    turned = jnp.transpose(flag_ref[...])

    def column(low, each):
        tall = jnp.concatenate([turned[low : low + each]] * many, 0)
        at = iota(tall.shape, 1) == iota(tall.shape, 0) // each
        return jnp.sum(jnp.where(at, tall, 0.0), 1, keepdims=True)

    keys_q = column(0, counts[0])
    valid = column(counts[0], counts[0])
    keys_p = column(2 * counts[0], counts[1])
    hot_q = hot(jnp.broadcast_to(keys_q, (totals[0], 128)) == iota((totals[0], 128), 1).astype(jnp.float32))
    hot_p = hot(jnp.broadcast_to(keys_p, (totals[1], 128)) == iota((totals[1], 128), 1).astype(jnp.float32))
    same = dot_last(hot_q, hot_p) > 0.5
    count = jnp.maximum(total_of(valid), 1.0)
    scale = 128 ** (-0.5)
    scores = dot_last(every_q, every_p) * scale
    index_q = iota(scores.shape, 0)
    index_p = iota(scores.shape, 1)
    target_qp = index_p == 2 * index_q
    target_pq = index_p // 2 == index_q
    grad_qp, loss_qp = score_terms(scores, same & ~target_qp, target_qp, valid, count, 1)
    drop_pq = (same | (jnp.broadcast_to(valid, scores.shape) == 0.0)) & ~target_pq
    weight_p = jnp.sum(jnp.where(target_qp, jnp.broadcast_to(valid, scores.shape), 0.0), 0, keepdims=True)
    grad_pq, loss_pq = score_terms(scores, drop_pq, target_pq, weight_p, count, 0)
    loss_ref[0] = jnp.max(loss_qp + loss_pq)
    count_ref[0] = jnp.max(count)
    d_q = (dot(grad_qp, every_p) + dot(grad_pq, every_p)) * scale
    d_p = (dot_rows(grad_pq, every_q) + dot_rows(grad_qp, every_q)) * scale

    d_mid[...] = jnp.zeros_like(d_mid)
    d_out[...] = jnp.zeros_like(d_out)
    d_ffn[...] = jnp.zeros_like(d_ffn)
    for enc, at, spot in parts:
        w_out, w_up, w_down = weights(enc)
        row = functools.partial(vector_row, vec_ref, enc)
        here = slice(spot, spot + chunk)

        def add(index, values):
            d_mid[index, enc : enc + 1, :] += jnp.sum(values, 0, keepdims=True)

        d_cls = d_q if enc == 0 else d_p[at : at + chunk]
        scaled = scaled_f[here, :]
        add(8, d_cls * scaled)
        add(9, d_cls)
        d_x_ffn = norm_back(d_cls * row(8), scaled, rate_f[here, :])
        d_branch = low16(d_x_ffn)
        add(7, d_branch.astype(jnp.float32))
        d_ffn[enc, 1] += dot_rows(d_branch, act_ref[here, :])
        d_act = dot(d_branch, w_down)
        pre = pre_ref[here, :]
        square = pre * pre
        bend = jnp.tanh(GELU_A * (pre + GELU_B * (square * pre)))
        slope = 0.5 * (1.0 + bend) + (0.5 * GELU_A) * pre * (1.0 - bend * bend) * (
            1.0 + (3.0 * GELU_B) * square
        )
        d_pre = low16(slope * d_act)
        up_bias = jnp.sum(d_pre.astype(jnp.float32), 0, keepdims=True)
        for cut in range(4):
            d_mid[10 + cut, enc : enc + 1, :] += up_bias[:, cut * 128 : (cut + 1) * 128]
        d_ffn[enc, 0] += dot_rows(low_ref[here, :], d_pre)
        d_h = d_x_ffn + dot_last(d_pre, w_up)
        scaled = scaled_a[here, :]
        add(5, d_h * scaled)
        add(6, d_h)
        d_x = norm_back(d_h * row(5), scaled, rate_a[here, :])
        if enc == 0:
            xa_q[...] = d_x
        else:
            xa_p[at : at + chunk, :] = d_x
        d_proj = low16(d_x)
        add(4, d_proj.astype(jnp.float32))
        d_out[enc] += dot_rows(held(mixed_ref, enc, at), d_proj)
        d_mixed = low16(dot_last(d_proj, w_out))
        each = counts[enc]
        low = 0 if enc == 0 else counts[0]
        grad_ref[at // each : (at + chunk) // each, low : low + each, :] = d_mixed.reshape(
            chunk // each, each, 128
        )


def class_stage(sizes, rows, mixed, every, positions, attention, feedforward, vectors):
    many = sizes.many
    n_q, n_p = (many * sizes.count[0], many * sizes.count[1])
    both = n_q + n_p
    f32 = jnp.float32
    return local_call(
        functools.partial(class_kernel, sizes),
        (
            jax.ShapeDtypeStruct((many, sum(sizes.count), 128), jnp.bfloat16),
            jax.ShapeDtypeStruct((n_q, 128), f32),
            jax.ShapeDtypeStruct((n_p, 128), f32),
            jax.ShapeDtypeStruct((2, 128, 128), f32),
            jax.ShapeDtypeStruct((2, 2, 128, 512), f32),
            jax.ShapeDtypeStruct((16, 2, 128), f32),
            jax.ShapeDtypeStruct((1,), f32),
            jax.ShapeDtypeStruct((1,), f32),
        ),
        (rows, mixed, every, positions, attention, feedforward, vectors),
        [
            pltpu.VMEM((both, 128), jnp.bfloat16),
            pltpu.VMEM((both, 128), f32),
            pltpu.VMEM((both, 128), f32),
            pltpu.VMEM((both, 128), f32),
            pltpu.VMEM((both, 128), f32),
            pltpu.VMEM((both, 512), f32),
            pltpu.VMEM((both, 512), jnp.bfloat16),
            pltpu.VMEM((both, 128), jnp.bfloat16),
            pltpu.VMEM((128, 128), f32),
        ],
        "class_stage",
        smem_out=(6, 7),
    )


def class_stage_large(sizes, rows_all, mixed_all, every, positions, attention, feedforward, vectors):
    many = sizes.many
    count_q, count_p = sizes.count
    counts = sizes.count
    width = rows_all.shape[2]
    flags_all = every[:, RAW_FLAGS, :].astype(jnp.int32)
    keys_q = flags_all[:, :count_q].reshape(-1)
    valid_all = flags_all[:, count_q : 2 * count_q].reshape(-1)
    keys_p = flags_all[:, 2 * count_q : 2 * count_q + count_p].reshape(-1)
    cuts = ((0, count_q), (count_q, count_q + count_p))
    cls, class_kept, mixes = ([], [], [])
    for enc in range(2):
        low, high = cuts[enc]
        rows = rows_all[:, low:high].reshape(-1, width)
        mixed = mixed_all[:, low:high].reshape(-1, width)
        low_cls, kept_cls = class_forward(
            rows, mixed, positions[0, enc], attention[0, enc], feedforward[0, enc], vectors[0, :, enc]
        )
        cls.append(low_cls)
        class_kept.append(kept_cls)
        mixes.append(mixed)
    d_q, d_p, loss_total, count = score_stage(cls[0], cls[1], keys_q, keys_p, valid_all)
    d_cls = (d_q, d_p)
    grads, xas, outs, ffns, mids = ([], [], [], [], [])
    for enc in range(2):
        d_mixed, d_x_attn, d_w_out, d_ffn, rows_mid, d_up_bias = class_backward(
            class_kept[enc], mixes[enc], attention[0, enc], feedforward[0, enc], vectors[0, :, enc], d_cls[enc]
        )
        grads.append(d_mixed.reshape(many, counts[enc], width))
        xas.append(d_x_attn)
        outs.append(d_w_out)
        ffns.append(d_ffn)
        mid = jnp.concatenate([jnp.stack(list(rows_mid)), d_up_bias.reshape(-1, width)])
        mids.append(jnp.pad(mid, ((4, 2), (0, 0))))
    return (
        jnp.concatenate(grads, 1),
        xas[0],
        xas[1],
        jnp.stack(outs),
        jnp.stack(ffns),
        jnp.stack(mids, 1),
        loss_total.reshape(1),
        count.reshape(1),
    )


def class_forward(rows, mixed, place, attn_w, ffn_w, vec):
    width = rows.shape[1]
    h_embed = layer_norm(rows.astype(jnp.float32) + place[:1], vec[0], vec[1])
    x_attn = h_embed + (dot(mixed, low16(attn_w[:, 3 * width :])) + vec[4])
    h_attn = layer_norm(x_attn, vec[5], vec[6])
    h_low = low16(h_attn)
    pre = dot(h_low, low16(ffn_w[0])) + vec[10:].reshape(-1)
    act = low16(gelu_tanh(pre))
    x_ffn = h_attn + (dot_last(act, low16(ffn_w[1])) + vec[7])
    h_out = layer_norm(x_ffn, vec[8], vec[9])
    return low16(h_out), (x_attn, h_low, pre, act, x_ffn)


def class_backward(kept, mixed, attn_w, ffn_w, vec, d_cls):
    x_attn, h_low, pre, act, x_ffn = kept
    width = x_attn.shape[1]
    unused, out_back = jax.vjp(layer_norm, x_ffn, vec[8], vec[9])
    d_x_ffn, d_gain_two, d_shift_two = out_back(d_cls)
    d_branch = low16(d_x_ffn)
    d_down_bias = jnp.sum(d_branch, 0, dtype=jnp.float32)
    d_down = dot_rows(d_branch, act)
    d_act = dot(d_branch, low16(ffn_w[1]))
    unused, gelu_back = jax.vjp(gelu_tanh, pre)
    d_pre = low16(gelu_back(d_act)[0])
    d_up_bias = jnp.sum(d_pre, 0, dtype=jnp.float32)
    d_up = dot_rows(h_low, d_pre)
    d_h_attn = d_x_ffn + dot_last(d_pre, low16(ffn_w[0]))
    unused, attn_back = jax.vjp(layer_norm, x_attn, vec[5], vec[6])
    d_x_attn, d_gain_one, d_shift_one = attn_back(d_h_attn)
    d_proj = low16(d_x_attn)
    d_out_bias = jnp.sum(d_proj, 0, dtype=jnp.float32)
    d_w_out = dot_rows(mixed, d_proj)
    d_mixed = low16(dot_last(d_proj, low16(attn_w[:, 3 * width :])))
    rows = (d_out_bias, d_gain_one, d_shift_one, d_down_bias, d_gain_two, d_shift_two)
    return d_mixed, d_x_attn, d_w_out, jnp.stack([d_up, d_down]), rows, d_up_bias


def softmax_terms(scores, drop, target, weight, count, axis):
    masked = jnp.where(drop, MASKED, scores)
    top = jnp.max(masked, axis, keepdims=True)
    expo = jnp.exp(masked - top)
    total = jnp.sum(expo, axis, keepdims=True)
    lse = top + jnp.log(total)
    picked = jnp.sum(jnp.where(target, scores, 0.0), axis, keepdims=True)
    loss = jnp.sum(weight * (lse - picked))
    grad = low16((weight / count) * (expo / total - target.astype(jnp.float32)))
    return grad, loss


def score_stage(every_q, every_p, keys_q, keys_p, valid_q):
    count = jnp.maximum(jnp.sum(valid_q).astype(jnp.float32), 1.0)
    scale = every_q.shape[1] ** (-0.5)
    index_q = jnp.arange(every_q.shape[0])[:, None]
    index_p = jnp.arange(every_p.shape[0])[None, :]
    scores = dot_last(every_q, every_p) * scale
    same = keys_q[:, None] == keys_p[None, :]
    target_qp = index_p == 2 * index_q
    valid = valid_q.astype(jnp.float32)[:, None]
    grad_qp, loss_qp = softmax_terms(scores, same & ~target_qp, target_qp, valid, count, 1)
    target_pq = index_p // 2 == index_q
    drop_pq = (same | (valid_q[:, None] == 0)) & ~target_pq
    owner_valid = jnp.repeat(valid_q, 2)
    weight_p = jnp.where(index_p[0] % 2 == 0, owner_valid, 0).astype(jnp.float32)[None, :]
    grad_pq, loss_pq = softmax_terms(scores, drop_pq, target_pq, weight_p, count, 0)
    d_q = (dot(grad_qp, every_p) + dot(grad_pq, every_p)) * scale
    d_p = (dot_rows(grad_pq, every_q) + dot_rows(grad_qp, every_q)) * scale
    return d_q, d_p, loss_qp + loss_pq, count


def body(
    question_ids,
    passage_ids,
    question_lengths,
    passage_lengths,
    question_keys,
    passage_keys,
    question_valid,
    word_table,
    positions,
    attention,
    feedforward,
    vectors,
    word_first,
    positions_first,
    attention_first,
    feedforward_first,
    vectors_first,
    word_second,
    positions_second,
    attention_second,
    feedforward_second,
    vectors_second,
    word_anchor,
    positions_anchor,
    attention_anchor,
    feedforward_anchor,
    vectors_anchor,
    word_outer,
    positions_outer,
    attention_outer,
    feedforward_outer,
    vectors_outer,
):
    many = lax.axis_size("dp")
    count_q = question_ids.shape[0]
    count_p = passage_ids.shape[0]
    table = word_table[0]
    sizes = Sizes(many, count_q, count_p, table.shape[0])
    swap = lambda values: jnp.swapaxes(values, -3, -2)
    vectors, vectors_first, vectors_second, vectors_anchor, vectors_outer = (
        swap(v) for v in (vectors, vectors_first, vectors_second, vectors_anchor, vectors_outer)
    )
    every, class_rows, kept, entry, counted = first_stage(
        sizes,
        question_ids,
        passage_ids,
        question_lengths,
        passage_lengths,
        question_keys,
        question_valid,
        passage_keys,
        table,
        positions,
    )
    part, lse_part, query, levels = tokens_forward(
        sizes, every, class_rows, kept, entry, counted, table, positions, attention, vectors
    )
    mixed_all, lse_all = exchange_mixed(sizes, part, lse_part)
    stage = class_stage if many * count_q <= 512 else class_stage_large
    grad_all, xa_q, xa_p, d_out, d_ffn, d_mid, loss_total, count = stage(
        sizes, class_rows, mixed_all, every, positions, attention, feedforward, vectors
    )
    d_query, d_table, slices = tokens_backward(
        sizes, levels, every, query, mixed_all, lse_all, grad_all, kept, entry, table, positions, attention, vectors
    )
    weights = (word_table, positions, attention, feedforward, vectors)
    firsts = (word_first, positions_first, attention_first, feedforward_first, vectors_first)
    seconds = (word_second, positions_second, attention_second, feedforward_second, vectors_second)
    anchors = (word_anchor, positions_anchor, attention_anchor, feedforward_anchor, vectors_anchor)
    outers = (word_outer, positions_outer, attention_outer, feedforward_outer, vectors_outer)
    done = finish(
        sizes,
        d_query,
        slices.reshape(many, sizes.lines, 128),
        d_table,
        class_rows,
        every,
        xa_q,
        xa_p,
        d_out,
        d_ffn,
        d_mid,
        (positions, attention, vectors),
        (weights, firsts, seconds, anchors),
    )
    norm = done[0]
    grads = (done[1], done[2], done[3], d_ffn, done[4])
    made, norm = make_outputs(
        norm, grads, firsts, seconds, anchors, outers, done[5:10], lax.axis_size("grp")
    )
    first_new, second_new, averages, outer_next, weight_next = (
        part[:4] + [swap(part[4])] for part in made
    )
    return (
        loss_total.reshape(1),
        count.reshape(1),
        norm.reshape(1),
        first_new[0],
        first_new[1],
        first_new[2],
        first_new[3],
        first_new[4],
        second_new[0],
        second_new[1],
        second_new[2],
        second_new[3],
        second_new[4],
        averages[0],
        averages[1],
        averages[2],
        averages[3],
        averages[4],
        outer_next[0],
        outer_next[1],
        outer_next[2],
        outer_next[3],
        outer_next[4],
        weight_next[0],
        weight_next[1],
        weight_next[2],
        weight_next[3],
        weight_next[4],
    )


def solution(mesh):
    placed = (
        P(("grp", "dp"), None),
        P(("grp", "dp"), None),
        P(("grp", "dp")),
        P(("grp", "dp")),
        P(("grp", "dp")),
        P(("grp", "dp")),
        P(("grp", "dp")),
        P("grp", "dp", None),
        P("grp", None, None, None),
        P("grp", None, None, None),
        P("grp", None, None, None, None),
        P("grp", None, None, None),
        P("grp", "dp", None),
        P("grp", None, None, None),
        P("grp", None, None, None),
        P("grp", None, None, None, None),
        P("grp", None, None, None),
        P("grp", "dp", None),
        P("grp", None, None, None),
        P("grp", None, None, None),
        P("grp", None, None, None, None),
        P("grp", None, None, None),
        P("dp", None),
        P(),
        P(),
        P(),
        P(),
        P("dp", None),
        P(),
        P(),
        P(),
        P(),
    )
    return jax.shard_map(
        body,
        mesh=mesh,
        in_specs=placed,
        out_specs=(
            P("grp"),
            P("grp"),
            P("grp"),
            P("grp", "dp", None),
            P("grp", None, None, None),
            P("grp", None, None, None),
            P("grp", None, None, None, None),
            P("grp", None, None, None),
            P("grp", "dp", None),
            P("grp", None, None, None),
            P("grp", None, None, None),
            P("grp", None, None, None, None),
            P("grp", None, None, None),
            P("dp", None),
            P(),
            P(),
            P(),
            P(),
            P("dp", None),
            P(),
            P(),
            P(),
            P(),
            P("grp", "dp", None),
            P("grp", None, None, None),
            P("grp", None, None, None),
            P("grp", None, None, None, None),
            P("grp", None, None, None),
        ),
        check_vma=False,
    )
```

```python
import functools
import math

import jax
import jax.numpy as jnp
from jax import lax
from jax.experimental import pallas as pl
from jax.experimental.pallas import tpu as pltpu
from jax.sharding import PartitionSpec as P

HEAD = 64
STEP = 5


NORM_EPS = 1e-05
MASKED = -1000000000.0
BETA_ONE = 0.9
BETA_TWO = 0.999
INNER_RATE = 0.05
WEIGHT_DECAY = 0.01
ADAM_EPS = 1e-08
CLIP_LIMIT = 0.01
OUTER_RATE = 0.7
OUTER_MU = 0.9
CONTRACT_ROWS = (((0,), (0,)), ((), ()))
CONTRACT_LAST = (((1,), (1,)), ((), ()))


def layer_norm(values, gain, shift):
    center = values - jnp.mean(values, -1, keepdims=True)
    spread = jnp.mean(center * center, -1, keepdims=True)
    return center * lax.rsqrt(spread + NORM_EPS) * gain + shift


def gelu_tanh(values):
    return jax.nn.gelu(values, approximate=True)


def low16(values):
    return values.astype(jnp.bfloat16)


NEG = -1e30
MESH = pl.DeviceIdType.MESH
VMEM_LIMIT = 60 * 1024 * 1024
WAYS = 4
SLOTS = 128
SPAN = WAYS * SLOTS
CHUNK = 256
UNROLL = 4
RAW_Q = 64
RAW_FLAGS = 72
RAW_ROWS = 80


def greet_all(many):
    me = lax.axis_index("dp")
    barrier = pltpu.get_barrier_semaphore()

    def greet(step, carry):
        peer = lax.rem(me + step, many)
        pl.semaphore_signal(barrier, inc=1, device_id={"dp": peer}, device_id_type=MESH)
        return carry

    lax.fori_loop(1, many, greet, 0)
    return me


def enter(many):
    me = greet_all(many)
    pl.semaphore_wait(pltpu.get_barrier_semaphore(), many - 1)
    return me


def copy_to(peer, src, dst, send, recv):
    return pltpu.make_async_remote_copy(
        src_ref=src,
        dst_ref=dst,
        send_sem=send,
        recv_sem=recv,
        device_id={"dp": peer},
        device_id_type=MESH,
    )


def spread_start(many, me, pairs, send, recv, slot):
    def step_start(step, carry):
        peer = lax.rem(me + step, many)
        for index, (source, landing) in enumerate(pairs):
            copy_to(
                peer,
                source(peer),
                landing.at[me],
                send.at[slot + index, peer],
                recv.at[slot + index, me],
            ).start()
        return carry

    lax.fori_loop(1, many, step_start, 0)


def spread_wait(many, me, pairs, send, recv, slot):
    def step_wait(step, carry):
        peer = lax.rem(me + step, many)
        for index, (source, landing) in enumerate(pairs):
            copy = copy_to(
                peer,
                source(peer),
                landing.at[peer],
                send.at[slot + index, peer],
                recv.at[slot + index, peer],
            )
            copy.wait_recv()
            copy.wait_send()
        return carry

    lax.fori_loop(1, many, step_wait, 0)


NEAR = 4


def place_of(many, me, far, near):
    row = lax.rem(me // NEAR + far, many // NEAR)
    return row * NEAR + lax.rem(lax.rem(me, NEAR) + near, NEAR)


def relay_start(many, me, source, landing, send, recv, slot):
    for near in range(NEAR):
        count = many // NEAR if near == 0 else 1

        def one(far, carry):
            peer = place_of(many, me, far, near)
            copy_to(peer, source, landing.at[me], send.at[slot, peer], recv.at[slot, me]).start()
            return carry

        lax.fori_loop(1 if near == 0 else 0, count, one, 0)


def relay_pass(many, me, source, landing, send, recv, slot):
    def one(far, carry):
        block = place_of(many, me, far, 0)
        copy_to(block, source, landing.at[block], send.at[slot, block], recv.at[slot, block]).wait_recv()
        for near in range(1, NEAR):
            peer = place_of(many, me, 0, near)
            key = place_of(many, me, far, near)
            copy_to(peer, landing.at[block], landing.at[block], send.at[slot, key], recv.at[slot, block]).start()
        return carry

    lax.fori_loop(1, many // NEAR, one, 0)


def relay_wait(many, me, source, landing, send, recv, slot):
    def one(far, carry):
        for near in range(NEAR):
            key = place_of(many, me, far, near)
            copy = copy_to(key, source, landing.at[key], send.at[slot, key], recv.at[slot, key])

            @pl.when((far > 0) | (near > 0))
            def _():
                copy.wait_send()

            if near > 0:
                copy.wait_recv()
        return carry

    lax.fori_loop(0, many // NEAR, one, 0)


def fold_start(many, me, blocks, landing, send, recv, slot):
    def one(row, carry):
        for near in range(1, NEAR):
            peer = place_of(many, me, 0, near)
            target = row * NEAR + lax.rem(peer, NEAR)
            copy_to(
                peer,
                blocks.at[target],
                landing.at[row * NEAR + lax.rem(me, NEAR)],
                send.at[slot, target],
                recv.at[slot, row * NEAR + lax.rem(me, NEAR)],
            ).start()
        mine = row * NEAR + lax.rem(me, NEAR)
        landing[mine] = blocks[mine]
        return carry

    lax.fori_loop(0, many // NEAR, one, 0)


def fold_pass(many, me, blocks, landing, halves, second, send, recv, slot, later):
    def one(row, carry):
        for near in range(1, NEAR):
            key = row * NEAR + lax.rem(place_of(many, me, 0, near), NEAR)
            copy = copy_to(
                place_of(many, me, 0, near), blocks.at[key], landing.at[key], send.at[slot, key], recv.at[slot, key]
            )
            copy.wait_recv()
            copy.wait_send()
        return carry

    lax.fori_loop(0, many // NEAR, one, 0)

    def two(far, carry):
        peer = place_of(many, me, far, 0)
        row = peer // NEAR
        total = landing[row * NEAR].astype(jnp.float32)
        for near in range(1, NEAR):
            total += landing[row * NEAR + near].astype(jnp.float32)
        halves[row] = total.astype(halves.dtype)

        @pl.when(far > 0)
        def _():
            copy_to(peer, halves.at[row], second.at[me // NEAR], send.at[later, row], recv.at[later, me // NEAR]).start()

        @pl.when(far == 0)
        def _():
            second[row] = halves[row]

        return carry

    lax.fori_loop(0, many // NEAR, two, 0)


def fold_wait(many, me, halves, second, send, recv, later):
    def one(far, carry):
        peer = place_of(many, me, far, 0)
        row = peer // NEAR
        copy = copy_to(peer, halves.at[row], second.at[row], send.at[later, row], recv.at[later, row])
        copy.wait_recv()
        copy.wait_send()
        return carry

    lax.fori_loop(1, many // NEAR, one, 0)
    return jnp.sum(second[...].astype(jnp.float32), 0)


def dot(left, right):
    return jnp.dot(left, right, preferred_element_type=jnp.float32)


def dot_rows(left, right):
    return lax.dot_general(left, right, CONTRACT_ROWS, preferred_element_type=jnp.float32)


def dot_last(left, right):
    return lax.dot_general(left, right, CONTRACT_LAST, preferred_element_type=jnp.float32)


def iota(shape, axis):
    return lax.broadcasted_iota(jnp.int32, shape, axis)


def hot(mask):
    return jnp.where(mask, 1.0, 0.0).astype(jnp.bfloat16)


def first_kernel(
    sizes,
    question_ref,
    passage_ref,
    length_q,
    length_p,
    key_q,
    valid_q,
    key_p,
    table_hbm,
    place_ref,
    every_ref,
    rows_ref,
    kept_ref,
    entry_ref,
    count_ref,
    stage,
    raw,
    ask,
    asks,
    low_ref,
    offer,
    landed,
    own,
    table_t,
    place_t,
    table_ref,
    fetch,
    send,
    recv,
):
    many = sizes.many
    count_q, count_p = sizes.count
    each = count_q + count_p
    depth = sizes.depth
    half = count_q // 2
    load = pltpu.make_async_copy(table_hbm, table_ref, fetch.at[0])
    load.start()
    me = greet_all(many)
    lane = iota((1, 128), 1)
    for seq in range(count_p):
        stop = length_p[seq]
        stage[seq : seq + 1, :] = jnp.where(lane < stop, passage_ref[seq : seq + 1, 0:128], -1)
        stage[count_p + seq : count_p + seq + 1, :] = jnp.where(
            lane + 128 < stop, passage_ref[seq : seq + 1, 128:256], -1
        )
    both = jnp.concatenate([question_ref[0:half, :], question_ref[half:count_q, :]], 1)
    for seq in range(half):
        stop = jnp.where(lane < 64, length_q[seq], length_q[half + seq] + 64)
        stage[RAW_Q + seq : RAW_Q + seq + 1, :] = jnp.where(lane < stop, both[seq : seq + 1], -1)
    flags = jnp.zeros((1, 128), jnp.int32)
    for spot in range(count_q):
        flags = jnp.where(lane == spot, key_q[spot], flags)
        flags = jnp.where(lane == count_q + spot, valid_q[spot], flags)
    for spot in range(count_p):
        flags = jnp.where(lane == 2 * count_q + spot, key_p[spot], flags)
    stage[RAW_FLAGS:RAW_ROWS, :] = jnp.broadcast_to(flags, (8, 128))
    raw[...] = stage[...].astype(jnp.int16)
    heads = jnp.concatenate([question_ref[:, 0:1], passage_ref[:, 0:1]], 0)
    diagonal = iota((each, 128), 0) == iota((each, 128), 1)
    heads = jnp.sum(jnp.where(diagonal, jnp.broadcast_to(heads, (each, 128)), 0), 0, keepdims=True)
    ask[...] = jnp.broadcast_to(heads, (8, 128))
    pl.semaphore_wait(pltpu.get_barrier_semaphore(), many - 1)
    ask_pairs = [(lambda peer: ask, asks)]
    spread_start(many, me, ask_pairs, send, recv, 0)
    relay_start(many, me, raw, every_ref, send, recv, 1)
    asks[me] = ask[...]
    every_ref[me] = raw[...]
    padded = sizes.padded
    if padded > depth:
        low_ref[...] = jnp.zeros_like(low_ref)
    load.wait()
    low_ref[0:depth, :] = low16(table_ref[...])
    first = me * depth
    block = math.gcd(many, 16)
    spread_wait(many, me, ask_pairs, send, recv, 0)
    relay_pass(many, me, raw, every_ref, send, recv, 1)

    def pick(step, carry):
        found = []
        for i in range(block):
            line = jnp.broadcast_to(asks[step * block + i][0:1, :].astype(jnp.float32), (each, 128))
            found.append(jnp.sum(jnp.where(diagonal, line, 0.0), 1, keepdims=True))
        place = jnp.concatenate(found, 0).astype(jnp.int32) - first
        spot = jnp.where((place >= 0) & (place < depth), place, -1)
        number = spot.shape[0]
        total = jnp.zeros((number, 128), jnp.float32)
        wide = jnp.broadcast_to(spot, (number, CHUNK))
        for at in range(padded // CHUNK):
            chosen = hot(wide == iota((number, CHUNK), 1) + at * CHUNK)
            total += dot(chosen, low_ref[at * CHUNK : (at + 1) * CHUNK, :])
        for i in range(block):
            offer[step * block + i] = low16(total[i * each : (i + 1) * each])
        return carry

    lax.fori_loop(0, many // block, pick, 0)
    offer_pairs = [(lambda peer: offer.at[peer], landed)]
    spread_start(many, me, offer_pairs, send, recv, 2)
    landed[me] = offer[me]
    if sizes.keep:
        prepare_tokens(sizes, table_ref, place_ref, table_t, place_t)
    relay_wait(many, me, raw, every_ref, send, recv, 1)

    row_pairs = [(lambda peer: own, rows_ref)]

    def send_rows():
        spread_wait(many, me, offer_pairs, send, recv, 2)
        own[...] = low16(jnp.sum(landed[...].astype(jnp.float32), 0))
        spread_start(many, me, row_pairs, send, recv, 3)
        rows_ref[me] = own[...]

    def spans_of(enc, count):
        def spans(turn, count):
            if enc == 1:
                pl.when(turn == 1)(send_rows)
            steps = [turn * sizes.unroll[enc] + u for u in range(sizes.unroll[enc])]
            packed = [pack_span(sizes, enc, s, 0, first, every_ref) for s in steps]
            found = [gather_span(sizes, enc, part[0], table_t, place_t) for part in packed]
            for part in packed:
                count = jnp.maximum(count, part[1])
            for u, s in enumerate(steps):
                at = s if enc == 0 else sizes.steps[0] + s
                kept_ref[at, 0:128, :] = found[u][0]
                kept_ref[at, 128:129, :] = found[u][1]
                entry_ref[at, 0:1, :] = packed[u][0]
            return count

        return lax.fori_loop(0, sizes.steps[enc] // sizes.unroll[enc], spans, count)

    count = jnp.zeros((8, 128), jnp.float32)
    if sizes.keep:
        count = spans_of(1, spans_of(0, count))
    else:
        send_rows()
    count_ref[...] = count
    spread_wait(many, me, row_pairs, send, recv, 3)


def first_stage(sizes, ids_q, ids_p, length_q, length_p, key_q, valid_q, key_p, table, positions):
    many = sizes.many
    padded = sizes.padded
    both = sum(sizes.count)
    vm = pl.BlockSpec(memory_space=pltpu.VMEM)
    sm = pl.BlockSpec(memory_space=pltpu.SMEM)
    kept = sizes.spans if sizes.keep else 1
    return pl.pallas_call(
        functools.partial(first_kernel, sizes),
        out_shape=(
            jax.ShapeDtypeStruct((many, RAW_ROWS, 128), jnp.int16),
            jax.ShapeDtypeStruct((many, both, 128), jnp.bfloat16),
            jax.ShapeDtypeStruct((kept, 136, SPAN), jnp.float32),
            jax.ShapeDtypeStruct((kept, 8, SPAN), jnp.int32),
            jax.ShapeDtypeStruct((8, 128), jnp.float32),
        ),
        in_specs=[vm, vm, sm, sm, sm, sm, sm, pl.BlockSpec(memory_space=pl.ANY), vm],
        out_specs=[vm] * 5,
        scratch_shapes=[
            pltpu.VMEM((RAW_ROWS, 128), jnp.int32),
            pltpu.VMEM((RAW_ROWS, 128), jnp.int16),
            pltpu.VMEM((8, 128), jnp.int32),
            pltpu.VMEM((many, 8, 128), jnp.int32),
            pltpu.VMEM((padded, 128), jnp.bfloat16),
            pltpu.VMEM((many, both, 128), jnp.bfloat16),
            pltpu.VMEM((many, both, 128), jnp.bfloat16),
            pltpu.VMEM((both, 128), jnp.bfloat16),
            pltpu.VMEM((128, padded), jnp.bfloat16),
            pltpu.VMEM((2, 2, 128, CHUNK), jnp.bfloat16),
            pltpu.VMEM((sizes.depth, 128), jnp.float32),
            pltpu.SemaphoreType.DMA((1,)),
            pltpu.SemaphoreType.DMA((4, many)),
            pltpu.SemaphoreType.DMA((4, many)),
        ],
        compiler_params=pltpu.CompilerParams(
            collective_id=1, has_side_effects=True, vmem_limit_bytes=VMEM_LIMIT
        ),
        name="first_stage",
    )(ids_q, ids_p, length_q, length_p, key_q, valid_q, key_p, table, positions)


def norm_rows(values, gain, shift):
    center = values - jnp.mean(values, -1, keepdims=True)
    spread = jnp.mean(center * center, -1, keepdims=True)
    return center * lax.rsqrt(spread + NORM_EPS) * gain + shift


def two_heads(values):
    lane = iota(values.shape, 1)
    low = jnp.where(lane < HEAD, values, jnp.zeros_like(values))
    high = jnp.where(lane >= HEAD, values, jnp.zeros_like(values))
    return jnp.concatenate([low, high], 0)


def merge_heads(both):
    half = both.shape[0] // 2
    lane = iota((half, both.shape[1]), 1)
    return jnp.where(lane < HEAD, both[:half], both[half:])


class Sizes:
    def __init__(self, many, count_q, count_p, depth):
        self.many = many
        self.count = (count_q, count_p)
        self.depth = depth
        self.padded = -(-depth // CHUNK) * CHUNK
        self.steps = (many // (2 * WAYS), many)
        self.unroll = tuple(math.gcd(UNROLL, step) for step in self.steps)
        self.spans = self.steps[0] + self.steps[1]
        self.devices = (2 * WAYS, 1)
        self.queries = (2 * WAYS * count_q, count_p)
        assert self.steps[1] // self.unroll[1] > 1
        self.lines = 1024 // many
        self.kind = jnp.bfloat16 if self.lines % 16 == 0 else jnp.float32
        self.keep = self.spans * 136 * SPAN * 4 <= 8 * 1024 * 1024


def vector_row(vec_ref, enc, row):
    return vec_ref[0, row, enc : enc + 1, :]


def prepare_tokens(sizes, table_ref, place_ref, table_t, place_t):
    depth = sizes.depth
    if sizes.padded > depth:
        table_t[...] = jnp.zeros_like(table_t)

    def turn(step, carry):
        spot = pl.ds(pl.multiple_of(step * 128, 128), 128)
        table_t[:, spot] = low16(jnp.transpose(table_ref[spot, :]))
        return carry

    whole = depth // 128
    lax.fori_loop(0, whole, turn, 0)
    rest = depth - whole * 128
    if rest:
        piece = jnp.concatenate([table_ref[whole * 128 :, :], jnp.zeros((128 - rest, 128), jnp.float32)], 0)
        table_t[:, whole * 128 : (whole + 1) * 128] = low16(jnp.transpose(piece))

    def turn_place(step, carry):
        enc, cut = (step // 2, step % 2)
        spot = pl.ds(pl.multiple_of(cut * 128, 128), 128)
        turned = jnp.transpose(place_ref[0, enc, spot, :])
        high = low16(turned)
        place_t[enc, 0, :, spot] = high
        place_t[enc, 1, :, spot] = low16(turned - high.astype(jnp.float32))
        return carry

    lax.fori_loop(0, 4, turn_place, 0)


def prepare_weights(attn_ref, vec_ref, w_kv, vec_t):
    for enc in range(2):
        for cut in range(2):
            w_kv[enc, cut * 128 : (cut + 1) * 128, :] = low16(
                jnp.transpose(attn_ref[0, enc, :, (cut + 1) * 128 : (cut + 2) * 128])
            )
        rows = [vector_row(vec_ref, enc, row) for row in range(4)]
        rows = jnp.concatenate(rows + [jnp.zeros((124, 128), jnp.float32)], 0)
        vec_t[enc] = jnp.transpose(rows)


def lane_pick(values, lanes):
    return jnp.take_along_axis(values, lanes, axis=1, mode="promise_in_bounds")


def pack_span(sizes, enc, step, level, first, raw_ref):
    if enc == 1:
        ids = raw_ref[step, 0:RAW_Q, :].astype(jnp.int32)
    else:
        ids = jnp.concatenate(
            [
                raw_ref[step * 8 + i, RAW_Q:RAW_ROWS, :].astype(jnp.int32)[0:8]
                for i in range(8)
            ],
            0,
        )
    place = ids - first
    owned = (place >= 0) & (place < sizes.depth)
    flag = hot(owned)
    inside = dot(flag, hot(iota((128, 128), 0) <= iota((128, 128), 1))).astype(jnp.int32)
    total = dot(flag, jnp.ones((128, 128), jnp.bfloat16))
    before = dot(hot(iota((64, 64), 1) < iota((64, 64), 0)), low16(total))
    start = before.astype(jnp.int32)
    stop = (before + total).astype(jnp.int32)
    line = iota((64, 128), 0)
    turn = iota((64, 128), 1)
    lane = jnp.zeros((64, 128), jnp.int32)
    for jump in (64, 32, 16, 8, 4, 2, 1):
        seen = lane_pick(inside, lane + (jump - 1))
        lane = jnp.where(seen <= turn, lane + jump, lane)
    row = lane_pick(place, lane)
    if enc == 1:
        where = (line >> 5) * 128 + lane
        seq = (line & 31) + 1
    else:
        where = lane & 63
        seq = (line >> 3) * sizes.count[0] + (lane >> 6) * 8 + (line & 7) + 1
    code = lane_pick((row << 16) + (where << 8) + seq, (turn - start) & 127)
    codes = []
    for window in range(WAYS):
        slot = turn + (window * SLOTS + level * SPAN)
        kept = jnp.where((slot >= start) & (slot < stop), code, 0)
        codes.append(jnp.sum(kept, 0, keepdims=True))
    return jnp.concatenate(codes, 1), (before + total)[56:64]


def gather_span(sizes, enc, code, table_t, place_t, short=False):
    rows = code >> 16
    where = (code >> 8) & 255
    x = jnp.zeros((128, SPAN), jnp.float32)
    wide = jnp.broadcast_to(rows, (CHUNK, SPAN))

    def add(cut, x):
        spot = pl.ds(pl.multiple_of(cut * CHUNK, CHUNK), CHUNK)
        return x + dot(table_t[:, spot], hot(wide == iota((CHUNK, SPAN), 0) + cut * CHUNK))

    x = lax.fori_loop(0, sizes.padded // CHUNK, add, x, unroll=not short)
    chosen = hot(jnp.broadcast_to(where, (CHUNK, SPAN)) == iota((CHUNK, SPAN), 0))
    x += dot(place_t[enc, 0], chosen) + dot(place_t[enc, 1], chosen)
    center = x - jnp.mean(x, 0, keepdims=True)
    rate = lax.rsqrt(jnp.mean(center * center, 0, keepdims=True) + NORM_EPS)
    return center * rate, rate


def project(enc, scaled, vec_t, w_kv):
    a_t = low16(scaled * vec_t[enc, :, 0:1] + vec_t[enc, :, 1:2])
    kv = dot(w_kv[enc], a_t)
    keys_t = low16(kv[:128])
    values_t = low16(kv[128:] + vec_t[enc, :, 3:4])
    return a_t, keys_t, values_t


def own_slots(code, number):
    line = iota((2 * number, SPAN), 0)
    line = jnp.where(line >= number, line - number, line)
    return line == (code & 255) - 1


def forward_kernel(
    sizes,
    raw_ref,
    rows_ref,
    kept_hbm,
    entry_hbm,
    count_ref,
    table_hbm,
    place_ref,
    attn_ref,
    vec_ref,
    out_ref,
    lse_ref,
    query_ref,
    levels_ref,
    table_t,
    place_t,
    w_kv,
    vec_t,
    query_q,
    total_q,
    top_q,
    mass_q,
    total_p,
    top_p,
    mass_p,
    kept_ref,
    entry_ref,
    load,
    table_ref,
    fetch,
):
    loads = load_kept(sizes, kept_hbm, entry_hbm, kept_ref, entry_ref, load)
    first = lax.axis_index("dp") * sizes.depth
    count_q, count_p = sizes.count
    prepare_weights(attn_ref, vec_ref, w_kv, vec_t)
    begin = 1 if sizes.keep else 0
    count = count_ref[...]
    block = math.gcd(sizes.many, 16)
    for enc in range(2):
        low, high = (0, count_q) if enc == 0 else (count_q, count_q + count_p)
        w_q = low16(attn_ref[0, enc, :, 0:128])

        def ask(step, carry):
            spot = pl.ds(step * block, block)
            held = rows_ref[spot, low:high, :].reshape(block * (high - low), 128)
            x = held.astype(jnp.float32) + place_ref[0, enc, 0:1, :]
            h = norm_rows(x, vector_row(vec_ref, enc, 0), vector_row(vec_ref, enc, 1))
            query = low16(dot(low16(h), w_q) + vector_row(vec_ref, enc, 2))
            query_ref[spot, low:high, :] = query.reshape(block, high - low, 128)
            if enc == 0:
                for half in range(block // 8):
                    query_q[step * (block // 8) + half] = query[half * 8 * count_q : (half + 1) * 8 * count_q]
            return carry

        lax.fori_loop(0, sizes.many // block, ask, 0)
    states = ((total_q, top_q, mass_q), (total_p, top_p, mass_p))
    lse_ref[...] = jnp.full_like(lse_ref, NEG)

    def close(enc, step, total, top, mass):
        some = mass > 0.0
        safe = jnp.where(some, mass, 1.0)
        mixed = merge_heads(total / safe)
        lse = jnp.where(some, top + jnp.log(safe), NEG)
        if enc == 1:
            out_ref[step, count_q:, :] = low16(mixed)
            at = iota(lse.shape, 0) == iota(lse.shape, 1)
            lse_ref[step, 0:1, :] = jnp.sum(jnp.where(at, lse, 0.0), 0, keepdims=True)
        else:
            half = lse.shape[0] // 2
            row = iota((count_q, 128), 0)
            lane = iota((count_q, 128), 1)
            for i in range(8):
                spot = slice(i * count_q, (i + 1) * count_q)
                out_ref[step * 8 + i, 0:count_q, :] = low16(mixed[spot])
                line = jnp.where(lane == row, lse[spot], 0.0) + jnp.where(
                    lane == row + count_q, lse[half + i * count_q : half + (i + 1) * count_q], 0.0
                )
                lse_ref[step * 8 + i, 1:2, :] = jnp.sum(line, 0, keepdims=True)

    def attend(enc, steps, codes, scaleds, olds):
        queries = [query_q[s] if enc == 0 else query_ref[s, count_q:, :] for s in steps]
        made = [project(enc, scaled, vec_t, w_kv) for scaled in scaleds]
        scores = [dot(two_heads(query), part[1]) * HEAD ** (-0.5) for query, part in zip(queries, made)]
        news = []
        for u, score in enumerate(scores):
            mine = own_slots(codes[u], queries[u].shape[0])
            score = jnp.where(mine, score, NEG)
            new = jnp.max(score, 1, keepdims=True)
            if olds is not None:
                new = jnp.maximum(olds[u][1][:, 0:1], new)
            expo = jnp.where(mine, jnp.exp(score - new), 0.0)
            total = dot_last(low16(expo), made[u][2])
            mass = jnp.sum(expo, 1, keepdims=True)
            if olds is not None:
                fade = jnp.exp(olds[u][1] - new)
                total = olds[u][0] * fade + total
                mass = olds[u][2] * fade + mass
            wide = (score.shape[0], 128)
            news.append((total, jnp.broadcast_to(new, wide), jnp.broadcast_to(mass, wide)))
        for u, s in enumerate(steps):
            for ref, value in zip(states[enc], news[u]):
                ref[s] = value
        return news

    for enc in range(2):
        if sizes.keep:
            for copy in loads[2 * enc : 2 * enc + 2]:
                copy.wait()

            def kept_spans(turn, carry):
                steps = [turn * sizes.unroll[enc] + u for u in range(sizes.unroll[enc])]
                ats = [s if enc == 0 else sizes.steps[0] + s for s in steps]
                news = attend(
                    enc, steps, [entry_ref[at, 0:1, :] for at in ats], [kept_ref[at, 0:128, :] for at in ats], None
                )
                for s, new in zip(steps, news):
                    close(enc, s, *new)
                return carry

            lax.fori_loop(0, sizes.steps[enc] // sizes.unroll[enc], kept_spans, 0)
        else:
            total, top, mass = states[enc]
            total[...] = jnp.zeros_like(total)
            mass[...] = jnp.zeros_like(mass)
            top[...] = jnp.full_like(top, NEG)

    def needed(count):
        return jnp.maximum((jnp.max(count).astype(jnp.int32) + SPAN - 1) // SPAN, 1)

    start = needed(count)
    levels_ref[0] = start

    @pl.when(start > begin)
    def _():
        copy = pltpu.make_async_copy(table_hbm, table_ref, fetch.at[0])
        copy.start()
        copy.wait()
        prepare_tokens(sizes, table_ref, place_ref, table_t, place_t)

        def one_level(state):
            level, unused, count = state
            for enc in range(2):

                def one_span(step, count):
                    code, found = pack_span(sizes, enc, step, level, first, raw_ref)
                    scaled = gather_span(sizes, enc, code, table_t, place_t, True)[0]
                    attend(enc, [step], [code], [scaled], [tuple(ref[step] for ref in states[enc])])
                    return jnp.maximum(count, found)

                count = lax.fori_loop(0, sizes.steps[enc], one_span, count)
            return level + 1, needed(count), count

        if sizes.keep:
            lax.fori_loop(
                begin, start, lambda level, carry: one_level((level, carry, count))[1], jnp.int32(0)
            )
        else:
            last = lax.while_loop(
                lambda state: state[0] < state[1], one_level, (jnp.int32(begin), start, count)
            )
            levels_ref[0] = last[1]
        for enc in range(2):

            def close_span(step, carry):
                close(enc, step, *(ref[step] for ref in states[enc]))
                return carry

            lax.fori_loop(0, sizes.steps[enc], close_span, 0)


def load_kept(sizes, kept_hbm, entry_hbm, kept_ref, entry_ref, load):
    if not sizes.keep:
        return []
    copies = []
    for enc, rows in enumerate((slice(0, sizes.steps[0]), slice(sizes.steps[0], sizes.spans))):
        for j, (source, target) in enumerate(((kept_hbm, kept_ref), (entry_hbm, entry_ref))):
            copy = pltpu.make_async_copy(source.at[rows], target.at[rows], load.at[enc, j])
            copy.start()
            copies.append(copy)
    return copies


def kept_scratch(sizes):
    kept = sizes.spans if sizes.keep else 1
    return [
        pltpu.VMEM((kept, 136, SPAN), jnp.float32),
        pltpu.VMEM((kept, 8, SPAN), jnp.int32),
        pltpu.SemaphoreType.DMA((2, 2)),
        pltpu.VMEM((sizes.depth, 128), jnp.float32),
        pltpu.SemaphoreType.DMA((1,)),
    ]


def token_scratch(sizes):
    return [
        pltpu.VMEM((128, sizes.padded), jnp.bfloat16),
        pltpu.VMEM((2, 2, 128, CHUNK), jnp.bfloat16),
        pltpu.VMEM((2, 256, 128), jnp.bfloat16),
        pltpu.VMEM((2, 128, 128), jnp.float32),
    ]


def local_call(kernel, out_shape, inputs, scratch, name, smem_in=(), smem_out=(), any_in=()):
    vm = pl.BlockSpec(memory_space=pltpu.VMEM)
    sm = pl.BlockSpec(memory_space=pltpu.SMEM)
    hbm = pl.BlockSpec(memory_space=pl.ANY)
    return pl.pallas_call(
        kernel,
        out_shape=out_shape,
        in_specs=[sm if i in smem_in else hbm if i in any_in else vm for i in range(len(inputs))],
        out_specs=[sm if i in smem_out else vm for i in range(len(out_shape))],
        scratch_shapes=scratch,
        compiler_params=pltpu.CompilerParams(vmem_limit_bytes=VMEM_LIMIT),
        name=name,
    )(*inputs)


def tokens_forward(sizes, every, rows, kept, entry, counted, table, positions, attention, vectors):
    many = sizes.many
    both = sum(sizes.count)
    state = []
    for enc in range(2):
        tall = 2 * sizes.queries[enc]
        state += [pltpu.VMEM((sizes.steps[enc], tall, 128), jnp.float32)] * 3
    return local_call(
        functools.partial(forward_kernel, sizes),
        (
            jax.ShapeDtypeStruct((many, both, 128), jnp.bfloat16),
            jax.ShapeDtypeStruct((many, 2, 128), jnp.float32),
            jax.ShapeDtypeStruct((many, both, 128), jnp.bfloat16),
            jax.ShapeDtypeStruct((1,), jnp.int32),
        ),
        (every, rows, kept, entry, counted, table, positions, attention, vectors),
        token_scratch(sizes)
        + [pltpu.VMEM((sizes.steps[0], sizes.queries[0], 128), jnp.bfloat16)]
        + state
        + kept_scratch(sizes),
        "tokens_forward",
        smem_out=(3,),
        any_in=(2, 3, 5),
    )


def mix_kernel(
    many, count_q, part_ref, lse_ref, mixed_ref, total_ref, landed, landed_lse, own, own_lse, send, recv
):
    me = enter(many)
    pairs = [
        (lambda peer: part_ref.at[peer], landed),
        (lambda peer: lse_ref.at[peer], landed_lse),
    ]
    spread_start(many, me, pairs, send, recv, 0)
    landed[me] = part_ref[me]
    landed_lse[me] = lse_ref[me]
    spread_wait(many, me, pairs, send, recv, 0)
    parts = landed_lse[...]
    top = jnp.max(parts, 0)
    total = top + jnp.log(jnp.sum(jnp.exp(parts - top[None]), 0))
    own_lse[...] = total
    share = jnp.exp(parts - total[None])
    count_p = part_ref.shape[1] - count_q
    mixed = jnp.zeros((count_q + count_p, 128), jnp.float32)
    for peer in range(many):
        factors = []
        for row, number in ((1, count_q), (0, count_p)):
            wide = (2 * number, 128)
            at = iota(wide, 0) == iota(wide, 1)
            line = jnp.broadcast_to(share[peer][row : row + 1], wide)
            column = jnp.sum(jnp.where(at, line, 0.0), 1, keepdims=True)
            lane = iota((number, 128), 1)
            factors.append(jnp.where(lane < HEAD, column[0:number], column[number:]))
        mixed += jnp.concatenate(factors, 0) * landed[peer].astype(jnp.float32)
    own[...] = low16(mixed)
    pairs = [(lambda peer: own, mixed_ref), (lambda peer: own_lse, total_ref)]
    spread_start(many, me, pairs, send, recv, 2)
    mixed_ref[me] = own[...]
    total_ref[me] = own_lse[...]
    spread_wait(many, me, pairs, send, recv, 2)


def remote_call(kernel, out_shape, inputs, scratch, lanes, many, ident, name):
    return pl.pallas_call(
        kernel,
        out_shape=out_shape,
        in_specs=[pl.BlockSpec(memory_space=pltpu.VMEM)] * len(inputs),
        out_specs=[pl.BlockSpec(memory_space=pltpu.VMEM)] * len(out_shape),
        scratch_shapes=scratch
        + [pltpu.SemaphoreType.DMA((lanes, many)), pltpu.SemaphoreType.DMA((lanes, many))],
        compiler_params=pltpu.CompilerParams(
            collective_id=ident, has_side_effects=True, vmem_limit_bytes=VMEM_LIMIT
        ),
        name=name,
    )(*inputs)


def exchange_mixed(sizes, part, lse):
    many = sizes.many
    both = sum(sizes.count)
    return remote_call(
        functools.partial(mix_kernel, many, sizes.count[0]),
        (
            jax.ShapeDtypeStruct((many, both, 128), jnp.bfloat16),
            jax.ShapeDtypeStruct((many, 2, 128), jnp.float32),
        ),
        (part, lse),
        [
            pltpu.VMEM((many, both, 128), jnp.bfloat16),
            pltpu.VMEM((many, 2, 128), jnp.float32),
            pltpu.VMEM((both, 128), jnp.bfloat16),
            pltpu.VMEM((2, 128), jnp.float32),
        ],
        4,
        many,
        2,
        "exchange_mixed",
    )


def backward_kernel(
    sizes,
    levels_ref,
    raw_ref,
    query_ref,
    mixed_ref,
    lse_ref,
    grad_ref,
    kept_hbm,
    entry_hbm,
    table_hbm,
    place_ref,
    attn_ref,
    vec_ref,
    d_query_ref,
    d_table_ref,
    slice_ref,
    table_t,
    place_t,
    w_kv,
    vec_t,
    d_place_ref,
    d_attn_ref,
    acc_gain,
    acc_shift,
    acc_value,
    d_query_q,
    d_query_p,
    kept_ref,
    entry_ref,
    load,
    table_ref,
    fetch,
):
    loads = load_kept(sizes, kept_hbm, entry_hbm, kept_ref, entry_ref, load)
    first = lax.axis_index("dp") * sizes.depth
    count_q, count_p = sizes.count
    prepare_weights(attn_ref, vec_ref, w_kv, vec_t)
    begin = 1 if sizes.keep else 0
    again = levels_ref[0] > begin

    @pl.when(again)
    def _():
        copy = pltpu.make_async_copy(table_hbm, table_ref, fetch.at[0])
        copy.start()
        copy.wait()
        prepare_tokens(sizes, table_ref, place_ref, table_t, place_t)

    for ref in (d_table_ref, d_place_ref, d_attn_ref, d_query_q, d_query_p, acc_gain, acc_shift, acc_value):
        ref[...] = jnp.zeros_like(ref)

    def ask_span(enc, step):
        if enc == 0:
            spot = pl.ds(step * 8, 8)
            shape = (8 * count_q, 128)
            found = [ref[spot, 0:count_q, :].reshape(shape) for ref in (query_ref, grad_ref, mixed_ref)]
            lines = [jnp.broadcast_to(lse_ref[step * 8 + i, 1:2, :], (count_q, 128)) for i in range(8)]
            lines = jnp.concatenate(lines, 0)
            row = iota(lines.shape, 0) % count_q
            lane = iota(lines.shape, 1)
            lse = [
                jnp.sum(jnp.where(lane == row + head * count_q, lines, 0.0), 1, keepdims=True)
                for head in range(2)
            ]
            lse = jnp.concatenate(lse, 0)
        else:
            found = [ref[step, count_q:, :] for ref in (query_ref, grad_ref, mixed_ref)]
            lines = jnp.broadcast_to(lse_ref[step, 0:1, :], (2 * count_p, 128))
            lse = jnp.sum(jnp.where(iota(lines.shape, 1) == iota(lines.shape, 0), lines, 0.0), 1, keepdims=True)
        return found + [lse]

    def work(enc, steps, codes, scaleds, rates, short=False):
        w_all = low16(attn_ref[0, enc, :, 128:384])
        asked = [ask_span(enc, step) for step in steps]
        made = [project(enc, scaled, vec_t, w_kv) for scaled in scaleds]
        d_queries, d_kvs = ([], [])
        for (query, grad, mixed, lse), code, (a_t, keys_t, values_t) in zip(asked, codes, made):
            both = two_heads(query)
            grads = two_heads(grad)
            base = jnp.sum(
                grads.astype(jnp.float32) * jnp.concatenate([mixed, mixed], 0).astype(jnp.float32),
                1,
                keepdims=True,
            )
            scores = dot(both, keys_t) * HEAD ** (-0.5)
            mine = own_slots(code, query.shape[0])
            probs = jnp.where(mine, jnp.exp(jnp.where(mine, scores, NEG) - lse), 0.0)
            d_probs = dot(grads, values_t)
            d_scores = low16(probs * (d_probs - base))
            d_values = low16(dot_rows(grads, low16(probs)))
            d_keys = low16(dot_rows(both, d_scores) * HEAD ** (-0.5))
            d_queries.append(merge_heads(dot_last(d_scores, keys_t)) * HEAD ** (-0.5))
            d_kvs.append(jnp.concatenate([d_keys, d_values], 0))
        for step, d_query in zip(steps, d_queries):
            if enc == 0:
                d_query_q[step] += d_query
            else:
                d_query_p[step] += d_query
        d_kv = jnp.concatenate(d_kvs, 1)
        a_t = jnp.concatenate([part[0] for part in made], 1)
        scaled = jnp.concatenate(scaleds, 1)
        rate = jnp.concatenate(rates, 1)
        code = jnp.concatenate(codes, 1)
        width = code.shape[1]
        d_attn_ref[enc] += dot_last(a_t, d_kv)
        d_h = dot(w_all, d_kv)
        fold = lambda values: sum(values[:, i * SPAN : (i + 1) * SPAN] for i in range(width // SPAN))
        acc_value[enc] += fold(d_kv[128:].astype(jnp.float32))
        acc_gain[enc] += fold(d_h * scaled)
        acc_shift[enc] += fold(d_h)
        d_scaled = d_h * vec_t[enc, :, 0:1]
        center = d_scaled - jnp.mean(d_scaled, 0, keepdims=True)
        slope = jnp.mean(d_scaled * scaled, 0, keepdims=True)
        d_x = low16((center - scaled * slope) * rate)
        rows = code >> 16
        where = (code >> 8) & 255
        chosen = hot(jnp.broadcast_to(where, (CHUNK, width)) == iota((CHUNK, width), 0))
        d_place_ref[enc] += dot_last(d_x, chosen)
        wide = jnp.broadcast_to(rows, (CHUNK, width))

        def add(cut, carry):
            spot = pl.ds(pl.multiple_of(cut * CHUNK, CHUNK), CHUNK)
            chosen = hot(wide == iota((CHUNK, width), 0) + cut * CHUNK)
            d_table_ref[spot, :] += dot_last(chosen, d_x)
            return carry

        lax.fori_loop(0, sizes.padded // CHUNK, add, 0, unroll=not short)

    for enc in range(2):
        if sizes.keep:
            for copy in loads[2 * enc : 2 * enc + 2]:
                copy.wait()

            def kept_spans(turn, carry):
                steps = [turn * sizes.unroll[enc] + u for u in range(sizes.unroll[enc])]
                ats = [s if enc == 0 else sizes.steps[0] + s for s in steps]
                work(
                    enc,
                    steps,
                    [entry_ref[at, 0:1, :] for at in ats],
                    [kept_ref[at, 0:128, :] for at in ats],
                    [kept_ref[at, 128:129, :] for at in ats],
                )
                return carry

            lax.fori_loop(0, sizes.steps[enc] // sizes.unroll[enc], kept_spans, 0)

        def more_level(level, carry_level):
            def one_span(step, carry):
                code = pack_span(sizes, enc, step, level, first, raw_ref)[0]
                scaled, rate = gather_span(sizes, enc, code, table_t, place_t, True)
                work(enc, [step], [code], [scaled], [rate], True)
                return carry

            return lax.fori_loop(0, sizes.steps[enc], one_span, carry_level)

        lax.fori_loop(begin, levels_ref[0], more_level, 0)

    for step in range(sizes.steps[0]):
        d_query_ref[step * 8 : step * 8 + 8, 0:count_q, :] = low16(d_query_q[step]).reshape(8, count_q, 128)
    d_query_ref[:, count_q:, :] = low16(d_query_p[...])
    for enc in range(2):
        for part, block in enumerate((d_place_ref, d_attn_ref)):
            for cut in range(2):
                slice_ref[enc, 2 * part + cut] = block[enc, :, cut * 128 : (cut + 1) * 128].astype(
                    slice_ref.dtype
                )
    slice_ref[0, 1] = jnp.zeros_like(slice_ref[0, 1])
    sums = []
    same = iota((128, 128), 0) == iota((128, 128), 1)
    for enc in range(2):
        for row, acc in enumerate((acc_gain, acc_shift, acc_value)):
            tall = jnp.broadcast_to(jnp.sum(acc[enc], 1, keepdims=True), (128, 128))
            sums.append(jnp.sum(jnp.where(same, tall, 0.0), 0, keepdims=True))
    sums = jnp.concatenate(sums + [jnp.zeros((10, 128), jnp.float32)], 0)
    slice_ref[0, 1, 0:16, :] = sums.astype(slice_ref.dtype)


def tokens_backward(sizes, levels, every, query, mixed, lse, grad, kept, entry, table, positions, attention, vectors):
    many = sizes.many
    count_p = sizes.count[1]
    both = sum(sizes.count)
    return local_call(
        functools.partial(backward_kernel, sizes),
        (
            jax.ShapeDtypeStruct((many, both, 128), jnp.bfloat16),
            jax.ShapeDtypeStruct((sizes.padded, 128), jnp.float32),
            jax.ShapeDtypeStruct((2, 4, 128, 128), sizes.kind),
        ),
        (levels, every, query, mixed, lse, grad, kept, entry, table, positions, attention, vectors),
        token_scratch(sizes)
        + [
            pltpu.VMEM((2, 128, CHUNK), jnp.float32),
            pltpu.VMEM((2, 128, 256), jnp.float32),
            pltpu.VMEM((2, 128, SPAN), jnp.float32),
            pltpu.VMEM((2, 128, SPAN), jnp.float32),
            pltpu.VMEM((2, 128, SPAN), jnp.float32),
            pltpu.VMEM((sizes.steps[0], sizes.queries[0], 128), jnp.float32),
            pltpu.VMEM((many, count_p, 128), jnp.float32),
        ]
        + kept_scratch(sizes),
        "tokens_backward",
        smem_in=(0,),
        any_in=(6, 7, 8),
    )


def adam(weight, grad, first, second):
    first_new = BETA_ONE * first + (1.0 - BETA_ONE) * grad
    second_new = BETA_TWO * second + (1.0 - BETA_TWO) * grad * grad
    fix_one = 1.0 - BETA_ONE**STEP
    fix_two = 1.0 - BETA_TWO**STEP
    ratio = first_new / fix_one / (jnp.sqrt(second_new / fix_two) + ADAM_EPS)
    return (first_new, second_new, weight - INNER_RATE * (ratio + WEIGHT_DECAY * weight))


def pieces_of(depth):
    blocks = [(1, (enc,)) for enc in range(2)] + [(2, (enc,)) for enc in range(2)]
    blocks += [(3, (enc, side)) for enc in range(2) for side in range(2)]
    return blocks + [(4, ())]


def square_sum(values):
    return jnp.sum(jnp.sum(values * values, 0, keepdims=True), 1, keepdims=True)


def finish_kernel(sizes, *refs):
    many = sizes.many
    count_q, count_p = sizes.count
    depth = sizes.depth
    (query_ref, slice_ref, d_table_hbm, rows_ref, raw_ref, xa_q, xa_p, d_out, d_ffn_hbm, d_mid) = refs[:10]
    place_ref, attn_ref, vec_ref = refs[10:13]
    state = refs[13:33]
    norm_ref, g_word, g_place, g_attn, g_vec = refs[33:38]
    joined = refs[38:43]
    held = refs[43:63]
    mine = refs[63:68]
    theirs = refs[68:73]
    (query_all, slice_all, scalar_all, land_query, land_slice, own_query, own_slice, tile, table_t) = refs[73:82]
    half_query, far_query, half_slice, far_slice, d_table_ref, d_ffn = refs[82:88]
    send, recv, load, pair_send, pair_recv = refs[88:93]
    loads, early = ([], [])
    for index, (source, target) in enumerate(((d_table_hbm, d_table_ref), (d_ffn_hbm, d_ffn))):
        copy = pltpu.make_async_copy(source, target, load.at[20 + index])
        copy.start()
        early.append(copy)
    for index in range(20):
        copy = pltpu.make_async_copy(state[index], held[index], load.at[index])
        copy.start()
        loads.append(copy)
    me = lax.axis_index("dp")
    other = 1 - lax.axis_index("grp")
    barrier = pltpu.get_barrier_semaphore()

    def greet(step, carry):
        peer = lax.rem(me + step, many)
        pl.semaphore_signal(barrier, inc=1, device_id={"dp": peer}, device_id_type=MESH)
        return carry

    lax.fori_loop(1, many, greet, 0)
    pl.semaphore_signal(barrier, inc=1, device_id={"grp": other}, device_id_type=MESH)
    pl.semaphore_wait(barrier, many)
    fold_start(many, me, query_ref, land_query, send, recv, 0)
    fold_start(many, me, slice_ref, land_slice, send, recv, 1)
    fold_pass(many, me, query_ref, land_query, half_query, far_query, send, recv, 0, 6)
    fold_pass(many, me, slice_ref, land_slice, half_slice, far_slice, send, recv, 1, 7)
    own_query[...] = low16(fold_wait(many, me, half_query, far_query, send, recv, 6))
    relay_start(many, me, own_query, query_all, send, recv, 3)
    query_all[me] = own_query[...]
    own_slice[...] = fold_wait(many, me, half_slice, far_slice, send, recv, 7).astype(own_slice.dtype)
    relay_start(many, me, own_slice, slice_all, send, recv, 4)
    slice_all[me] = own_slice[...]
    relay_pass(many, me, own_query, query_all, send, recv, 3)
    relay_pass(many, me, own_slice, slice_all, send, recv, 4)
    relay_wait(many, me, own_query, query_all, send, recv, 3)

    g_vec[...] = d_mid[...]
    tops = []
    for copy in early:
        copy.wait()
    first = me * depth
    table_t[...] = jnp.zeros_like(table_t)
    rest = jnp.zeros((1, 1), jnp.float32)
    places = []
    for enc in range(2):
        low, high = (0, count_q) if enc == 0 else (count_q, count_q + count_p)
        number = many * (high - low)
        d_query = query_all[:, low:high, :].reshape(number, 128)
        x = rows_ref[:, low:high, :].reshape(number, 128).astype(jnp.float32) + place_ref[0, enc, 0:1, :]
        center = x - jnp.mean(x, -1, keepdims=True)
        rate = lax.rsqrt(jnp.mean(center * center, -1, keepdims=True) + NORM_EPS)
        scaled = center * rate
        gain = vector_row(vec_ref, enc, 0)
        a_low = low16(scaled * gain + vector_row(vec_ref, enc, 1))
        xa = xa_q if enc == 0 else xa_p
        d_h = xa[...] + dot_last(d_query, low16(attn_ref[0, enc, :, 0:128]))
        d_scaled = d_h * gain
        slope = jnp.mean(d_scaled * scaled, -1, keepdims=True)
        d_x = (d_scaled - jnp.mean(d_scaled, -1, keepdims=True) - scaled * slope) * rate
        d_place = jnp.sum(d_x, 0, keepdims=True)
        places.append(d_place)
        g_attn[enc, :, 0:128] = dot_rows(a_low, d_query)
        g_attn[enc, :, 384:512] = d_out[enc]
        spot = slice(enc, enc + 1)
        g_vec[2, spot, :] = jnp.sum(d_query.astype(jnp.float32), 0, keepdims=True)
        tops.append((jnp.sum(d_h * scaled, 0, keepdims=True), jnp.sum(d_h, 0, keepdims=True)))
        if enc == 0:
            columns = [
                part
                for peer in range(many)
                for part in (
                    raw_ref[peer, RAW_Q : RAW_Q + 16, 0:1].astype(jnp.int32)[0 : count_q // 2],
                    raw_ref[peer, RAW_Q : RAW_Q + 16, 64:65].astype(jnp.int32)[0 : count_q // 2],
                )
            ]
        else:
            columns = [raw_ref[peer, 0:count_p, 0:1].astype(jnp.int32) for peer in range(many)]
        spot = jnp.concatenate(columns, 0) - first
        spot = jnp.where(spot < depth, spot, -1)
        d_low = low16(d_x)
        wide = jnp.broadcast_to(spot, (number, CHUNK))
        for cut in range(sizes.padded // CHUNK):
            chosen = hot(wide == iota((number, CHUNK), 1) + cut * CHUNK)
            table_t[:, cut * CHUNK : (cut + 1) * CHUNK] += dot_rows(d_low, chosen)
        rest += square_sum(d_ffn[enc, 0]) + square_sum(d_ffn[enc, 1])
    for cut in range(0, depth, 128):
        top = min(cut + 128, depth)
        g_word[cut:top, :] = d_table_ref[cut:top, :] + jnp.transpose(table_t[:, cut : cut + 128])[0 : top - cut]
    tile[...] = jnp.broadcast_to(square_sum(g_word[...]), (8, 128))
    pairs = [(lambda peer: tile, scalar_all)]
    spread_start(many, me, pairs, send, recv, 5)
    scalar_all[me] = tile[...]
    relay_wait(many, me, own_slice, slice_all, send, recv, 4)
    blocks = slice_all[...].astype(jnp.float32).reshape(8, 128, 128)
    for enc in range(2):
        spot = slice(enc, enc + 1)
        g_vec[0, spot, :] = blocks[1][enc * 3 : enc * 3 + 1] + tops[enc][0]
        g_vec[1, spot, :] = blocks[1][enc * 3 + 1 : enc * 3 + 2] + tops[enc][1]
        g_vec[3, spot, :] = blocks[1][enc * 3 + 2 : enc * 3 + 3]
        g_place[enc, 0:128, :] = jnp.transpose(blocks[enc * 4])
        if enc == 0:
            g_place[enc, 128:256, :] = jnp.zeros((128, 128), jnp.float32)
        else:
            g_place[enc, 128:256, :] = jnp.transpose(blocks[enc * 4 + 1])
        g_place[enc, 0:1, :] += places[enc]
        g_attn[enc, :, 128:256] = blocks[enc * 4 + 2]
        g_attn[enc, :, 256:384] = blocks[enc * 4 + 3]
        rest += square_sum(g_place[enc]) + square_sum(g_attn[enc])
    small = jnp.sum(g_vec[...] * g_vec[...], 0)
    rest += jnp.sum(jnp.sum(small, 0, keepdims=True), 1, keepdims=True)
    for copy in loads:
        copy.wait()
    spread_wait(many, me, pairs, send, recv, 5)
    norm = jnp.sqrt(jnp.sum(scalar_all[...], 0)[0:1, 0:1] + rest)
    norm_ref[...] = jnp.broadcast_to(norm, (8, 128))
    factor = CLIP_LIMIT / jnp.maximum(norm, CLIP_LIMIT)
    grads = (g_word, g_place, g_attn, d_ffn, g_vec)

    def differ(kind, at, rows):
        weight, moment, square, anchor = (held[kind * 4 + j] for j in range(4))
        grad = grads[kind][at + (rows,)] * factor
        inner = adam(weight[(0,) + at + (rows,)], grad, moment[(0,) + at + (rows,)], square[(0,) + at + (rows,)])[2]
        mine[kind][at + (rows,)] = (anchor[at + (rows,)] - inner).astype(mine[kind].dtype)

    size = math.gcd(depth, 128)

    def table_block(step, carry):
        differ(0, (), pl.ds(pl.multiple_of(step * size, size), size))
        return carry

    lax.fori_loop(0, depth // size, table_block, 0)
    ways = []

    def hand(kind):
        copy = pltpu.make_async_remote_copy(
            src_ref=mine[kind],
            dst_ref=theirs[kind],
            send_sem=pair_send.at[kind],
            recv_sem=pair_recv.at[kind],
            device_id={"grp": other},
            device_id_type=MESH,
        )
        copy.start()
        ways.append(copy)

    hand(0)
    for kind in range(1, 5):
        for found, at in pieces_of(depth):
            if found == kind:
                differ(kind, at, slice(0, 14) if kind == 4 else slice(None))
        hand(kind)
    def join(kind, spot):
        joined[kind][spot] = mine[kind][spot].astype(jnp.float32) + theirs[kind][spot].astype(jnp.float32)

    def table_add(step, carry):
        join(0, pl.ds(pl.multiple_of(step * size, size), size))
        return carry

    ways[0].wait()
    lax.fori_loop(0, depth // size, table_add, 0)
    for kind in range(1, 5):
        ways[kind].wait()
        for found, at in pieces_of(depth):
            if found == kind:
                join(kind, at if at else slice(None))


def finish(sizes, query, slices, d_table, rows, every, xa_q, xa_p, d_out, d_ffn, d_mid, params, state):
    many = sizes.many
    both = sum(sizes.count)
    inputs = (query, slices, d_table, rows, every, xa_q, xa_p, d_out, d_ffn, d_mid) + params
    flat = tuple(state[j][kind] for kind in range(5) for j in range(4))
    shapes = [state[3][kind].shape for kind in range(5)]
    vm = pl.BlockSpec(memory_space=pltpu.VMEM)
    hbm = pl.BlockSpec(memory_space=pl.ANY)
    f32 = jnp.float32
    return pl.pallas_call(
        functools.partial(finish_kernel, sizes),
        out_shape=tuple(
            jax.ShapeDtypeStruct(shape, f32)
            for shape in [(8, 128), shapes[0], shapes[1], shapes[2], (16, 2, 128)] + shapes
        ),
        in_specs=[hbm if i in (2, 8) else vm for i in range(len(inputs))] + [hbm] * 20,
        out_specs=[vm] * 10,
        scratch_shapes=[pltpu.VMEM(value.shape, f32) for value in flat]
        + [pltpu.VMEM(shape, jnp.bfloat16 if kind < 4 else f32) for kind, shape in enumerate(shapes)] * 2
        + [
            pltpu.VMEM((many, both, 128), jnp.bfloat16),
            pltpu.VMEM((many, sizes.lines, 128), sizes.kind),
            pltpu.VMEM((many, 8, 128), f32),
            pltpu.VMEM((many, both, 128), jnp.bfloat16),
            pltpu.VMEM((many, sizes.lines, 128), sizes.kind),
            pltpu.VMEM((both, 128), jnp.bfloat16),
            pltpu.VMEM((sizes.lines, 128), sizes.kind),
            pltpu.VMEM((8, 128), f32),
            pltpu.VMEM((128, sizes.padded), f32),
            pltpu.VMEM((many // NEAR, both, 128), jnp.bfloat16),
            pltpu.VMEM((many // NEAR, both, 128), jnp.bfloat16),
            pltpu.VMEM((many // NEAR, sizes.lines, 128), sizes.kind),
            pltpu.VMEM((many // NEAR, sizes.lines, 128), sizes.kind),
            pltpu.VMEM(d_table.shape, f32),
            pltpu.VMEM(d_ffn.shape, f32),
            pltpu.SemaphoreType.DMA((8, many)),
            pltpu.SemaphoreType.DMA((8, many)),
            pltpu.SemaphoreType.DMA((22,)),
            pltpu.SemaphoreType.DMA((5,)),
            pltpu.SemaphoreType.DMA((5,)),
        ],
        compiler_params=pltpu.CompilerParams(
            collective_id=3, has_side_effects=True, vmem_limit_bytes=VMEM_LIMIT
        ),
        name="finish",
    )(*inputs, *flat)


def output_parts(depth):
    rows = depth // 3 if depth % 24 == 0 else depth
    parts = [(0, slice(at, at + rows)) for at in range(0, depth, rows)]
    return parts + [(kind, None) for kind in (3, 2, 1, 4)]


def outputs_kernel(depth, groups, *refs):
    norm_ref, g_vec = refs[:2]
    ins = refs[2:31]
    outs = refs[31:56]
    total_ref = refs[56]
    held = refs[57:86]
    made = refs[86:111]
    load, store = refs[111:113]
    parts = output_parts(depth)
    loads, stores = ([], [])
    for number, (kind, rows) in enumerate(parts):
        group = []
        for j in range(6 if kind < 4 else 5):
            index = kind * 5 + j if j < 5 else 25 + kind
            source, target = (ins[index], held[index])
            if rows is not None:
                lead = (0,) if len(source.shape) == 3 else ()
                source, target = (source.at[lead + (rows,)], target.at[lead + (rows,)])
            copy = pltpu.make_async_copy(source, target, load.at[number, j])
            copy.start()
            group.append(copy)
        loads.append(group)
    total_ref[0] = jnp.max(norm_ref[...])
    norm = norm_ref[0:1, 0:1]
    factor = CLIP_LIMIT / jnp.maximum(norm, CLIP_LIMIT)
    grads = tuple(held[25:29]) + (g_vec,)

    def work(kind, at, rows):
        moment, square, anchor, outer, summed = (held[kind * 5 + j] for j in range(5))
        first, second, average, momentum, weight = (made[kind * 5 + j] for j in range(5))
        spot = at + (rows,)
        deep = (0,) + spot
        grad = grads[kind][spot] * factor
        first[deep] = BETA_ONE * moment[deep] + (1.0 - BETA_ONE) * grad
        second[deep] = BETA_TWO * square[deep] + (1.0 - BETA_TWO) * grad * grad
        mean = summed[spot] / groups
        speed = OUTER_MU * outer[spot] + mean
        average[spot] = mean
        momentum[spot] = speed
        weight[deep] = anchor[spot] - OUTER_RATE * (mean + OUTER_MU * speed)

    for number, (kind, rows) in enumerate(parts):
        for copy in loads[number]:
            copy.wait()
        if kind == 0:
            size = math.gcd(rows.stop - rows.start, 128)

            def table_block(step, carry):
                work(0, (), pl.ds(pl.multiple_of(rows.start + step * size, size), size))
                return carry

            lax.fori_loop(0, (rows.stop - rows.start) // size, table_block, 0)
        else:
            for found, at in pieces_of(depth):
                if found == kind:
                    work(kind, at, slice(0, 14) if kind == 4 else slice(None))
        for j in range(5):
            source, target = (made[kind * 5 + j], outs[kind * 5 + j])
            if rows is not None:
                lead = (0,) if len(source.shape) == 3 else ()
                source, target = (source.at[lead + (rows,)], target.at[lead + (rows,)])
            copy = pltpu.make_async_copy(source, target, store.at[number, j])
            copy.start()
            stores.append(copy)
    for copy in stores:
        copy.wait()


def make_outputs(norm, grads, firsts, seconds, anchors, outers, summed, groups):
    kinds = range(5)
    flat = tuple(v for kind in kinds for v in (firsts[kind], seconds[kind], anchors[kind], outers[kind], summed[kind]))
    flat += tuple(grads[:4])
    out = tuple(
        jax.ShapeDtypeStruct(shape, jnp.float32)
        for kind in kinds
        for shape in (firsts[kind].shape, firsts[kind].shape, anchors[kind].shape, anchors[kind].shape, firsts[kind].shape)
    )
    vm = pl.BlockSpec(memory_space=pltpu.VMEM)
    hbm = pl.BlockSpec(memory_space=pl.ANY)
    got = pl.pallas_call(
        functools.partial(outputs_kernel, anchors[0].shape[0], groups),
        out_shape=out + (jax.ShapeDtypeStruct((1,), jnp.float32),),
        in_specs=[vm] * 2 + [hbm] * 29,
        out_specs=[hbm] * 25 + [pl.BlockSpec(memory_space=pltpu.SMEM)],
        scratch_shapes=[pltpu.VMEM(v.shape, jnp.float32) for v in flat]
        + [pltpu.VMEM(v.shape, jnp.float32) for v in out]
        + [pltpu.SemaphoreType.DMA((7, 6)), pltpu.SemaphoreType.DMA((7, 5))],
        compiler_params=pltpu.CompilerParams(vmem_limit_bytes=VMEM_LIMIT),
        name="make_outputs",
    )(norm, grads[4], *flat)
    return [[got[kind * 5 + j] for kind in kinds] for j in range(5)], got[25]


def square_norm(values):
    center = values - jnp.mean(values, -1, keepdims=True)
    rate = lax.rsqrt(jnp.mean(center * center, -1, keepdims=True) + NORM_EPS)
    return center * rate, rate


def norm_back(d_scaled, scaled, rate):
    slope = jnp.mean(d_scaled * scaled, -1, keepdims=True)
    return (d_scaled - jnp.mean(d_scaled, -1, keepdims=True) - scaled * slope) * rate


def total_of(values):
    return jnp.sum(jnp.sum(values, 0, keepdims=True), 1, keepdims=True)


def score_terms(scores, drop, target, weight, count, axis):
    masked = jnp.where(drop, MASKED, scores)
    top = jnp.max(masked, axis, keepdims=True)
    expo = jnp.exp(masked - top)
    total = jnp.sum(expo, axis, keepdims=True)
    picked = jnp.sum(jnp.where(target, scores, 0.0), axis, keepdims=True)
    loss = total_of(weight * (top + jnp.log(total) - picked))
    grad = low16((weight / count) * (expo / total - jnp.where(target, 1.0, 0.0)))
    return grad, loss


GELU_A = math.sqrt(2.0 / math.pi)
GELU_B = 0.044715


def class_kernel(
    sizes,
    rows_ref,
    mixed_ref,
    raw_ref,
    place_ref,
    attn_ref,
    ffn_ref,
    vec_ref,
    grad_ref,
    xa_q,
    xa_p,
    d_out,
    d_ffn,
    d_mid,
    loss_ref,
    count_ref,
    cls_ref,
    scaled_a,
    rate_a,
    scaled_f,
    rate_f,
    pre_ref,
    act_ref,
    low_ref,
    flag_ref,
):
    many = sizes.many
    counts = sizes.count
    totals = (many * counts[0], many * counts[1])
    chunk = totals[0]
    parts = [(0, 0, 0)] + [(1, at, totals[0] + at) for at in range(0, totals[1], chunk)]

    def held(ref, enc, at):
        each = counts[enc]
        low = 0 if enc == 0 else counts[0]
        return ref[at // each : (at + chunk) // each, low : low + each, :].reshape(chunk, 128)

    def weights(enc):
        return (
            low16(attn_ref[0, enc, :, 384:512]),
            low16(ffn_ref[0, enc, 0]),
            low16(ffn_ref[0, enc, 1]),
        )

    for enc, at, spot in parts:
        w_out, w_up, w_down = weights(enc)
        row = functools.partial(vector_row, vec_ref, enc)
        here = slice(spot, spot + chunk)
        x = held(rows_ref, enc, at).astype(jnp.float32) + place_ref[0, enc, 0:1, :]
        h_embed = norm_rows(x, row(0), row(1))
        scaled, rate = square_norm(h_embed + (dot(held(mixed_ref, enc, at), w_out) + row(4)))
        scaled_a[here, :] = scaled
        rate_a[here, :] = jnp.broadcast_to(rate, (chunk, 128))
        h_attn = scaled * row(5) + row(6)
        h_low = low16(h_attn)
        low_ref[here, :] = h_low
        pre = dot(h_low, w_up) + jnp.concatenate([row(10), row(11), row(12), row(13)], 1)
        pre_ref[here, :] = pre
        act = low16(0.5 * pre * (1.0 + jnp.tanh(GELU_A * (pre + GELU_B * (pre * pre * pre)))))
        act_ref[here, :] = act
        scaled, rate = square_norm(h_attn + (dot_last(act, w_down) + row(7)))
        scaled_f[here, :] = scaled
        rate_f[here, :] = jnp.broadcast_to(rate, (chunk, 128))
        cls_ref[here, :] = low16(scaled * row(8) + row(9))

    every_q = cls_ref[0 : totals[0], :]
    every_p = cls_ref[totals[0] :, :]
    flag_ref[...] = jnp.zeros_like(flag_ref)
    for peer in range(many):
        flag_ref[peer : peer + 1, :] = raw_ref[peer, RAW_Q:RAW_ROWS, :].astype(jnp.float32)[8:9]
    turned = jnp.transpose(flag_ref[...])

    def column(low, each):
        tall = jnp.concatenate([turned[low : low + each]] * many, 0)
        at = iota(tall.shape, 1) == iota(tall.shape, 0) // each
        return jnp.sum(jnp.where(at, tall, 0.0), 1, keepdims=True)

    keys_q = column(0, counts[0])
    valid = column(counts[0], counts[0])
    keys_p = column(2 * counts[0], counts[1])
    hot_q = hot(jnp.broadcast_to(keys_q, (totals[0], 128)) == iota((totals[0], 128), 1).astype(jnp.float32))
    hot_p = hot(jnp.broadcast_to(keys_p, (totals[1], 128)) == iota((totals[1], 128), 1).astype(jnp.float32))
    same = dot_last(hot_q, hot_p) > 0.5
    count = jnp.maximum(total_of(valid), 1.0)
    scale = 128 ** (-0.5)
    scores = dot_last(every_q, every_p) * scale
    index_q = iota(scores.shape, 0)
    index_p = iota(scores.shape, 1)
    target_qp = index_p == 2 * index_q
    target_pq = index_p // 2 == index_q
    grad_qp, loss_qp = score_terms(scores, same & ~target_qp, target_qp, valid, count, 1)
    drop_pq = (same | (jnp.broadcast_to(valid, scores.shape) == 0.0)) & ~target_pq
    weight_p = jnp.sum(jnp.where(target_qp, jnp.broadcast_to(valid, scores.shape), 0.0), 0, keepdims=True)
    grad_pq, loss_pq = score_terms(scores, drop_pq, target_pq, weight_p, count, 0)
    loss_ref[0] = jnp.max(loss_qp + loss_pq)
    count_ref[0] = jnp.max(count)
    d_q = (dot(grad_qp, every_p) + dot(grad_pq, every_p)) * scale
    d_p = (dot_rows(grad_pq, every_q) + dot_rows(grad_qp, every_q)) * scale

    d_mid[...] = jnp.zeros_like(d_mid)
    d_out[...] = jnp.zeros_like(d_out)
    d_ffn[...] = jnp.zeros_like(d_ffn)
    for enc, at, spot in parts:
        w_out, w_up, w_down = weights(enc)
        row = functools.partial(vector_row, vec_ref, enc)
        here = slice(spot, spot + chunk)

        def add(index, values):
            d_mid[index, enc : enc + 1, :] += jnp.sum(values, 0, keepdims=True)

        d_cls = d_q if enc == 0 else d_p[at : at + chunk]
        scaled = scaled_f[here, :]
        add(8, d_cls * scaled)
        add(9, d_cls)
        d_x_ffn = norm_back(d_cls * row(8), scaled, rate_f[here, :])
        d_branch = low16(d_x_ffn)
        add(7, d_branch.astype(jnp.float32))
        d_ffn[enc, 1] += dot_rows(d_branch, act_ref[here, :])
        d_act = dot(d_branch, w_down)
        pre = pre_ref[here, :]
        square = pre * pre
        bend = jnp.tanh(GELU_A * (pre + GELU_B * (square * pre)))
        slope = 0.5 * (1.0 + bend) + (0.5 * GELU_A) * pre * (1.0 - bend * bend) * (
            1.0 + (3.0 * GELU_B) * square
        )
        d_pre = low16(slope * d_act)
        up_bias = jnp.sum(d_pre.astype(jnp.float32), 0, keepdims=True)
        for cut in range(4):
            d_mid[10 + cut, enc : enc + 1, :] += up_bias[:, cut * 128 : (cut + 1) * 128]
        d_ffn[enc, 0] += dot_rows(low_ref[here, :], d_pre)
        d_h = d_x_ffn + dot_last(d_pre, w_up)
        scaled = scaled_a[here, :]
        add(5, d_h * scaled)
        add(6, d_h)
        d_x = norm_back(d_h * row(5), scaled, rate_a[here, :])
        if enc == 0:
            xa_q[...] = d_x
        else:
            xa_p[at : at + chunk, :] = d_x
        d_proj = low16(d_x)
        add(4, d_proj.astype(jnp.float32))
        d_out[enc] += dot_rows(held(mixed_ref, enc, at), d_proj)
        d_mixed = low16(dot_last(d_proj, w_out))
        each = counts[enc]
        low = 0 if enc == 0 else counts[0]
        grad_ref[at // each : (at + chunk) // each, low : low + each, :] = d_mixed.reshape(
            chunk // each, each, 128
        )


def class_stage(sizes, rows, mixed, every, positions, attention, feedforward, vectors):
    many = sizes.many
    n_q, n_p = (many * sizes.count[0], many * sizes.count[1])
    both = n_q + n_p
    f32 = jnp.float32
    return local_call(
        functools.partial(class_kernel, sizes),
        (
            jax.ShapeDtypeStruct((many, sum(sizes.count), 128), jnp.bfloat16),
            jax.ShapeDtypeStruct((n_q, 128), f32),
            jax.ShapeDtypeStruct((n_p, 128), f32),
            jax.ShapeDtypeStruct((2, 128, 128), f32),
            jax.ShapeDtypeStruct((2, 2, 128, 512), f32),
            jax.ShapeDtypeStruct((16, 2, 128), f32),
            jax.ShapeDtypeStruct((1,), f32),
            jax.ShapeDtypeStruct((1,), f32),
        ),
        (rows, mixed, every, positions, attention, feedforward, vectors),
        [
            pltpu.VMEM((both, 128), jnp.bfloat16),
            pltpu.VMEM((both, 128), f32),
            pltpu.VMEM((both, 128), f32),
            pltpu.VMEM((both, 128), f32),
            pltpu.VMEM((both, 128), f32),
            pltpu.VMEM((both, 512), f32),
            pltpu.VMEM((both, 512), jnp.bfloat16),
            pltpu.VMEM((both, 128), jnp.bfloat16),
            pltpu.VMEM((128, 128), f32),
        ],
        "class_stage",
        smem_out=(6, 7),
    )


def class_stage_large(sizes, rows_all, mixed_all, every, positions, attention, feedforward, vectors):
    many = sizes.many
    count_q, count_p = sizes.count
    counts = sizes.count
    width = rows_all.shape[2]
    flags_all = every[:, RAW_FLAGS, :].astype(jnp.int32)
    keys_q = flags_all[:, :count_q].reshape(-1)
    valid_all = flags_all[:, count_q : 2 * count_q].reshape(-1)
    keys_p = flags_all[:, 2 * count_q : 2 * count_q + count_p].reshape(-1)
    cuts = ((0, count_q), (count_q, count_q + count_p))
    cls, class_kept, mixes = ([], [], [])
    for enc in range(2):
        low, high = cuts[enc]
        rows = rows_all[:, low:high].reshape(-1, width)
        mixed = mixed_all[:, low:high].reshape(-1, width)
        low_cls, kept_cls = class_forward(
            rows, mixed, positions[0, enc], attention[0, enc], feedforward[0, enc], vectors[0, :, enc]
        )
        cls.append(low_cls)
        class_kept.append(kept_cls)
        mixes.append(mixed)
    d_q, d_p, loss_total, count = score_stage(cls[0], cls[1], keys_q, keys_p, valid_all)
    d_cls = (d_q, d_p)
    grads, xas, outs, ffns, mids = ([], [], [], [], [])
    for enc in range(2):
        d_mixed, d_x_attn, d_w_out, d_ffn, rows_mid, d_up_bias = class_backward(
            class_kept[enc], mixes[enc], attention[0, enc], feedforward[0, enc], vectors[0, :, enc], d_cls[enc]
        )
        grads.append(d_mixed.reshape(many, counts[enc], width))
        xas.append(d_x_attn)
        outs.append(d_w_out)
        ffns.append(d_ffn)
        mid = jnp.concatenate([jnp.stack(list(rows_mid)), d_up_bias.reshape(-1, width)])
        mids.append(jnp.pad(mid, ((4, 2), (0, 0))))
    return (
        jnp.concatenate(grads, 1),
        xas[0],
        xas[1],
        jnp.stack(outs),
        jnp.stack(ffns),
        jnp.stack(mids, 1),
        loss_total.reshape(1),
        count.reshape(1),
    )


def class_forward(rows, mixed, place, attn_w, ffn_w, vec):
    width = rows.shape[1]
    h_embed = layer_norm(rows.astype(jnp.float32) + place[:1], vec[0], vec[1])
    x_attn = h_embed + (dot(mixed, low16(attn_w[:, 3 * width :])) + vec[4])
    h_attn = layer_norm(x_attn, vec[5], vec[6])
    h_low = low16(h_attn)
    pre = dot(h_low, low16(ffn_w[0])) + vec[10:].reshape(-1)
    act = low16(gelu_tanh(pre))
    x_ffn = h_attn + (dot_last(act, low16(ffn_w[1])) + vec[7])
    h_out = layer_norm(x_ffn, vec[8], vec[9])
    return low16(h_out), (x_attn, h_low, pre, act, x_ffn)


def class_backward(kept, mixed, attn_w, ffn_w, vec, d_cls):
    x_attn, h_low, pre, act, x_ffn = kept
    width = x_attn.shape[1]
    unused, out_back = jax.vjp(layer_norm, x_ffn, vec[8], vec[9])
    d_x_ffn, d_gain_two, d_shift_two = out_back(d_cls)
    d_branch = low16(d_x_ffn)
    d_down_bias = jnp.sum(d_branch, 0, dtype=jnp.float32)
    d_down = dot_rows(d_branch, act)
    d_act = dot(d_branch, low16(ffn_w[1]))
    unused, gelu_back = jax.vjp(gelu_tanh, pre)
    d_pre = low16(gelu_back(d_act)[0])
    d_up_bias = jnp.sum(d_pre, 0, dtype=jnp.float32)
    d_up = dot_rows(h_low, d_pre)
    d_h_attn = d_x_ffn + dot_last(d_pre, low16(ffn_w[0]))
    unused, attn_back = jax.vjp(layer_norm, x_attn, vec[5], vec[6])
    d_x_attn, d_gain_one, d_shift_one = attn_back(d_h_attn)
    d_proj = low16(d_x_attn)
    d_out_bias = jnp.sum(d_proj, 0, dtype=jnp.float32)
    d_w_out = dot_rows(mixed, d_proj)
    d_mixed = low16(dot_last(d_proj, low16(attn_w[:, 3 * width :])))
    rows = (d_out_bias, d_gain_one, d_shift_one, d_down_bias, d_gain_two, d_shift_two)
    return d_mixed, d_x_attn, d_w_out, jnp.stack([d_up, d_down]), rows, d_up_bias


def softmax_terms(scores, drop, target, weight, count, axis):
    masked = jnp.where(drop, MASKED, scores)
    top = jnp.max(masked, axis, keepdims=True)
    expo = jnp.exp(masked - top)
    total = jnp.sum(expo, axis, keepdims=True)
    lse = top + jnp.log(total)
    picked = jnp.sum(jnp.where(target, scores, 0.0), axis, keepdims=True)
    loss = jnp.sum(weight * (lse - picked))
    grad = low16((weight / count) * (expo / total - target.astype(jnp.float32)))
    return grad, loss


def score_stage(every_q, every_p, keys_q, keys_p, valid_q):
    count = jnp.maximum(jnp.sum(valid_q).astype(jnp.float32), 1.0)
    scale = every_q.shape[1] ** (-0.5)
    index_q = jnp.arange(every_q.shape[0])[:, None]
    index_p = jnp.arange(every_p.shape[0])[None, :]
    scores = dot_last(every_q, every_p) * scale
    same = keys_q[:, None] == keys_p[None, :]
    target_qp = index_p == 2 * index_q
    valid = valid_q.astype(jnp.float32)[:, None]
    grad_qp, loss_qp = softmax_terms(scores, same & ~target_qp, target_qp, valid, count, 1)
    target_pq = index_p // 2 == index_q
    drop_pq = (same | (valid_q[:, None] == 0)) & ~target_pq
    owner_valid = jnp.repeat(valid_q, 2)
    weight_p = jnp.where(index_p[0] % 2 == 0, owner_valid, 0).astype(jnp.float32)[None, :]
    grad_pq, loss_pq = softmax_terms(scores, drop_pq, target_pq, weight_p, count, 0)
    d_q = (dot(grad_qp, every_p) + dot(grad_pq, every_p)) * scale
    d_p = (dot_rows(grad_pq, every_q) + dot_rows(grad_qp, every_q)) * scale
    return d_q, d_p, loss_qp + loss_pq, count


def body(
    question_ids,
    passage_ids,
    question_lengths,
    passage_lengths,
    question_keys,
    passage_keys,
    question_valid,
    word_table,
    positions,
    attention,
    feedforward,
    vectors,
    word_first,
    positions_first,
    attention_first,
    feedforward_first,
    vectors_first,
    word_second,
    positions_second,
    attention_second,
    feedforward_second,
    vectors_second,
    word_anchor,
    positions_anchor,
    attention_anchor,
    feedforward_anchor,
    vectors_anchor,
    word_outer,
    positions_outer,
    attention_outer,
    feedforward_outer,
    vectors_outer,
):
    many = lax.axis_size("dp")
    count_q = question_ids.shape[0]
    count_p = passage_ids.shape[0]
    table = word_table[0]
    sizes = Sizes(many, count_q, count_p, table.shape[0])
    swap = lambda values: jnp.swapaxes(values, -3, -2)
    vectors, vectors_first, vectors_second, vectors_anchor, vectors_outer = (
        swap(v) for v in (vectors, vectors_first, vectors_second, vectors_anchor, vectors_outer)
    )
    every, class_rows, kept, entry, counted = first_stage(
        sizes,
        question_ids,
        passage_ids,
        question_lengths,
        passage_lengths,
        question_keys,
        question_valid,
        passage_keys,
        table,
        positions,
    )
    part, lse_part, query, levels = tokens_forward(
        sizes, every, class_rows, kept, entry, counted, table, positions, attention, vectors
    )
    mixed_all, lse_all = exchange_mixed(sizes, part, lse_part)
    stage = class_stage if many * count_q <= 512 else class_stage_large
    grad_all, xa_q, xa_p, d_out, d_ffn, d_mid, loss_total, count = stage(
        sizes, class_rows, mixed_all, every, positions, attention, feedforward, vectors
    )
    d_query, d_table, slices = tokens_backward(
        sizes, levels, every, query, mixed_all, lse_all, grad_all, kept, entry, table, positions, attention, vectors
    )
    weights = (word_table, positions, attention, feedforward, vectors)
    firsts = (word_first, positions_first, attention_first, feedforward_first, vectors_first)
    seconds = (word_second, positions_second, attention_second, feedforward_second, vectors_second)
    anchors = (word_anchor, positions_anchor, attention_anchor, feedforward_anchor, vectors_anchor)
    outers = (word_outer, positions_outer, attention_outer, feedforward_outer, vectors_outer)
    done = finish(
        sizes,
        d_query,
        slices.reshape(many, sizes.lines, 128),
        d_table,
        class_rows,
        every,
        xa_q,
        xa_p,
        d_out,
        d_ffn,
        d_mid,
        (positions, attention, vectors),
        (weights, firsts, seconds, anchors),
    )
    norm = done[0]
    grads = (done[1], done[2], done[3], d_ffn, done[4])
    made, norm = make_outputs(
        norm, grads, firsts, seconds, anchors, outers, done[5:10], lax.axis_size("grp")
    )
    first_new, second_new, averages, outer_next, weight_next = (
        part[:4] + [swap(part[4])] for part in made
    )
    return (
        loss_total.reshape(1),
        count.reshape(1),
        norm.reshape(1),
        first_new[0],
        first_new[1],
        first_new[2],
        first_new[3],
        first_new[4],
        second_new[0],
        second_new[1],
        second_new[2],
        second_new[3],
        second_new[4],
        averages[0],
        averages[1],
        averages[2],
        averages[3],
        averages[4],
        outer_next[0],
        outer_next[1],
        outer_next[2],
        outer_next[3],
        outer_next[4],
        weight_next[0],
        weight_next[1],
        weight_next[2],
        weight_next[3],
        weight_next[4],
    )


def solution(mesh):
    placed = (
        P(("grp", "dp"), None),
        P(("grp", "dp"), None),
        P(("grp", "dp")),
        P(("grp", "dp")),
        P(("grp", "dp")),
        P(("grp", "dp")),
        P(("grp", "dp")),
        P("grp", "dp", None),
        P("grp", None, None, None),
        P("grp", None, None, None),
        P("grp", None, None, None, None),
        P("grp", None, None, None),
        P("grp", "dp", None),
        P("grp", None, None, None),
        P("grp", None, None, None),
        P("grp", None, None, None, None),
        P("grp", None, None, None),
        P("grp", "dp", None),
        P("grp", None, None, None),
        P("grp", None, None, None),
        P("grp", None, None, None, None),
        P("grp", None, None, None),
        P("dp", None),
        P(),
        P(),
        P(),
        P(),
        P("dp", None),
        P(),
        P(),
        P(),
        P(),
    )
    return jax.shard_map(
        body,
        mesh=mesh,
        in_specs=placed,
        out_specs=(
            P("grp"),
            P("grp"),
            P("grp"),
            P("grp", "dp", None),
            P("grp", None, None, None),
            P("grp", None, None, None),
            P("grp", None, None, None, None),
            P("grp", None, None, None),
            P("grp", "dp", None),
            P("grp", None, None, None),
            P("grp", None, None, None),
            P("grp", None, None, None, None),
            P("grp", None, None, None),
            P("dp", None),
            P(),
            P(),
            P(),
            P(),
            P("dp", None),
            P(),
            P(),
            P(),
            P(),
            P("grp", "dp", None),
            P("grp", None, None, None),
            P("grp", None, None, None),
            P("grp", None, None, None, None),
            P("grp", None, None, None),
        ),
        check_vma=False,
    )
```
